32 devices in a mesh: seq: 32 (over z, y, x, core).
Axes of the slice: x: 2, y: 2, z: 4, core: 2. Of those that a mesh axis runs over, the one named last changes fastest.
Arguments:
- lengths: int32 [3], replicated, may hold values from 120 to 15888, as said below
- tokens: bfloat16 [16384, 512], P('seq'), may hold values from -6 to 6
- ln1_gain: bfloat16 [512], P('seq'), may hold values from 0.5 to 1.5
- ln1_bias: bfloat16 [512], P('seq'), may hold values from -1.5 to 1.5
- w_qkv: bfloat16 [512, 1536], P('seq'), may hold values from -0.25 to 0.25
- w_out: bfloat16 [512, 512], P('seq'), may hold values from -0.75 to 0.75
- out_bias: bfloat16 [512], P('seq'), may hold values from -1.5 to 1.5
- ln2_gain: bfloat16 [512], P('seq'), may hold values from 0.5 to 1.5
- ln2_bias: bfloat16 [512], P('seq'), may hold values from -1.5 to 1.5
- w_in: bfloat16 [512, 2048], P('seq'), may hold values from -0.25 to 0.25
- in_bias: bfloat16 [2048], P('seq'), may hold values from -2.5 to 2.5
- w_back: bfloat16 [2048, 512], P('seq'), may hold values from -0.125 to 0.125
- back_bias: bfloat16 [512], P('seq'), may hold values from -1.5 to 1.5
- cotangent: bfloat16 [16384, 512], P('seq'), may hold values from -6 to 6
Outputs:
- result: bfloat16 [16384, 512], P('seq')
- grad_tokens: float32 [16384, 512], P('seq')
- grad_ln1_gain: float32 [512], P('seq')
- grad_ln1_bias: float32 [512], P('seq')
- grad_w_qkv: float32 [512, 1536], P('seq')
- grad_w_out: float32 [512, 512], P('seq')
- grad_out_bias: float32 [512], P('seq')
- grad_ln2_gain: float32 [512], P('seq')
- grad_ln2_bias: float32 [512], P('seq')
- grad_w_in: float32 [512, 2048], P('seq')
- grad_in_bias: float32 [2048], P('seq')
- grad_w_back: float32 [2048, 512], P('seq')
- grad_back_bias: float32 [512], P('seq')
The draws below stay inside these ranges and needn't reach their ends.
Inputs may be any that keep to these rules, and one draw needn't show every extreme that they name: `lengths`: one sequence, at a position drawn from the seed, has exactly 15888 tokens; the two others have 120 to 240 each.
All inputs are finite; a program needn't handle non-finite values.
Results may differ from the reference program's by a relative error of at most 0.011.
Values may be sent and summed in bfloat16 or wider, within the bound.
No kernel may reach another device: no remote copies, remote signals or barrier semaphores. Data moves between devices by JAX's collectives and lax.ppermute only.
A program may use at most 192 MiB of HBM per device.

```python
import math
import jax
import jax.numpy as jnp
from jax import lax

D = 512
HEADS = 8
HEAD_DIM = 64
FF = 2048
LEVELS = 5
TOKENS = 16384
LONG_LEN = 15888
SHORT_MOST = 240
MIN_LEN = 120


def draw_lengths(key, part):
    key = jax.random.fold_in(key, 17)
    pieces = jax.random.split(key, 2)
    shorts = jax.random.randint(pieces[0], (2,), MIN_LEN, SHORT_MOST + 1)
    chosen = jax.random.randint(pieces[1], (), 0, 3)
    places = jnp.arange(3, dtype=jnp.int32)
    short_index = jnp.clip(places - (places > chosen).astype(jnp.int32), 0, 1)
    return jnp.where(places == chosen, LONG_LEN, shorts[short_index]).astype(jnp.int32)


def shard_levels(key, dims, cuts, least, largest):
    factor_of = 1.0
    for position, shards_of in cuts:
        heights = jax.random.uniform(jax.random.fold_in(jax.random.fold_in(key, 6), position), (shards_of,), jnp.float32, least / len(cuts), largest / len(cuts))
        factor_of = factor_of * jnp.repeat(jnp.exp(heights), dims[position] // shards_of).reshape((-1,) + (1,) * (len(dims) - 1 - position))
    return factor_of


def gaussian(rng, dims, scale, limit, cuts=(), held_as=jnp.bfloat16):
    loudness = shard_levels(rng, dims, cuts, -0.22, 0.18) if cuts else 1.0
    drawn = jax.random.normal(rng, dims, jnp.float32) * scale * loudness
    return jnp.minimum(jnp.maximum(drawn, -limit), limit).astype(held_as)


def setup_inputs(seed: int = 0) -> dict:
    key_list = jax.random.split(jax.random.key(seed), 15)
    lengths = draw_lengths(jax.random.fold_in(key_list[14], 71), 0)
    tokens = gaussian(key_list[1], (TOKENS, D), 1.0, 6.0, ((0, 32),))
    ln1_gain = jnp.clip(1.0 + 0.1 * jax.random.normal(key_list[2], (D,), jnp.float32), 0.5, 1.5).astype(jnp.bfloat16)
    ln1_bias = gaussian(key_list[3], (D,), 0.3, 1.5, ((0, 32),))
    w_qkv = gaussian(key_list[4], (D, 3 * D), D ** -0.5, 0.25, ((0, 32),))
    w_out = gaussian(key_list[5], (D, D), (D // 8) ** -0.5, 0.75, ((0, 32),))
    out_bias = gaussian(key_list[6], (D,), 0.3, 1.5, ((0, 32),))
    ln2_gain = jnp.clip(1.0 + 0.1 * jax.random.normal(key_list[7], (D,), jnp.float32), 0.5, 1.5).astype(jnp.bfloat16)
    ln2_bias = gaussian(key_list[8], (D,), 0.3, 1.5, ((0, 32),))
    w_in = gaussian(key_list[9], (D, FF), D ** -0.5, 0.25, ((0, 32),))
    in_bias = gaussian(key_list[10], (FF,), 0.5, 2.5, ((0, 32),))
    w_back = gaussian(key_list[11], (FF, D), FF ** -0.5, 0.125, ((0, 32),))
    back_bias = gaussian(key_list[12], (D,), 0.3, 1.5, ((0, 32),))
    cotangent = gaussian(key_list[13], (TOKENS, D), 1.0, 6.0, ((0, 32),))
    return {"lengths": lengths, "tokens": tokens, "ln1_gain": ln1_gain, "ln1_bias": ln1_bias, "w_qkv": w_qkv, "w_out": w_out, "out_bias": out_bias, "ln2_gain": ln2_gain, "ln2_bias": ln2_bias, "w_in": w_in, "in_bias": in_bias, "w_back": w_back, "back_bias": back_bias, "cotangent": cotangent}


@jax.custom_vjp
def low(v):
    return lax.optimization_barrier(v.astype(jnp.bfloat16)).astype(jnp.float32)

@jax.custom_vjp
def low_back(v):
    return v

def low_keep(v):
    return (low(v), None)

def low_pass(kept, grad):
    return (grad,)

def back_keep(v):
    return (v, None)

def back_low(kept, grad):
    return (low(grad),)
low.defvjp(low_keep, low_pass)
low_back.defvjp(back_keep, back_low)
exactness = lax.Precision.HIGHEST

def layer_norm(values, gain, shift):
    center = values - lax.optimization_barrier(jnp.mean(values, axis=-1, keepdims=True))
    spread = lax.optimization_barrier(jnp.mean(center * center, axis=-1, keepdims=True))
    return center * lax.rsqrt(spread + 1e-05) * gain + shift

def gelu_exact(values):
    return jax.nn.gelu(values, approximate=False)

def slot_info(lengths, places, total):
    number_seqs = lengths.shape[0]
    padded = (lengths + 15) // 16 * 16
    ends = jnp.cumsum(padded, dtype=jnp.int32)
    number = lax.optimization_barrier(jnp.sum((places[:, None] >= ends[None, :]).astype(jnp.int32), axis=1, dtype=jnp.int32))
    picked = (jnp.arange(number_seqs, dtype=jnp.int32)[None, :] == number[:, None]).astype(jnp.int32)
    begin = lax.optimization_barrier(jnp.sum(picked * (ends - padded)[None, :], axis=1, dtype=jnp.int32))
    length = lax.optimization_barrier(jnp.sum(picked * lengths[None, :], axis=1, dtype=jnp.int32))
    inside = (places >= 0) & (places < total) & (number < number_seqs)
    return (jnp.where(inside, number, -1), places - begin, jnp.where(inside, length, 0))

def level_info(lengths, first, count, level, total):
    span = 2 ** level
    coarse = first + jnp.arange(count, dtype=jnp.int32)
    seqid, offset, length = slot_info(lengths, coarse * span, total)
    weight = jnp.where(seqid >= 0, jnp.clip(length - offset, 0, span), 0).astype(jnp.float32)
    return (seqid, offset // span, weight)

def windows(extended, count):
    tiles = extended.reshape((count + 4, 16) + extended.shape[1:])
    return jnp.concatenate([tiles[shift:shift + count] for shift in range(5)], axis=1)

def admit(seq_query, pos_query, seq_key, pos_key, level):
    same = (seq_query[:, :, None] == seq_key[:, None, :]) & (seq_query[:, :, None] >= 0)
    near = jnp.abs(pos_query[:, :, None] // 16 - pos_key[:, None, :] // 16) <= 1
    if level > 0:
        near = near & (jnp.abs(pos_query[:, :, None] // 8 - pos_key[:, None, :] // 8) >= 2)
    return same & near

def halves(values):
    pairs = values.reshape(values.shape[0] // 2, 2, values.shape[1])
    return (pairs[:, 0] + pairs[:, 1]) * 0.5

def pair_sums(values):
    pairs = values.reshape(values.shape[0] // 2, 2, values.shape[1])
    return pairs[:, 0] + pairs[:, 1]

def level_block(query, keys, values, counts, seq_query, pos_query, seq_key, pos_key, level):
    count = query.shape[0] // 16
    heads = query.shape[1] // HEAD_DIM
    q_tiles = query.reshape(count, 16, heads, HEAD_DIM)
    k_tiles = windows(keys, count).reshape(count, 80, heads, HEAD_DIM)
    v_tiles = windows(values, count).reshape(count, 80, heads, HEAD_DIM)
    c_tiles = windows(counts, count)
    allowed = admit(seq_query.reshape(count, 16), pos_query.reshape(count, 16), windows(seq_key, count), windows(pos_key, count), level)[:, None]
    score = low_back(jnp.einsum('tqhd,tkhd->thqk', q_tiles, k_tiles, precision=exactness) / math.sqrt(HEAD_DIM))
    weight = jnp.where(allowed, jnp.exp(jnp.where(allowed, score, 0.0)), 0.0)
    probs = low(weight)
    numer = low_back(jnp.einsum('thqk,tkhd->tqhd', probs, v_tiles, precision=exactness))
    denom = jnp.einsum('thqk,tk->tqh', probs, c_tiles, precision=exactness)
    return (numer.reshape(count * 16, heads * HEAD_DIM), denom.reshape(count * 16, heads))

def level_whole(query, keys, values, counts, seq_query, pos_query, seq_key, pos_key, level):
    total_rows = query.shape[0]
    group = min(512, total_rows)

    def one_group(index):
        start = index * group
        return level_block(lax.dynamic_slice_in_dim(query, start, group, 0), lax.dynamic_slice_in_dim(keys, start, group + 64, 0), lax.dynamic_slice_in_dim(values, start, group + 64, 0), lax.dynamic_slice_in_dim(counts, start, group + 64, 0), lax.dynamic_slice_in_dim(seq_query, start, group, 0), lax.dynamic_slice_in_dim(pos_query, start, group, 0), lax.dynamic_slice_in_dim(seq_key, start, group + 64, 0), lax.dynamic_slice_in_dim(pos_key, start, group + 64, 0), level)
    numer, denom = lax.map(jax.checkpoint(one_group), jnp.arange(total_rows // group, dtype=jnp.int32))
    return (numer.reshape(total_rows, numer.shape[-1]), denom.reshape(total_rows, denom.shape[-1]))

def forward(lengths, tokens, ln1_gain, ln1_bias, w_qkv, w_out, out_bias, ln2_gain, ln2_bias, w_in, in_bias, w_back, back_bias):
    total = tokens.shape[0]
    normed = low(layer_norm(tokens, ln1_gain, ln1_bias))
    joined = low(low_back(jnp.dot(normed, w_qkv, precision=exactness)))
    query = joined[:, :D]
    keys = joined[:, D:2 * D]
    values = joined[:, 2 * D:]
    seq_all, pos_all, live = level_info(lengths, 0, total, 0, total)
    level_query = query
    level_keys = keys
    level_values = values * live[:, None]
    numer_sum = jnp.zeros((total, D), jnp.float32)
    denom_sum = jnp.zeros((total, HEADS), jnp.float32)
    border = ((32, 32), (0, 0))
    for level in range(LEVELS):
        if level > 0:
            level_query = halves(level_query)
            level_keys = halves(level_keys)
            level_values = pair_sums(level_values)
            used_query, used_keys, used_values = (low(level_query), low(level_keys), low(level_values))
        else:
            used_query, used_keys, used_values = (level_query, level_keys, level_values)
        level_rows = total // 2 ** level
        seq_query, pos_query, query_counts = level_info(lengths, 0, level_rows, level, total)
        seq_key, pos_key, key_counts = level_info(lengths, -32, level_rows + 64, level, total)
        numer, denom = level_whole(used_query, jnp.pad(used_keys, border), jnp.pad(used_values, border), key_counts, seq_query, pos_query, seq_key, pos_key, level)
        numer_sum = numer_sum + jnp.repeat(numer, 2 ** level, axis=0)
        denom_sum = denom_sum + jnp.repeat(denom, 2 ** level, axis=0)
    live_rows = live[:, None]
    scale = live_rows / (denom_sum + 1.0 - live_rows)
    mixed = (numer_sum.reshape(total, HEADS, HEAD_DIM) * scale[:, :, None]).reshape(total, D)
    attended = low(mixed)
    branch = low_back(jnp.dot(attended, w_out, precision=exactness) + out_bias)
    resid = tokens + branch
    normed_two = low(layer_norm(resid, ln2_gain, ln2_bias))
    inner = low_back(jnp.dot(normed_two, w_in, precision=exactness) + in_bias)
    active = low(gelu_exact(inner))
    outer = low_back(jnp.dot(active, w_back, precision=exactness) + back_bias)
    return resid + outer

def reference(lengths, tokens, ln1_gain, ln1_bias, w_qkv, w_out, out_bias, ln2_gain, ln2_bias, w_in, in_bias, w_back, back_bias, cotangent):
    floats = [item.astype(jnp.float32) for item in (tokens, ln1_gain, ln1_bias, w_qkv, w_out, out_bias, ln2_gain, ln2_bias, w_in, in_bias, w_back, back_bias)]

    def apply(*params):
        return forward(lengths, *params)
    output, pull = jax.vjp(apply, *floats)
    grads = pull(cotangent.astype(jnp.float32))
    return (output.astype(jnp.bfloat16), grads[0], grads[1], grads[2], grads[3], grads[4], grads[5], grads[6], grads[7], grads[8], grads[9], grads[10], grads[11])
```

```python
import functools
import math

import jax
import jax.numpy as jnp
import numpy as np
from jax import lax
from jax.experimental import pallas as pl
from jax.experimental.pallas import tpu as pltpu
from jax.sharding import PartitionSpec as P

HEAD_DIM = 64
LEVELS = 5
HALO = 32
BLOCK = 64
WINDOW = BLOCK + 2 * HALO
QUAD = 4
QUAD_WIDTH = QUAD * HEAD_DIM
FAR = 1 << 26
SEQ_STEP = 1 << 21
VMEM_LIMIT = 56 * 1024 * 1024

f32 = jnp.float32
bf16 = jnp.bfloat16


class Plan:
    def __init__(self, rows):
        self.rows = rows
        self.counts = [rows >> level for level in range(LEVELS)]
        self.padded = [-(-count // BLOCK) * BLOCK for count in self.counts]
        self.query_at = [sum(self.padded[:level]) for level in range(LEVELS)]
        self.query_rows = sum(self.padded)
        self.key_at = [self.query_at[level] + 2 * HALO * level for level in range(LEVELS)]
        self.key_rows = self.query_rows + 2 * HALO * LEVELS
        self.blocks = [
            (level, part)
            for level in range(LEVELS)
            for part in range(self.padded[level] // BLOCK)
        ]


def dot_nn(a, b):
    return lax.dot_general(a, b, (((1,), (0,)), ((), ())), preferred_element_type=f32)


def dot_nt(a, b):
    return lax.dot_general(a, b, (((1,), (1,)), ((), ())), preferred_element_type=f32)


def dot_tn(a, b):
    return lax.dot_general(a, b, (((0,), (0,)), ((), ())), preferred_element_type=f32)


def spec(count):
    return [pl.BlockSpec(memory_space=pltpu.VMEM)] * count


SCALARS = pl.BlockSpec(memory_space=pltpu.SMEM)


def slot_facts(info, slot, total):
    number = jnp.zeros(slot.shape, jnp.int32)
    for s in range(3):
        number = number + (slot >= info[7 + s]).astype(jnp.int32)
    begin = jnp.where(number == 0, info[4], jnp.where(number == 1, info[5], info[6]))
    length = jnp.where(number == 0, info[1], jnp.where(number == 1, info[2], info[3]))
    inside = (slot >= 0) & (slot < total) & (number < 3)
    return number, slot - begin, length, inside


def tile_codes(info, coarse, level, total, outside):
    number, offset, _, inside = slot_facts(info, coarse << level, total)
    wide = jnp.where(inside, number * SEQ_STEP + (offset >> (level + 4)), outside)
    fine = number * SEQ_STEP + (offset >> (level + 3))
    return wide, fine


def admitted(query_codes, key_codes, level):
    near = jnp.abs(query_codes[0] - key_codes[0]) <= 1
    if level > 0:
        near = near & (jnp.abs(query_codes[1] - key_codes[1]) >= 2)
    return jnp.where(near, 1.0, 0.0)


def live_counts(info, coarse, level, total):
    _, offset, length, inside = slot_facts(info, coarse << level, total)
    span = 1 << level
    return jnp.where(inside, jnp.clip(length - offset, 0, span), 0).astype(f32)


def head_masks(rows):
    lane = lax.broadcasted_iota(jnp.int32, (rows, QUAD_WIDTH), 1) // HEAD_DIM
    return [jnp.where(lane == h, 1.0, 0.0) for h in range(QUAD)]


def spread_heads(block, masks):
    return jnp.concatenate([block * m for m in masks], axis=0)


def gather_heads(stacked, masks):
    rows = stacked.shape[0] // QUAD
    total = stacked[:rows] * masks[0]
    for h in range(1, QUAD):
        total = total + stacked[h * rows : (h + 1) * rows] * masks[h]
    return total


def put(chunks, rows, quad, block):
    for part in range(QUAD_WIDTH // 128):
        chunk = quad * (QUAD_WIDTH // 128) + part
        chunks[chunk, rows, :] = block[:, part * 128 : part * 128 + 128]


def take(chunks, rows, quad):
    first = quad * (QUAD_WIDTH // 128)
    return jnp.concatenate(
        [chunks[first + part, rows, :] for part in range(QUAD_WIDTH // 128)], axis=1
    )


def fill_extended(plan, own, before, after, extended):
    for level in range(LEVELS):
        at, count, mine = plan.key_at[level], plan.counts[level], plan.query_at[level]
        halo = pl.ds(HALO * level, HALO)
        extended[pl.ds(at, HALO), :] = before[halo, :]
        extended[pl.ds(at + HALO, count), :] = own[pl.ds(mine, count), :]
        extended[pl.ds(at + HALO + count, HALO), :] = after[halo, :]
        rest = plan.padded[level] - count
        if rest:
            extended[pl.ds(at + 2 * HALO + count, rest), :] = jnp.zeros(
                (rest, extended.shape[1]), bf16
            )


def project_kernel(plan, total, info, tokens, gain, bias, weight, normed, query, pairs, head, tail):
    rows, width = tokens.shape
    device = info[0]
    values = tokens[...].astype(f32)
    center = values - jnp.mean(values, axis=-1, keepdims=True)
    spread = jnp.mean(center * center, axis=-1, keepdims=True)
    low = (center * lax.rsqrt(spread + 1e-05) * gain[...] + bias[...]).astype(bf16)
    normed[...] = low
    pooled_rows = plan.query_rows - plan.query_at[1]
    row = lax.broadcasted_iota(jnp.int32, (pooled_rows, rows), 0)
    slot = lax.broadcasted_iota(jnp.int32, (pooled_rows, rows), 1)
    first = jnp.zeros((pooled_rows, rows), jnp.int32)
    shift = jnp.zeros((pooled_rows, rows), jnp.int32)
    share = jnp.zeros((pooled_rows, 1), f32)
    row_one = lax.broadcasted_iota(jnp.int32, (pooled_rows, 1), 0)
    for level in range(1, LEVELS):
        at = plan.query_at[level] - plan.query_at[1]
        first = jnp.where(row >= at, at, first)
        shift = jnp.where(row >= at, level, shift)
        share = jnp.where(row_one >= at, 0.5**level, share)
    pool = jnp.where((slot >> shift) == row - first, 1.0, 0.0).astype(bf16)
    places = device * rows + lax.broadcasted_iota(jnp.int32, (rows, QUAD_WIDTH), 0)
    live = live_counts(info, places, 0, total)
    lanes = QUAD_WIDTH
    for part in range(3 * width // lanes):
        columns = pl.ds(part * lanes, lanes)
        block = dot_nn(low, weight[:, columns]).astype(bf16)
        if part * lanes >= 2 * width:
            block = (block.astype(f32) * live).astype(bf16)
        pooled = dot_nn(pool, block)
        if part * lanes < 2 * width:
            pooled = pooled * share
        if part * lanes < width:
            scale = 1.0 / math.sqrt(HEAD_DIM)
            query[pl.ds(0, rows), columns] = (block.astype(f32) * scale).astype(bf16)
            query[pl.ds(rows, pooled_rows), columns] = (pooled * scale).astype(bf16)
        else:
            there = pl.ds(part * lanes - width, lanes)
            pairs[pl.ds(0, rows), there] = block
            pairs[pl.ds(rows, pooled_rows), there] = pooled.astype(bf16)
    for level in range(LEVELS):
        at, count = plan.query_at[level], plan.counts[level]
        halo = pl.ds(HALO * level, HALO)
        head[halo, :] = pairs[pl.ds(at, HALO), :]
        tail[halo, :] = pairs[pl.ds(at + count - HALO, HALO), :]


def project(plan, total, info, tokens, gain, bias, weight):
    rows, width = tokens.shape
    halo = LEVELS * HALO
    return pl.pallas_call(
        functools.partial(project_kernel, plan, total),
        out_shape=(
            jax.ShapeDtypeStruct((rows, width), bf16),
            jax.ShapeDtypeStruct((plan.query_rows, width), bf16),
            jax.ShapeDtypeStruct((plan.query_rows, 2 * width), bf16),
            jax.ShapeDtypeStruct((halo, 2 * width), bf16),
            jax.ShapeDtypeStruct((halo, 2 * width), bf16),
        ),
        in_specs=[SCALARS] + spec(4),
        out_specs=tuple(spec(5)),
        compiler_params=pltpu.CompilerParams(vmem_limit_bytes=VMEM_LIMIT),
        name="project",
    )(info, tokens, gain, bias, weight)


def attend_kernel(
    plan, total, info, query, pairs, before, after, attended, mixed, scale, extended, numer, denom
):
    rows = plan.rows
    width = query.shape[1]
    device = info[0]
    fill_extended(plan, pairs, before, after, extended)
    masks = head_masks(BLOCK)
    low_masks = [m.astype(bf16) for m in masks]
    for level, part in plan.blocks:
        count = plan.counts[level]
        at = plan.query_at[level] + BLOCK * part
        window = plan.key_at[level] + BLOCK * part
        first = device * count + BLOCK * part
        row = first + lax.broadcasted_iota(jnp.int32, (BLOCK, WINDOW), 0)
        column = first - HALO + lax.broadcasted_iota(jnp.int32, (BLOCK, WINDOW), 1)
        allowed = admitted(
            tile_codes(info, row, level, total, FAR),
            tile_codes(info, column, level, total, -FAR),
            level,
        )
        allowed = jnp.concatenate([allowed] * QUAD, axis=0) > 0.0
        key_row = first - HALO + lax.broadcasted_iota(jnp.int32, (WINDOW, 128), 0)
        counts = live_counts(info, key_row, level, total).astype(bf16)
        counts = jnp.concatenate([counts] * (QUAD_WIDTH // 128), axis=1)
        for quad in range(width // QUAD_WIDTH):
            columns = pl.ds(quad * QUAD_WIDTH, QUAD_WIDTH)
            value_columns = pl.ds(width + quad * QUAD_WIDTH, QUAD_WIDTH)
            q = spread_heads(query[pl.ds(at, BLOCK), columns], low_masks)
            k = extended[pl.ds(window, WINDOW), columns]
            v = extended[pl.ds(window, WINDOW), value_columns]
            weight = jnp.where(allowed, jnp.exp(dot_nt(q, k)), 0.0).astype(bf16)
            put(numer, pl.ds(at, BLOCK), quad, gather_heads(dot_nn(weight, v), masks))
            put(denom, pl.ds(at, BLOCK), quad, gather_heads(dot_nn(weight, counts), masks))
    for sums in (numer, denom):
        for level in range(LEVELS - 1, 0, -1):
            count = plan.counts[level]
            for chunk in range(width // 128):
                upper = sums[chunk, pl.ds(plan.query_at[level], count), :]
                for parity in range(2):
                    there = pl.ds(plan.query_at[level - 1] + parity, count, stride=2)
                    sums[chunk, there, :] = sums[chunk, there, :] + upper
    places = device * rows + lax.broadcasted_iota(jnp.int32, (rows, 128), 0)
    live = live_counts(info, places, 0, total)
    for chunk in range(width // 128):
        lanes = pl.ds(chunk * 128, 128)
        factor = live / (denom[chunk, pl.ds(0, rows), :] + 1.0 - live)
        value = numer[chunk, pl.ds(0, rows), :] * factor
        scale[:, lanes] = factor
        mixed[:, lanes] = value
        attended[:, lanes] = value.astype(bf16)


def attend(plan, total, info, query, pairs, before, after):
    rows, width = plan.rows, query.shape[1]
    return pl.pallas_call(
        functools.partial(attend_kernel, plan, total),
        out_shape=(
            jax.ShapeDtypeStruct((rows, width), bf16),
            jax.ShapeDtypeStruct((rows, width), f32),
            jax.ShapeDtypeStruct((rows, width), f32),
        ),
        in_specs=[SCALARS] + spec(4),
        out_specs=tuple(spec(3)),
        scratch_shapes=[
            pltpu.VMEM((plan.key_rows, 2 * width), bf16),
            pltpu.VMEM((width // 128, plan.query_rows, 128), f32),
            pltpu.VMEM((width // 128, plan.query_rows, 128), f32),
        ],
        compiler_params=pltpu.CompilerParams(vmem_limit_bytes=VMEM_LIMIT),
        name="attend",
    )(info, query, pairs, before, after)


def attend_back_kernel(
    plan,
    total,
    info,
    query,
    pairs,
    before,
    after,
    grad_mixed,
    scale,
    mixed,
    grad_query,
    grad_pairs,
    grad_head,
    grad_tail,
    extended,
    grad_extended,
    grad_numer,
    grad_denom,
):
    rows = plan.rows
    width = query.shape[1]
    device = info[0]
    fill_extended(plan, pairs, before, after, extended)
    grad_extended[...] = jnp.zeros(grad_extended.shape, f32)
    own = pl.ds(0, rows)
    for chunk in range(width // 128):
        lanes = pl.ds(chunk * 128, 128)
        value = grad_mixed[:, lanes] * scale[:, lanes]
        grad_numer[chunk, own, :] = value
        grad_denom[chunk, own, :] = -(value * mixed[:, lanes])
        for sums in (grad_numer, grad_denom):
            for level in range(1, LEVELS):
                count, at = plan.counts[level], plan.query_at[level]
                even = sums[chunk, pl.ds(plan.query_at[level - 1], count, stride=2), :]
                odd = sums[chunk, pl.ds(plan.query_at[level - 1] + 1, count, stride=2), :]
                sums[chunk, pl.ds(at, count), :] = even + odd
                rest = plan.padded[level] - count
                if rest:
                    sums[chunk, pl.ds(at + count, rest), :] = jnp.zeros((rest, 128), f32)
    masks = head_masks(BLOCK)
    low_masks = [m.astype(bf16) for m in masks]
    for level, part in plan.blocks:
        count = plan.counts[level]
        at = plan.query_at[level] + BLOCK * part
        window = plan.key_at[level] + BLOCK * part
        first = device * count + BLOCK * part
        key_row = first - HALO + lax.broadcasted_iota(jnp.int32, (WINDOW, 128), 0)
        lane = lax.broadcasted_iota(jnp.int32, (WINDOW, 128), 1)
        row = first + (lane & (BLOCK - 1))
        allowed = admitted(
            tile_codes(info, row, level, total, FAR),
            tile_codes(info, key_row, level, total, -FAR),
            level,
        )
        allowed = jnp.concatenate([allowed] * (QUAD * BLOCK // 128), axis=1) > 0.0
        counts = live_counts(info, key_row, level, total).astype(bf16)
        for quad in range(width // QUAD_WIDTH):
            columns = pl.ds(quad * QUAD_WIDTH, QUAD_WIDTH)
            value_columns = pl.ds(width + quad * QUAD_WIDTH, QUAD_WIDTH)
            here = pl.ds(at, BLOCK)
            there = pl.ds(window, WINDOW)
            q = spread_heads(query[here, columns], low_masks)
            g = spread_heads(take(grad_numer, here, quad).astype(bf16), low_masks)
            d = spread_heads(take(grad_denom, here, quad).astype(bf16), low_masks)
            k = extended[there, columns]
            v = extended[there, value_columns]
            value_and_count = jnp.concatenate([v] + [counts] * (QUAD_WIDTH // 128), axis=1)
            weight = jnp.where(allowed, jnp.exp(dot_nt(k, q)), 0.0)
            probs = weight.astype(bf16)
            grad_probs = dot_nt(value_and_count, jnp.concatenate([g, d], axis=1))
            grad_score = (grad_probs * weight).astype(bf16)
            grad_query[here, columns] = gather_heads(dot_tn(grad_score, k), masks) * (
                1.0 / math.sqrt(HEAD_DIM)
            )
            grad_extended[there, columns] += dot_nn(grad_score, q)
            grad_extended[there, value_columns] += dot_nn(probs, g)
    for level in range(LEVELS):
        at, count, mine = plan.key_at[level], plan.counts[level], plan.query_at[level]
        halo = pl.ds(HALO * level, HALO)
        grad_head[halo, :] = grad_extended[pl.ds(at, HALO), :].astype(bf16)
        grad_tail[halo, :] = grad_extended[pl.ds(at + HALO + count, HALO), :].astype(bf16)
        grad_pairs[pl.ds(mine, count), :] = grad_extended[pl.ds(at + HALO, count), :]


def attend_back(plan, total, info, query, pairs, before, after, grad_mixed, scale, mixed):
    width = query.shape[1]
    halo = LEVELS * HALO
    return pl.pallas_call(
        functools.partial(attend_back_kernel, plan, total),
        out_shape=(
            jax.ShapeDtypeStruct((plan.query_rows, width), f32),
            jax.ShapeDtypeStruct((plan.query_rows, 2 * width), f32),
            jax.ShapeDtypeStruct((halo, 2 * width), bf16),
            jax.ShapeDtypeStruct((halo, 2 * width), bf16),
        ),
        in_specs=[SCALARS] + spec(7),
        out_specs=tuple(spec(4)),
        scratch_shapes=[
            pltpu.VMEM((plan.key_rows, 2 * width), bf16),
            pltpu.VMEM((plan.key_rows, 2 * width), f32),
            pltpu.VMEM((width // 128, plan.query_rows, 128), f32),
            pltpu.VMEM((width // 128, plan.query_rows, 128), f32),
        ],
        compiler_params=pltpu.CompilerParams(vmem_limit_bytes=VMEM_LIMIT),
        name="attend_back",
    )(info, query, pairs, before, after, grad_mixed, scale, mixed)


def combine_kernel(plan, total, info, grad_query, grad_pairs, from_below, from_above, joined, work):
    rows = plan.rows
    width = grad_query.shape[1]
    device = info[0]
    places = device * rows + lax.broadcasted_iota(jnp.int32, (rows, 128), 0)
    live = live_counts(info, places, 0, total)
    for chunk in range(3 * width // 128):
        if chunk * 128 < width:
            work[chunk] = grad_query[:, pl.ds(chunk * 128, 128)]
        else:
            lanes = pl.ds(chunk * 128 - width, 128)
            work[chunk] = grad_pairs[:, lanes]
            for level in range(LEVELS):
                at, count = plan.query_at[level], plan.counts[level]
                halo = pl.ds(HALO * level, HALO)
                work[chunk, pl.ds(at, HALO), :] += from_below[halo, lanes].astype(f32)
                last = pl.ds(at + count - HALO, HALO)
                work[chunk, last, :] += from_above[halo, lanes].astype(f32)
        for level in range(LEVELS - 1, 0, -1):
            count = plan.counts[level]
            upper = work[chunk, pl.ds(plan.query_at[level], count), :]
            if chunk * 128 < 2 * width:
                upper = upper * 0.5
            for parity in range(2):
                there = pl.ds(plan.query_at[level - 1] + parity, count, stride=2)
                work[chunk, there, :] = work[chunk, there, :] + upper
        value = work[chunk, pl.ds(0, rows), :]
        if chunk * 128 >= 2 * width:
            value = value * live
        joined[:, pl.ds(chunk * 128, 128)] = value.astype(bf16)


def combine(plan, total, info, grad_query, grad_pairs, from_below, from_above):
    width = grad_query.shape[1]
    return pl.pallas_call(
        functools.partial(combine_kernel, plan, total),
        out_shape=jax.ShapeDtypeStruct((plan.rows, 3 * width), bf16),
        in_specs=[SCALARS] + spec(4),
        out_specs=spec(1)[0],
        scratch_shapes=[pltpu.VMEM((3 * width // 128, plan.query_rows, 128), f32)],
        compiler_params=pltpu.CompilerParams(vmem_limit_bytes=VMEM_LIMIT),
        name="combine",
    )(info, grad_query, grad_pairs, from_below, from_above)


def layer_norm(values, gain, shift):
    center = values - jnp.mean(values, axis=-1, keepdims=True)
    spread = jnp.mean(center * center, axis=-1, keepdims=True)
    return center * lax.rsqrt(spread + 1e-05) * gain + shift


def gelu_exact(values):
    return jax.nn.gelu(values, approximate=False)


def exchange(to_above, to_below):
    count = lax.axis_size("seq")
    up = [(i, i + 1) for i in range(count - 1)]
    down = [(i + 1, i) for i in range(count - 1)]
    return lax.ppermute(to_above, "seq", up), lax.ppermute(to_below, "seq", down)


def per_device(
    lengths,
    tokens,
    ln1_gain,
    ln1_bias,
    w_qkv,
    w_out,
    out_bias,
    ln2_gain,
    ln2_bias,
    w_in,
    in_bias,
    w_back,
    back_bias,
    cotangent,
):
    devices = lax.axis_size("seq")
    device = lax.axis_index("seq")
    rows = tokens.shape[0]
    total = rows * devices
    plan = Plan(rows)
    padded = (lengths + 15) // 16 * 16
    ends = jnp.cumsum(padded, dtype=jnp.int32)
    info = jnp.concatenate([device[None].astype(jnp.int32), lengths, ends - padded, ends])
    (
        gain_one,
        bias_one,
        joint_weight,
        out_weight,
        out_shift,
        gain_two,
        bias_two,
        in_weight,
        in_shift,
        back_weight,
        back_shift,
    ) = (
        lax.all_gather(item, "seq", axis=0, tiled=True)
        for item in (
            ln1_gain,
            ln1_bias,
            w_qkv,
            w_out,
            out_bias,
            ln2_gain,
            ln2_bias,
            w_in,
            in_bias,
            w_back,
            back_bias,
        )
    )
    gain_one, bias_one = gain_one.astype(f32), bias_one.astype(f32)
    normed_low, query, pairs, head, tail = project(
        plan, total, info, tokens, gain_one[None], bias_one[None], joint_weight
    )
    before, after = exchange(tail, head)
    attended, mixed, scale = attend(plan, total, info, query, pairs, before, after)
    inputs = tokens.astype(f32)
    branch = jnp.dot(attended, out_weight, preferred_element_type=f32) + out_shift.astype(f32)
    resid = inputs + branch
    normed_two, norm_two_pull = jax.vjp(
        layer_norm, resid, gain_two.astype(f32), bias_two.astype(f32)
    )
    normed_two_low = normed_two.astype(bf16)
    inner = jnp.dot(normed_two_low, in_weight, preferred_element_type=f32) + in_shift.astype(f32)
    active, gelu_pull = jax.vjp(gelu_exact, inner)
    active_low = active.astype(bf16)
    outer = jnp.dot(active_low, back_weight, preferred_element_type=f32) + back_shift.astype(f32)
    result = (resid + outer).astype(bf16)
    grad_out = cotangent.astype(f32)
    grad_back_shift = jnp.sum(grad_out, axis=0)
    grad_back_weight = jnp.einsum("rf,rd->fd", active_low, cotangent, preferred_element_type=f32)
    grad_active = jnp.dot(cotangent, back_weight.T, preferred_element_type=f32)
    grad_inner = gelu_pull(grad_active)[0].astype(bf16)
    grad_in_shift = jnp.sum(grad_inner.astype(f32), axis=0)
    grad_in_weight = jnp.einsum("rd,rf->df", normed_two_low, grad_inner, preferred_element_type=f32)
    grad_normed_two = jnp.dot(grad_inner, in_weight.T, preferred_element_type=f32)
    grad_resid_part, grad_gain_two, grad_bias_two = norm_two_pull(grad_normed_two)
    grad_resid = grad_out + grad_resid_part
    grad_branch = grad_resid.astype(bf16)
    grad_out_shift = jnp.sum(grad_branch.astype(f32), axis=0)
    grad_out_weight = jnp.einsum("rd,re->de", attended, grad_branch, preferred_element_type=f32)
    grad_mixed = jnp.dot(grad_branch, out_weight.T, preferred_element_type=f32)
    grad_query, grad_pairs, grad_head, grad_tail = attend_back(
        plan, total, info, query, pairs, before, after, grad_mixed, scale, mixed
    )
    from_below, from_above = exchange(grad_tail, grad_head)
    grad_joined = combine(plan, total, info, grad_query, grad_pairs, from_below, from_above)
    grad_joint_weight = jnp.einsum(
        "rd,rf->df", normed_low, grad_joined, preferred_element_type=f32
    )
    grad_normed = jnp.dot(grad_joined, joint_weight.T, preferred_element_type=f32)
    _, norm_one_pull = jax.vjp(layer_norm, inputs, gain_one, bias_one)
    grad_input_part, grad_gain_one, grad_bias_one = norm_one_pull(grad_normed)
    grad_tokens = grad_resid + grad_input_part
    return (result, grad_tokens) + tuple(
        lax.psum_scatter(item, "seq", scatter_dimension=0, tiled=True)
        for item in (
            grad_gain_one,
            grad_bias_one,
            grad_joint_weight,
            grad_out_weight,
            grad_out_shift,
            grad_gain_two,
            grad_bias_two,
            grad_in_weight,
            grad_in_shift,
            grad_back_weight,
            grad_back_shift,
        )
    )


def solution(mesh):
    flat, wide = P("seq"), P("seq", None)
    weights = (flat, flat, wide, wide, flat, flat, flat, wide, flat, wide, flat)
    return jax.shard_map(
        per_device,
        mesh=mesh,
        in_specs=(P(), wide) + weights + (wide,),
        out_specs=(wide, wide) + weights,
        check_vma=False,
    )
```

```python
import functools
import math

import jax
import jax.numpy as jnp
import numpy as np
from jax import lax
from jax.experimental import pallas as pl
from jax.experimental.pallas import tpu as pltpu
from jax.sharding import PartitionSpec as P

HEAD_DIM = 64
LEVELS = 5
HALO = 32
BLOCK = 64
WINDOW = BLOCK + 2 * HALO
QUAD = 4
QUAD_WIDTH = QUAD * HEAD_DIM
PIECES = 4
BLOCKS = 32
FAR = 1 << 26
SEQ_STEP = 1 << 21
VMEM_LIMIT = 56 * 1024 * 1024

f32 = jnp.float32
bf16 = jnp.bfloat16


class Plan:
    def __init__(self, rows):
        self.rows = rows
        self.counts = [rows >> level for level in range(LEVELS)]
        self.padded = [-(-count // BLOCK) * BLOCK for count in self.counts]
        self.query_at = [sum(self.padded[:level]) for level in range(LEVELS)]
        self.query_rows = sum(self.padded)
        self.key_at = [self.query_at[level] + 2 * HALO * level for level in range(LEVELS)]
        self.key_rows = self.query_rows + 2 * HALO * LEVELS
        self.blocks = [
            (level, part)
            for level in range(LEVELS)
            for part in range(self.padded[level] // BLOCK)
        ]


def dot_nn(a, b):
    return lax.dot_general(a, b, (((1,), (0,)), ((), ())), preferred_element_type=f32)


def dot_nt(a, b):
    return lax.dot_general(a, b, (((1,), (1,)), ((), ())), preferred_element_type=f32)


def dot_tn(a, b):
    return lax.dot_general(a, b, (((0,), (0,)), ((), ())), preferred_element_type=f32)


def spec(count):
    return [pl.BlockSpec(memory_space=pltpu.VMEM)] * count


SCALARS = pl.BlockSpec(memory_space=pltpu.SMEM)


def slot_facts(info, slot, total):
    number = jnp.zeros(slot.shape, jnp.int32)
    for s in range(3):
        number = number + (slot >= info[7 + s]).astype(jnp.int32)
    begin = jnp.where(number == 0, info[4], jnp.where(number == 1, info[5], info[6]))
    length = jnp.where(number == 0, info[1], jnp.where(number == 1, info[2], info[3]))
    inside = (slot >= 0) & (slot < total) & (number < 3)
    return number, slot - begin, length, inside


def tile_codes(info, coarse, level, total, outside):
    number, offset, _, inside = slot_facts(info, coarse << level, total)
    wide = jnp.where(inside, number * SEQ_STEP + (offset >> (level + 4)), outside)
    fine = number * SEQ_STEP + (offset >> (level + 3))
    return wide, fine


def admitted(query_codes, key_codes, level):
    near = jnp.abs(query_codes[0] - key_codes[0]) <= 1
    if level > 0:
        near = near & (jnp.abs(query_codes[1] - key_codes[1]) >= 2)
    return jnp.where(near, 1.0, 0.0)


def live_counts(info, coarse, level, total):
    _, offset, length, inside = slot_facts(info, coarse << level, total)
    span = 1 << level
    return jnp.where(inside, jnp.clip(length - offset, 0, span), 0).astype(f32)


def head_masks(rows):
    lane = lax.broadcasted_iota(jnp.int32, (rows, QUAD_WIDTH), 1) // HEAD_DIM
    return [jnp.where(lane == h, 1.0, 0.0) for h in range(QUAD)]


def spread_heads(block, masks):
    return jnp.concatenate([block * m for m in masks], axis=0)


def gather_heads(stacked, masks):
    rows = stacked.shape[0] // QUAD
    total = stacked[:rows] * masks[0]
    for h in range(1, QUAD):
        total = total + stacked[h * rows : (h + 1) * rows] * masks[h]
    return total


def put(chunks, rows, quad, block):
    for part in range(QUAD_WIDTH // 128):
        chunk = quad * (QUAD_WIDTH // 128) + part
        chunks[chunk, rows, :] = block[:, part * 128 : part * 128 + 128]


def take(chunks, rows, quad):
    first = quad * (QUAD_WIDTH // 128)
    return jnp.concatenate(
        [chunks[first + part, rows, :] for part in range(QUAD_WIDTH // 128)], axis=1
    )


def fill_extended(plan, own, before, after, extended):
    for level in range(LEVELS):
        at, count, mine = plan.key_at[level], plan.counts[level], plan.query_at[level]
        halo = pl.ds(HALO * level, HALO)
        extended[pl.ds(at, HALO), :] = before[halo, :]
        extended[pl.ds(at + HALO, count), :] = own[pl.ds(mine, count), :]
        extended[pl.ds(at + HALO + count, HALO), :] = after[halo, :]
        rest = plan.padded[level] - count
        if rest:
            extended[pl.ds(at + 2 * HALO + count, rest), :] = jnp.zeros(
                (rest, extended.shape[1]), bf16
            )


def ln_stats(values):
    center = values - jnp.mean(values, axis=-1, keepdims=True)
    spread = jnp.mean(center * center, axis=-1, keepdims=True)
    return center, lax.rsqrt(spread + 1e-05)


def ln_back(grad, center, rstd, gain):
    hat = center * rstd
    scaled = grad * gain
    mean_one = jnp.mean(scaled, axis=-1, keepdims=True)
    mean_two = jnp.mean(scaled * hat, axis=-1, keepdims=True)
    return rstd * (scaled - mean_one - hat * mean_two), grad * hat


def column_sum(values):
    return jnp.sum(values, axis=0, keepdims=True)


def unpack_vectors(table, wide):
    blocks, lanes = table.shape

    def one(first, each):
        length = blocks * each
        source = lax.broadcasted_iota(jnp.int32, (lanes, length), 0)
        target = lax.broadcasted_iota(jnp.int32, (lanes, length), 1)
        pick = jnp.where(source == first + (target & (each - 1)), 1.0, 0.0).astype(bf16)
        spreaded = dot_nn(table, pick)
        block = lax.broadcasted_iota(jnp.int32, (blocks, length), 0)
        lane = lax.broadcasted_iota(jnp.int32, (blocks, length), 1)
        return column_sum(jnp.where(lane // each == block, spreaded, 0.0))

    size = wide // 4
    return [one(k * size, size) for k in range(6)], one(6 * size, wide)


def pack_vectors(vectors, last, blocks, lanes):
    size = last.shape[1] // blocks // 4

    def one(row, first, each):
        length = blocks * each
        source = lax.broadcasted_iota(jnp.int32, (length, lanes), 0)
        target = lax.broadcasted_iota(jnp.int32, (length, lanes), 1)
        pick = jnp.where(target == first + (source & (each - 1)), 1.0, 0.0).astype(bf16)
        block = lax.broadcasted_iota(jnp.int32, (blocks, length), 0)
        lane = lax.broadcasted_iota(jnp.int32, (blocks, length), 1)
        spreaded = jnp.where(lane // each == block, row, 0.0)
        total = jnp.zeros((blocks, lanes), f32)
        for _ in range(3):
            part = spreaded.astype(bf16)
            total = total + dot_nn(part, pick)
            spreaded = spreaded - part.astype(f32)
        return total

    total = one(last, 6 * size, 4 * size)
    for k, vector in enumerate(vectors):
        total = total + one(vector, k * size, size)
    return total


def project_kernel(
    plan, total, info, inverse, tokens, *refs
):
    weight_pieces, vector_pieces = refs[:PIECES], refs[PIECES : 2 * PIECES]
    normed, query, pairs, head, tail, weight, vectors, shift_out, table = refs[2 * PIECES :]
    rows, width = tokens.shape
    device = info[0]
    each = weight_pieces[0].shape[0]
    block_rows = weight_pieces[0].shape[1]
    for p in range(PIECES * each):
        i = inverse[p]
        there = pl.ds(pl.multiple_of(i * block_rows, block_rows), block_rows)
        weight[there, :] = weight_pieces[p // each][p % each]
        table[pl.ds(i, 1), :] = vector_pieces[p // each][p % each].astype(f32)
    singles, wide = unpack_vectors(table[...].astype(bf16), 4 * block_rows)
    for k, single in enumerate(singles):
        vectors[pl.ds(k, 1), :] = single
    shift_out[...] = wide
    values = tokens[...].astype(f32)
    center, rstd = ln_stats(values)
    low = (center * rstd * singles[0] + singles[1]).astype(bf16)
    normed[...] = low
    pooled_rows = plan.query_rows - plan.query_at[1]
    row = lax.broadcasted_iota(jnp.int32, (pooled_rows, rows), 0)
    slot = lax.broadcasted_iota(jnp.int32, (pooled_rows, rows), 1)
    first = jnp.zeros((pooled_rows, rows), jnp.int32)
    shift = jnp.zeros((pooled_rows, rows), jnp.int32)
    share = jnp.zeros((pooled_rows, 1), f32)
    row_one = lax.broadcasted_iota(jnp.int32, (pooled_rows, 1), 0)
    for level in range(1, LEVELS):
        at = plan.query_at[level] - plan.query_at[1]
        first = jnp.where(row >= at, at, first)
        shift = jnp.where(row >= at, level, shift)
        share = jnp.where(row_one >= at, 0.5**level, share)
    pool = jnp.where((slot >> shift) == row - first, 1.0, 0.0).astype(bf16)
    places = device * rows + lax.broadcasted_iota(jnp.int32, (rows, QUAD_WIDTH), 0)
    live = live_counts(info, places, 0, total)
    lanes = QUAD_WIDTH
    for part in range(3 * width // lanes):
        columns = pl.ds(part * lanes, lanes)
        block = dot_nn(low, weight[:, columns]).astype(bf16)
        if part * lanes >= 2 * width:
            block = (block.astype(f32) * live).astype(bf16)
        pooled = dot_nn(pool, block)
        if part * lanes < 2 * width:
            pooled = pooled * share
        if part * lanes < width:
            scale = 1.0 / math.sqrt(HEAD_DIM)
            query[pl.ds(0, rows), columns] = (block.astype(f32) * scale).astype(bf16)
            query[pl.ds(rows, pooled_rows), columns] = (pooled * scale).astype(bf16)
        else:
            there = pl.ds(part * lanes - width, lanes)
            pairs[pl.ds(0, rows), there] = block
            pairs[pl.ds(rows, pooled_rows), there] = pooled.astype(bf16)
    for level in range(LEVELS):
        at, count = plan.query_at[level], plan.counts[level]
        halo = pl.ds(HALO * level, HALO)
        head[halo, :] = pairs[pl.ds(at, HALO), :]
        tail[halo, :] = pairs[pl.ds(at + count - HALO, HALO), :]


def project(plan, total, info, inverse, tokens, weight_pieces, vector_pieces):
    rows, width = tokens.shape
    halo = LEVELS * HALO
    blocks = PIECES * weight_pieces[0].shape[0]
    depth = blocks * weight_pieces[0].shape[1]
    lanes = vector_pieces[0].shape[-1]
    return pl.pallas_call(
        functools.partial(project_kernel, plan, total),
        out_shape=(
            jax.ShapeDtypeStruct((rows, width), bf16),
            jax.ShapeDtypeStruct((plan.query_rows, width), bf16),
            jax.ShapeDtypeStruct((plan.query_rows, 2 * width), bf16),
            jax.ShapeDtypeStruct((halo, 2 * width), bf16),
            jax.ShapeDtypeStruct((halo, 2 * width), bf16),
            jax.ShapeDtypeStruct((depth, weight_pieces[0].shape[2]), bf16),
            jax.ShapeDtypeStruct((8, depth), f32),
            jax.ShapeDtypeStruct((1, 4 * depth), f32),
        ),
        in_specs=[SCALARS, SCALARS] + spec(1 + 2 * PIECES),
        out_specs=tuple(spec(8)),
        scratch_shapes=[pltpu.VMEM((blocks, lanes), f32)],
        compiler_params=pltpu.CompilerParams(vmem_limit_bytes=VMEM_LIMIT),
        name="project",
    )(info, inverse, tokens, *weight_pieces, *vector_pieces)


def attend_kernel(
    plan, total, info, query, pairs, before, after, attended, mixed, scale, extended, numer, denom
):
    rows = plan.rows
    width = query.shape[1]
    device = info[0]
    fill_extended(plan, pairs, before, after, extended)
    masks = head_masks(BLOCK)
    low_masks = [m.astype(bf16) for m in masks]
    for level, part in plan.blocks:
        count = plan.counts[level]
        at = plan.query_at[level] + BLOCK * part
        window = plan.key_at[level] + BLOCK * part
        first = device * count + BLOCK * part
        row = first + lax.broadcasted_iota(jnp.int32, (BLOCK, WINDOW), 0)
        column = first - HALO + lax.broadcasted_iota(jnp.int32, (BLOCK, WINDOW), 1)
        allowed = admitted(
            tile_codes(info, row, level, total, FAR),
            tile_codes(info, column, level, total, -FAR),
            level,
        )
        allowed = jnp.concatenate([allowed] * QUAD, axis=0) > 0.0
        key_row = first - HALO + lax.broadcasted_iota(jnp.int32, (WINDOW, 128), 0)
        counts = live_counts(info, key_row, level, total).astype(bf16)
        counts = jnp.concatenate([counts] * (QUAD_WIDTH // 128), axis=1)
        for quad in range(width // QUAD_WIDTH):
            columns = pl.ds(quad * QUAD_WIDTH, QUAD_WIDTH)
            value_columns = pl.ds(width + quad * QUAD_WIDTH, QUAD_WIDTH)
            q = spread_heads(query[pl.ds(at, BLOCK), columns], low_masks)
            k = extended[pl.ds(window, WINDOW), columns]
            v = extended[pl.ds(window, WINDOW), value_columns]
            weight = jnp.where(allowed, jnp.exp(dot_nt(q, k)), 0.0).astype(bf16)
            put(numer, pl.ds(at, BLOCK), quad, gather_heads(dot_nn(weight, v), masks))
            put(denom, pl.ds(at, BLOCK), quad, gather_heads(dot_nn(weight, counts), masks))
    for sums in (numer, denom):
        for level in range(LEVELS - 1, 0, -1):
            count = plan.counts[level]
            for chunk in range(width // 128):
                upper = sums[chunk, pl.ds(plan.query_at[level], count), :]
                for parity in range(2):
                    there = pl.ds(plan.query_at[level - 1] + parity, count, stride=2)
                    sums[chunk, there, :] = sums[chunk, there, :] + upper
    places = device * rows + lax.broadcasted_iota(jnp.int32, (rows, 128), 0)
    live = live_counts(info, places, 0, total)
    for chunk in range(width // 128):
        lanes = pl.ds(chunk * 128, 128)
        factor = live / (denom[chunk, pl.ds(0, rows), :] + 1.0 - live)
        value = numer[chunk, pl.ds(0, rows), :] * factor
        scale[:, lanes] = factor
        mixed[:, lanes] = value
        attended[:, lanes] = value.astype(bf16)


def attend(plan, total, info, query, pairs, before, after):
    rows, width = plan.rows, query.shape[1]
    return pl.pallas_call(
        functools.partial(attend_kernel, plan, total),
        out_shape=(
            jax.ShapeDtypeStruct((rows, width), bf16),
            jax.ShapeDtypeStruct((rows, width), f32),
            jax.ShapeDtypeStruct((rows, width), f32),
        ),
        in_specs=[SCALARS] + spec(4),
        out_specs=tuple(spec(3)),
        scratch_shapes=[
            pltpu.VMEM((plan.key_rows, 2 * width), bf16),
            pltpu.VMEM((width // 128, plan.query_rows, 128), f32),
            pltpu.VMEM((width // 128, plan.query_rows, 128), f32),
        ],
        compiler_params=pltpu.CompilerParams(vmem_limit_bytes=VMEM_LIMIT),
        name="attend",
    )(info, query, pairs, before, after)


def middle_kernel(
    inverse,
    tokens,
    cotangent,
    attended,
    vectors,
    shift_in,
    *refs,
):
    pieces = refs[:PIECES]
    result, grad_resid, grad_mixed, own, other, sums, sum_in = refs[PIECES : PIECES + 7]
    w_out, w_in, w_back, gelu_low, normed_two, grad_normed, outer, tall, flat = refs[PIECES + 7 :]
    width = tokens.shape[1]
    each, stack = pieces[0].shape[0], pieces[0].shape[1]
    half = own.shape[0]
    chunks = w_in.shape[0]
    block = width // (PIECES * each)
    tall_block = chunks * block
    in_at, back_at = block, block + tall_block
    for p in range(PIECES * each):
        piece, q = pieces[p // each], p % each
        i = inverse[p]
        rows = pl.ds(pl.multiple_of(i * block, block), block)
        w_out[rows, :] = piece[q, pl.ds(0, block), :]
        for c in range(chunks):
            w_in[c, rows, :] = piece[q, pl.ds(in_at + block * c, block), :]
        rows = pl.ds(pl.multiple_of(i * tall_block, tall_block), tall_block)
        w_back[rows, :] = piece[q, pl.ds(back_at, tall_block), :]
    gain = vectors[pl.ds(3, 1), :]
    resid = tokens[...].astype(f32) + dot_nn(attended[...], w_out[...]) + vectors[pl.ds(2, 1), :]
    center, rstd = ln_stats(resid)
    normed_two[...] = (center * rstd * gain + vectors[pl.ds(4, 1), :]).astype(bf16)
    grad_resid[...] = resid
    outer[...] = jnp.zeros(outer.shape, f32)
    grad_normed[...] = jnp.zeros(grad_normed.shape, f32)

    def chunk_step(c, carry):
        there = pl.ds(pl.multiple_of(c * width, width), width)
        inner = dot_nn(normed_two[...], w_in[c]) + shift_in[:, there]
        cdf = 0.5 * (1.0 + lax.erf(inner * math.sqrt(0.5)))
        active = (inner * cdf).astype(bf16)
        slope = cdf + inner * (jnp.exp(-0.5 * inner * inner) * (1.0 / math.sqrt(2.0 * math.pi)))
        gelu_low[...] = active
        back = w_back[there, :]
        grad_inner = slope * dot_nt(cotangent[...], back)
        low = grad_inner.astype(bf16)
        outer[...] += dot_nn(active, back)
        tall[there, :] = dot_tn(active, cotangent[...])
        sum_in[:, there] = column_sum(low.astype(f32))
        flat[...] = dot_tn(normed_two[...], low)
        for p in range(2 * half):
            i = inverse[p]
            rows = flat[pl.ds(pl.multiple_of(i * block, block), block), :]
            at = pl.ds(pl.multiple_of(in_at + c * block, block), block)
            if p < half:
                own[p, at, :] = rows
            else:
                other[p - half, at, :] = rows.astype(bf16)
        grad_normed[...] += dot_nt(low, w_in[c])
        return carry

    lax.fori_loop(0, chunks, chunk_step, 0)
    resid = grad_resid[...]
    result[...] = (resid + outer[...] + vectors[pl.ds(5, 1), :]).astype(bf16)
    center, rstd = ln_stats(resid)
    grad_in, gain_terms = ln_back(grad_normed[...], center, rstd, gain)
    grad_out = cotangent[...].astype(f32)
    total = grad_out + grad_in
    grad_resid[...] = total
    low = total.astype(bf16)
    sums[pl.ds(0, 1), :] = jnp.zeros((1, width), f32)
    sums[pl.ds(1, 1), :] = jnp.zeros((1, width), f32)
    sums[pl.ds(2, 1), :] = column_sum(low.astype(f32))
    sums[pl.ds(3, 1), :] = column_sum(gain_terms)
    sums[pl.ds(4, 1), :] = column_sum(grad_normed[...])
    sums[pl.ds(5, 1), :] = column_sum(grad_out)
    grad_mixed[...] = dot_nt(low, w_out[...])
    flat[...] = dot_tn(attended[...], low)
    for p in range(2 * half):
        i = inverse[p]
        rows = flat[pl.ds(pl.multiple_of(i * block, block), block), :]
        tall_rows = tall[pl.ds(pl.multiple_of(i * tall_block, tall_block), tall_block), :]
        if p < half:
            own[p, pl.ds(0, block), :] = rows
            own[p, pl.ds(back_at, tall_block), :] = tall_rows
        else:
            other[p - half, pl.ds(0, block), :] = rows.astype(bf16)
            other[p - half, pl.ds(back_at, tall_block), :] = tall_rows.astype(bf16)


def middle(inverse, tokens, cotangent, attended, vectors, shift_in, pieces):
    rows, width = tokens.shape
    hidden = shift_in.shape[1]
    chunks = hidden // width
    blocks = PIECES * pieces[0].shape[0]
    stack = pieces[0].shape[1]
    return pl.pallas_call(
        middle_kernel,
        out_shape=(
            jax.ShapeDtypeStruct((rows, width), bf16),
            jax.ShapeDtypeStruct((rows, width), f32),
            jax.ShapeDtypeStruct((rows, width), f32),
            jax.ShapeDtypeStruct((blocks // 2, stack, width), f32),
            jax.ShapeDtypeStruct((blocks // 2, stack, width), bf16),
            jax.ShapeDtypeStruct((8, width), f32),
            jax.ShapeDtypeStruct((1, hidden), f32),
        ),
        in_specs=[SCALARS] + spec(5 + PIECES),
        out_specs=tuple(spec(7)),
        scratch_shapes=[
            pltpu.VMEM((width, width), bf16),
            pltpu.VMEM((chunks, width, width), bf16),
            pltpu.VMEM((hidden, width), bf16),
            pltpu.VMEM((rows, width), bf16),
            pltpu.VMEM((rows, width), bf16),
            pltpu.VMEM((rows, width), f32),
            pltpu.VMEM((rows, width), f32),
            pltpu.VMEM((hidden, width), f32),
            pltpu.VMEM((width, width), f32),
        ],
        compiler_params=pltpu.CompilerParams(vmem_limit_bytes=VMEM_LIMIT),
        name="middle",
    )(inverse, tokens, cotangent, attended, vectors, shift_in, *pieces)


def attend_back_kernel(
    plan,
    total,
    info,
    query,
    pairs,
    before,
    after,
    grad_mixed,
    scale,
    mixed,
    grad_query,
    grad_pairs,
    grad_head,
    grad_tail,
    extended,
    grad_extended,
    grad_numer,
    grad_denom,
):
    rows = plan.rows
    width = query.shape[1]
    device = info[0]
    fill_extended(plan, pairs, before, after, extended)
    grad_extended[...] = jnp.zeros(grad_extended.shape, f32)
    own = pl.ds(0, rows)
    for chunk in range(width // 128):
        lanes = pl.ds(chunk * 128, 128)
        value = grad_mixed[:, lanes] * scale[:, lanes]
        grad_numer[chunk, own, :] = value
        grad_denom[chunk, own, :] = -(value * mixed[:, lanes])
        for sums in (grad_numer, grad_denom):
            for level in range(1, LEVELS):
                count, at = plan.counts[level], plan.query_at[level]
                even = sums[chunk, pl.ds(plan.query_at[level - 1], count, stride=2), :]
                odd = sums[chunk, pl.ds(plan.query_at[level - 1] + 1, count, stride=2), :]
                sums[chunk, pl.ds(at, count), :] = even + odd
                rest = plan.padded[level] - count
                if rest:
                    sums[chunk, pl.ds(at + count, rest), :] = jnp.zeros((rest, 128), f32)
    masks = head_masks(BLOCK)
    low_masks = [m.astype(bf16) for m in masks]
    for level, part in plan.blocks:
        count = plan.counts[level]
        at = plan.query_at[level] + BLOCK * part
        window = plan.key_at[level] + BLOCK * part
        first = device * count + BLOCK * part
        key_row = first - HALO + lax.broadcasted_iota(jnp.int32, (WINDOW, 128), 0)
        lane = lax.broadcasted_iota(jnp.int32, (WINDOW, 128), 1)
        row = first + (lane & (BLOCK - 1))
        allowed = admitted(
            tile_codes(info, row, level, total, FAR),
            tile_codes(info, key_row, level, total, -FAR),
            level,
        )
        allowed = jnp.concatenate([allowed] * (QUAD * BLOCK // 128), axis=1) > 0.0
        counts = live_counts(info, key_row, level, total).astype(bf16)
        for quad in range(width // QUAD_WIDTH):
            columns = pl.ds(quad * QUAD_WIDTH, QUAD_WIDTH)
            value_columns = pl.ds(width + quad * QUAD_WIDTH, QUAD_WIDTH)
            here = pl.ds(at, BLOCK)
            there = pl.ds(window, WINDOW)
            q = spread_heads(query[here, columns], low_masks)
            g = spread_heads(take(grad_numer, here, quad).astype(bf16), low_masks)
            d = spread_heads(take(grad_denom, here, quad).astype(bf16), low_masks)
            k = extended[there, columns]
            v = extended[there, value_columns]
            value_and_count = jnp.concatenate([v] + [counts] * (QUAD_WIDTH // 128), axis=1)
            weight = jnp.where(allowed, jnp.exp(dot_nt(k, q)), 0.0)
            probs = weight.astype(bf16)
            grad_probs = dot_nt(value_and_count, jnp.concatenate([g, d], axis=1))
            grad_score = (grad_probs * weight).astype(bf16)
            grad_query[here, columns] = gather_heads(dot_tn(grad_score, k), masks) * (
                1.0 / math.sqrt(HEAD_DIM)
            )
            grad_extended[there, columns] += dot_nn(grad_score, q)
            grad_extended[there, value_columns] += dot_nn(probs, g)
    for level in range(LEVELS):
        at, count, mine = plan.key_at[level], plan.counts[level], plan.query_at[level]
        halo = pl.ds(HALO * level, HALO)
        grad_head[halo, :] = grad_extended[pl.ds(at, HALO), :].astype(bf16)
        grad_tail[halo, :] = grad_extended[pl.ds(at + HALO + count, HALO), :].astype(bf16)
        grad_pairs[pl.ds(mine, count), :] = grad_extended[pl.ds(at + HALO, count), :]


def attend_back(plan, total, info, query, pairs, before, after, grad_mixed, scale, mixed):
    width = query.shape[1]
    halo = LEVELS * HALO
    return pl.pallas_call(
        functools.partial(attend_back_kernel, plan, total),
        out_shape=(
            jax.ShapeDtypeStruct((plan.query_rows, width), f32),
            jax.ShapeDtypeStruct((plan.query_rows, 2 * width), f32),
            jax.ShapeDtypeStruct((halo, 2 * width), bf16),
            jax.ShapeDtypeStruct((halo, 2 * width), bf16),
        ),
        in_specs=[SCALARS] + spec(7),
        out_specs=tuple(spec(4)),
        scratch_shapes=[
            pltpu.VMEM((plan.key_rows, 2 * width), bf16),
            pltpu.VMEM((plan.key_rows, 2 * width), f32),
            pltpu.VMEM((width // 128, plan.query_rows, 128), f32),
            pltpu.VMEM((width // 128, plan.query_rows, 128), f32),
        ],
        compiler_params=pltpu.CompilerParams(vmem_limit_bytes=VMEM_LIMIT),
        name="attend_back",
    )(info, query, pairs, before, after, grad_mixed, scale, mixed)


def finish_kernel(
    plan,
    total,
    info,
    inverse,
    tokens,
    weight,
    vectors,
    grad_resid,
    sums,
    sum_in,
    grad_query,
    grad_pairs,
    from_below,
    from_above,
    grad_tokens,
    own,
    other,
    own_vector,
    other_vector,
    work,
    joined,
    flat,
    table,
):
    rows = plan.rows
    width = grad_query.shape[1]
    device = info[0]
    places = device * rows + lax.broadcasted_iota(jnp.int32, (rows, 128), 0)
    live = live_counts(info, places, 0, total)
    for chunk in range(3 * width // 128):
        if chunk * 128 < width:
            work[chunk] = grad_query[:, pl.ds(chunk * 128, 128)]
        else:
            lanes = pl.ds(chunk * 128 - width, 128)
            work[chunk] = grad_pairs[:, lanes]
            for level in range(LEVELS):
                at, count = plan.query_at[level], plan.counts[level]
                halo = pl.ds(HALO * level, HALO)
                work[chunk, pl.ds(at, HALO), :] += from_below[halo, lanes].astype(f32)
                last = pl.ds(at + count - HALO, HALO)
                work[chunk, last, :] += from_above[halo, lanes].astype(f32)
        for level in range(LEVELS - 1, 0, -1):
            count = plan.counts[level]
            upper = work[chunk, pl.ds(plan.query_at[level], count), :]
            if chunk * 128 < 2 * width:
                upper = upper * 0.5
            for parity in range(2):
                there = pl.ds(plan.query_at[level - 1] + parity, count, stride=2)
                work[chunk, there, :] = work[chunk, there, :] + upper
        value = work[chunk, pl.ds(0, rows), :]
        if chunk * 128 >= 2 * width:
            value = value * live
        joined[:, pl.ds(chunk * 128, 128)] = value.astype(bf16)
    values = tokens[...].astype(f32)
    center, rstd = ln_stats(values)
    gain = vectors[pl.ds(0, 1), :]
    normed = (center * rstd * gain + vectors[pl.ds(1, 1), :]).astype(bf16)
    half, block = own.shape[0], own.shape[1]
    for part in range(3):
        columns = pl.ds(part * width, width)
        flat[...] = dot_tn(normed, joined[:, columns])
        for p in range(2 * half):
            i = inverse[p]
            lines = flat[pl.ds(pl.multiple_of(i * block, block), block), :]
            if p < half:
                own[p, :, columns] = lines
            else:
                other[p - half, :, columns] = lines.astype(bf16)
    grad_normed = dot_nt(joined[...], weight[...])
    grad_in, gain_terms = ln_back(grad_normed, center, rstd, gain)
    grad_tokens[...] = grad_resid[...] + grad_in
    singles = [column_sum(gain_terms), column_sum(grad_normed)]
    singles += [sums[pl.ds(k, 1), :] for k in range(2, 6)]
    table[...] = pack_vectors(singles, sum_in[...], 2 * half, table.shape[1])
    for p in range(2 * half):
        line = table[pl.ds(inverse[p], 1), :]
        if p < half:
            own_vector[p] = line
        else:
            other_vector[p - half] = line


def finish(plan, total, info, inverse, lanes, blocks, tokens, weight, *rest):
    rows, width = tokens.shape
    half = blocks // 2
    block = width // blocks
    return pl.pallas_call(
        functools.partial(finish_kernel, plan, total),
        out_shape=(
            jax.ShapeDtypeStruct((rows, width), f32),
            jax.ShapeDtypeStruct((half, block, 3 * width), f32),
            jax.ShapeDtypeStruct((half, block, 3 * width), bf16),
            jax.ShapeDtypeStruct((half, 1, lanes), f32),
            jax.ShapeDtypeStruct((half, 1, lanes), f32),
        ),
        in_specs=[SCALARS, SCALARS] + spec(2 + len(rest)),
        out_specs=tuple(spec(5)),
        scratch_shapes=[
            pltpu.VMEM((3 * width // 128, plan.query_rows, 128), f32),
            pltpu.VMEM((rows, 3 * width), bf16),
            pltpu.VMEM((width, width), f32),
            pltpu.VMEM((blocks, lanes), f32),
        ],
        compiler_params=pltpu.CompilerParams(vmem_limit_bytes=VMEM_LIMIT),
        name="finish",
    )(info, inverse, tokens, weight, *rest)


class Ring:
    def __init__(self, devices):
        self.devices = devices
        bits = [1 << k for k in range(devices.bit_length() - 2, 0, -1)]
        self.orders = (bits, bits[-1:] + bits[:-1])
        self.stages = len(bits)

    def partner(self, stage):
        return [(i, i ^ self.orders[i & 1][stage]) for i in range(self.devices)]

    def twin(self):
        return [(i, i ^ 1) for i in range(self.devices)]

    def table(self):
        rows = []
        for device in range(self.devices):
            row = []
            for base in (device, device ^ 1):
                order = self.orders[base & 1]
                for position in range(1 << self.stages):
                    block = base
                    for stage in range(self.stages):
                        if position >> stage & 1:
                            block ^= order[stage]
                    row.append(block)
            rows.append(row)
        return np.array(rows, np.int32)

    def gather(self, arrays):
        held = [item[None] for item in arrays]
        for stage in range(self.stages - 1):
            route = self.partner(stage)
            came = [lax.ppermute(item, "seq", route) for item in held]
            held = [jnp.concatenate(pair) for pair in zip(held, came)]
        route = self.partner(self.stages - 1)
        came = [lax.ppermute(item, "seq", route) for item in held]
        twin_held = [lax.ppermute(item, "seq", self.twin()) for item in held]
        twin_came = [lax.ppermute(item, "seq", self.twin()) for item in came]
        return [list(four) for four in zip(held, came, twin_held, twin_came)]

    def scatter(self, own, other):
        came = [lax.ppermute(item, "seq", self.twin()) for item in other]
        for stage in range(self.stages - 1, -1, -1):
            half = 1 << stage
            route = self.partner(stage)
            sent = [
                (mine[half:] + more[half:].astype(f32)).astype(more.dtype)
                for mine, more in zip(own, came)
            ]
            kept = [mine[:half] + more[:half].astype(f32) for mine, more in zip(own, came)]
            came = [lax.ppermute(item, "seq", route) for item in sent]
            own = kept
        return [mine[0] + more[0].astype(f32) for mine, more in zip(own, came)]


def lanes_of(vectors, axis):
    joined = jnp.concatenate(vectors, axis=axis)
    rest = -joined.shape[axis] % 128
    pads = [(0, 0)] * joined.ndim
    pads[axis] = (0, rest)
    return jnp.pad(joined, pads)


def exchange(to_above, to_below):
    count = lax.axis_size("seq")
    up = [(i, i + 1) for i in range(count - 1)]
    down = [(i + 1, i) for i in range(count - 1)]
    return lax.ppermute(to_above, "seq", up), lax.ppermute(to_below, "seq", down)


def per_device(
    lengths,
    tokens,
    ln1_gain,
    ln1_bias,
    w_qkv,
    w_out,
    out_bias,
    ln2_gain,
    ln2_bias,
    w_in,
    in_bias,
    w_back,
    back_bias,
    cotangent,
):
    devices = lax.axis_size("seq")
    device = lax.axis_index("seq")
    rows, width = tokens.shape
    total = rows * devices
    plan = Plan(rows)
    padded = (lengths + 15) // 16 * 16
    ends = jnp.cumsum(padded, dtype=jnp.int32)
    info = jnp.concatenate([device[None].astype(jnp.int32), lengths, ends - padded, ends])
    block = width // BLOCKS
    chunks = w_in.shape[1] // width
    small = (ln1_gain, ln1_bias, out_bias, ln2_gain, ln2_bias, back_bias, in_bias)
    direct = devices == BLOCKS
    if direct:
        ring = Ring(devices)
        inverse = lax.dynamic_index_in_dim(jnp.array(ring.table()), device, keepdims=False)
        line = lanes_of(small, 0)[None]
        one, vector_pieces = ring.gather([w_qkv, line])
        stack = jnp.concatenate(
            [w_out] + [w_in[:, c * width : (c + 1) * width] for c in range(chunks)] + [w_back]
        )
        (two,) = ring.gather([stack])
    else:
        inverse = jnp.arange(BLOCKS, dtype=jnp.int32)

        def whole(item):
            return lax.all_gather(item, "seq", axis=0, tiled=True)

        def quarters(item):
            return [item[k * 8 : (k + 1) * 8] for k in range(PIECES)]

        line = lanes_of([whole(item).reshape(BLOCKS, -1) for item in small], 1)
        vector_pieces = quarters(line[:, None])
        one = quarters(whole(w_qkv).reshape(BLOCKS, block, -1))
        full_in = whole(w_in).reshape(BLOCKS, block, chunks, width)
        full_in = full_in.transpose(0, 2, 1, 3).reshape(BLOCKS, chunks * block, width)
        two = quarters(
            jnp.concatenate(
                [
                    whole(w_out).reshape(BLOCKS, block, width),
                    full_in,
                    whole(w_back).reshape(BLOCKS, chunks * block, width),
                ],
                axis=1,
            )
        )
    normed, query, pairs, head, tail, weight, vectors, shift_in = project(
        plan, total, info, inverse, tokens, one, vector_pieces
    )
    before, after = exchange(tail, head)
    attended, mixed, scale = attend(plan, total, info, query, pairs, before, after)
    result, grad_resid, grad_mixed, own_two, other_two, sums, sum_in = middle(
        inverse, tokens, cotangent, attended, vectors, shift_in, two
    )
    grad_query, grad_pairs, grad_head, grad_tail = attend_back(
        plan, total, info, query, pairs, before, after, grad_mixed, scale, mixed
    )
    from_below, from_above = exchange(grad_tail, grad_head)
    grad_tokens, own_one, other_one, own_line, other_line = finish(
        plan,
        total,
        info,
        inverse,
        line.shape[-1],
        BLOCKS,
        tokens,
        weight,
        vectors,
        grad_resid,
        sums,
        sum_in,
        grad_query,
        grad_pairs,
        from_below,
        from_above,
    )
    if direct:
        (grad_two,) = ring.scatter([own_two], [other_two])
        grad_w_qkv, grad_line = ring.scatter([own_one, own_line], [other_one, other_line])
        each = [item.shape[0] for item in small]
        starts = [sum(each[:k]) for k in range(len(each))]
        parts = [grad_line[0, at : at + size] for at, size in zip(starts, each)]
        grad_w_out = grad_two[:block]
        grad_w_in = jnp.concatenate(
            [grad_two[block * (c + 1) : block * (c + 2)] for c in range(chunks)], axis=1
        )
        grad_w_back = grad_two[block * (chunks + 1) :]
    else:

        def spread(own, other):
            return jnp.concatenate([own, other.astype(f32)])

        def shared(item):
            return lax.psum_scatter(item, "seq", scatter_dimension=0, tiled=True)

        full_line = spread(own_line, other_line)[:, 0]
        each = [block] * 6 + [block * chunks]
        starts = [sum(each[:k]) for k in range(len(each))]
        parts = [
            shared(full_line[:, at : at + size].reshape(-1)) for at, size in zip(starts, each)
        ]
        grad_w_qkv = shared(spread(own_one, other_one).reshape(width, 3 * width))
        full_two = spread(own_two, other_two)
        grad_w_out = shared(full_two[:, :block].reshape(width, width))
        full_in = full_two[:, block : block * (chunks + 1)]
        full_in = full_in.reshape(BLOCKS, chunks, block, width).transpose(0, 2, 1, 3)
        grad_w_in = shared(full_in.reshape(width, chunks * width))
        grad_w_back = shared(full_two[:, block * (chunks + 1) :].reshape(chunks * width, width))
    gain_one, bias_one, shift_out, gain_two, bias_two, shift_back, shift_hidden = parts
    return (
        result,
        grad_tokens,
        gain_one,
        bias_one,
        grad_w_qkv,
        grad_w_out,
        shift_out,
        gain_two,
        bias_two,
        grad_w_in,
        shift_hidden,
        grad_w_back,
        shift_back,
    )


def solution(mesh):
    flat, wide = P("seq"), P("seq", None)
    weights = (flat, flat, wide, wide, flat, flat, flat, wide, flat, wide, flat)
    return jax.shard_map(
        per_device,
        mesh=mesh,
        in_specs=(P(), wide) + weights + (wide,),
        out_specs=(wide, wide) + weights,
        check_vma=False,
    )
```

```python
import functools
import math

import jax
import jax.numpy as jnp
from jax import lax
from jax.experimental import pallas as pl
from jax.experimental.pallas import tpu as pltpu
from jax.sharding import PartitionSpec as P

HEAD_DIM = 64
LEVELS = 5
HALO = 32
BLOCK = 64
WINDOW = BLOCK + 2 * HALO
QUAD = 4
QUAD_WIDTH = QUAD * HEAD_DIM
PIECES = 4
BLOCKS = 32
LINE = 128
FAR = 1 << 26
SEQ_STEP = 1 << 21
MIB = 1024 * 1024

f32 = jnp.float32
bf16 = jnp.bfloat16


class Plan:
    def __init__(self, rows):
        self.rows = rows
        self.counts = [rows >> level for level in range(LEVELS)]
        self.padded = [-(-count // BLOCK) * BLOCK for count in self.counts]
        self.query_at = [sum(self.padded[:level]) for level in range(LEVELS)]
        self.query_rows = sum(self.padded)
        self.key_at = [self.query_at[level] + 2 * HALO * level for level in range(LEVELS)]
        self.key_rows = self.query_rows + 2 * HALO * LEVELS
        self.blocks = [
            (level, part)
            for level in range(LEVELS)
            for part in range(self.padded[level] // BLOCK)
        ]


def dot_nn(a, b):
    return lax.dot_general(a, b, (((1,), (0,)), ((), ())), preferred_element_type=f32)


def dot_nt(a, b):
    return lax.dot_general(a, b, (((1,), (1,)), ((), ())), preferred_element_type=f32)


def dot_tn(a, b):
    return lax.dot_general(a, b, (((0,), (0,)), ((), ())), preferred_element_type=f32)


def spec(count):
    return [pl.BlockSpec(memory_space=pltpu.VMEM)] * count


SCALARS = pl.BlockSpec(memory_space=pltpu.SMEM)


def slot_facts(info, slot, total):
    number = jnp.zeros(slot.shape, jnp.int32)
    for s in range(3):
        number = number + (slot >= info[7 + s]).astype(jnp.int32)
    begin = jnp.where(number == 0, info[4], jnp.where(number == 1, info[5], info[6]))
    length = jnp.where(number == 0, info[1], jnp.where(number == 1, info[2], info[3]))
    inside = (slot >= 0) & (slot < total) & (number < 3)
    return number, slot - begin, length, inside


def tile_codes(info, coarse, level, total, outside):
    number, offset, _, inside = slot_facts(info, coarse << level, total)
    wide = jnp.where(inside, number * SEQ_STEP + (offset >> (level + 4)), outside)
    fine = number * SEQ_STEP + (offset >> (level + 3))
    return wide, fine


def admitted(query_codes, key_codes, level):
    near = jnp.abs(query_codes[0] - key_codes[0]) <= 1
    if level > 0:
        near = near & (jnp.abs(query_codes[1] - key_codes[1]) >= 2)
    return jnp.where(near, 1.0, 0.0)


def live_counts(info, coarse, level, total):
    _, offset, length, inside = slot_facts(info, coarse << level, total)
    span = 1 << level
    return jnp.where(inside, jnp.clip(length - offset, 0, span), 0).astype(f32)


def head_masks(rows):
    lane = lax.broadcasted_iota(jnp.int32, (rows, QUAD_WIDTH), 1) // HEAD_DIM
    return [jnp.where(lane == h, 1.0, 0.0) for h in range(QUAD)]


def spread_heads(block, masks):
    return jnp.concatenate([block * m for m in masks], axis=0)


def gather_heads(stacked, masks):
    rows = stacked.shape[0] // QUAD
    total = stacked[:rows] * masks[0]
    for h in range(1, QUAD):
        total = total + stacked[h * rows : (h + 1) * rows] * masks[h]
    return total


def put(chunks, rows, block):
    for part in range(QUAD_WIDTH // 128):
        chunks[part, rows, :] = block[:, part * 128 : part * 128 + 128]


def take(chunks, rows):
    return jnp.concatenate([chunks[part, rows, :] for part in range(QUAD_WIDTH // 128)], axis=1)


def is_even(info):
    return (info[0] & 1) == 0


def params(size):
    return pltpu.CompilerParams(vmem_limit_bytes=size * MIB)


def cost(micros):
    return pl.CostEstimate(flops=1, bytes_accessed=1, transcendentals=0)


def fill_extended(plan, info, own, from_twin, from_other, extended):
    even = is_even(info)
    for level in range(LEVELS):
        at, count, mine = plan.key_at[level], plan.counts[level], plan.query_at[level]
        halo = pl.ds(HALO * level, HALO)
        after = at + HALO + count
        twin_at = pl.multiple_of(jnp.where(even, after, at), HALO)
        other_at = pl.multiple_of(jnp.where(even, at, after), HALO)
        extended[pl.ds(at + HALO, count), :] = own[pl.ds(mine, count), :]
        extended[pl.ds(twin_at, HALO), :] = from_twin[halo, :]
        extended[pl.ds(other_at, HALO), :] = from_other[halo, :]
        rest = plan.padded[level] - count
        if rest:
            extended[pl.ds(at + 2 * HALO + count, rest), :] = jnp.zeros(
                (rest, extended.shape[1]), bf16
            )


def ln_stats(values):
    center = values - jnp.mean(values, axis=-1, keepdims=True)
    spread = jnp.mean(center * center, axis=-1, keepdims=True)
    return center, lax.rsqrt(spread + 1e-05)


def ln_back(grad, center, rstd, gain):
    hat = center * rstd
    scaled = grad * gain
    mean_one = jnp.mean(scaled, axis=-1, keepdims=True)
    mean_two = jnp.mean(scaled * hat, axis=-1, keepdims=True)
    return rstd * (scaled - mean_one - hat * mean_two), grad * hat


def column_sum(values):
    return jnp.sum(values, axis=0, keepdims=True)


def unpack_vectors(table, wide):
    blocks, lanes = table.shape

    def one(first, each):
        length = blocks * each
        source = lax.broadcasted_iota(jnp.int32, (lanes, length), 0)
        target = lax.broadcasted_iota(jnp.int32, (lanes, length), 1)
        pick = jnp.where(source == first + (target & (each - 1)), 1.0, 0.0).astype(bf16)
        spreaded = dot_nn(table, pick)
        block = lax.broadcasted_iota(jnp.int32, (blocks, length), 0)
        lane = lax.broadcasted_iota(jnp.int32, (blocks, length), 1)
        return column_sum(jnp.where(lane // each == block, spreaded, 0.0))

    size = wide // 4
    return [one(k * size, size) for k in range(6)], one(LINE, wide)


def pack_vectors(vectors, last, blocks, lanes):
    size = last.shape[1] // blocks // 4

    def one(row, first, each):
        length = blocks * each
        source = lax.broadcasted_iota(jnp.int32, (length, lanes), 0)
        target = lax.broadcasted_iota(jnp.int32, (length, lanes), 1)
        pick = jnp.where(target == first + (source & (each - 1)), 1.0, 0.0).astype(bf16)
        block = lax.broadcasted_iota(jnp.int32, (blocks, length), 0)
        lane = lax.broadcasted_iota(jnp.int32, (blocks, length), 1)
        spreaded = jnp.where(lane // each == block, row, 0.0)
        total = jnp.zeros((blocks, lanes), f32)
        for _ in range(3):
            part = spreaded.astype(bf16)
            total = total + dot_nn(part, pick)
            spreaded = spreaded - part.astype(f32)
        return total

    total = one(last, LINE, 4 * size)
    for k, vector in enumerate(vectors):
        total = total + one(vector, k * size, size)
    return total


def project_kernel(
    plan, total, info, inverse, tokens, *refs
):
    pieces, outs = refs[:PIECES], refs[PIECES:]
    queries, pairs, twins, others = (outs[2 * k : 2 * k + 2] for k in range(4))
    weight, vectors, shift_out, table = outs[8:]
    rows, width = tokens.shape
    device = info[0]
    each = pieces[0].shape[0]
    block_rows = pieces[0].shape[1]
    main = pl.ds(0, 3 * width)
    side = pl.ds(3 * width, LINE)
    for p in range(PIECES * each):
        i = inverse[p]
        there = pl.ds(pl.multiple_of(i * block_rows, block_rows), block_rows)
        weight[there, :] = pieces[p // each][p % each, :, main]
        line = pieces[p // each][p % each, :, side].astype(f32)
        table[pl.ds(i, 1), :] = jnp.concatenate([line[0:1], line[1:2]], axis=1)
    singles, wide = unpack_vectors(table[...].astype(bf16), 4 * block_rows)
    for k, single in enumerate(singles):
        vectors[pl.ds(k, 1), :] = single
    shift_out[...] = wide
    values = tokens[...].astype(f32)
    center, rstd = ln_stats(values)
    low = (center * rstd * singles[0] + singles[1]).astype(bf16)
    pooled_rows = plan.query_rows - plan.query_at[1]
    row = lax.broadcasted_iota(jnp.int32, (pooled_rows, rows), 0)
    slot = lax.broadcasted_iota(jnp.int32, (pooled_rows, rows), 1)
    first = jnp.zeros((pooled_rows, rows), jnp.int32)
    shift = jnp.zeros((pooled_rows, rows), jnp.int32)
    share = jnp.zeros((pooled_rows, 1), f32)
    row_one = lax.broadcasted_iota(jnp.int32, (pooled_rows, 1), 0)
    for level in range(1, LEVELS):
        at = plan.query_at[level] - plan.query_at[1]
        first = jnp.where(row >= at, at, first)
        shift = jnp.where(row >= at, level, shift)
        share = jnp.where(row_one >= at, 0.5**level, share)
    pool = jnp.where((slot >> shift) == row - first, 1.0, 0.0).astype(bf16)
    places = device * rows + lax.broadcasted_iota(jnp.int32, (rows, QUAD_WIDTH), 0)
    live = live_counts(info, places, 0, total)
    lanes = QUAD_WIDTH
    for part in range(3 * width // lanes):
        columns = pl.ds(part * lanes, lanes)
        block = dot_nn(low, weight[:, columns]).astype(bf16)
        if part * lanes >= 2 * width:
            block = (block.astype(f32) * live).astype(bf16)
        pooled = dot_nn(pool, block)
        if part * lanes < 2 * width:
            pooled = pooled * share
        quad = part % 2
        if part * lanes < width:
            scale = 1.0 / math.sqrt(HEAD_DIM)
            queries[quad][pl.ds(0, rows), :] = (block.astype(f32) * scale).astype(bf16)
            queries[quad][pl.ds(rows, pooled_rows), :] = (pooled * scale).astype(bf16)
        else:
            there = pl.ds((part * lanes // width - 1) * lanes, lanes)
            pairs[quad][pl.ds(0, rows), there] = block
            pairs[quad][pl.ds(rows, pooled_rows), there] = pooled.astype(bf16)
    even = is_even(info)
    for quad in range(2):
        for level in range(LEVELS):
            at, count = plan.query_at[level], plan.counts[level]
            halo = pl.ds(HALO * level, HALO)
            last = at + count - HALO
            twin_at = pl.multiple_of(jnp.where(even, last, at), HALO)
            other_at = pl.multiple_of(jnp.where(even, at, last), HALO)
            twins[quad][halo, :] = pairs[quad][pl.ds(twin_at, HALO), :]
            others[quad][halo, :] = pairs[quad][pl.ds(other_at, HALO), :]


def project(plan, total, info, inverse, tokens, pieces):
    rows, width = tokens.shape
    halo = LEVELS * HALO
    blocks = PIECES * pieces[0].shape[0]
    depth = blocks * pieces[0].shape[1]
    half = width // 2
    outs = pl.pallas_call(
        functools.partial(project_kernel, plan, total),
        out_shape=(
            [jax.ShapeDtypeStruct((plan.query_rows, half), bf16)] * 2
            + [jax.ShapeDtypeStruct((plan.query_rows, 2 * half), bf16)] * 2
            + [jax.ShapeDtypeStruct((halo, 2 * half), bf16)] * 4
            + [
                jax.ShapeDtypeStruct((depth, 3 * width), bf16),
                jax.ShapeDtypeStruct((8, depth), f32),
                jax.ShapeDtypeStruct((1, 4 * depth), f32),
            ]
        ),
        in_specs=[SCALARS, SCALARS] + spec(1 + PIECES),
        out_specs=spec(11),
        scratch_shapes=[pltpu.VMEM((blocks, 2 * LINE), f32)],
        compiler_params=params(16),
        name="project",
        cost_estimate=cost(3.3),
    )(info, inverse, tokens, *pieces)
    return [outs[2 * k : 2 * k + 2] for k in range(4)] + list(outs[8:])


def attend_kernel(
    plan,
    total,
    info,
    query,
    pairs,
    from_twin,
    from_other,
    attended,
    mixed,
    scale,
    extended,
    numer,
    denom,
):
    rows = plan.rows
    width = query.shape[1]
    device = info[0]
    fill_extended(plan, info, pairs, from_twin, from_other, extended)
    masks = head_masks(BLOCK)
    low_masks = [m.astype(bf16) for m in masks]
    for level, part in plan.blocks:
        count = plan.counts[level]
        at = plan.query_at[level] + BLOCK * part
        window = plan.key_at[level] + BLOCK * part
        first = device * count + BLOCK * part
        row = first + lax.broadcasted_iota(jnp.int32, (BLOCK, WINDOW), 0)
        column = first - HALO + lax.broadcasted_iota(jnp.int32, (BLOCK, WINDOW), 1)
        allowed = admitted(
            tile_codes(info, row, level, total, FAR),
            tile_codes(info, column, level, total, -FAR),
            level,
        )
        allowed = jnp.concatenate([allowed] * QUAD, axis=0) > 0.0
        key_row = first - HALO + lax.broadcasted_iota(jnp.int32, (WINDOW, 128), 0)
        counts = live_counts(info, key_row, level, total).astype(bf16)
        counts = jnp.concatenate([counts] * (QUAD_WIDTH // 128), axis=1)
        here = pl.ds(at, BLOCK)
        q = spread_heads(query[here, :], low_masks)
        k = extended[pl.ds(window, WINDOW), pl.ds(0, width)]
        v = extended[pl.ds(window, WINDOW), pl.ds(width, width)]
        weight = jnp.where(allowed, jnp.exp(dot_nt(q, k)), 0.0).astype(bf16)
        put(numer, here, gather_heads(dot_nn(weight, v), masks))
        put(denom, here, gather_heads(dot_nn(weight, counts), masks))
    for sums in (numer, denom):
        for level in range(LEVELS - 1, 0, -1):
            count = plan.counts[level]
            for chunk in range(width // 128):
                upper = sums[chunk, pl.ds(plan.query_at[level], count), :]
                for parity in range(2):
                    there = pl.ds(plan.query_at[level - 1] + parity, count, stride=2)
                    sums[chunk, there, :] = sums[chunk, there, :] + upper
    places = device * rows + lax.broadcasted_iota(jnp.int32, (rows, 128), 0)
    live = live_counts(info, places, 0, total)
    for chunk in range(width // 128):
        lanes = pl.ds(chunk * 128, 128)
        factor = live / (denom[chunk, pl.ds(0, rows), :] + 1.0 - live)
        value = numer[chunk, pl.ds(0, rows), :] * factor
        scale[:, lanes] = factor
        mixed[:, lanes] = value
        attended[:, lanes] = value.astype(bf16)


def attend(plan, total, info, query, pairs, from_twin, from_other):
    rows, width = plan.rows, query.shape[1]
    return pl.pallas_call(
        functools.partial(attend_kernel, plan, total),
        out_shape=(
            jax.ShapeDtypeStruct((rows, width), bf16),
            jax.ShapeDtypeStruct((rows, width), f32),
            jax.ShapeDtypeStruct((rows, width), f32),
        ),
        in_specs=[SCALARS] + spec(4),
        out_specs=tuple(spec(3)),
        scratch_shapes=[
            pltpu.VMEM((plan.key_rows, 2 * width), bf16),
            pltpu.VMEM((width // 128, plan.query_rows, 128), f32),
            pltpu.VMEM((width // 128, plan.query_rows, 128), f32),
        ],
        compiler_params=params(12),
        name="attend",
        cost_estimate=cost(5),
    )(info, query, pairs, from_twin, from_other)


def middle_kernel(
    parts,
    inverse,
    tokens,
    cotangent,
    attended_a,
    attended_b,
    vectors,
    shift_in,
    *refs,
):
    pieces = refs[:parts]
    result, grad_resid, mixed_a, mixed_b, own, low_half, high_half, sums, sum_in = refs[
        parts : parts + 9
    ]
    w_out, w_in, w_back, normed_two, grad_normed, outer, tall, flat = refs[parts + 9 :]
    other = (low_half, high_half)
    width = tokens.shape[1]
    wide = width // 2
    each, stack = pieces[0].shape[0], pieces[0].shape[1]
    half = own.shape[0]
    chunks = w_in.shape[0]
    block = width // (parts * each)
    tall_block = chunks * block
    in_at, back_at = block, block + tall_block
    for p in range(parts * each):
        piece, q = pieces[p // each], p % each
        i = inverse[p]
        rows = pl.ds(pl.multiple_of(i * block, block), block)
        w_out[rows, :] = piece[q, pl.ds(0, block), :]
        for c in range(chunks):
            w_in[c, rows, :] = piece[q, pl.ds(in_at + block * c, block), :]
        rows = pl.ds(pl.multiple_of(i * tall_block, tall_block), tall_block)
        w_back[rows, :] = piece[q, pl.ds(back_at, tall_block), :]
    gain = vectors[pl.ds(3, 1), :]
    resid = tokens[...].astype(f32) + dot_nn(attended_a[...], w_out[pl.ds(0, wide), :])
    resid = resid + dot_nn(attended_b[...], w_out[pl.ds(wide, wide), :]) + vectors[pl.ds(2, 1), :]
    center, rstd = ln_stats(resid)
    normed_two[...] = (center * rstd * gain + vectors[pl.ds(4, 1), :]).astype(bf16)
    grad_resid[...] = resid
    outer[...] = jnp.zeros(outer.shape, f32)
    grad_normed[...] = jnp.zeros(grad_normed.shape, f32)

    def chunk_step(c, carry):
        there = pl.ds(pl.multiple_of(c * width, width), width)
        inner = dot_nn(normed_two[...], w_in[c]) + shift_in[:, there]
        cdf = 0.5 * (1.0 + lax.erf(inner * math.sqrt(0.5)))
        active = (inner * cdf).astype(bf16)
        slope = cdf + inner * (jnp.exp(-0.5 * inner * inner) * (1.0 / math.sqrt(2.0 * math.pi)))
        back = w_back[there, :]
        grad_inner = slope * dot_nt(cotangent[...], back)
        low = grad_inner.astype(bf16)
        outer[...] += dot_nn(active, back)
        tall[there, :] = dot_tn(active, cotangent[...])
        sum_in[:, there] = column_sum(low.astype(f32))
        flat[...] = dot_tn(normed_two[...], low)
        for p in range(2 * half):
            i = inverse[p]
            rows = flat[pl.ds(pl.multiple_of(i * block, block), block), :]
            at = pl.ds(pl.multiple_of(in_at + c * block, block), block)
            if p < half:
                own[p, at, :] = rows
            else:
                other[(p - half) // 8][(p - half) % 8, at, :] = rows.astype(bf16)
        grad_normed[...] += dot_nt(low, w_in[c])
        return carry

    lax.fori_loop(0, chunks, chunk_step, 0)
    resid = grad_resid[...]
    result[...] = (resid + outer[...] + vectors[pl.ds(5, 1), :]).astype(bf16)
    center, rstd = ln_stats(resid)
    grad_in, gain_terms = ln_back(grad_normed[...], center, rstd, gain)
    grad_out = cotangent[...].astype(f32)
    total = grad_out + grad_in
    grad_resid[...] = total
    low = total.astype(bf16)
    sums[pl.ds(0, 1), :] = jnp.zeros((1, width), f32)
    sums[pl.ds(1, 1), :] = jnp.zeros((1, width), f32)
    sums[pl.ds(2, 1), :] = column_sum(low.astype(f32))
    sums[pl.ds(3, 1), :] = column_sum(gain_terms)
    sums[pl.ds(4, 1), :] = column_sum(grad_normed[...])
    sums[pl.ds(5, 1), :] = column_sum(grad_out)
    for part, (attended, mixed) in enumerate(((attended_a, mixed_a), (attended_b, mixed_b))):
        lines = pl.ds(part * wide, wide)
        mixed[...] = dot_nt(low, w_out[lines, :])
        flat[lines, :] = dot_tn(attended[...], low)
    for p in range(2 * half):
        i = inverse[p]
        rows = flat[pl.ds(pl.multiple_of(i * block, block), block), :]
        tall_rows = tall[pl.ds(pl.multiple_of(i * tall_block, tall_block), tall_block), :]
        if p < half:
            own[p, pl.ds(0, block), :] = rows
            own[p, pl.ds(back_at, tall_block), :] = tall_rows
        else:
            there = other[(p - half) // 8]
            there[(p - half) % 8, pl.ds(0, block), :] = rows.astype(bf16)
            there[(p - half) % 8, pl.ds(back_at, tall_block), :] = tall_rows.astype(bf16)


def middle(inverse, tokens, cotangent, attended, vectors, shift_in, pieces):
    parts = len(pieces)
    rows, width = tokens.shape
    hidden = shift_in.shape[1]
    chunks = hidden // width
    blocks = parts * pieces[0].shape[0]
    stack = pieces[0].shape[1]
    return pl.pallas_call(
        functools.partial(middle_kernel, parts),
        out_shape=(
            jax.ShapeDtypeStruct((rows, width), bf16),
            jax.ShapeDtypeStruct((rows, width), f32),
            jax.ShapeDtypeStruct((rows, width // 2), f32),
            jax.ShapeDtypeStruct((rows, width // 2), f32),
            jax.ShapeDtypeStruct((blocks // 2, stack, width), f32),
            jax.ShapeDtypeStruct((blocks // 4, stack, width), bf16),
            jax.ShapeDtypeStruct((blocks // 4, stack, width), bf16),
            jax.ShapeDtypeStruct((8, width), f32),
            jax.ShapeDtypeStruct((1, hidden), f32),
        ),
        in_specs=[SCALARS] + spec(6 + parts),
        out_specs=tuple(spec(9)),
        scratch_shapes=[
            pltpu.VMEM((width, width), bf16),
            pltpu.VMEM((chunks, width, width), bf16),
            pltpu.VMEM((hidden, width), bf16),
            pltpu.VMEM((rows, width), bf16),
            pltpu.VMEM((rows, width), f32),
            pltpu.VMEM((rows, width), f32),
            pltpu.VMEM((hidden, width), f32),
            pltpu.VMEM((width, width), f32),
        ],
        compiler_params=params(34),
        name="middle",
        cost_estimate=cost(12),
    )(inverse, tokens, cotangent, *attended, vectors, shift_in, *pieces)


def attend_back_kernel(
    plan,
    total,
    info,
    query,
    pairs,
    from_twin,
    from_other,
    grad_mixed,
    scale,
    mixed,
    grad_query,
    grad_pairs,
    grad_twin,
    grad_other,
    extended,
    grad_extended,
    grad_numer,
    grad_denom,
):
    rows = plan.rows
    width = query.shape[1]
    device = info[0]
    fill_extended(plan, info, pairs, from_twin, from_other, extended)
    grad_extended[...] = jnp.zeros(grad_extended.shape, f32)
    own = pl.ds(0, rows)
    for chunk in range(width // 128):
        lanes = pl.ds(chunk * 128, 128)
        value = grad_mixed[:, lanes] * scale[:, lanes]
        grad_numer[chunk, own, :] = value
        grad_denom[chunk, own, :] = -(value * mixed[:, lanes])
        for sums in (grad_numer, grad_denom):
            for level in range(1, LEVELS):
                count, at = plan.counts[level], plan.query_at[level]
                even = sums[chunk, pl.ds(plan.query_at[level - 1], count, stride=2), :]
                odd = sums[chunk, pl.ds(plan.query_at[level - 1] + 1, count, stride=2), :]
                sums[chunk, pl.ds(at, count), :] = even + odd
                rest = plan.padded[level] - count
                if rest:
                    sums[chunk, pl.ds(at + count, rest), :] = jnp.zeros((rest, 128), f32)
    masks = head_masks(BLOCK)
    low_masks = [m.astype(bf16) for m in masks]
    for level, part in plan.blocks:
        count = plan.counts[level]
        at = plan.query_at[level] + BLOCK * part
        window = plan.key_at[level] + BLOCK * part
        first = device * count + BLOCK * part
        key_row = first - HALO + lax.broadcasted_iota(jnp.int32, (WINDOW, 128), 0)
        lane = lax.broadcasted_iota(jnp.int32, (WINDOW, 128), 1)
        row = first + (lane & (BLOCK - 1))
        allowed = admitted(
            tile_codes(info, row, level, total, FAR),
            tile_codes(info, key_row, level, total, -FAR),
            level,
        )
        allowed = jnp.concatenate([allowed] * (QUAD * BLOCK // 128), axis=1) > 0.0
        counts = live_counts(info, key_row, level, total).astype(bf16)
        here = pl.ds(at, BLOCK)
        there = pl.ds(window, WINDOW)
        keys = pl.ds(0, width)
        values = pl.ds(width, width)
        q = spread_heads(query[here, :], low_masks)
        g = spread_heads(take(grad_numer, here).astype(bf16), low_masks)
        d = spread_heads(take(grad_denom, here).astype(bf16), low_masks)
        k = extended[there, keys]
        v = extended[there, values]
        value_and_count = jnp.concatenate([v] + [counts] * (QUAD_WIDTH // 128), axis=1)
        weight = jnp.where(allowed, jnp.exp(dot_nt(k, q)), 0.0)
        probs = weight.astype(bf16)
        grad_probs = dot_nt(value_and_count, jnp.concatenate([g, d], axis=1))
        grad_score = (grad_probs * weight).astype(bf16)
        grad_query[here, :] = gather_heads(dot_tn(grad_score, k), masks) * (
            1.0 / math.sqrt(HEAD_DIM)
        )
        grad_extended[there, keys] += dot_nn(grad_score, q)
        grad_extended[there, values] += dot_nn(probs, g)
    even = is_even(info)
    for level in range(LEVELS):
        at, count, mine = plan.key_at[level], plan.counts[level], plan.query_at[level]
        halo = pl.ds(HALO * level, HALO)
        last = at + HALO + count
        twin_at = pl.multiple_of(jnp.where(even, last, at), HALO)
        other_at = pl.multiple_of(jnp.where(even, at, last), HALO)
        grad_twin[halo, :] = grad_extended[pl.ds(twin_at, HALO), :].astype(bf16)
        grad_other[halo, :] = grad_extended[pl.ds(other_at, HALO), :].astype(bf16)
        grad_pairs[pl.ds(mine, count), :] = grad_extended[pl.ds(at + HALO, count), :]


def attend_back(plan, total, info, query, pairs, from_twin, from_other, grad_mixed, scale, mixed):
    width = query.shape[1]
    halo = LEVELS * HALO
    return pl.pallas_call(
        functools.partial(attend_back_kernel, plan, total),
        out_shape=(
            jax.ShapeDtypeStruct((plan.query_rows, width), f32),
            jax.ShapeDtypeStruct((plan.query_rows, 2 * width), f32),
            jax.ShapeDtypeStruct((halo, 2 * width), bf16),
            jax.ShapeDtypeStruct((halo, 2 * width), bf16),
        ),
        in_specs=[SCALARS] + spec(7),
        out_specs=tuple(spec(4)),
        scratch_shapes=[
            pltpu.VMEM((plan.key_rows, 2 * width), bf16),
            pltpu.VMEM((plan.key_rows, 2 * width), f32),
            pltpu.VMEM((width // 128, plan.query_rows, 128), f32),
            pltpu.VMEM((width // 128, plan.query_rows, 128), f32),
        ],
        compiler_params=params(18),
        name="attend_back",
        cost_estimate=cost(6.4),
    )(info, query, pairs, from_twin, from_other, grad_mixed, scale, mixed)


def finish_kernel(
    plan,
    total,
    info,
    inverse,
    tokens,
    weight,
    vectors,
    grad_resid,
    sums,
    sum_in,
    queries_a,
    queries_b,
    pairs_a,
    pairs_b,
    twin_a,
    twin_b,
    other_a,
    other_b,
    grad_tokens,
    own,
    low_half,
    high_half,
    work,
    joined,
    flat,
    table,
):
    rows, width = tokens.shape
    device = info[0]
    even = is_even(info)
    half_width = width // 2
    places = device * rows + lax.broadcasted_iota(jnp.int32, (rows, 128), 0)
    live = live_counts(info, places, 0, total)
    for chunk in range(3 * width // 128):
        part, lane = divmod(chunk * 128, width)
        quad, lane = divmod(lane, half_width)
        if part == 0:
            work[chunk] = (queries_a, queries_b)[quad][:, pl.ds(lane, 128)]
        else:
            lanes = pl.ds((part - 1) * half_width + lane, 128)
            work[chunk] = (pairs_a, pairs_b)[quad][:, lanes]
            for level in range(LEVELS):
                at, count = plan.query_at[level], plan.counts[level]
                halo = pl.ds(HALO * level, HALO)
                last = at + count - HALO
                twin_at = pl.multiple_of(jnp.where(even, last, at), HALO)
                other_at = pl.multiple_of(jnp.where(even, at, last), HALO)
                there = pl.ds(twin_at, HALO)
                work[chunk, there, :] += (twin_a, twin_b)[quad][halo, lanes].astype(f32)
                there = pl.ds(other_at, HALO)
                work[chunk, there, :] += (other_a, other_b)[quad][halo, lanes].astype(f32)
        for level in range(LEVELS - 1, 0, -1):
            count = plan.counts[level]
            upper = work[chunk, pl.ds(plan.query_at[level], count), :]
            if chunk * 128 < 2 * width:
                upper = upper * 0.5
            for parity in range(2):
                there = pl.ds(plan.query_at[level - 1] + parity, count, stride=2)
                work[chunk, there, :] = work[chunk, there, :] + upper
        value = work[chunk, pl.ds(0, rows), :]
        if chunk * 128 >= 2 * width:
            value = value * live
        joined[:, pl.ds(chunk * 128, 128)] = value.astype(bf16)
    values = tokens[...].astype(f32)
    center, rstd = ln_stats(values)
    gain = vectors[pl.ds(0, 1), :]
    normed = (center * rstd * gain + vectors[pl.ds(1, 1), :]).astype(bf16)
    half, block = own.shape[0], own.shape[1]
    other = (low_half, high_half)
    for part in range(3):
        columns = pl.ds(part * width, width)
        flat[...] = dot_tn(normed, joined[:, columns])
        for p in range(2 * half):
            i = inverse[p]
            lines = flat[pl.ds(pl.multiple_of(i * block, block), block), :]
            if p < half:
                own[p, :, columns] = lines
            else:
                other[(p - half) // 8][(p - half) % 8, :, columns] = lines.astype(bf16)
    grad_normed = dot_nt(joined[...], weight[...])
    grad_in, gain_terms = ln_back(grad_normed, center, rstd, gain)
    grad_tokens[...] = grad_resid[...] + grad_in
    singles = [column_sum(gain_terms), column_sum(grad_normed)]
    singles += [sums[pl.ds(k, 1), :] for k in range(2, 6)]
    table[...] = pack_vectors(singles, sum_in[...], 2 * half, table.shape[1])
    row = lax.broadcasted_iota(jnp.int32, (block, LINE), 0)
    side = pl.ds(3 * width, LINE)
    for p in range(2 * half):
        line = table[pl.ds(inverse[p], 1), :]
        lines = jnp.where(row == 0, line[:, :LINE], jnp.where(row == 1, line[:, LINE:], 0.0))
        if p < half:
            own[p, :, side] = lines
        else:
            other[(p - half) // 8][(p - half) % 8, :, side] = lines.astype(bf16)


def finish(plan, total, info, inverse, tokens, weight, *rest):
    rows, width = tokens.shape
    half = BLOCKS // 2
    block = width // BLOCKS
    return pl.pallas_call(
        functools.partial(finish_kernel, plan, total),
        out_shape=(
            jax.ShapeDtypeStruct((rows, width), f32),
            jax.ShapeDtypeStruct((half, block, 3 * width + LINE), f32),
            jax.ShapeDtypeStruct((half // 2, block, 3 * width + LINE), bf16),
            jax.ShapeDtypeStruct((half // 2, block, 3 * width + LINE), bf16),
        ),
        in_specs=[SCALARS, SCALARS] + spec(2 + len(rest)),
        out_specs=tuple(spec(4)),
        scratch_shapes=[
            pltpu.VMEM((3 * width // 128, plan.query_rows, 128), f32),
            pltpu.VMEM((rows, 3 * width), bf16),
            pltpu.VMEM((width, width), f32),
            pltpu.VMEM((BLOCKS, 2 * LINE), f32),
        ],
        compiler_params=params(28),
        name="finish",
        cost_estimate=cost(6.2),
    )(info, inverse, tokens, weight, *rest)


class Ring:
    def __init__(self, devices):
        self.devices = devices
        bits = [1 << k for k in range(devices.bit_length() - 2, 0, -1)]
        self.orders = (bits, bits[-1:] + bits[:-1])
        self.stages = len(bits)

    def partner(self, stage):
        return [(i, i ^ self.orders[i & 1][stage]) for i in range(self.devices)]

    def twin(self):
        return [(i, i ^ 1) for i in range(self.devices)]

    def places(self, device):
        found = []
        even = (device & 1) == 0
        for base, swap in ((device, False), (device ^ 1, True)):
            for position in range(1 << self.stages):
                masks = [
                    sum(order[k] for k in range(self.stages) if position >> k & 1)
                    for order in self.orders
                ]
                if swap:
                    masks = masks[::-1]
                found.append(base ^ jnp.where(even, *masks))
        return found

    def step(self, stage, arrays):
        route = self.twin() if stage == self.stages else self.partner(stage)
        return [lax.ppermute(item, "seq", route) for item in arrays]

    def fold(self, stage, own, low, high):
        half = 1 << stage
        sent = (own[half:] + high.astype(f32)).astype(bf16)
        kept = own[:half] + low.astype(f32)
        return kept, sent


def halves(item):
    half = item.shape[0] // 2
    return item[:half], item[half:]


def join(held, came):
    return [jnp.concatenate(pair) for pair in zip(held, came)]


def pack_kernel(ring, lengths, w_qkv, w_out, w_in, w_back, *refs):
    vectors, (info, inverse, first, second, staged) = refs[:-5], refs[-5:]
    device = lax.axis_index("seq")
    info[0] = device
    start = jnp.int32(0)
    for k in range(3):
        length = lengths[k]
        info[1 + k] = length
        info[4 + k] = start
        start = start + (length + 15) // 16 * 16
        info[7 + k] = start
    for place, block in enumerate(ring.places(device)):
        inverse[place] = block
    block, width = w_qkv.shape
    first[0, :, pl.ds(0, width)] = w_qkv[...]
    staged[...] = jnp.zeros(staged.shape, f32)
    for k, vector in enumerate(vectors):
        size = vector.shape[0]
        row, lane = (0, k * block) if k < 6 else (1, 0)
        staged[pl.ds(row, 1), pl.ds(lane, size)] = vector[...].astype(f32).reshape(1, size)
    first[0, :, pl.ds(width, LINE)] = staged[...].astype(bf16)
    block, width = w_out.shape
    chunks = w_in.shape[1] // width
    second[0, pl.ds(0, block), :] = w_out[...]
    for c in range(chunks):
        second[0, pl.ds(block * (c + 1), block), :] = w_in[:, pl.ds(c * width, width)]
    second[0, pl.ds(block * (chunks + 1), block * chunks), :] = w_back[...]


def pack(ring, lengths, w_qkv, w_out, w_in, w_back, vectors):
    block, width = w_out.shape
    rows = block + w_in.shape[1] // width * block + w_back.shape[0]
    return pl.pallas_call(
        functools.partial(pack_kernel, ring),
        out_shape=(
            jax.ShapeDtypeStruct((10,), jnp.int32),
            jax.ShapeDtypeStruct((BLOCKS,), jnp.int32),
            jax.ShapeDtypeStruct((1, block, w_qkv.shape[1] + LINE), bf16),
            jax.ShapeDtypeStruct((1, rows, width), bf16),
        ),
        in_specs=[SCALARS] + spec(4 + len(vectors)),
        out_specs=(SCALARS, SCALARS) + tuple(spec(2)),
        scratch_shapes=[pltpu.VMEM((block, LINE), f32)],
        compiler_params=params(62),
        name="pack",
        cost_estimate=cost(1.5),
    )(lengths, w_qkv, w_out, w_in, w_back, *vectors)


def unpack_kernel(kept_one, came_one, kept_two, came_two, *outs):
    block, width = kept_one.shape[1] , kept_two.shape[2]
    w_qkv, w_out, w_in, w_back = outs[:4]
    main = pl.ds(0, 3 * width)
    w_qkv[...] = kept_one[0, :, main] + came_one[0, :, main].astype(f32)
    side = pl.ds(3 * width, LINE)
    lines = kept_one[0, :, side] + came_one[0, :, side].astype(f32)
    for k, out in enumerate(outs[4:]):
        size = out.shape[0]
        row, lane = (0, k * block) if k < 6 else (1, 0)
        out[...] = lines[row : row + 1, lane : lane + size].reshape(size)
    chunks = w_in.shape[1] // width

    def total(at, size):
        rows = pl.ds(at, size)
        return kept_two[0, rows, :] + came_two[0, rows, :].astype(f32)

    w_out[...] = total(0, block)
    for c in range(chunks):
        w_in[:, pl.ds(c * width, width)] = total(block * (c + 1), block)
    w_back[...] = total(block * (chunks + 1), block * chunks)


def unpack(kept_one, came_one, kept_two, came_two, like):
    return pl.pallas_call(
        unpack_kernel,
        out_shape=[jax.ShapeDtypeStruct(item.shape, f32) for item in like],
        in_specs=spec(4),
        out_specs=spec(len(like)),
        compiler_params=params(62),
        name="unpack",
        cost_estimate=cost(1.5),
    )(kept_one, came_one, kept_two, came_two)


def exchange(to_twin, to_other):
    count = lax.axis_size("seq")
    twin = [(i, i ^ 1) for i in range(count)]
    other = [(i, i + 1) for i in range(1, count - 1, 2)]
    other += [(j, i) for i, j in other]
    return (
        [lax.ppermute(item, "seq", other) for item in to_other],
        [lax.ppermute(item, "seq", twin) for item in to_twin],
    )


def order(items, *after):
    return lax.optimization_barrier((items, after))[0]


def per_device(
    lengths,
    tokens,
    ln1_gain,
    ln1_bias,
    w_qkv,
    w_out,
    out_bias,
    ln2_gain,
    ln2_bias,
    w_in,
    in_bias,
    w_back,
    back_bias,
    cotangent,
):
    devices = lax.axis_size("seq")
    device = lax.axis_index("seq")
    rows, width = tokens.shape
    total = rows * devices
    plan = Plan(rows)
    block = width // BLOCKS
    chunks = w_in.shape[1] // width
    small = (ln1_gain, ln1_bias, out_bias, ln2_gain, ln2_bias, back_bias, in_bias)
    direct = devices == BLOCKS
    ring = Ring(BLOCKS)
    last = ring.stages - 1
    core = ring.stages
    if direct:
        info, inverse, a, b = pack(ring, lengths, w_qkv, w_out, w_in, w_back, small)
        a_came, b_came = ring.step(0, [a, b])
        a, b = join([a, b], [a_came, b_came])
        a = order(a, b)
        a_came, b_came = ring.step(1, [a, b])
        (a,) = join([a], [a_came])
        (a_came,) = ring.step(2, [a])
        (a,) = join([a], [a_came])
        (b,) = join([b], [b_came])
        a = order(a, b)
        (a_came,) = ring.step(3, [a])
        (b_came,) = ring.step(2, [b])
        one = [a, a_came] + ring.step(core, [a, a_came])
        one = order(one, b_came)
    else:
        padded = (lengths + 15) // 16 * 16
        ends = jnp.cumsum(padded, dtype=jnp.int32)
        info = jnp.concatenate([device[None].astype(jnp.int32), lengths, ends - padded, ends])
        inverse = jnp.arange(BLOCKS, dtype=jnp.int32)

        def whole(item):
            return lax.all_gather(item, "seq", axis=0, tiled=True)

        def split(item, parts):
            each = BLOCKS // parts
            return [item[k * each : (k + 1) * each] for k in range(parts)]

        full = [whole(item).reshape(BLOCKS, 1, -1) for item in small]
        top = jnp.concatenate(full[:6], axis=2)
        top = jnp.pad(top, ((0, 0), (0, 0), (0, LINE - top.shape[2])))
        under = jnp.pad(full[6], ((0, 0), (0, block - 2), (0, LINE - full[6].shape[2])))
        line = jnp.concatenate([top, under], axis=1)
        one = whole(w_qkv).reshape(BLOCKS, block, -1)
        one = split(jnp.concatenate([one, line], axis=2), PIECES)
        full_in = whole(w_in).reshape(BLOCKS, block, chunks, width)
        full_in = full_in.transpose(0, 2, 1, 3).reshape(BLOCKS, chunks * block, width)
        full_two = [
            whole(w_out).reshape(BLOCKS, block, width),
            full_in,
            whole(w_back).reshape(BLOCKS, chunks * block, width),
        ]
        two = split(jnp.concatenate(full_two, axis=1), 2 * PIECES)
    queries, pairs, twins, others, weight, vectors, shift_in = project(
        plan, total, info, inverse, tokens, one
    )
    from_other, from_twin = exchange(twins, others)
    ready = queries[0]
    if direct:
        b, b_came = order((b, b_came), from_other)
        early, late = ring.step(last, [b, b_came])
        twin_early = ring.step(core, [b, b_came])
        ready = order(ready, b_came)
    outs = [attend(plan, total, info, ready, pairs[0], from_twin[0], from_other[0])]
    outs.append(
        attend(plan, total, info, queries[1], pairs[1], from_twin[1], from_other[1])
    )
    attended, mixed, scale = zip(*outs)
    if direct:
        early, late = order((early, late), attended)
        two = [b, b_came, early, late] + twin_early + ring.step(core, [early, late])
    result, grad_resid, mixed_a, mixed_b, own_two, low_two, high_two, sums, sum_in = middle(
        inverse, tokens, cotangent, attended, vectors, shift_in, two
    )
    grad_mixed = [mixed_a, mixed_b]

    def back(quad):
        return attend_back(
            plan,
            total,
            info,
            queries[quad],
            pairs[quad],
            from_twin[quad],
            from_other[quad],
            grad_mixed[quad],
            scale[quad],
            mixed[quad],
        )

    backs = [back(0)]
    if direct:
        high, low = ring.step(core, [high_two, low_two])
        low, high = order((low, high), backs[0][0])
        kept, sent = ring.fold(last, own_two, low, high)
        (came,) = ring.step(last, [sent])
        grad_mixed[1] = order(grad_mixed[1], sent)
    backs.append(back(1))
    twins, others = [item[2] for item in backs], [item[3] for item in backs]
    other_halo, twin_halo = exchange(twins, others)
    if direct:
        came = order(came, other_halo)
        kept, sent = ring.fold(last - 1, kept, *halves(came))
        (came,) = ring.step(last - 1, [sent])
        other_halo = order(other_halo, sent)
    grad_tokens, own_one, low_one, high_one = finish(
        plan,
        total,
        info,
        inverse,
        tokens,
        weight,
        vectors,
        grad_resid,
        sums,
        sum_in,
        backs[0][0],
        backs[1][0],
        backs[0][1],
        backs[1][1],
        *twin_halo,
        *other_halo,
    )
    if direct:
        high_one, low_one = ring.step(core, [high_one, low_one])
        came = order(came, grad_tokens)
        kept, sent = ring.fold(last - 2, kept, *halves(came))
        (came,) = ring.step(last - 2, [sent])
        high_one, low_one = order((high_one, low_one), sent)
        own_one, sent_one = ring.fold(last, own_one, low_one, high_one)
        (came_one,) = ring.step(last, [sent_one])
        own_one, sent_one = ring.fold(last - 1, own_one, *halves(came_one))
        (came_one,) = ring.step(last - 1, [sent_one])
        came = order(came, came_one)
        kept, sent = ring.fold(last - 3, kept, *halves(came))
        (came,) = ring.step(last - 3, [sent])
        own_one, sent_one = ring.fold(last - 2, own_one, *halves(came_one))
        sent_one = order(sent_one, sent)
        (came_one,) = ring.step(last - 2, [sent_one])
        own_one, sent_one = ring.fold(last - 3, own_one, *halves(came_one))
        (came_one,) = ring.step(last - 3, [sent_one])
        grads = unpack(own_one, came_one, kept, came, (w_qkv, w_out, w_in, w_back) + small)
        grad_w_qkv, grad_w_out, grad_w_in, grad_w_back = grads[:4]
        parts = grads[4:]
    else:

        def shared(item):
            return lax.psum_scatter(item, "seq", scatter_dimension=0, tiled=True)

        full = jnp.concatenate([own_one] + [x.astype(f32) for x in (low_one, high_one)])
        line = full[:, :, 3 * width :]
        parts = [shared(line[:, 0, k * block : (k + 1) * block].reshape(-1)) for k in range(6)]
        parts.append(shared(line[:, 1, : chunks * block].reshape(-1)))
        grad_w_qkv = shared(full[:, :, : 3 * width].reshape(width, 3 * width))
        full = jnp.concatenate([own_two] + [x.astype(f32) for x in (low_two, high_two)])
        grad_w_out = shared(full[:, :block].reshape(width, width))
        full_in = full[:, block : block * (chunks + 1)]
        full_in = full_in.reshape(BLOCKS, chunks, block, width).transpose(0, 2, 1, 3)
        grad_w_in = shared(full_in.reshape(width, chunks * width))
        grad_w_back = shared(full[:, block * (chunks + 1) :].reshape(chunks * width, width))
    gain_one, bias_one, shift_out, gain_two, bias_two, shift_back, shift_hidden = parts
    return (
        result,
        grad_tokens,
        gain_one,
        bias_one,
        grad_w_qkv,
        grad_w_out,
        shift_out,
        gain_two,
        bias_two,
        grad_w_in,
        shift_hidden,
        grad_w_back,
        shift_back,
    )


def solution(mesh):
    flat, wide = P("seq"), P("seq", None)
    weights = (flat, flat, wide, wide, flat, flat, flat, wide, flat, wide, flat)
    return jax.shard_map(
        per_device,
        mesh=mesh,
        in_specs=(P(), wide) + weights + (wide,),
        out_specs=(wide, wide) + weights,
        check_vma=False,
    )
```

```python
import functools
import math

import jax
import jax.numpy as jnp
from jax import lax
from jax.experimental import pallas as pl
from jax.experimental.pallas import tpu as pltpu
from jax.sharding import PartitionSpec as P

HEAD_DIM = 64
LEVELS = 5
HALO = 32
BLOCK = 64
WINDOW = BLOCK + 2 * HALO
QUAD = 4
QUAD_WIDTH = QUAD * HEAD_DIM
PIECES = 4
BLOCKS = 32
LINE = 128
FAR = 1 << 26
SEQ_STEP = 1 << 21
MIB = 1024 * 1024

f32 = jnp.float32
bf16 = jnp.bfloat16


class Plan:
    def locate(self, block):
        firsts = [at // BLOCK for at in self.query_at]
        level = sum((block >= first).astype(jnp.int32) for first in firsts[1:])
        start = sum(
            jnp.where(level == k, first, 0) for k, first in enumerate(firsts)
        )
        return level, block - start

    def __init__(self, rows):
        self.rows = rows
        self.counts = [rows >> level for level in range(LEVELS)]
        self.padded = [-(-count // BLOCK) * BLOCK for count in self.counts]
        self.query_at = [sum(self.padded[:level]) for level in range(LEVELS)]
        self.query_rows = sum(self.padded)
        self.key_at = [self.query_at[level] + 2 * HALO * level for level in range(LEVELS)]
        self.key_rows = self.query_rows + 2 * HALO * LEVELS
        self.blocks = [
            (level, part)
            for level in range(LEVELS)
            for part in range(self.padded[level] // BLOCK)
        ]


def dot_nn(a, b):
    return lax.dot_general(a, b, (((1,), (0,)), ((), ())), preferred_element_type=f32)


def dot_nt(a, b):
    return lax.dot_general(a, b, (((1,), (1,)), ((), ())), preferred_element_type=f32)


def dot_tn(a, b):
    return lax.dot_general(a, b, (((0,), (0,)), ((), ())), preferred_element_type=f32)


def spec(count):
    return [pl.BlockSpec(memory_space=pltpu.VMEM)] * count


SCALARS = pl.BlockSpec(memory_space=pltpu.SMEM)


def slot_facts(info, slot, total):
    number = jnp.zeros(slot.shape, jnp.int32)
    for s in range(3):
        number = number + (slot >= info[7 + s]).astype(jnp.int32)
    begin = jnp.where(number == 0, info[4], jnp.where(number == 1, info[5], info[6]))
    length = jnp.where(number == 0, info[1], jnp.where(number == 1, info[2], info[3]))
    inside = (slot >= 0) & (slot < total) & (number < 3)
    return number, slot - begin, length, inside


def tile_codes(info, coarse, level, total, outside):
    number, offset, _, inside = slot_facts(info, coarse << level, total)
    wide = jnp.where(inside, number * SEQ_STEP + (offset >> (level + 4)), outside)
    fine = number * SEQ_STEP + (offset >> (level + 3))
    return wide, fine


def admitted(query_codes, key_codes, level):
    near = jnp.abs(query_codes[0] - key_codes[0]) <= 1
    least = jnp.where(level > 0, 2, 0)
    near = near & (jnp.abs(query_codes[1] - key_codes[1]) >= least)
    return jnp.where(near, 1.0, 0.0)


def live_counts(info, coarse, level, total):
    _, offset, length, inside = slot_facts(info, coarse << level, total)
    span = 1 << level
    return jnp.where(inside, jnp.clip(length - offset, 0, span), 0).astype(f32)


def head_masks(rows):
    lane = lax.broadcasted_iota(jnp.int32, (rows, QUAD_WIDTH), 1) // HEAD_DIM
    return [jnp.where(lane == h, 1.0, 0.0).astype(bf16) for h in range(QUAD)]


def spread_heads(block, masks):
    return jnp.concatenate([block * m for m in masks], axis=0)


def join_pair(stacked, first):
    rows = stacked.shape[0] // 2
    return jnp.where(first, stacked[:rows], stacked[rows:])


def is_even(info):
    return (info[0] & 1) == 0


def params(size):
    return pltpu.CompilerParams(vmem_limit_bytes=size * MIB)


def cost(micros):
    return pl.CostEstimate(flops=1, bytes_accessed=1, transcendentals=0)


def fill_extended(plan, own, halos, extended):
    for level in range(LEVELS):
        at, count, mine = plan.key_at[level], plan.counts[level], plan.query_at[level]
        extended[pl.ds(at, HALO), :] = halos[pl.ds(HALO * level, HALO), :]
        extended[pl.ds(at + HALO, count), :] = own[pl.ds(mine, count), :]
        extended[pl.ds(at + HALO + count, HALO), :] = halos[pl.ds(HALO * (LEVELS + level), HALO), :]
        rest = plan.padded[level] - count
        if rest:
            extended[pl.ds(at + 2 * HALO + count, rest), :] = jnp.zeros(
                (rest, extended.shape[1]), bf16
            )


def place_halos(info, from_twin, from_other, halos):
    even = is_even(info)
    size = LEVELS * HALO
    halos[pl.ds(pl.multiple_of(jnp.where(even, size, 0), size), size), :] = from_twin[...]
    halos[pl.ds(pl.multiple_of(jnp.where(even, 0, size), size), size), :] = from_other[...]


def hand_out(info, ends, to_twin, to_other):
    even = is_even(info)
    size = LEVELS * HALO
    to_twin[...] = ends[pl.ds(pl.multiple_of(jnp.where(even, size, 0), size), size), :]
    to_other[...] = ends[pl.ds(pl.multiple_of(jnp.where(even, 0, size), size), size), :]


def ln_stats(values):
    center = values - jnp.mean(values, axis=-1, keepdims=True)
    spread = jnp.mean(center * center, axis=-1, keepdims=True)
    return center, lax.rsqrt(spread + 1e-05)


def ln_back(grad, center, rstd, gain):
    hat = center * rstd
    scaled = grad * gain
    mean_one = jnp.mean(scaled, axis=-1, keepdims=True)
    mean_two = jnp.mean(scaled * hat, axis=-1, keepdims=True)
    return rstd * (scaled - mean_one - hat * mean_two), grad * hat


def column_sum(values):
    return jnp.sum(values, axis=0, keepdims=True)


def unpack_vectors(table, wide):
    blocks, lanes = table.shape

    def one(first, each):
        length = blocks * each
        source = lax.broadcasted_iota(jnp.int32, (lanes, length), 0)
        target = lax.broadcasted_iota(jnp.int32, (lanes, length), 1)
        pick = jnp.where(source == first + (target & (each - 1)), 1.0, 0.0).astype(bf16)
        spreaded = dot_nn(table, pick)
        block = lax.broadcasted_iota(jnp.int32, (blocks, length), 0)
        lane = lax.broadcasted_iota(jnp.int32, (blocks, length), 1)
        return column_sum(jnp.where(lane // each == block, spreaded, 0.0))

    size = wide // 4
    return [one(k * size, size) for k in range(6)], one(6 * size, wide)


def pack_vectors(vectors, last, blocks, lanes):
    size = last.shape[1] // blocks // 4

    def one(row, first, each):
        length = blocks * each
        source = lax.broadcasted_iota(jnp.int32, (length, lanes), 0)
        target = lax.broadcasted_iota(jnp.int32, (length, lanes), 1)
        pick = jnp.where(target == first + (source & (each - 1)), 1.0, 0.0).astype(bf16)
        block = lax.broadcasted_iota(jnp.int32, (blocks, length), 0)
        lane = lax.broadcasted_iota(jnp.int32, (blocks, length), 1)
        spreaded = jnp.where(lane // each == block, row, 0.0)
        total = jnp.zeros((blocks, lanes), f32)
        for _ in range(3):
            part = spreaded.astype(bf16)
            total = total + dot_nn(part, pick)
            spreaded = spreaded - part.astype(f32)
        return total

    total = one(last, 6 * size, 4 * size)
    for k, vector in enumerate(vectors):
        total = total + one(vector, k * size, size)
    return total


def edge_sums_kernel(plan, total, info, tokens, to_twin, to_other, ends):
    rows, width = tokens.shape
    center, rstd = ln_stats(tokens[...].astype(f32))
    plain = (center * rstd).astype(bf16)
    places = info[0] * rows + lax.broadcasted_iota(jnp.int32, (rows, width), 0)
    living = (plain.astype(f32) * live_counts(info, places, 0, total)).astype(bf16)
    size = 2 * LEVELS * HALO
    row = lax.broadcasted_iota(jnp.int32, (size, rows), 0)
    slot = lax.broadcasted_iota(jnp.int32, (size, rows), 1)
    row_one = lax.broadcasted_iota(jnp.int32, (size, 1), 0)
    wanted = jnp.zeros((size, rows), jnp.int32)
    shift = jnp.zeros((size, rows), jnp.int32)
    share = jnp.zeros((size, 1), f32)
    for k in range(2 * LEVELS):
        level, at = k % LEVELS, k * HALO
        first = 0 if k < LEVELS else plan.counts[level] - HALO
        wanted = jnp.where(row >= at, row - at + first, wanted)
        shift = jnp.where(row >= at, level, shift)
        share = jnp.where(row_one >= at, 0.5**level, share)
    pool = jnp.where((slot >> shift) == wanted, 1.0, 0.0).astype(bf16)
    ends[:, pl.ds(0, width)] = (dot_nn(pool, plain) * share).astype(bf16)
    ends[:, pl.ds(width, width)] = dot_nn(pool, living).astype(bf16)
    hand_out(info, ends, to_twin, to_other)


def edge_sums(plan, total, info, tokens):
    width = tokens.shape[1]
    size = LEVELS * HALO
    return pl.pallas_call(
        functools.partial(edge_sums_kernel, plan, total),
        out_shape=[jax.ShapeDtypeStruct((size, 2 * width), bf16)] * 2,
        in_specs=[SCALARS] + spec(1),
        out_specs=spec(2),
        scratch_shapes=[pltpu.VMEM((2 * size, 2 * width), bf16)],
        compiler_params=params(10),
        name="edge_sums",
        cost_estimate=cost(1.5),
    )(info, tokens)


def project_kernel(
    plan, total, info, inverse, tokens, from_twin, from_other, *refs
):
    pieces, outs = refs[:PIECES], refs[PIECES:]
    queries, pairs, halo_queries, halo_pairs = (outs[2 * k : 2 * k + 2] for k in range(4))
    weight, vectors, shift_out, table, edges, halos = outs[8:]
    rows, width = tokens.shape
    device = info[0]
    each = pieces[0].shape[0]
    block_rows = pieces[0].shape[1] // 4
    for p in range(PIECES * each):
        i = inverse[p]
        there = pl.ds(pl.multiple_of(i * block_rows, block_rows), block_rows)
        piece, q = pieces[p // each], p % each
        for c in range(3):
            weight[there, pl.ds(c * width, width)] = piece[q, pl.ds(block_rows * c, block_rows), :]
        line = piece[q, pl.ds(block_rows * 3, block_rows), pl.ds(0, 2 * LINE)].astype(f32)
        table[pl.ds(i, 1), :] = line[0:1]
    singles, wide = unpack_vectors(table[...].astype(bf16), 4 * block_rows)
    for k, single in enumerate(singles):
        vectors[pl.ds(k, 1), :] = single
    shift_out[...] = wide
    values = tokens[...].astype(f32)
    center, rstd = ln_stats(values)
    low = (center * rstd * singles[0] + singles[1]).astype(bf16)
    pooled_rows = plan.query_rows - plan.query_at[1]
    row = lax.broadcasted_iota(jnp.int32, (pooled_rows, rows), 0)
    slot = lax.broadcasted_iota(jnp.int32, (pooled_rows, rows), 1)
    first = jnp.zeros((pooled_rows, rows), jnp.int32)
    shift = jnp.zeros((pooled_rows, rows), jnp.int32)
    share = jnp.zeros((pooled_rows, 1), f32)
    row_one = lax.broadcasted_iota(jnp.int32, (pooled_rows, 1), 0)
    for level in range(1, LEVELS):
        at = plan.query_at[level] - plan.query_at[1]
        first = jnp.where(row >= at, at, first)
        shift = jnp.where(row >= at, level, shift)
        share = jnp.where(row_one >= at, 0.5**level, share)
    pool = jnp.where((slot >> shift) == row - first, 1.0, 0.0).astype(bf16)
    places = device * rows + lax.broadcasted_iota(jnp.int32, (rows, QUAD_WIDTH), 0)
    live = live_counts(info, places, 0, total)
    place_halos(info, from_twin, from_other, edges)
    size = LEVELS * HALO
    halos[:, pl.ds(0, width)] = (
        edges[:, pl.ds(0, width)].astype(f32) * singles[0] + singles[1]
    ).astype(bf16)
    for k in range(2 * LEVELS):
        level, here = k % LEVELS, pl.ds(k * HALO, HALO)
        count = plan.counts[level]
        first = device * count + (-HALO if k < LEVELS else count)
        place = first + lax.broadcasted_iota(jnp.int32, (HALO, 128), 0)
        counts = live_counts(info, place, level, total)
        counts = jnp.concatenate([counts] * (width // 128), axis=1)
        halos[here, pl.ds(width, width)] = (
            edges[here, pl.ds(width, width)].astype(f32) * singles[0] + counts * singles[1]
        ).astype(bf16)
    lanes = QUAD_WIDTH
    scale = 1.0 / math.sqrt(HEAD_DIM)
    for part in range(3 * width // lanes):
        columns = pl.ds(part * lanes, lanes)
        block = dot_nn(low, weight[:, columns]).astype(bf16)
        kind, quad = divmod(part, 2)
        if kind == 2:
            block = (block.astype(f32) * live).astype(bf16)
        pooled = dot_nn(pool, block)
        if kind < 2:
            pooled = pooled * share
        side = dot_nn(halos[:, pl.ds(width if kind == 2 else 0, width)], weight[:, columns])
        if kind == 0:
            queries[quad][pl.ds(0, rows), :] = (block.astype(f32) * scale).astype(bf16)
            queries[quad][pl.ds(rows, pooled_rows), :] = (pooled * scale).astype(bf16)
            halo_queries[quad][...] = (side * scale).astype(bf16)
        else:
            there = pl.ds((kind - 1) * lanes, lanes)
            pairs[quad][pl.ds(0, rows), there] = block
            pairs[quad][pl.ds(rows, pooled_rows), there] = pooled.astype(bf16)
            halo_pairs[quad][:, there] = side.astype(bf16)


def project(plan, total, info, inverse, tokens, from_twin, from_other, pieces):
    rows, width = tokens.shape
    halo = LEVELS * HALO
    blocks = PIECES * pieces[0].shape[0]
    depth = blocks * pieces[0].shape[1] // 4
    half = width // 2
    outs = pl.pallas_call(
        functools.partial(project_kernel, plan, total),
        out_shape=(
            [jax.ShapeDtypeStruct((plan.query_rows, half), bf16)] * 2
            + [jax.ShapeDtypeStruct((plan.query_rows, 2 * half), bf16)] * 2
            + [jax.ShapeDtypeStruct((2 * halo, half), bf16)] * 2
            + [jax.ShapeDtypeStruct((2 * halo, 2 * half), bf16)] * 2
            + [
                jax.ShapeDtypeStruct((depth, 3 * width), bf16),
                jax.ShapeDtypeStruct((8, depth), f32),
                jax.ShapeDtypeStruct((1, 4 * depth), f32),
            ]
        ),
        in_specs=[SCALARS, SCALARS] + spec(3 + PIECES),
        out_specs=spec(11),
        scratch_shapes=[
            pltpu.VMEM((blocks, 2 * LINE), f32),
            pltpu.VMEM((2 * halo, 2 * width), bf16),
            pltpu.VMEM((2 * halo, 2 * width), bf16),
        ],
        compiler_params=params(18),
        name="project",
        cost_estimate=cost(3.3),
    )(info, inverse, tokens, from_twin, from_other, *pieces)
    return [outs[2 * k : 2 * k + 2] for k in range(4)] + list(outs[8:])


def attend_kernel(plan, total, info, *refs):
    queries, pairs, halos, attended, mixed, scale, extended = (
        refs[2 * k : 2 * k + 2] for k in range(7)
    )
    numer, denom = refs[14:]
    rows = plan.rows
    device = info[0]
    for quad in range(2):
        fill_extended(plan, pairs[quad], halos[quad], extended[quad])
    first_head = lax.broadcasted_iota(jnp.int32, (BLOCK, 128), 1) < HEAD_DIM
    masks = head_masks(BLOCK)

    def prepare(block):
        level, part = plan.locate(block)
        here = pl.ds(pl.multiple_of(BLOCK * block, BLOCK), BLOCK)
        there = pl.ds(pl.multiple_of(BLOCK * block + 2 * HALO * level, BLOCK), WINDOW)
        first = device * (rows >> level) + BLOCK * part
        row = first + lax.broadcasted_iota(jnp.int32, (BLOCK, WINDOW), 0)
        column = first - HALO + lax.broadcasted_iota(jnp.int32, (BLOCK, WINDOW), 1)
        allowed = admitted(
            tile_codes(info, row, level, total, FAR),
            tile_codes(info, column, level, total, -FAR),
            level,
        )
        key_row = first - HALO + lax.broadcasted_iota(jnp.int32, (WINDOW, 128), 0)
        counts = live_counts(info, key_row, level, total).astype(bf16)
        return here, there, allowed, counts

    def block_step(step, carry):
        work = []
        for k in range(4):
            here, there, allowed, counts = prepare(step * 4 + k)
            allowed = jnp.concatenate([allowed] * 4, axis=0) > 0.0
            for part in range(8 // 4):
                work.append((here, there, allowed, counts, part))
        scores = []
        for here, there, allowed, counts, part in work:
            wide = 4 * HEAD_DIM
            quad, half = divmod(part * wide, QUAD_WIDTH)
            lanes = pl.ds(half, wide)
            q = spread_heads(queries[quad][here, lanes], masks)
            scores.append(dot_nt(q, extended[quad][there, lanes]))
        weights = [
            jnp.where(item[2], jnp.exp(score), 0.0).astype(bf16)
            for item, score in zip(work, scores)
        ]
        for (here, there, allowed, counts, part), weight in zip(work, weights):
            wide = 4 * HEAD_DIM
            for sub in range(4 // 2):
                pair = part * (4 // 2) + sub
                quad, half = divmod(pair, 2)
                v = extended[quad][there, pl.ds(QUAD_WIDTH + 128 * half, 128)]
                both = dot_nn(
                    weight[128 * sub : 128 * sub + 128], jnp.concatenate([v, counts], axis=1)
                )
                numer[pair, here, :] = join_pair(both[:, :128], first_head)
                denom[pair, here, :] = join_pair(both[:, 128:], first_head)
        return carry

    lax.fori_loop(0, len(plan.blocks) // 4, block_step, 0, unroll=1)
    places = device * rows + lax.broadcasted_iota(jnp.int32, (rows, 128), 0)
    live = live_counts(info, places, 0, total)
    for pair in range(4):
        for sums in (numer, denom):
            for level in range(LEVELS - 1, 0, -1):
                count = plan.counts[level]
                upper = sums[pair, pl.ds(plan.query_at[level], count), :]
                for parity in range(2):
                    there = pl.ds(plan.query_at[level - 1] + parity, count, stride=2)
                    sums[pair, there, :] = sums[pair, there, :] + upper
        quad, half = divmod(pair, 2)
        lanes = pl.ds(128 * half, 128)
        factor = live / (denom[pair, pl.ds(0, rows), :] + 1.0 - live)
        value = numer[pair, pl.ds(0, rows), :] * factor
        scale[quad][:, lanes] = factor
        mixed[quad][:, lanes] = value
        attended[quad][:, lanes] = value.astype(bf16)


def attend(plan, total, info, queries, pairs, halos):
    rows, width = plan.rows, queries[0].shape[1]
    outs = pl.pallas_call(
        functools.partial(attend_kernel, plan, total),
        out_shape=[jax.ShapeDtypeStruct((rows, width), bf16)] * 2
        + [jax.ShapeDtypeStruct((rows, width), f32)] * 4,
        in_specs=[SCALARS] + spec(6),
        out_specs=spec(6),
        scratch_shapes=[
            pltpu.VMEM((plan.key_rows, 2 * width), bf16),
            pltpu.VMEM((plan.key_rows, 2 * width), bf16),
            pltpu.VMEM((2 * width // 128, plan.query_rows, 128), f32),
            pltpu.VMEM((2 * width // 128, plan.query_rows, 128), f32),
        ],
        compiler_params=params(20),
        name="attend",
        cost_estimate=cost(8),
    )(info, *queries, *pairs, *halos)
    return outs[:2], outs[2:4], outs[4:]


def forward_kernel(
    parts,
    inverse,
    sums_inverse,
    tokens,
    cotangent,
    attended_a,
    attended_b,
    vectors,
    shift_in,
    *refs,
):
    pieces = refs[:parts]
    result, resid_out, grad_normed, w_out, own, low_half, high_half, sum_in = refs[
        parts : parts + 8
    ]
    w_in, w_back, normed_two, outer, tall, flat = refs[parts + 8 :]
    other = (low_half, high_half)
    width = tokens.shape[1]
    wide = width // 2
    each = pieces[0].shape[0]
    half = own.shape[0]
    chunks = w_in.shape[0]
    block = width // (parts * each)
    tall_block = chunks * block
    back_at = block + tall_block
    for p in range(parts * each):
        piece, q = pieces[p // each], p % each
        i = inverse[p]
        rows = pl.ds(pl.multiple_of(i * block, block), block)
        w_out[rows, :] = piece[q, pl.ds(0, block), :]
        for c in range(chunks):
            w_in[c, rows, :] = piece[q, pl.ds(block * (c + 1), block), :]
        rows = pl.ds(pl.multiple_of(i * tall_block, tall_block), tall_block)
        w_back[rows, :] = piece[q, pl.ds(back_at, tall_block), :]
    gain = vectors[pl.ds(3, 1), :]
    resid = tokens[...].astype(f32) + dot_nn(attended_a[...], w_out[pl.ds(0, wide), :])
    resid = resid + dot_nn(attended_b[...], w_out[pl.ds(wide, wide), :]) + vectors[pl.ds(2, 1), :]
    center, rstd = ln_stats(resid)
    normed_two[...] = (center * rstd * gain + vectors[pl.ds(4, 1), :]).astype(bf16)
    resid_out[...] = resid
    outer[...] = jnp.zeros(outer.shape, f32)
    grad_normed[...] = jnp.zeros(grad_normed.shape, f32)

    def chunk_step(c, carry):
        there = pl.ds(pl.multiple_of(c * width, width), width)
        inner = dot_nn(normed_two[...], w_in[c]) + shift_in[:, there]
        cdf = 0.5 * (1.0 + lax.erf(inner * math.sqrt(0.5)))
        active = (inner * cdf).astype(bf16)
        slope = cdf + inner * (jnp.exp(-0.5 * inner * inner) * (1.0 / math.sqrt(2.0 * math.pi)))
        back = w_back[there, :]
        grad_inner = slope * dot_nt(cotangent[...], back)
        low = grad_inner.astype(bf16)
        outer[...] += dot_nn(active, back)
        tall[there, :] = dot_tn(active, cotangent[...]).astype(bf16)
        sum_in[:, there] = column_sum(low.astype(f32))
        flat[...] = dot_tn(normed_two[...], low).astype(bf16)
        for p in range(2 * half):
            i = sums_inverse[p]
            rows = flat[pl.ds(pl.multiple_of(i * block, block), block), :]
            at = pl.ds(pl.multiple_of(c * block, block), block)
            if p < half:
                own[p, at, :] = rows
            else:
                other[(p - half) // 8][(p - half) % 8, at, :] = rows
        grad_normed[...] += dot_nt(low, w_in[c])
        return carry

    lax.fori_loop(0, chunks, chunk_step, 0)
    result[...] = (resid_out[...] + outer[...] + vectors[pl.ds(5, 1), :]).astype(bf16)
    for p in range(2 * half):
        i = sums_inverse[p]
        rows = tall[pl.ds(pl.multiple_of(i * tall_block, tall_block), tall_block), :]
        there = pl.ds(tall_block, tall_block)
        if p < half:
            own[p, there, :] = rows
        else:
            other[(p - half) // 8][(p - half) % 8, there, :] = rows


def feed_forward(inverses, tokens, cotangent, attended, vectors, shift_in, pieces):
    parts = len(pieces)
    rows, width = tokens.shape
    hidden = shift_in.shape[1]
    chunks = hidden // width
    blocks = parts * pieces[0].shape[0]
    stack = pieces[0].shape[1] - width // blocks
    return pl.pallas_call(
        functools.partial(forward_kernel, parts),
        out_shape=(
            jax.ShapeDtypeStruct((rows, width), bf16),
            jax.ShapeDtypeStruct((rows, width), f32),
            jax.ShapeDtypeStruct((rows, width), f32),
            jax.ShapeDtypeStruct((width, width), bf16),
            jax.ShapeDtypeStruct((blocks // 2, stack, width), bf16),
            jax.ShapeDtypeStruct((blocks // 4, stack, width), bf16),
            jax.ShapeDtypeStruct((blocks // 4, stack, width), bf16),
            jax.ShapeDtypeStruct((1, hidden), f32),
        ),
        in_specs=[SCALARS] * 2 + spec(6 + parts),
        out_specs=tuple(spec(8)),
        scratch_shapes=[
            pltpu.VMEM((chunks, width, width), bf16),
            pltpu.VMEM((hidden, width), bf16),
            pltpu.VMEM((rows, width), bf16),
            pltpu.VMEM((rows, width), f32),
            pltpu.VMEM((hidden, width), bf16),
            pltpu.VMEM((width, width), bf16),
        ],
        compiler_params=params(30),
        name="feed_forward",
        cost_estimate=cost(10),
    )(*inverses, tokens, cotangent, *attended, vectors, shift_in, *pieces)


def middle_kernel(
    plan,
    info,
    sums_inverse,
    cotangent,
    attended_a,
    attended_b,
    mixed_a,
    mixed_b,
    scale_a,
    scale_b,
    vectors,
    resid,
    grad_normed,
    w_out,
    grad_resid,
    grads_a,
    grads_b,
    to_twin,
    to_other,
    sums,
    own,
    low_half,
    high_half,
    levels,
    ends,
    denoms,
    flat,
):
    width = cotangent.shape[1]
    wide = width // 2
    center, rstd = ln_stats(resid[...])
    grad_in, gain_terms = ln_back(grad_normed[...], center, rstd, vectors[pl.ds(3, 1), :])
    grad_out = cotangent[...].astype(f32)
    total = grad_out + grad_in
    grad_resid[...] = total
    low = total.astype(bf16)
    sums[pl.ds(0, 1), :] = jnp.zeros((1, width), f32)
    sums[pl.ds(1, 1), :] = jnp.zeros((1, width), f32)
    sums[pl.ds(2, 1), :] = column_sum(low.astype(f32))
    sums[pl.ds(3, 1), :] = column_sum(gain_terms)
    sums[pl.ds(4, 1), :] = column_sum(grad_normed[...])
    sums[pl.ds(5, 1), :] = column_sum(grad_out)
    for quad in range(2):
        lines = pl.ds(quad * wide, wide)
        flat[lines, :] = dot_tn((attended_a, attended_b)[quad][...], low).astype(bf16)
        numer = dot_nt(low, w_out[lines, :]) * (scale_a, scale_b)[quad][...]
        denom = -(numer * (mixed_a, mixed_b)[quad][...])
        for chunk in range(2 * wide // 128):
            source = numer if chunk < wide // 128 else denom
            lane = chunk * 128 % wide
            levels[chunk, pl.ds(0, plan.rows), :] = source[:, lane : lane + 128]
            for level in range(1, LEVELS):
                count, at = plan.counts[level], plan.query_at[level]
                below = plan.query_at[level - 1]
                levels[chunk, pl.ds(at, count), :] = (
                    levels[chunk, pl.ds(below, count, stride=2), :]
                    + levels[chunk, pl.ds(below + 1, count, stride=2), :]
                )
                rest = plan.padded[level] - count
                if rest:
                    levels[chunk, pl.ds(at + count, rest), :] = jnp.zeros((rest, 128), f32)
            grads = (grads_a, grads_b)[quad]
            grads[:, pl.ds(chunk * 128, 128)] = levels[chunk].astype(bf16)
        for k in range(2 * LEVELS):
            level, here = k % LEVELS, pl.ds(k * HALO, HALO)
            at = plan.query_at[level] + (0 if k < LEVELS else plan.counts[level] - HALO)
            there = pl.ds(at, HALO)
            ends[here, pl.ds(quad * wide, wide)] = (grads_a, grads_b)[quad][there, pl.ds(0, wide)]
            for chunk in range(wide // 128):
                lanes = pl.ds(quad * wide + chunk * 128, 128)
                denoms[here, lanes] = levels[wide // 128 + chunk, there, :]
    feature = lax.broadcasted_iota(jnp.int32, (width, LINE), 0)
    lane = lax.broadcasted_iota(jnp.int32, (width, LINE), 1)
    pick = jnp.where(lane == feature // HEAD_DIM, 1.0, 0.0).astype(bf16)
    heads = width // HEAD_DIM
    values = denoms[...]
    first = values.astype(bf16)
    values = dot_nn(first, pick) + dot_nn((values - first.astype(f32)).astype(bf16), pick)
    first = values.astype(bf16).astype(f32)
    both = jnp.concatenate([first[:, :heads], (values - first)[:, :heads]], axis=1)
    both = jnp.concatenate([both, jnp.zeros((both.shape[0], LINE - 2 * heads), f32)], axis=1)
    ends[:, pl.ds(width, LINE)] = both.astype(bf16)
    hand_out(info, ends, to_twin, to_other)
    half, block = own.shape[0], own.shape[1]
    other = (low_half, high_half)
    for p in range(2 * half):
        rows = flat[pl.ds(pl.multiple_of(sums_inverse[p] * block, block), block), :]
        if p < half:
            own[p] = rows
        else:
            other[(p - half) // 8][(p - half) % 8] = rows


def middle(plan, info, sums_inverse, cotangent, attended, mixed, scale, vectors, resid, grad_normed, w_out):
    rows, width = cotangent.shape
    size = LEVELS * HALO
    return pl.pallas_call(
        functools.partial(middle_kernel, plan),
        out_shape=(
            jax.ShapeDtypeStruct((rows, width), f32),
            jax.ShapeDtypeStruct((plan.query_rows, width), bf16),
            jax.ShapeDtypeStruct((plan.query_rows, width), bf16),
            jax.ShapeDtypeStruct((size, width + LINE), bf16),
            jax.ShapeDtypeStruct((size, width + LINE), bf16),
            jax.ShapeDtypeStruct((8, width), f32),
            jax.ShapeDtypeStruct((BLOCKS // 2, width // BLOCKS, width), bf16),
            jax.ShapeDtypeStruct((BLOCKS // 4, width // BLOCKS, width), bf16),
            jax.ShapeDtypeStruct((BLOCKS // 4, width // BLOCKS, width), bf16),
        ),
        in_specs=[SCALARS] * 2 + spec(11),
        out_specs=tuple(spec(9)),
        scratch_shapes=[
            pltpu.VMEM((width // 128, plan.query_rows, 128), f32),
            pltpu.VMEM((2 * size, width + LINE), bf16),
            pltpu.VMEM((2 * size, width), f32),
            pltpu.VMEM((width, width), bf16),
        ],
        compiler_params=params(20),
        name="middle",
        cost_estimate=cost(3),
    )(info, sums_inverse, cotangent, *attended, *mixed, *scale, vectors, resid, grad_normed, w_out)


def attend_back_kernel(plan, total, info, *refs):
    queries, pairs, halos, grads, grad_queries, grad_extended, extended = (
        refs[2 * k : 2 * k + 2] for k in range(7)
    )
    device = info[0]
    width = QUAD_WIDTH
    for quad in range(2):
        fill_extended(plan, pairs[quad], halos[quad], extended[quad])
        grad_extended[quad][...] = jnp.zeros(grad_extended[quad].shape, f32)
    masks = head_masks(BLOCK)
    first_head = lax.broadcasted_iota(jnp.int32, (BLOCK, 128), 1) < HEAD_DIM
    keys = pl.ds(0, width)
    values = pl.ds(width, width)

    def prepare(block):
        level, part = plan.locate(block)
        here = pl.ds(pl.multiple_of(BLOCK * block, BLOCK), BLOCK)
        there = pl.ds(pl.multiple_of(BLOCK * block + 2 * HALO * level, BLOCK), WINDOW)
        first = device * (plan.rows >> level) + BLOCK * part
        key_row = first - HALO + lax.broadcasted_iota(jnp.int32, (WINDOW, 128), 0)
        lane = lax.broadcasted_iota(jnp.int32, (WINDOW, 128), 1)
        row = first + (lane & (BLOCK - 1))
        allowed = admitted(
            tile_codes(info, row, level, total, FAR),
            tile_codes(info, key_row, level, total, -FAR),
            level,
        )
        allowed = jnp.concatenate([allowed] * (QUAD * BLOCK // 128), axis=1) > 0.0
        counts = live_counts(info, key_row, level, total).astype(bf16)
        return here, there, allowed, counts

    def block_step(step, carry):
        work = []
        for k in range(4):
            here, there, allowed, counts = prepare(step * 4 + k)
            for quad in range(2):
                q = spread_heads(queries[quad][here, :], masks)
                g = spread_heads(grads[quad][here, keys], masks)
                d = spread_heads(grads[quad][here, values], masks)
                work.append((quad, here, there, allowed, counts, q, g, d))
        scores, grad_probs = [], []
        for quad, here, there, allowed, counts, q, g, d in work:
            scores.append(dot_nt(extended[quad][there, keys], q))
            v = extended[quad][there, values]
            value_and_count = jnp.concatenate([v] + [counts] * (width // 128), axis=1)
            grad_probs.append(dot_nt(value_and_count, jnp.concatenate([g, d], axis=1)))
        weights = [
            jnp.where(item[3], jnp.exp(score), 0.0) for item, score in zip(work, scores)
        ]
        grad_scores = [(x * y).astype(bf16) for x, y in zip(grad_probs, weights)]
        probs = [weight.astype(bf16) for weight in weights]
        keys_of = [extended[item[0]][item[2], keys] for item in work]
        to_queries = [
            [
                dot_tn(grad_score[:, 128 * half : 128 * half + 128], k[:, 128 * half : 128 * half + 128])
                for half in range(2)
            ]
            for grad_score, k in zip(grad_scores, keys_of)
        ]
        to_keys = [dot_nn(grad_score, item[5]) for grad_score, item in zip(grad_scores, work)]
        to_values = [dot_nn(prob, item[6]) for prob, item in zip(probs, work)]
        for item, parts, to_key, to_value in zip(work, to_queries, to_keys, to_values):
            quad, here, there = item[:3]
            for half in range(2):
                grad_queries[quad][here, pl.ds(128 * half, 128)] = join_pair(
                    parts[half], first_head
                ) * (1.0 / math.sqrt(HEAD_DIM))
            grad_extended[quad][there, keys] += to_key
            grad_extended[quad][there, values] += to_value
        return carry

    lax.fori_loop(0, len(plan.blocks) // 4, block_step, 0, unroll=1)


def attend_back(plan, total, info, queries, pairs, halos, grads):
    width = queries[0].shape[1]
    outs = pl.pallas_call(
        functools.partial(attend_back_kernel, plan, total),
        out_shape=[jax.ShapeDtypeStruct((plan.query_rows, width), f32)] * 2
        + [jax.ShapeDtypeStruct((plan.key_rows, 2 * width), f32)] * 2,
        in_specs=[SCALARS] + spec(8),
        out_specs=spec(4),
        scratch_shapes=[
            pltpu.VMEM((plan.key_rows, 2 * width), bf16),
            pltpu.VMEM((plan.key_rows, 2 * width), bf16),
        ],
        compiler_params=params(24),
        name="attend_back",
        cost_estimate=cost(12),
    )(info, *queries, *pairs, *halos, *grads)
    return outs[:2], outs[2:]


def edge_back_kernel(
    plan,
    total,
    info,
    queries_a,
    queries_b,
    pairs_a,
    pairs_b,
    from_twin,
    from_other,
    low,
    high,
    grads,
):
    width = queries_a.shape[1]
    device = info[0]
    place_halos(info, from_twin, from_other, grads)
    two = 2 * HALO
    masks = head_masks(two)
    keys = pl.ds(0, width)
    key = lax.broadcasted_iota(jnp.int32, (two, 128), 0)
    lane = lax.broadcasted_iota(jnp.int32, (two, 128), 1) & (two - 1)
    heads = 2 * width // HEAD_DIM
    source = lax.broadcasted_iota(jnp.int32, (LINE, width), 0)
    target = lax.broadcasted_iota(jnp.int32, (LINE, width), 1)
    picks = []
    for quad in range(2):
        head = target // HEAD_DIM + quad * QUAD
        wanted = jnp.where(target % HEAD_DIM == 0, head, -1)
        wanted = jnp.where(target % HEAD_DIM == 1, head + heads, wanted)
        picks.append(jnp.where(source == wanted, 1.0, 0.0).astype(bf16))
    facing = jnp.where((key < HALO) == (lane < HALO), 1.0, 0.0)
    for level in range(LEVELS):
        count, at = plan.counts[level], plan.query_at[level]
        start = device * count
        key_row = start + jnp.where(key < HALO, key, count - two + key)
        row = start + jnp.where(lane < HALO, lane - HALO, count - HALO + lane)
        allowed = facing * admitted(
            tile_codes(info, row, level, total, FAR),
            tile_codes(info, key_row, level, total, -FAR),
            level,
        )
        allowed = jnp.concatenate([allowed] * (QUAD * two // 128), axis=1) > 0.0
        counts = live_counts(info, key_row, level, total).astype(bf16)
        ahead = pl.ds(HALO * level, HALO)
        behind = pl.ds(HALO * (LEVELS + level), HALO)

        def both(source, lanes):
            return jnp.concatenate([source[ahead, lanes], source[behind, lanes]], axis=0)

        denoms = both(grads, pl.ds(2 * width, LINE))
        for quad in range(2):
            pairs = (pairs_a, pairs_b)[quad]
            own = jnp.concatenate(
                [pairs[pl.ds(at, HALO), :], pairs[pl.ds(at + count - HALO, HALO), :]], axis=0
            )
            k, v = own[:, :width], own[:, width:]
            q = spread_heads(both((queries_a, queries_b)[quad], keys), masks)
            g = spread_heads(both(grads, pl.ds(quad * width, width)), masks)
            d = spread_heads(dot_nn(denoms, picks[quad]).astype(bf16), masks)
            value_and_count = jnp.concatenate([v] + [counts] * (width // 128), axis=1)
            weight = jnp.where(allowed, jnp.exp(dot_nt(k, q)), 0.0)
            grad_probs = dot_nt(value_and_count, jnp.concatenate([g, d], axis=1))
            grad_score = (grad_probs * weight).astype(bf16)
            there = pl.ds(HALO * (quad * LEVELS + level), HALO)
            grad_keys = dot_nn(grad_score, q)
            grad_values = dot_nn(weight.astype(bf16), g)
            low[there, keys] = grad_keys[:HALO]
            high[there, keys] = grad_keys[HALO:]
            low[there, pl.ds(width, width)] = grad_values[:HALO]
            high[there, pl.ds(width, width)] = grad_values[HALO:]


def edge_back(plan, total, info, queries, pairs, from_twin, from_other):
    width = queries[0].shape[1]
    size = 2 * LEVELS * HALO
    return pl.pallas_call(
        functools.partial(edge_back_kernel, plan, total),
        out_shape=[jax.ShapeDtypeStruct((size, 2 * width), f32)] * 2,
        in_specs=[SCALARS] + spec(6),
        out_specs=spec(2),
        scratch_shapes=[pltpu.VMEM((size, 2 * width + LINE), bf16)],
        compiler_params=params(10),
        name="edge_back",
        cost_estimate=cost(2.5),
    )(info, *queries, *pairs, from_twin, from_other)


def finish_kernel(
    plan,
    total,
    info,
    inverse,
    tokens,
    weight,
    vectors,
    grad_resid,
    sums,
    sum_in,
    queries_a,
    queries_b,
    pairs_a,
    pairs_b,
    edge_low,
    edge_high,
    grad_tokens,
    own,
    low_half,
    high_half,
    work,
    joined,
    flat,
    table,
):
    rows, width = tokens.shape
    device = info[0]
    half_width = width // 2
    places = device * rows + lax.broadcasted_iota(jnp.int32, (rows, 128), 0)
    live = live_counts(info, places, 0, total)
    for chunk in range(3 * width // 128):
        part, lane = divmod(chunk * 128, width)
        quad, lane = divmod(lane, half_width)
        if part == 0:
            work[chunk] = (queries_a, queries_b)[quad][:, pl.ds(lane, 128)]
        else:
            lanes = pl.ds((part - 1) * half_width + lane, 128)
            for level in range(LEVELS):
                at, count = plan.query_at[level], plan.counts[level]
                own_rows = pl.ds(plan.key_at[level] + HALO, count)
                work[chunk, pl.ds(at, count), :] = (pairs_a, pairs_b)[quad][own_rows, lanes]
                halo = pl.ds(HALO * (quad * LEVELS + level), HALO)
                work[chunk, pl.ds(at, HALO), :] += edge_low[halo, lanes]
                work[chunk, pl.ds(at + count - HALO, HALO), :] += edge_high[halo, lanes]
        for level in range(LEVELS - 1, 0, -1):
            count = plan.counts[level]
            upper = work[chunk, pl.ds(plan.query_at[level], count), :]
            if chunk * 128 < 2 * width:
                upper = upper * 0.5
            for parity in range(2):
                there = pl.ds(plan.query_at[level - 1] + parity, count, stride=2)
                work[chunk, there, :] = work[chunk, there, :] + upper
        value = work[chunk, pl.ds(0, rows), :]
        if chunk * 128 >= 2 * width:
            value = value * live
        joined[:, pl.ds(chunk * 128, 128)] = value.astype(bf16)
    values = tokens[...].astype(f32)
    center, rstd = ln_stats(values)
    gain = vectors[pl.ds(0, 1), :]
    normed = (center * rstd * gain + vectors[pl.ds(1, 1), :]).astype(bf16)
    half, block = own.shape[0], own.shape[1] // 4
    other = (low_half, high_half)
    for part in range(3):
        columns = pl.ds(part * width, width)
        flat[...] = dot_tn(normed, joined[:, columns])
        for p in range(2 * half):
            i = inverse[p]
            lines = flat[pl.ds(pl.multiple_of(i * block, block), block), :]
            there = pl.ds(part * block, block)
            if p < half:
                own[p, there, :] = lines.astype(bf16)
            else:
                other[(p - half) // 8][(p - half) % 8, there, :] = lines.astype(bf16)
    grad_normed = dot_nt(joined[...], weight[...])
    grad_in, gain_terms = ln_back(grad_normed, center, rstd, gain)
    grad_tokens[...] = grad_resid[...] + grad_in
    singles = [column_sum(gain_terms), column_sum(grad_normed)]
    singles += [sums[pl.ds(k, 1), :] for k in range(2, 6)]
    table[...] = pack_vectors(singles, sum_in[...], 2 * half, table.shape[1])
    row = lax.broadcasted_iota(jnp.int32, (block, 2 * LINE), 0)
    there = pl.ds(3 * block, block)
    for p in range(2 * half):
        i = inverse[p]
        line = table[pl.ds(i, 1), :]
        lines = jnp.where(row == 0, line, 0.0)
        lines = jnp.concatenate([lines, jnp.zeros((block, width - 2 * LINE), f32)], axis=1)
        if p < half:
            own[p, there, :] = lines.astype(bf16)
        else:
            other[(p - half) // 8][(p - half) % 8, there, :] = lines.astype(bf16)


def finish(plan, total, info, inverse, tokens, weight, *rest):
    rows, width = tokens.shape
    half = BLOCKS // 2
    block = width // BLOCKS
    return pl.pallas_call(
        functools.partial(finish_kernel, plan, total),
        out_shape=(
            jax.ShapeDtypeStruct((rows, width), f32),
            jax.ShapeDtypeStruct((half, 4 * block, width), bf16),
            jax.ShapeDtypeStruct((half // 2, 4 * block, width), bf16),
            jax.ShapeDtypeStruct((half // 2, 4 * block, width), bf16),
        ),
        in_specs=[SCALARS, SCALARS] + spec(2 + len(rest)),
        out_specs=tuple(spec(4)),
        scratch_shapes=[
            pltpu.VMEM((3 * width // 128, plan.query_rows, 128), f32),
            pltpu.VMEM((rows, 3 * width), bf16),
            pltpu.VMEM((width, width), f32),
            pltpu.VMEM((BLOCKS, 2 * LINE), f32),
        ],
        compiler_params=params(28),
        name="finish",
        cost_estimate=cost(6.2),
    )(info, inverse, tokens, weight, *rest)


class Ring:
    def __init__(self, devices, *orders):
        self.devices = devices
        self.orders = orders
        self.stages = len(orders[0])

    def partner(self, stage):
        return [(i, i ^ self.orders[i & 1][stage]) for i in range(self.devices)]

    def twin(self):
        return [(i, i ^ 1) for i in range(self.devices)]

    def places(self, device):
        found = []
        even = (device & 1) == 0
        for base, swap in ((device, False), (device ^ 1, True)):
            for position in range(1 << self.stages):
                masks = [
                    sum(order[k] for k in range(self.stages) if position >> k & 1)
                    for order in self.orders
                ]
                if swap:
                    masks = masks[::-1]
                found.append(base ^ jnp.where(even, *masks))
        return found

    def step(self, stage, arrays):
        route = self.twin() if stage == self.stages else self.partner(stage)
        return [lax.ppermute(item, "seq", route) for item in arrays]

    def fold(self, stage, own, low, high):
        half = 1 << stage
        sent = (own[half:].astype(f32) + high.astype(f32)).astype(bf16)
        kept = own[:half].astype(f32) + low.astype(f32)
        return kept, sent


def halves(item):
    half = item.shape[0] // 2
    return item[:half], item[half:]


def join(held, came):
    return [jnp.concatenate(pair) for pair in zip(held, came)]


def pack_kernel(rings, lengths, w_qkv, w_out, w_in, w_back, *refs):
    vectors, (info, *inverses, payload, staged) = refs[:-5], refs[-5:]
    device = lax.axis_index("seq")
    info[0] = device
    start = jnp.int32(0)
    for k in range(3):
        length = lengths[k]
        info[1 + k] = length
        info[4 + k] = start
        start = start + (length + 15) // 16 * 16
        info[7 + k] = start
    for ring, inverse in zip(rings, inverses):
        for place, block in enumerate(ring.places(device)):
            inverse[place] = block
    block, width = w_out.shape
    chunks = w_in.shape[1] // width
    staged[...] = jnp.zeros(staged.shape, f32)
    for k, vector in enumerate(vectors):
        size = vector.shape[0]
        lane = k * block
        staged[pl.ds(0, 1), pl.ds(lane, size)] = vector[...].astype(f32).reshape(1, size)
    for c in range(3):
        payload[0, pl.ds(block * c, block), :] = w_qkv[:, pl.ds(c * width, width)]
    payload[0, pl.ds(block * 3, block), :] = staged[...].astype(bf16)
    payload[0, pl.ds(block * 4, block), :] = w_out[...]
    for c in range(chunks):
        payload[0, pl.ds(block * (c + 5), block), :] = w_in[:, pl.ds(c * width, width)]
    payload[0, pl.ds(block * (chunks + 5), block * chunks), :] = w_back[...]


def pack(rings, lengths, w_qkv, w_out, w_in, w_back, vectors):
    block, width = w_out.shape
    rows = 5 * block + w_in.shape[1] // width * block + w_back.shape[0]
    return pl.pallas_call(
        functools.partial(pack_kernel, rings),
        out_shape=(
            jax.ShapeDtypeStruct((10,), jnp.int32),
            jax.ShapeDtypeStruct((BLOCKS,), jnp.int32),
            jax.ShapeDtypeStruct((BLOCKS,), jnp.int32),
            jax.ShapeDtypeStruct((1, rows, width), bf16),
        ),
        in_specs=[SCALARS] + spec(4 + len(vectors)),
        out_specs=(SCALARS,) * 3 + tuple(spec(1)),
        scratch_shapes=[pltpu.VMEM((block, width), f32)],
        compiler_params=params(62),
        name="pack",
        cost_estimate=cost(1.5),
    )(lengths, w_qkv, w_out, w_in, w_back, *vectors)


def unpack_kernel(kept_one, came_one, kept_two, came_two, *outs):
    block, width = kept_one.shape[1] // 4, kept_two.shape[2]
    w_qkv, w_out, w_in, w_back = outs[:4]
    for c in range(3):
        rows = pl.ds(block * c, block)
        w_qkv[:, pl.ds(c * width, width)] = kept_one[0, rows, :] + came_one[0, rows, :].astype(f32)
    rows = pl.ds(block * 3, block)
    lines = kept_one[0, rows, :] + came_one[0, rows, :].astype(f32)
    for k, out in enumerate(outs[4:]):
        size = out.shape[0]
        lane = k * block
        out[...] = lines[0:1, lane : lane + size].reshape(size)
    chunks = w_in.shape[1] // width

    def total(at, size):
        rows = pl.ds(at, size)
        return kept_two[0, rows, :] + came_two[0, rows, :].astype(f32)

    w_out[...] = total(2 * block * chunks, block)
    for c in range(chunks):
        w_in[:, pl.ds(c * width, width)] = total(block * c, block)
    w_back[...] = total(block * chunks, block * chunks)


def unpack(kept_one, came_one, kept_two, came_two, like):
    return pl.pallas_call(
        unpack_kernel,
        out_shape=[jax.ShapeDtypeStruct(item.shape, f32) for item in like],
        in_specs=spec(4),
        out_specs=spec(len(like)),
        compiler_params=params(62),
        name="unpack",
        cost_estimate=cost(1.5),
    )(kept_one, came_one, kept_two, came_two)


def exchange(to_twin, to_other):
    count = lax.axis_size("seq")
    twin = [(i, i ^ 1) for i in range(count)]
    other = [(i, i + 1) for i in range(1, count - 1, 2)]
    other += [(j, i) for i, j in other]
    return lax.ppermute(to_other, "seq", other), lax.ppermute(to_twin, "seq", twin)


def order(items, *after):
    return lax.optimization_barrier((items, after))[0]


def per_device(
    lengths,
    tokens,
    ln1_gain,
    ln1_bias,
    w_qkv,
    w_out,
    out_bias,
    ln2_gain,
    ln2_bias,
    w_in,
    in_bias,
    w_back,
    back_bias,
    cotangent,
):
    devices = lax.axis_size("seq")
    device = lax.axis_index("seq")
    rows, width = tokens.shape
    total = rows * devices
    plan = Plan(rows)
    block = width // BLOCKS
    chunks = w_in.shape[1] // width
    small = (ln1_gain, ln1_bias, out_bias, ln2_gain, ln2_bias, back_bias, in_bias)
    direct = devices == BLOCKS
    ring = Ring(BLOCKS, (16, 8, 4, 2), (2, 16, 8, 4))
    sums_ring = Ring(BLOCKS, (16, 8, 4, 2), (2, 16, 8, 4))
    last = ring.stages - 1
    core = ring.stages
    if direct:
        info, inverse, sums_inverse, payload = pack(
            (ring, sums_ring), lengths, w_qkv, w_out, w_in, w_back, small
        )
        from_other, from_twin = exchange(*edge_sums(plan, total, info, order(tokens, payload)))
        (payload,) = join([payload], ring.step(0, [payload]))
        a, b = payload[:, : 4 * block], payload[:, 4 * block :]
        a_came, b_came = ring.step(1, [a, b])
        (a,) = join([a], [a_came])
        a = order(a, from_other, from_twin)
        (a_came,) = ring.step(2, [a])
        (a,) = join([a], [a_came])
        (b,) = join([b], [b_came])
        a = order(a, b)
        (b_came,) = ring.step(2, [b])
        (a_came,) = ring.step(3, [a])
        one = [a, a_came] + ring.step(core, [a, a_came])
        (b,) = join([b], [b_came])
        b = order(b, one)
    else:
        padded = (lengths + 15) // 16 * 16
        ends = jnp.cumsum(padded, dtype=jnp.int32)
        info = jnp.concatenate([device[None].astype(jnp.int32), lengths, ends - padded, ends])
        inverse = sums_inverse = jnp.arange(BLOCKS, dtype=jnp.int32)
        from_other, from_twin = exchange(*edge_sums(plan, total, info, tokens))

        def whole(item):
            return lax.all_gather(item, "seq", axis=0, tiled=True)

        def split(item, parts):
            each = BLOCKS // parts
            return [item[k * each : (k + 1) * each] for k in range(parts)]

        line = jnp.concatenate([whole(item).reshape(BLOCKS, 1, -1) for item in small], axis=2)
        line = jnp.pad(line, ((0, 0), (0, block - 1), (0, width - line.shape[2])))
        one = whole(w_qkv).reshape(BLOCKS, block, 3, width).transpose(0, 2, 1, 3)
        one = one.reshape(BLOCKS, 3 * block, width)
        one = split(jnp.concatenate([one, line], axis=1), PIECES)
        full_in = whole(w_in).reshape(BLOCKS, block, chunks, width)
        full_in = full_in.transpose(0, 2, 1, 3).reshape(BLOCKS, chunks * block, width)
        full_two = [
            whole(w_out).reshape(BLOCKS, block, width),
            full_in,
            whole(w_back).reshape(BLOCKS, chunks * block, width),
        ]
        two = split(jnp.concatenate(full_two, axis=1), PIECES)
    queries, pairs, halo_queries, halo_pairs, weight, vectors, shift_in = project(
        plan, total, info, inverse, tokens, from_twin, from_other, one
    )
    ready = queries[0]
    if direct:
        (b_came,) = ring.step(last, [b])
        (b_twin,) = ring.step(core, [b])
        ready = order(ready, b)
    attended, mixed, scale = attend(plan, total, info, (ready, queries[1]), pairs, halo_pairs)
    if direct:
        b_came = order(b_came, attended)
        two = [b, b_came, b_twin] + ring.step(core, [b_came])
    result, resid, grad_normed, out_weight, own_two, low_two, high_two, sum_in = feed_forward(
        (inverse, sums_inverse), tokens, cotangent, attended, vectors, shift_in, two
    )
    if direct:
        high, low = sums_ring.step(core, [high_two, low_two])
    (
        grad_resid,
        grads_a,
        grads_b,
        to_twin,
        to_other,
        sums,
        own_out,
        low_out,
        high_out,
    ) = middle(
        plan,
        info,
        sums_inverse,
        cotangent,
        attended,
        mixed,
        scale,
        vectors,
        resid,
        grad_normed,
        out_weight,
    )
    from_other, from_twin = exchange(to_twin, to_other)

    def with_out(item, out):
        return jnp.concatenate([item, out], axis=1)

    if direct:
        high_out, low_out = sums_ring.step(core, [high_out, low_out])
        kept, sent = sums_ring.fold(
            last, with_out(own_two, own_out), with_out(low, low_out), with_out(high, high_out)
        )
        sent_low, sent_high = halves(sent)
        (high,) = sums_ring.step(last, [sent_high])
        grads_a = order(grads_a, sent_high)
    grad_queries, grad_pairs = attend_back(
        plan, total, info, queries, pairs, halo_pairs, (grads_a, grads_b)
    )
    from_other, from_twin = order((from_other, from_twin), grad_queries)
    if direct:
        sent_low, high = order((sent_low, high), grad_queries, from_other, from_twin)
        (low,) = sums_ring.step(last, [sent_low])
        kept, kept_high = halves(kept)
        sent = (kept_high + high.astype(f32)).astype(bf16)
        (came,) = sums_ring.step(last - 1, [sent])
        from_other, from_twin = order((from_other, from_twin), sent_low, sent)
    edges = edge_back(plan, total, info, halo_queries, pairs, from_twin, from_other)
    grad_tokens, own_one, low_one, high_one = finish(
        plan,
        total,
        info,
        sums_inverse,
        tokens,
        weight,
        vectors,
        grad_resid,
        sums,
        sum_in,
        *grad_queries,
        *grad_pairs,
        *edges,
    )
    if direct:
        high_one, low_one = sums_ring.step(core, [high_one, low_one])
        low, came = order((low, came), grad_tokens)
        kept = kept + low.astype(f32)
        kept, sent = sums_ring.fold(last - 2, kept, *halves(came))
        (came,) = sums_ring.step(last - 2, [sent])
        high_one, low_one = order((high_one, low_one), sent)
        own_one, sent_one = sums_ring.fold(last, own_one, low_one, high_one)
        (came_one,) = sums_ring.step(last, [sent_one])
        own_one, sent_one = sums_ring.fold(last - 1, own_one, *halves(came_one))
        (came_one,) = sums_ring.step(last - 1, [sent_one])
        came = order(came, sent_one)
        kept, sent = sums_ring.fold(0, kept, *halves(came))
        (came,) = sums_ring.step(0, [sent])
        came_one = order(came_one, sent)
        own_one, sent_one = sums_ring.fold(last - 2, own_one, *halves(came_one))
        (came_one,) = sums_ring.step(last - 2, [sent_one])
        own_one, sent_one = sums_ring.fold(0, own_one, *halves(came_one))
        (came_one,) = sums_ring.step(0, [sent_one])
        grads = unpack(own_one, came_one, kept, came, (w_qkv, w_out, w_in, w_back) + small)
        grad_w_qkv, grad_w_out, grad_w_in, grad_w_back = grads[:4]
        parts = grads[4:]
    else:

        def shared(item):
            return lax.psum_scatter(item, "seq", scatter_dimension=0, tiled=True)

        full = jnp.concatenate([x.astype(f32) for x in (own_one, low_one, high_one)])
        line = full[:, 3 * block]
        sizes = [block] * 6 + [chunks * block]
        starts = [k * block for k in range(7)]
        parts = [
            shared(line[:, at : at + size].reshape(-1)) for at, size in zip(starts, sizes)
        ]
        grad_w_qkv = full[:, : 3 * block].reshape(BLOCKS, 3, block, width).transpose(0, 2, 1, 3)
        grad_w_qkv = shared(grad_w_qkv.reshape(width, 3 * width))
        full = jnp.concatenate([x.astype(f32) for x in (own_out, low_out, high_out)])
        grad_w_out = shared(full.reshape(width, width))
        full = jnp.concatenate([x.astype(f32) for x in (own_two, low_two, high_two)])
        full_in = full[:, : block * chunks]
        full_in = full_in.reshape(BLOCKS, chunks, block, width).transpose(0, 2, 1, 3)
        grad_w_in = shared(full_in.reshape(width, chunks * width))
        grad_w_back = shared(full[:, block * chunks :].reshape(chunks * width, width))
    gain_one, bias_one, shift_out, gain_two, bias_two, shift_back, shift_hidden = parts
    return (
        result,
        grad_tokens,
        gain_one,
        bias_one,
        grad_w_qkv,
        grad_w_out,
        shift_out,
        gain_two,
        bias_two,
        grad_w_in,
        shift_hidden,
        grad_w_back,
        shift_back,
    )


def solution(mesh):
    flat, wide = P("seq"), P("seq", None)
    weights = (flat, flat, wide, wide, flat, flat, flat, wide, flat, wide, flat)
    return jax.shard_map(
        per_device,
        mesh=mesh,
        in_specs=(P(), wide) + weights + (wide,),
        out_specs=(wide, wide) + weights,
        check_vma=False,
    )
```

```python
import functools
import math

import jax
import jax.numpy as jnp
from jax import lax
from jax.experimental import pallas as pl
from jax.experimental.pallas import tpu as pltpu
from jax.sharding import PartitionSpec as P

HEAD_DIM = 64
LEVELS = 5
HALO = 32
BLOCK = 64
WINDOW = BLOCK + 2 * HALO
QUAD = 4
QUAD_WIDTH = QUAD * HEAD_DIM
PIECES = 4
BLOCKS = 32
LINE = 128
FAR = 1 << 26
SEQ_STEP = 1 << 21
MIB = 1024 * 1024

f32 = jnp.float32
bf16 = jnp.bfloat16


class Plan:
    def locate(self, block):
        firsts = [at // BLOCK for at in self.query_at]
        level = sum((block >= first).astype(jnp.int32) for first in firsts[1:])
        start = sum(
            jnp.where(level == k, first, 0) for k, first in enumerate(firsts)
        )
        return level, block - start

    def __init__(self, rows):
        self.rows = rows
        self.counts = [rows >> level for level in range(LEVELS)]
        self.padded = [-(-count // BLOCK) * BLOCK for count in self.counts]
        self.query_at = [sum(self.padded[:level]) for level in range(LEVELS)]
        self.query_rows = sum(self.padded)
        self.key_at = [self.query_at[level] + 2 * HALO * level for level in range(LEVELS)]
        self.key_rows = self.query_rows + 2 * HALO * LEVELS
        self.blocks = [
            (level, part)
            for level in range(LEVELS)
            for part in range(self.padded[level] // BLOCK)
        ]


def dot_nn(a, b):
    return lax.dot_general(a, b, (((1,), (0,)), ((), ())), preferred_element_type=f32)


def dot_nt(a, b):
    return lax.dot_general(a, b, (((1,), (1,)), ((), ())), preferred_element_type=f32)


def dot_tn(a, b):
    return lax.dot_general(a, b, (((0,), (0,)), ((), ())), preferred_element_type=f32)


def spec(count):
    return [pl.BlockSpec(memory_space=pltpu.VMEM)] * count


SCALARS = pl.BlockSpec(memory_space=pltpu.SMEM)


def slot_facts(info, slot, total):
    number = jnp.zeros(slot.shape, jnp.int32)
    for s in range(3):
        number = number + (slot >= info[7 + s]).astype(jnp.int32)
    begin = jnp.where(number == 0, info[4], jnp.where(number == 1, info[5], info[6]))
    length = jnp.where(number == 0, info[1], jnp.where(number == 1, info[2], info[3]))
    inside = (slot >= 0) & (slot < total) & (number < 3)
    return number, slot - begin, length, inside


def tile_codes(info, coarse, level, total, outside):
    number, offset, _, inside = slot_facts(info, coarse << level, total)
    wide = jnp.where(inside, number * SEQ_STEP + (offset >> (level + 4)), outside)
    fine = number * SEQ_STEP + (offset >> (level + 3))
    return wide, fine


def admitted(query_codes, key_codes, level):
    near = jnp.abs(query_codes[0] - key_codes[0]) <= 1
    least = jnp.where(level > 0, 2, 0)
    near = near & (jnp.abs(query_codes[1] - key_codes[1]) >= least)
    return jnp.where(near, 1.0, 0.0)


def live_counts(info, coarse, level, total):
    _, offset, length, inside = slot_facts(info, coarse << level, total)
    span = 1 << level
    return jnp.where(inside, jnp.clip(length - offset, 0, span), 0).astype(f32)


def head_masks(rows):
    lane = lax.broadcasted_iota(jnp.int32, (rows, QUAD_WIDTH), 1) // HEAD_DIM
    return [jnp.where(lane == h, 1.0, 0.0).astype(bf16) for h in range(QUAD)]


def spread_heads(block, masks):
    return jnp.concatenate([block * m for m in masks], axis=0)


def join_pair(stacked, first):
    rows = stacked.shape[0] // 2
    return jnp.where(first, stacked[:rows], stacked[rows:])


def is_even(info):
    return (info[0] & 1) == 0


def params(size):
    return pltpu.CompilerParams(vmem_limit_bytes=size * MIB)


def cost(micros):
    return pl.CostEstimate(flops=1, bytes_accessed=1, transcendentals=0)


def fill_extended(plan, own, halos, extended):
    for level in range(LEVELS):
        at, count, mine = plan.key_at[level], plan.counts[level], plan.query_at[level]
        extended[pl.ds(at, HALO), :] = halos[pl.ds(HALO * level, HALO), :]
        extended[pl.ds(at + HALO, count), :] = own[pl.ds(mine, count), :]
        extended[pl.ds(at + HALO + count, HALO), :] = halos[pl.ds(HALO * (LEVELS + level), HALO), :]
        rest = plan.padded[level] - count
        if rest:
            extended[pl.ds(at + 2 * HALO + count, rest), :] = jnp.zeros(
                (rest, extended.shape[1]), bf16
            )


def place_halos(info, from_twin, from_other, halos):
    even = is_even(info)
    size = LEVELS * HALO
    halos[pl.ds(pl.multiple_of(jnp.where(even, size, 0), size), size), :] = from_twin[...]
    halos[pl.ds(pl.multiple_of(jnp.where(even, 0, size), size), size), :] = from_other[...]


def hand_out(info, ends, to_twin, to_other):
    even = is_even(info)
    size = LEVELS * HALO
    to_twin[...] = ends[pl.ds(pl.multiple_of(jnp.where(even, size, 0), size), size), :]
    to_other[...] = ends[pl.ds(pl.multiple_of(jnp.where(even, 0, size), size), size), :]


def ln_stats(values):
    center = values - jnp.mean(values, axis=-1, keepdims=True)
    spread = jnp.mean(center * center, axis=-1, keepdims=True)
    return center, lax.rsqrt(spread + 1e-05)


def ln_back(grad, hat, rstd, gain):
    scaled = grad * gain
    mean_one = jnp.mean(scaled, axis=-1, keepdims=True)
    mean_two = jnp.mean(scaled * hat, axis=-1, keepdims=True)
    return rstd * (scaled - mean_one - hat * mean_two), grad * hat


def column_sum(values):
    return jnp.sum(values, axis=0, keepdims=True)


def unpack_vectors(table, wide):
    blocks, lanes = table.shape

    def one(first, each):
        length = blocks * each
        source = lax.broadcasted_iota(jnp.int32, (lanes, length), 0)
        target = lax.broadcasted_iota(jnp.int32, (lanes, length), 1)
        pick = jnp.where(source == first + (target & (each - 1)), 1.0, 0.0).astype(bf16)
        spreaded = dot_nn(table, pick)
        block = lax.broadcasted_iota(jnp.int32, (blocks, length), 0)
        lane = lax.broadcasted_iota(jnp.int32, (blocks, length), 1)
        return column_sum(jnp.where(lane // each == block, spreaded, 0.0))

    size = wide // 4
    return [one(k * size, size) for k in range(6)], one(6 * size, wide)


def pack_vectors(vectors, last, blocks, lanes):
    size = last.shape[1] // blocks // 4

    def one(row, first, each):
        length = blocks * each
        source = lax.broadcasted_iota(jnp.int32, (length, lanes), 0)
        target = lax.broadcasted_iota(jnp.int32, (length, lanes), 1)
        pick = jnp.where(target == first + (source & (each - 1)), 1.0, 0.0).astype(bf16)
        block = lax.broadcasted_iota(jnp.int32, (blocks, length), 0)
        lane = lax.broadcasted_iota(jnp.int32, (blocks, length), 1)
        return dot_nn(jnp.where(lane // each == block, row, 0.0).astype(bf16), pick)

    total = one(last, 6 * size, 4 * size)
    for k, vector in enumerate(vectors):
        total = total + one(vector, k * size, size)
    return total


def edge_sums_kernel(plan, total, info, tokens, to_twin, to_other, ends):
    rows, width = tokens.shape
    center, rstd = ln_stats(tokens[...].astype(f32))
    plain = (center * rstd).astype(bf16)
    places = info[0] * rows + lax.broadcasted_iota(jnp.int32, (rows, width), 0)
    living = (plain.astype(f32) * live_counts(info, places, 0, total)).astype(bf16)
    size = 2 * LEVELS * HALO
    row = lax.broadcasted_iota(jnp.int32, (size, rows), 0)
    slot = lax.broadcasted_iota(jnp.int32, (size, rows), 1)
    row_one = lax.broadcasted_iota(jnp.int32, (size, 1), 0)
    wanted = jnp.zeros((size, rows), jnp.int32)
    shift = jnp.zeros((size, rows), jnp.int32)
    share = jnp.zeros((size, 1), f32)
    for k in range(2 * LEVELS):
        level, at = k % LEVELS, k * HALO
        first = 0 if k < LEVELS else plan.counts[level] - HALO
        wanted = jnp.where(row >= at, row - at + first, wanted)
        shift = jnp.where(row >= at, level, shift)
        share = jnp.where(row_one >= at, 0.5**level, share)
    pool = jnp.where((slot >> shift) == wanted, 1.0, 0.0).astype(bf16)
    ends[:, pl.ds(0, width)] = (dot_nn(pool, plain) * share).astype(bf16)
    ends[:, pl.ds(width, width)] = dot_nn(pool, living).astype(bf16)
    hand_out(info, ends, to_twin, to_other)


def edge_sums(plan, total, info, tokens):
    width = tokens.shape[1]
    size = LEVELS * HALO
    return pl.pallas_call(
        functools.partial(edge_sums_kernel, plan, total),
        out_shape=[jax.ShapeDtypeStruct((size, 2 * width), bf16)] * 2,
        in_specs=[SCALARS] + spec(1),
        out_specs=spec(2),
        scratch_shapes=[pltpu.VMEM((2 * size, 2 * width), bf16)],
        compiler_params=params(10),
        name="edge_sums",
        cost_estimate=cost(1.5),
    )(info, tokens)


def prepare_kernel(
    plan,
    total,
    info,
    tokens,
    standard,
    spread,
    pool,
    allowed,
    allowed_back,
    counts,
    edge_allowed,
    edge_counts,
):
    rows = plan.rows
    device = info[0]
    center, rstd = ln_stats(tokens[...].astype(f32))
    standard[...] = center * rstd
    spread[...] = jnp.broadcast_to(rstd, spread.shape)
    pooled_rows = pool.shape[0]
    row = lax.broadcasted_iota(jnp.int32, (pooled_rows, rows), 0)
    slot = lax.broadcasted_iota(jnp.int32, (pooled_rows, rows), 1)
    first = jnp.zeros((pooled_rows, rows), jnp.int32)
    shift = jnp.zeros((pooled_rows, rows), jnp.int32)
    for level in range(1, LEVELS):
        at = plan.query_at[level] - plan.query_at[1]
        first = jnp.where(row >= at, at, first)
        shift = jnp.where(row >= at, level, shift)
    pool[...] = jnp.where((slot >> shift) == row - first, 1.0, 0.0).astype(bf16)

    def block_step(block, carry):
        level, part = plan.locate(block)
        first = device * (rows >> level) + BLOCK * part
        here = pl.ds(pl.multiple_of(BLOCK * block, BLOCK), BLOCK)
        there = pl.ds(pl.multiple_of(WINDOW * block, WINDOW), WINDOW)
        row = first + lax.broadcasted_iota(jnp.int32, (BLOCK, WINDOW), 0)
        column = first - HALO + lax.broadcasted_iota(jnp.int32, (BLOCK, WINDOW), 1)
        allowed[here, :] = admitted(
            tile_codes(info, row, level, total, FAR),
            tile_codes(info, column, level, total, -FAR),
            level,
        )
        key_row = first - HALO + lax.broadcasted_iota(jnp.int32, (WINDOW, 128), 0)
        lane = lax.broadcasted_iota(jnp.int32, (WINDOW, 128), 1)
        row = first + (lane & (BLOCK - 1))
        allowed_back[there, :] = admitted(
            tile_codes(info, row, level, total, FAR),
            tile_codes(info, key_row, level, total, -FAR),
            level,
        )
        counts[there, :] = live_counts(info, key_row, level, total).astype(bf16)
        return carry

    lax.fori_loop(0, len(plan.blocks), block_step, 0, unroll=2)
    two = 2 * HALO
    key = lax.broadcasted_iota(jnp.int32, (two, 128), 0)
    lane = lax.broadcasted_iota(jnp.int32, (two, 128), 1) & (two - 1)
    facing = jnp.where((key < HALO) == (lane < HALO), 1.0, 0.0)
    for level in range(LEVELS):
        count = plan.counts[level]
        start = device * count
        key_row = start + jnp.where(key < HALO, key, count - two + key)
        row = start + jnp.where(lane < HALO, lane - HALO, count - HALO + lane)
        here = pl.ds(two * level, two)
        edge_allowed[here, :] = facing * admitted(
            tile_codes(info, row, level, total, FAR),
            tile_codes(info, key_row, level, total, -FAR),
            level,
        )
        edge_counts[here, :] = live_counts(info, key_row, level, total).astype(bf16)


def prepare(plan, total, info, tokens):
    rows, width = tokens.shape
    blocks = len(plan.blocks)
    return pl.pallas_call(
        functools.partial(prepare_kernel, plan, total),
        out_shape=(
            jax.ShapeDtypeStruct((rows, width), f32),
            jax.ShapeDtypeStruct((rows, 128), f32),
            jax.ShapeDtypeStruct((plan.query_rows - plan.query_at[1], rows), bf16),
            jax.ShapeDtypeStruct((BLOCK * blocks, WINDOW), f32),
            jax.ShapeDtypeStruct((WINDOW * blocks, 128), f32),
            jax.ShapeDtypeStruct((WINDOW * blocks, 128), bf16),
            jax.ShapeDtypeStruct((2 * HALO * LEVELS, 128), f32),
            jax.ShapeDtypeStruct((2 * HALO * LEVELS, 128), bf16),
        ),
        in_specs=[SCALARS] + spec(1),
        out_specs=tuple(spec(8)),
        compiler_params=params(8),
        name="prepare",
        cost_estimate=cost(4),
    )(info, tokens)


def project_kernel(
    plan, total, info, inverse, standard, pool, from_twin, from_other, *refs
):
    pieces, outs = refs[:PIECES], refs[PIECES:]
    queries, pairs, halo_queries, halo_pairs = (outs[2 * k : 2 * k + 2] for k in range(4))
    weight, vectors, shift_out, table, edges, halos = outs[8:]
    rows, width = standard.shape
    device = info[0]
    each = pieces[0].shape[0]
    block_rows = pieces[0].shape[1] // 4
    for p in range(PIECES * each):
        i = inverse[p]
        there = pl.ds(pl.multiple_of(i * block_rows, block_rows), block_rows)
        piece, q = pieces[p // each], p % each
        for c in range(3):
            weight[there, pl.ds(c * width, width)] = piece[q, pl.ds(block_rows * c, block_rows), :]
        line = piece[q, pl.ds(block_rows * 3, block_rows), pl.ds(0, 2 * LINE)].astype(f32)
        table[pl.ds(i, 1), :] = line[0:1]
    singles, wide = unpack_vectors(table[...].astype(bf16), 4 * block_rows)
    for k, single in enumerate(singles):
        vectors[pl.ds(k, 1), :] = single
    shift_out[...] = wide
    low = (standard[...] * singles[0] + singles[1]).astype(bf16)
    pooled_rows = pool.shape[0]
    share = jnp.zeros((pooled_rows, 1), f32)
    row_one = lax.broadcasted_iota(jnp.int32, (pooled_rows, 1), 0)
    for level in range(1, LEVELS):
        at = plan.query_at[level] - plan.query_at[1]
        share = jnp.where(row_one >= at, 0.5**level, share)
    places = device * rows + lax.broadcasted_iota(jnp.int32, (rows, QUAD_WIDTH), 0)
    live = live_counts(info, places, 0, total)
    place_halos(info, from_twin, from_other, edges)
    size = LEVELS * HALO
    halos[:, pl.ds(0, width)] = (
        edges[:, pl.ds(0, width)].astype(f32) * singles[0] + singles[1]
    ).astype(bf16)
    for k in range(2 * LEVELS):
        level, here = k % LEVELS, pl.ds(k * HALO, HALO)
        count = plan.counts[level]
        first = device * count + (-HALO if k < LEVELS else count)
        place = first + lax.broadcasted_iota(jnp.int32, (HALO, 128), 0)
        counts = live_counts(info, place, level, total)
        counts = jnp.concatenate([counts] * (width // 128), axis=1)
        halos[here, pl.ds(width, width)] = (
            edges[here, pl.ds(width, width)].astype(f32) * singles[0] + counts * singles[1]
        ).astype(bf16)
    lanes = QUAD_WIDTH
    scale = 1.0 / math.sqrt(HEAD_DIM)
    for part in range(3 * width // lanes):
        columns = pl.ds(part * lanes, lanes)
        block = dot_nn(low, weight[:, columns]).astype(bf16)
        kind, quad = divmod(part, 2)
        if kind == 2:
            block = (block.astype(f32) * live).astype(bf16)
        pooled = dot_nn(pool[...], block)
        if kind < 2:
            pooled = pooled * share
        side = dot_nn(halos[:, pl.ds(width if kind == 2 else 0, width)], weight[:, columns])
        if kind == 0:
            queries[quad][pl.ds(0, rows), :] = (block.astype(f32) * scale).astype(bf16)
            queries[quad][pl.ds(rows, pooled_rows), :] = (pooled * scale).astype(bf16)
            halo_queries[quad][...] = (side * scale).astype(bf16)
        else:
            there = pl.ds((kind - 1) * lanes, lanes)
            pairs[quad][pl.ds(0, rows), there] = block
            pairs[quad][pl.ds(rows, pooled_rows), there] = pooled.astype(bf16)
            halo_pairs[quad][:, there] = side.astype(bf16)


def project(plan, total, info, inverse, standard, pool, from_twin, from_other, pieces):
    rows, width = standard.shape
    halo = LEVELS * HALO
    blocks = PIECES * pieces[0].shape[0]
    depth = blocks * pieces[0].shape[1] // 4
    half = width // 2
    outs = pl.pallas_call(
        functools.partial(project_kernel, plan, total),
        out_shape=(
            [jax.ShapeDtypeStruct((plan.query_rows, half), bf16)] * 2
            + [jax.ShapeDtypeStruct((plan.query_rows, 2 * half), bf16)] * 2
            + [jax.ShapeDtypeStruct((2 * halo, half), bf16)] * 2
            + [jax.ShapeDtypeStruct((2 * halo, 2 * half), bf16)] * 2
            + [
                jax.ShapeDtypeStruct((depth, 3 * width), bf16),
                jax.ShapeDtypeStruct((8, depth), f32),
                jax.ShapeDtypeStruct((1, 4 * depth), f32),
            ]
        ),
        in_specs=[SCALARS, SCALARS] + spec(4 + PIECES),
        out_specs=spec(11),
        scratch_shapes=[
            pltpu.VMEM((blocks, 2 * LINE), f32),
            pltpu.VMEM((2 * halo, 2 * width), bf16),
            pltpu.VMEM((2 * halo, 2 * width), bf16),
        ],
        compiler_params=params(18),
        name="project",
        cost_estimate=cost(3.3),
    )(info, inverse, standard, pool, from_twin, from_other, *pieces)
    return [outs[2 * k : 2 * k + 2] for k in range(4)] + list(outs[8:])


def attend_kernel(plan, total, info, mask, counts_of, *refs):
    queries, pairs, halos, attended, mixed, scale, extended = (
        refs[2 * k : 2 * k + 2] for k in range(7)
    )
    numer, denom = refs[14:]
    rows = plan.rows
    device = info[0]
    for quad in range(2):
        fill_extended(plan, pairs[quad], halos[quad], extended[quad])
    first_head = lax.broadcasted_iota(jnp.int32, (BLOCK, 128), 1) < HEAD_DIM
    masks = head_masks(BLOCK)

    def prepare(block):
        level, part = plan.locate(block)
        here = pl.ds(pl.multiple_of(BLOCK * block, BLOCK), BLOCK)
        there = pl.ds(pl.multiple_of(BLOCK * block + 2 * HALO * level, BLOCK), WINDOW)
        allowed = mask[here, :]
        counts = counts_of[pl.ds(pl.multiple_of(WINDOW * block, WINDOW), WINDOW), :]
        return here, there, allowed, counts

    def block_step(step, carry):
        work = []
        for k in range(4):
            here, there, allowed, counts = prepare(step * 4 + k)
            allowed = jnp.concatenate([allowed] * 4, axis=0) > 0.0
            for part in range(8 // 4):
                work.append((here, there, allowed, counts, part))
        scores = []
        for here, there, allowed, counts, part in work:
            wide = 4 * HEAD_DIM
            quad, half = divmod(part * wide, QUAD_WIDTH)
            lanes = pl.ds(half, wide)
            q = spread_heads(queries[quad][here, lanes], masks)
            scores.append(dot_nt(q, extended[quad][there, lanes]))
        weights = [
            jnp.where(item[2], jnp.exp(score), 0.0).astype(bf16)
            for item, score in zip(work, scores)
        ]
        for (here, there, allowed, counts, part), weight in zip(work, weights):
            wide = 4 * HEAD_DIM
            for sub in range(4 // 2):
                pair = part * (4 // 2) + sub
                quad, half = divmod(pair, 2)
                v = extended[quad][there, pl.ds(QUAD_WIDTH + 128 * half, 128)]
                both = dot_nn(
                    weight[128 * sub : 128 * sub + 128], jnp.concatenate([v, counts], axis=1)
                )
                numer[pair, here, :] = join_pair(both[:, :128], first_head)
                denom[pair, here, :] = join_pair(both[:, 128:], first_head)
        return carry

    lax.fori_loop(0, len(plan.blocks) // 4, block_step, 0, unroll=1)
    places = device * rows + lax.broadcasted_iota(jnp.int32, (rows, 128), 0)
    live = live_counts(info, places, 0, total)
    for pair in range(4):
        for sums in (numer, denom):
            for level in range(LEVELS - 1, 0, -1):
                count = plan.counts[level]
                upper = sums[pair, pl.ds(plan.query_at[level], count), :]
                for parity in range(2):
                    there = pl.ds(plan.query_at[level - 1] + parity, count, stride=2)
                    sums[pair, there, :] = sums[pair, there, :] + upper
        quad, half = divmod(pair, 2)
        lanes = pl.ds(128 * half, 128)
        factor = live / (denom[pair, pl.ds(0, rows), :] + 1.0 - live)
        value = numer[pair, pl.ds(0, rows), :] * factor
        scale[quad][:, lanes] = factor
        mixed[quad][:, lanes] = value
        attended[quad][:, lanes] = value.astype(bf16)


def attend(plan, total, info, mask, counts, queries, pairs, halos):
    rows, width = plan.rows, queries[0].shape[1]
    outs = pl.pallas_call(
        functools.partial(attend_kernel, plan, total),
        out_shape=[jax.ShapeDtypeStruct((rows, width), bf16)] * 2
        + [jax.ShapeDtypeStruct((rows, width), f32)] * 4,
        in_specs=[SCALARS] + spec(8),
        out_specs=spec(6),
        scratch_shapes=[
            pltpu.VMEM((plan.key_rows, 2 * width), bf16),
            pltpu.VMEM((plan.key_rows, 2 * width), bf16),
            pltpu.VMEM((2 * width // 128, plan.query_rows, 128), f32),
            pltpu.VMEM((2 * width // 128, plan.query_rows, 128), f32),
        ],
        compiler_params=params(20),
        name="attend",
        cost_estimate=cost(8),
    )(info, mask, counts, *queries, *pairs, *halos)
    return outs[:2], outs[2:4], outs[4:]


def forward_kernel(
    parts,
    inverse,
    sums_inverse,
    tokens,
    cotangent,
    attended_a,
    attended_b,
    vectors,
    shift_in,
    *refs,
):
    pieces = refs[:parts]
    result, resid_out, grad_normed, w_out, own, low_half, high_half, sum_in = refs[
        parts : parts + 8
    ]
    w_in, w_back, normed_two, outer, tall, flat, turned, cot_turned = refs[parts + 8 :]
    other = (low_half, high_half)
    width = tokens.shape[1]
    wide = width // 2
    each = pieces[0].shape[0]
    half = own.shape[0]
    chunks = w_in.shape[0]
    block = width // (parts * each)
    tall_block = chunks * block
    back_at = block + tall_block
    for p in range(parts * each):
        piece, q = pieces[p // each], p % each
        i = inverse[p]
        rows = pl.ds(pl.multiple_of(i * block, block), block)
        w_out[rows, :] = piece[q, pl.ds(0, block), :]
        for c in range(chunks):
            w_in[c, rows, :] = piece[q, pl.ds(block * (c + 1), block), :]
        rows = pl.ds(pl.multiple_of(i * tall_block, tall_block), tall_block)
        w_back[rows, :] = piece[q, pl.ds(back_at, tall_block), :]
    gain = vectors[pl.ds(3, 1), :]
    resid = tokens[...].astype(f32) + dot_nn(attended_a[...], w_out[pl.ds(0, wide), :])
    resid = resid + dot_nn(attended_b[...], w_out[pl.ds(wide, wide), :]) + vectors[pl.ds(2, 1), :]
    center, rstd = ln_stats(resid)
    normed_two[...] = (center * rstd * gain + vectors[pl.ds(4, 1), :]).astype(bf16)
    turned[...] = normed_two[...].T
    resid_out[...] = resid
    outer[...] = jnp.zeros(outer.shape, f32)
    grad_normed[...] = jnp.zeros(grad_normed.shape, f32)

    def chunk_step(c, carry):
        there = pl.ds(pl.multiple_of(c * width, width), width)
        inner = dot_nn(normed_two[...], w_in[c]) + shift_in[:, there]
        cdf = 0.5 * (1.0 + lax.erf(inner * math.sqrt(0.5)))
        active = (inner * cdf).astype(bf16)
        slope = cdf + inner * (jnp.exp(-0.5 * inner * inner) * (1.0 / math.sqrt(2.0 * math.pi)))
        back = w_back[there, :]
        grad_inner = slope * dot_nt(cotangent[...], back)
        low = grad_inner.astype(bf16)
        outer[...] += dot_nn(active, back)
        tall[there, :] = dot_tn(active, cotangent[...]).astype(bf16)
        sum_in[:, there] = column_sum(low.astype(f32))
        flat[...] = dot_nn(turned[...], low).astype(bf16)
        for p in range(2 * half):
            i = sums_inverse[p]
            rows = flat[pl.ds(pl.multiple_of(i * block, block), block), :]
            at = pl.ds(pl.multiple_of(c * block, block), block)
            if p < half:
                own[p, at, :] = rows
            else:
                other[(p - half) // 8][(p - half) % 8, at, :] = rows
        grad_normed[...] += dot_nt(low, w_in[c])
        return carry

    lax.fori_loop(0, chunks, chunk_step, 0, unroll=4)
    result[...] = (resid_out[...] + outer[...] + vectors[pl.ds(5, 1), :]).astype(bf16)
    for p in range(2 * half):
        i = sums_inverse[p]
        rows = tall[pl.ds(pl.multiple_of(i * tall_block, tall_block), tall_block), :]
        there = pl.ds(tall_block, tall_block)
        if p < half:
            own[p, there, :] = rows
        else:
            other[(p - half) // 8][(p - half) % 8, there, :] = rows


def feed_forward(inverses, tokens, cotangent, attended, vectors, shift_in, pieces):
    parts = len(pieces)
    rows, width = tokens.shape
    hidden = shift_in.shape[1]
    chunks = hidden // width
    blocks = parts * pieces[0].shape[0]
    stack = pieces[0].shape[1] - width // blocks
    return pl.pallas_call(
        functools.partial(forward_kernel, parts),
        out_shape=(
            jax.ShapeDtypeStruct((rows, width), bf16),
            jax.ShapeDtypeStruct((rows, width), f32),
            jax.ShapeDtypeStruct((rows, width), f32),
            jax.ShapeDtypeStruct((width, width), bf16),
            jax.ShapeDtypeStruct((blocks // 2, stack, width), bf16),
            jax.ShapeDtypeStruct((blocks // 4, stack, width), bf16),
            jax.ShapeDtypeStruct((blocks // 4, stack, width), bf16),
            jax.ShapeDtypeStruct((1, hidden), f32),
        ),
        in_specs=[SCALARS] * 2 + spec(6 + parts),
        out_specs=tuple(spec(8)),
        scratch_shapes=[
            pltpu.VMEM((chunks, width, width), bf16),
            pltpu.VMEM((hidden, width), bf16),
            pltpu.VMEM((rows, width), bf16),
            pltpu.VMEM((rows, width), f32),
            pltpu.VMEM((hidden, width), bf16),
            pltpu.VMEM((width, width), bf16),
            pltpu.VMEM((width, rows), bf16),
            pltpu.VMEM((width, rows), bf16),
        ],
        compiler_params=params(30),
        name="feed_forward",
        cost_estimate=cost(10),
    )(*inverses, tokens, cotangent, *attended, vectors, shift_in, *pieces)


def middle_kernel(
    plan,
    info,
    sums_inverse,
    cotangent,
    attended_a,
    attended_b,
    mixed_a,
    mixed_b,
    scale_a,
    scale_b,
    vectors,
    resid,
    grad_normed,
    w_out,
    grad_resid,
    grads_a,
    grads_b,
    to_twin,
    to_other,
    sums,
    own,
    low_half,
    high_half,
    levels,
    ends,
    denoms,
    flat,
):
    width = cotangent.shape[1]
    wide = width // 2
    center, rstd = ln_stats(resid[...])
    grad_in, gain_terms = ln_back(grad_normed[...], center * rstd, rstd, vectors[pl.ds(3, 1), :])
    grad_out = cotangent[...].astype(f32)
    total = grad_out + grad_in
    grad_resid[...] = total
    low = total.astype(bf16)
    sums[pl.ds(0, 1), :] = jnp.zeros((1, width), f32)
    sums[pl.ds(1, 1), :] = jnp.zeros((1, width), f32)
    sums[pl.ds(2, 1), :] = column_sum(low.astype(f32))
    sums[pl.ds(3, 1), :] = column_sum(gain_terms)
    sums[pl.ds(4, 1), :] = column_sum(grad_normed[...])
    sums[pl.ds(5, 1), :] = column_sum(grad_out)
    for quad in range(2):
        lines = pl.ds(quad * wide, wide)
        flat[lines, :] = dot_tn((attended_a, attended_b)[quad][...], low).astype(bf16)
        numer = dot_nt(low, w_out[lines, :]) * (scale_a, scale_b)[quad][...]
        denom = -(numer * (mixed_a, mixed_b)[quad][...])
        for chunk in range(2 * wide // 128):
            source = numer if chunk < wide // 128 else denom
            lane = chunk * 128 % wide
            levels[chunk, pl.ds(0, plan.rows), :] = source[:, lane : lane + 128]
            for level in range(1, LEVELS):
                count, at = plan.counts[level], plan.query_at[level]
                below = plan.query_at[level - 1]
                levels[chunk, pl.ds(at, count), :] = (
                    levels[chunk, pl.ds(below, count, stride=2), :]
                    + levels[chunk, pl.ds(below + 1, count, stride=2), :]
                )
                rest = plan.padded[level] - count
                if rest:
                    levels[chunk, pl.ds(at + count, rest), :] = jnp.zeros((rest, 128), f32)
            grads = (grads_a, grads_b)[quad]
            grads[:, pl.ds(chunk * 128, 128)] = levels[chunk].astype(bf16)
        for k in range(2 * LEVELS):
            level, here = k % LEVELS, pl.ds(k * HALO, HALO)
            at = plan.query_at[level] + (0 if k < LEVELS else plan.counts[level] - HALO)
            there = pl.ds(at, HALO)
            ends[here, pl.ds(quad * wide, wide)] = (grads_a, grads_b)[quad][there, pl.ds(0, wide)]
            for chunk in range(wide // 128):
                lanes = pl.ds(quad * wide + chunk * 128, 128)
                denoms[here, lanes] = levels[wide // 128 + chunk, there, :]
    feature = lax.broadcasted_iota(jnp.int32, (width, LINE), 0)
    lane = lax.broadcasted_iota(jnp.int32, (width, LINE), 1)
    pick = jnp.where(lane == feature // HEAD_DIM, 1.0, 0.0).astype(bf16)
    heads = width // HEAD_DIM
    values = denoms[...]
    first = values.astype(bf16)
    values = dot_nn(first, pick) + dot_nn((values - first.astype(f32)).astype(bf16), pick)
    first = values.astype(bf16).astype(f32)
    both = jnp.concatenate([first[:, :heads], (values - first)[:, :heads]], axis=1)
    both = jnp.concatenate([both, jnp.zeros((both.shape[0], LINE - 2 * heads), f32)], axis=1)
    ends[:, pl.ds(width, LINE)] = both.astype(bf16)
    hand_out(info, ends, to_twin, to_other)
    half, block = own.shape[0], own.shape[1]
    other = (low_half, high_half)
    for p in range(2 * half):
        rows = flat[pl.ds(pl.multiple_of(sums_inverse[p] * block, block), block), :]
        if p < half:
            own[p] = rows
        else:
            other[(p - half) // 8][(p - half) % 8] = rows


def middle(plan, info, sums_inverse, cotangent, attended, mixed, scale, vectors, resid, grad_normed, w_out):
    rows, width = cotangent.shape
    size = LEVELS * HALO
    return pl.pallas_call(
        functools.partial(middle_kernel, plan),
        out_shape=(
            jax.ShapeDtypeStruct((rows, width), f32),
            jax.ShapeDtypeStruct((plan.query_rows, width), bf16),
            jax.ShapeDtypeStruct((plan.query_rows, width), bf16),
            jax.ShapeDtypeStruct((size, width + LINE), bf16),
            jax.ShapeDtypeStruct((size, width + LINE), bf16),
            jax.ShapeDtypeStruct((8, width), f32),
            jax.ShapeDtypeStruct((BLOCKS // 2, width // BLOCKS, width), bf16),
            jax.ShapeDtypeStruct((BLOCKS // 4, width // BLOCKS, width), bf16),
            jax.ShapeDtypeStruct((BLOCKS // 4, width // BLOCKS, width), bf16),
        ),
        in_specs=[SCALARS] * 2 + spec(11),
        out_specs=tuple(spec(9)),
        scratch_shapes=[
            pltpu.VMEM((width // 128, plan.query_rows, 128), f32),
            pltpu.VMEM((2 * size, width + LINE), bf16),
            pltpu.VMEM((2 * size, width), f32),
            pltpu.VMEM((width, width), bf16),
        ],
        compiler_params=params(20),
        name="middle",
        cost_estimate=cost(3),
    )(info, sums_inverse, cotangent, *attended, *mixed, *scale, vectors, resid, grad_normed, w_out)


def attend_back_kernel(plan, total, mask, counts_of, *refs):
    queries, pairs, halos, grads, grad_queries, grad_extended, extended = (
        refs[2 * k : 2 * k + 2] for k in range(7)
    )
    width = QUAD_WIDTH
    for quad in range(2):
        fill_extended(plan, pairs[quad], halos[quad], extended[quad])
        grad_extended[quad][...] = jnp.zeros(grad_extended[quad].shape, f32)
    masks = head_masks(BLOCK)
    first_head = lax.broadcasted_iota(jnp.int32, (BLOCK, 128), 1) < HEAD_DIM
    keys = pl.ds(0, width)
    values = pl.ds(width, width)

    def prepare(block):
        level, part = plan.locate(block)
        here = pl.ds(pl.multiple_of(BLOCK * block, BLOCK), BLOCK)
        there = pl.ds(pl.multiple_of(BLOCK * block + 2 * HALO * level, BLOCK), WINDOW)
        window = pl.ds(pl.multiple_of(WINDOW * block, WINDOW), WINDOW)
        allowed = jnp.concatenate([mask[window, :]] * (QUAD * BLOCK // 128), axis=1) > 0.0
        counts = counts_of[window, :]
        return here, there, allowed, counts

    def block_step(step, carry):
        work = []
        for k in range(4):
            here, there, allowed, counts = prepare(step * 4 + k)
            for quad in range(2):
                q = spread_heads(queries[quad][here, :], masks)
                g = spread_heads(grads[quad][here, keys], masks)
                d = spread_heads(grads[quad][here, values], masks)
                work.append((quad, here, there, allowed, counts, q, g, d))
        scores, grad_probs = [], []
        for quad, here, there, allowed, counts, q, g, d in work:
            scores.append(dot_nt(extended[quad][there, keys], q))
            v = extended[quad][there, values]
            value_and_count = jnp.concatenate([v] + [counts] * (width // 128), axis=1)
            grad_probs.append(dot_nt(value_and_count, jnp.concatenate([g, d], axis=1)))
        weights = [
            jnp.where(item[3], jnp.exp(score), 0.0) for item, score in zip(work, scores)
        ]
        grad_scores = [(x * y).astype(bf16) for x, y in zip(grad_probs, weights)]
        probs = [weight.astype(bf16) for weight in weights]
        keys_of = [extended[item[0]][item[2], keys] for item in work]
        to_queries = [
            [
                dot_tn(grad_score[:, 128 * half : 128 * half + 128], k[:, 128 * half : 128 * half + 128])
                for half in range(2)
            ]
            for grad_score, k in zip(grad_scores, keys_of)
        ]
        to_keys = [dot_nn(grad_score, item[5]) for grad_score, item in zip(grad_scores, work)]
        to_values = [dot_nn(prob, item[6]) for prob, item in zip(probs, work)]
        for item, parts, to_key, to_value in zip(work, to_queries, to_keys, to_values):
            quad, here, there = item[:3]
            for half in range(2):
                grad_queries[quad][here, pl.ds(128 * half, 128)] = join_pair(
                    parts[half], first_head
                ) * (1.0 / math.sqrt(HEAD_DIM))
            grad_extended[quad][there, keys] += to_key
            grad_extended[quad][there, values] += to_value
        return carry

    lax.fori_loop(0, len(plan.blocks) // 4, block_step, 0, unroll=1)


def attend_back(plan, total, mask, counts, queries, pairs, halos, grads):
    width = queries[0].shape[1]
    outs = pl.pallas_call(
        functools.partial(attend_back_kernel, plan, total),
        out_shape=[jax.ShapeDtypeStruct((plan.query_rows, width), f32)] * 2
        + [jax.ShapeDtypeStruct((plan.key_rows, 2 * width), f32)] * 2,
        in_specs=spec(10),
        out_specs=spec(4),
        scratch_shapes=[
            pltpu.VMEM((plan.key_rows, 2 * width), bf16),
            pltpu.VMEM((plan.key_rows, 2 * width), bf16),
        ],
        compiler_params=params(24),
        name="attend_back",
        cost_estimate=cost(12),
    )(mask, counts, *queries, *pairs, *halos, *grads)
    return outs[:2], outs[2:]


def edge_back_kernel(
    plan,
    info,
    mask,
    counts_of,
    queries_a,
    queries_b,
    pairs_a,
    pairs_b,
    from_twin,
    from_other,
    low,
    high,
    grads,
):
    width = queries_a.shape[1]
    place_halos(info, from_twin, from_other, grads)
    two = 2 * HALO
    masks = head_masks(two)
    keys = pl.ds(0, width)
    heads = 2 * width // HEAD_DIM
    source = lax.broadcasted_iota(jnp.int32, (LINE, width), 0)
    target = lax.broadcasted_iota(jnp.int32, (LINE, width), 1)
    picks = []
    for quad in range(2):
        head = target // HEAD_DIM + quad * QUAD
        wanted = jnp.where(target % HEAD_DIM == 0, head, -1)
        wanted = jnp.where(target % HEAD_DIM == 1, head + heads, wanted)
        picks.append(jnp.where(source == wanted, 1.0, 0.0).astype(bf16))
    denoms = [dot_nn(grads[:, pl.ds(2 * width, LINE)], pick).astype(bf16) for pick in picks]
    work = []
    for level in range(LEVELS):
        count, at = plan.counts[level], plan.query_at[level]
        here = pl.ds(two * level, two)
        allowed = jnp.concatenate([mask[here, :]] * (QUAD * two // 128), axis=1) > 0.0
        counts = counts_of[here, :]
        ahead, behind = HALO * level, HALO * (LEVELS + level)

        def both(item, lanes):
            parts = [item[pl.ds(first, HALO), lanes] for first in (ahead, behind)]
            return jnp.concatenate(parts, axis=0)

        for quad in range(2):
            pairs = (pairs_a, pairs_b)[quad]
            own = jnp.concatenate(
                [pairs[pl.ds(at, HALO), :], pairs[pl.ds(at + count - HALO, HALO), :]], axis=0
            )
            k, v = own[:, :width], own[:, width:]
            d = denoms[quad]
            d = jnp.concatenate([d[ahead : ahead + HALO], d[behind : behind + HALO]], axis=0)
            q = spread_heads(both((queries_a, queries_b)[quad], keys), masks)
            g = spread_heads(both(grads, pl.ds(quad * width, width)), masks)
            d = spread_heads(d, masks)
            value_and_count = jnp.concatenate([v] + [counts] * (width // 128), axis=1)
            there = pl.ds(HALO * (quad * LEVELS + level), HALO)
            work.append((there, allowed, q, g, d, k, value_and_count))
    scores = [dot_nt(item[5], item[2]) for item in work]
    grad_probs = [
        dot_nt(item[6], jnp.concatenate([item[3], item[4]], axis=1)) for item in work
    ]
    weights = [jnp.where(item[1], jnp.exp(score), 0.0) for item, score in zip(work, scores)]
    grad_scores = [(x * y).astype(bf16) for x, y in zip(grad_probs, weights)]
    to_keys = [dot_nn(grad_score, item[2]) for grad_score, item in zip(grad_scores, work)]
    to_values = [dot_nn(weight.astype(bf16), item[3]) for weight, item in zip(weights, work)]
    for item, to_key, to_value in zip(work, to_keys, to_values):
        there = item[0]
        low[there, keys] = to_key[:HALO]
        high[there, keys] = to_key[HALO:]
        low[there, pl.ds(width, width)] = to_value[:HALO]
        high[there, pl.ds(width, width)] = to_value[HALO:]


def edge_back(plan, info, mask, counts, queries, pairs, from_twin, from_other):
    width = queries[0].shape[1]
    size = 2 * LEVELS * HALO
    return pl.pallas_call(
        functools.partial(edge_back_kernel, plan),
        out_shape=[jax.ShapeDtypeStruct((size, 2 * width), f32)] * 2,
        in_specs=[SCALARS] + spec(8),
        out_specs=spec(2),
        scratch_shapes=[pltpu.VMEM((size, 2 * width + LINE), bf16)],
        compiler_params=params(12),
        name="edge_back",
        cost_estimate=cost(2.5),
    )(info, mask, counts, *queries, *pairs, from_twin, from_other)


def finish_kernel(
    plan,
    total,
    info,
    inverse,
    standard,
    spread,
    weight,
    vectors,
    grad_resid,
    sums,
    sum_in,
    queries_a,
    queries_b,
    pairs_a,
    pairs_b,
    edge_low,
    edge_high,
    grad_tokens,
    own,
    low_half,
    high_half,
    work,
    joined,
    flat,
    table,
):
    rows, width = standard.shape
    device = info[0]
    half_width = width // 2
    places = device * rows + lax.broadcasted_iota(jnp.int32, (rows, 128), 0)
    live = live_counts(info, places, 0, total)
    for chunk in range(3 * width // 128):
        part, lane = divmod(chunk * 128, width)
        quad, lane = divmod(lane, half_width)
        if part == 0:
            work[chunk] = (queries_a, queries_b)[quad][:, pl.ds(lane, 128)]
        else:
            lanes = pl.ds((part - 1) * half_width + lane, 128)
            for level in range(LEVELS):
                at, count = plan.query_at[level], plan.counts[level]
                own_rows = pl.ds(plan.key_at[level] + HALO, count)
                work[chunk, pl.ds(at, count), :] = (pairs_a, pairs_b)[quad][own_rows, lanes]
                halo = pl.ds(HALO * (quad * LEVELS + level), HALO)
                work[chunk, pl.ds(at, HALO), :] += edge_low[halo, lanes]
                work[chunk, pl.ds(at + count - HALO, HALO), :] += edge_high[halo, lanes]
        for level in range(LEVELS - 1, 0, -1):
            count = plan.counts[level]
            upper = work[chunk, pl.ds(plan.query_at[level], count), :]
            if chunk * 128 < 2 * width:
                upper = upper * 0.5
            for parity in range(2):
                there = pl.ds(plan.query_at[level - 1] + parity, count, stride=2)
                work[chunk, there, :] = work[chunk, there, :] + upper
        value = work[chunk, pl.ds(0, rows), :]
        if chunk * 128 >= 2 * width:
            value = value * live
        joined[:, pl.ds(chunk * 128, 128)] = value.astype(bf16)
    hat = standard[...]
    gain = vectors[pl.ds(0, 1), :]
    normed = (hat * gain + vectors[pl.ds(1, 1), :]).astype(bf16)
    half, block = own.shape[0], own.shape[1] // 4
    other = (low_half, high_half)
    for part in range(3):
        columns = pl.ds(part * width, width)
        flat[...] = dot_tn(normed, joined[:, columns])
        for p in range(2 * half):
            i = inverse[p]
            lines = flat[pl.ds(pl.multiple_of(i * block, block), block), :]
            there = pl.ds(part * block, block)
            if p < half:
                own[p, there, :] = lines.astype(bf16)
            else:
                other[(p - half) // 8][(p - half) % 8, there, :] = lines.astype(bf16)
    grad_normed = dot_nt(joined[...], weight[...])
    grad_in, gain_terms = ln_back(grad_normed, hat, spread[:, :1], gain)
    grad_tokens[...] = grad_resid[...] + grad_in
    singles = [column_sum(gain_terms), column_sum(grad_normed)]
    singles += [sums[pl.ds(k, 1), :] for k in range(2, 6)]
    table[...] = pack_vectors(singles, sum_in[...], 2 * half, table.shape[1])
    row = lax.broadcasted_iota(jnp.int32, (block, 2 * LINE), 0)
    there = pl.ds(3 * block, block)
    for p in range(2 * half):
        i = inverse[p]
        line = table[pl.ds(i, 1), :]
        lines = jnp.where(row == 0, line, 0.0)
        lines = jnp.concatenate([lines, jnp.zeros((block, width - 2 * LINE), f32)], axis=1)
        if p < half:
            own[p, there, :] = lines.astype(bf16)
        else:
            other[(p - half) // 8][(p - half) % 8, there, :] = lines.astype(bf16)


def finish(plan, total, info, inverse, standard, spread, weight, *rest):
    rows, width = standard.shape
    half = BLOCKS // 2
    block = width // BLOCKS
    return pl.pallas_call(
        functools.partial(finish_kernel, plan, total),
        out_shape=(
            jax.ShapeDtypeStruct((rows, width), f32),
            jax.ShapeDtypeStruct((half, 4 * block, width), bf16),
            jax.ShapeDtypeStruct((half // 2, 4 * block, width), bf16),
            jax.ShapeDtypeStruct((half // 2, 4 * block, width), bf16),
        ),
        in_specs=[SCALARS, SCALARS] + spec(3 + len(rest)),
        out_specs=tuple(spec(4)),
        scratch_shapes=[
            pltpu.VMEM((3 * width // 128, plan.query_rows, 128), f32),
            pltpu.VMEM((rows, 3 * width), bf16),
            pltpu.VMEM((width, width), f32),
            pltpu.VMEM((BLOCKS, 2 * LINE), f32),
        ],
        compiler_params=params(28),
        name="finish",
        cost_estimate=cost(6.2),
    )(info, inverse, standard, spread, weight, *rest)


class Ring:
    def __init__(self, devices, *orders):
        self.devices = devices
        self.orders = orders
        self.stages = len(orders[0])

    def partner(self, stage):
        return [(i, i ^ self.orders[i & 1][stage]) for i in range(self.devices)]

    def twin(self):
        return [(i, i ^ 1) for i in range(self.devices)]

    def places(self, device):
        found = []
        even = (device & 1) == 0
        for base, swap in ((device, False), (device ^ 1, True)):
            for position in range(1 << self.stages):
                masks = [
                    sum(order[k] for k in range(self.stages) if position >> k & 1)
                    for order in self.orders
                ]
                if swap:
                    masks = masks[::-1]
                found.append(base ^ jnp.where(even, *masks))
        return found

    def step(self, stage, arrays):
        route = self.twin() if stage == self.stages else self.partner(stage)
        return [lax.ppermute(item, "seq", route) for item in arrays]

    def fold(self, stage, own, low, high):
        half = 1 << stage
        sent = (own[half:].astype(f32) + high.astype(f32)).astype(bf16)
        kept = own[:half].astype(f32) + low.astype(f32)
        return kept, sent


def halves(item):
    half = item.shape[0] // 2
    return item[:half], item[half:]


def join(held, came):
    return [jnp.concatenate(pair) for pair in zip(held, came)]


def pack_kernel(rings, lengths, w_qkv, w_out, w_in, w_back, *refs):
    vectors, (info, *inverses, payload, staged) = refs[:-5], refs[-5:]
    device = lax.axis_index("seq")
    info[0] = device
    start = jnp.int32(0)
    for k in range(3):
        length = lengths[k]
        info[1 + k] = length
        info[4 + k] = start
        start = start + (length + 15) // 16 * 16
        info[7 + k] = start
    for ring, inverse in zip(rings, inverses):
        for place, block in enumerate(ring.places(device)):
            inverse[place] = block
    block, width = w_out.shape
    chunks = w_in.shape[1] // width
    staged[...] = jnp.zeros(staged.shape, f32)
    for k, vector in enumerate(vectors):
        size = vector.shape[0]
        lane = k * block
        staged[pl.ds(0, 1), pl.ds(lane, size)] = vector[...].astype(f32).reshape(1, size)
    for c in range(3):
        payload[0, pl.ds(block * c, block), :] = w_qkv[:, pl.ds(c * width, width)]
    payload[0, pl.ds(block * 3, block), :] = staged[...].astype(bf16)
    payload[0, pl.ds(block * 4, block), :] = w_out[...]
    for c in range(chunks):
        payload[0, pl.ds(block * (c + 5), block), :] = w_in[:, pl.ds(c * width, width)]
    payload[0, pl.ds(block * (chunks + 5), block * chunks), :] = w_back[...]


def pack(rings, lengths, w_qkv, w_out, w_in, w_back, vectors):
    block, width = w_out.shape
    rows = 5 * block + w_in.shape[1] // width * block + w_back.shape[0]
    return pl.pallas_call(
        functools.partial(pack_kernel, rings),
        out_shape=(
            jax.ShapeDtypeStruct((10,), jnp.int32),
            jax.ShapeDtypeStruct((BLOCKS,), jnp.int32),
            jax.ShapeDtypeStruct((BLOCKS,), jnp.int32),
            jax.ShapeDtypeStruct((1, rows, width), bf16),
        ),
        in_specs=[SCALARS] + spec(4 + len(vectors)),
        out_specs=(SCALARS,) * 3 + tuple(spec(1)),
        scratch_shapes=[pltpu.VMEM((block, width), f32)],
        compiler_params=params(62),
        name="pack",
        cost_estimate=cost(1.5),
    )(lengths, w_qkv, w_out, w_in, w_back, *vectors)


def unpack_kernel(kept_one, came_one, kept_two, came_two, *outs):
    block, width = kept_one.shape[1] // 4, kept_two.shape[2]
    w_qkv, w_out, w_in, w_back = outs[:4]
    for c in range(3):
        rows = pl.ds(block * c, block)
        w_qkv[:, pl.ds(c * width, width)] = kept_one[0, rows, :] + came_one[0, rows, :].astype(f32)
    rows = pl.ds(block * 3, block)
    lines = kept_one[0, rows, :] + came_one[0, rows, :].astype(f32)
    for k, out in enumerate(outs[4:]):
        size = out.shape[0]
        lane = k * block
        out[...] = lines[0:1, lane : lane + size].reshape(size)
    chunks = w_in.shape[1] // width

    def total(at, size):
        rows = pl.ds(at, size)
        return kept_two[0, rows, :] + came_two[0, rows, :].astype(f32)

    w_out[...] = total(2 * block * chunks, block)
    for c in range(chunks):
        w_in[:, pl.ds(c * width, width)] = total(block * c, block)
    w_back[...] = total(block * chunks, block * chunks)


def unpack(kept_one, came_one, kept_two, came_two, like):
    return pl.pallas_call(
        unpack_kernel,
        out_shape=[jax.ShapeDtypeStruct(item.shape, f32) for item in like],
        in_specs=spec(4),
        out_specs=spec(len(like)),
        compiler_params=params(8),
        name="unpack",
        cost_estimate=cost(1.5),
    )(kept_one, came_one, kept_two, came_two)


def exchange(to_twin, to_other):
    count = lax.axis_size("seq")
    twin = [(i, i ^ 1) for i in range(count)]
    other = [(i, i + 1) for i in range(1, count - 1, 2)]
    other += [(j, i) for i, j in other]
    return lax.ppermute(to_other, "seq", other), lax.ppermute(to_twin, "seq", twin)


def order(items, *after):
    return lax.optimization_barrier((items, after))[0]


def per_device(
    lengths,
    tokens,
    ln1_gain,
    ln1_bias,
    w_qkv,
    w_out,
    out_bias,
    ln2_gain,
    ln2_bias,
    w_in,
    in_bias,
    w_back,
    back_bias,
    cotangent,
):
    devices = lax.axis_size("seq")
    device = lax.axis_index("seq")
    rows, width = tokens.shape
    total = rows * devices
    plan = Plan(rows)
    block = width // BLOCKS
    chunks = w_in.shape[1] // width
    small = (ln1_gain, ln1_bias, out_bias, ln2_gain, ln2_bias, back_bias, in_bias)
    direct = devices == BLOCKS
    ring = Ring(BLOCKS, (16, 2, 8, 4), (4, 16, 2, 8))
    sums_ring = Ring(BLOCKS, (16, 8, 4, 2), (2, 16, 8, 4))
    last = ring.stages - 1
    core = ring.stages
    if direct:
        info, inverse, sums_inverse, payload = pack(
            (ring, sums_ring), lengths, w_qkv, w_out, w_in, w_back, small
        )
        from_other, from_twin = exchange(*edge_sums(plan, total, info, order(tokens, payload)))
        ready = prepare(plan, total, info, order(tokens, payload))
        (payload,) = join([payload], ring.step(0, [payload]))
        a, b = payload[:, : 4 * block], payload[:, 4 * block :]
        a_came, b_came = ring.step(1, [a, b])
        (a,) = join([a], [a_came])
        a = order(a, from_other, from_twin)
        (a_came,) = ring.step(2, [a])
        (a,) = join([a], [a_came])
        (b,) = join([b], [b_came])
        a = order(a, b, ready)
        (b_came,) = ring.step(2, [b])
        (a_came,) = ring.step(3, [a])
        one = [a, a_came] + ring.step(core, [a, a_came])
        (b,) = join([b], [b_came])
        b = order(b, a_came)
    else:
        padded = (lengths + 15) // 16 * 16
        ends = jnp.cumsum(padded, dtype=jnp.int32)
        info = jnp.concatenate([device[None].astype(jnp.int32), lengths, ends - padded, ends])
        inverse = sums_inverse = jnp.arange(BLOCKS, dtype=jnp.int32)
        from_other, from_twin = exchange(*edge_sums(plan, total, info, tokens))
        ready = prepare(plan, total, info, tokens)

        def whole(item):
            return lax.all_gather(item, "seq", axis=0, tiled=True)

        def split(item, parts):
            each = BLOCKS // parts
            return [item[k * each : (k + 1) * each] for k in range(parts)]

        line = jnp.concatenate([whole(item).reshape(BLOCKS, 1, -1) for item in small], axis=2)
        line = jnp.pad(line, ((0, 0), (0, block - 1), (0, width - line.shape[2])))
        one = whole(w_qkv).reshape(BLOCKS, block, 3, width).transpose(0, 2, 1, 3)
        one = one.reshape(BLOCKS, 3 * block, width)
        one = split(jnp.concatenate([one, line], axis=1), PIECES)
        full_in = whole(w_in).reshape(BLOCKS, block, chunks, width)
        full_in = full_in.transpose(0, 2, 1, 3).reshape(BLOCKS, chunks * block, width)
        full_two = [
            whole(w_out).reshape(BLOCKS, block, width),
            full_in,
            whole(w_back).reshape(BLOCKS, chunks * block, width),
        ]
        two = split(jnp.concatenate(full_two, axis=1), PIECES)
    standard, spread, pool, allowed, allowed_back, counts, edge_allowed, edge_counts = ready
    queries, pairs, halo_queries, halo_pairs, weight, vectors, shift_in = project(
        plan, total, info, inverse, standard, pool, from_twin, from_other, one
    )
    if direct:
        (b_came,) = ring.step(last, [b])
        (b_twin,) = ring.step(core, [b])
        allowed = order(allowed, b)
    attended, mixed, scale = attend(
        plan, total, info, allowed, counts, queries, pairs, halo_pairs
    )
    if direct:
        b_came = order(b_came, attended)
        two = [b, b_came, b_twin] + ring.step(core, [b_came])
    result, resid, grad_normed, out_weight, own_two, low_two, high_two, sum_in = feed_forward(
        (inverse, sums_inverse), tokens, cotangent, attended, vectors, shift_in, two
    )
    if direct:
        high, low = sums_ring.step(core, [high_two, low_two])
    (
        grad_resid,
        grads_a,
        grads_b,
        to_twin,
        to_other,
        sums,
        own_out,
        low_out,
        high_out,
    ) = middle(
        plan,
        info,
        sums_inverse,
        cotangent,
        attended,
        mixed,
        scale,
        vectors,
        resid,
        grad_normed,
        out_weight,
    )
    from_other, from_twin = exchange(to_twin, to_other)

    def with_out(item, out):
        return jnp.concatenate([item, out], axis=1)

    if direct:
        high_out, low_out = sums_ring.step(core, [high_out, low_out])
        kept, sent = sums_ring.fold(
            last, with_out(own_two, own_out), with_out(low, low_out), with_out(high, high_out)
        )
        sent_low, sent_high = halves(sent)
        sent_low, sent_high = order((sent_low, sent_high), from_twin)
        high, low = sums_ring.step(last, [sent_high, sent_low])
        grads_a = order(grads_a, sent_high, sent_low)
    grad_queries, grad_pairs = attend_back(
        plan, total, allowed_back, counts, queries, pairs, halo_pairs, (grads_a, grads_b)
    )
    from_other, from_twin = order((from_other, from_twin), grad_queries)
    if direct:
        high = order(high, grad_queries, from_other, from_twin)
        kept, kept_high = halves(kept)
        sent = (kept_high + high.astype(f32)).astype(bf16)
        (came,) = sums_ring.step(last - 1, [sent])
        from_other, from_twin = order((from_other, from_twin), sent)
    edges = edge_back(
        plan, info, edge_allowed, edge_counts, halo_queries, pairs, from_twin, from_other
    )
    grad_tokens, own_one, low_one, high_one = finish(
        plan,
        total,
        info,
        sums_inverse,
        standard,
        spread,
        weight,
        vectors,
        grad_resid,
        sums,
        sum_in,
        *grad_queries,
        *grad_pairs,
        *edges,
    )
    if direct:
        high_one, low_one = sums_ring.step(core, [high_one, low_one])
        low, came = order((low, came), grad_tokens)
        kept = kept + low.astype(f32)
        kept, sent = sums_ring.fold(last - 2, kept, *halves(came))
        (came,) = sums_ring.step(last - 2, [sent])
        high_one, low_one = order((high_one, low_one), sent)
        own_one, sent_one = sums_ring.fold(last, own_one, low_one, high_one)
        (came_one,) = sums_ring.step(last, [sent_one])
        own_one, sent_one = sums_ring.fold(last - 1, own_one, *halves(came_one))
        (came_one,) = sums_ring.step(last - 1, [sent_one])
        came = order(came, sent_one)
        kept, sent = sums_ring.fold(0, kept, *halves(came))
        (came,) = sums_ring.step(0, [sent])
        came_one = order(came_one, sent)
        own_one, sent_one = sums_ring.fold(last - 2, own_one, *halves(came_one))
        (came_one,) = sums_ring.step(last - 2, [sent_one])
        own_one, sent_one = sums_ring.fold(0, own_one, *halves(came_one))
        (came_one,) = sums_ring.step(0, [sent_one])
        grads = unpack(own_one, came_one, kept, came, (w_qkv, w_out, w_in, w_back) + small)
        grad_w_qkv, grad_w_out, grad_w_in, grad_w_back = grads[:4]
        parts = grads[4:]
    else:

        def shared(item):
            return lax.psum_scatter(item, "seq", scatter_dimension=0, tiled=True)

        full = jnp.concatenate([x.astype(f32) for x in (own_one, low_one, high_one)])
        line = full[:, 3 * block]
        sizes = [block] * 6 + [chunks * block]
        starts = [k * block for k in range(7)]
        parts = [
            shared(line[:, at : at + size].reshape(-1)) for at, size in zip(starts, sizes)
        ]
        grad_w_qkv = full[:, : 3 * block].reshape(BLOCKS, 3, block, width).transpose(0, 2, 1, 3)
        grad_w_qkv = shared(grad_w_qkv.reshape(width, 3 * width))
        full = jnp.concatenate([x.astype(f32) for x in (own_out, low_out, high_out)])
        grad_w_out = shared(full.reshape(width, width))
        full = jnp.concatenate([x.astype(f32) for x in (own_two, low_two, high_two)])
        full_in = full[:, : block * chunks]
        full_in = full_in.reshape(BLOCKS, chunks, block, width).transpose(0, 2, 1, 3)
        grad_w_in = shared(full_in.reshape(width, chunks * width))
        grad_w_back = shared(full[:, block * chunks :].reshape(chunks * width, width))
    gain_one, bias_one, shift_out, gain_two, bias_two, shift_back, shift_hidden = parts
    return (
        result,
        grad_tokens,
        gain_one,
        bias_one,
        grad_w_qkv,
        grad_w_out,
        shift_out,
        gain_two,
        bias_two,
        grad_w_in,
        shift_hidden,
        grad_w_back,
        shift_back,
    )


def solution(mesh):
    flat, wide = P("seq"), P("seq", None)
    weights = (flat, flat, wide, wide, flat, flat, flat, wide, flat, wide, flat)
    return jax.shard_map(
        per_device,
        mesh=mesh,
        in_specs=(P(), wide) + weights + (wide,),
        out_specs=(wide, wide) + weights,
        check_vma=False,
    )
```

```python
import functools
import math

import jax
import jax.numpy as jnp
from jax import lax
from jax.experimental import pallas as pl
from jax.experimental.pallas import tpu as pltpu
from jax.sharding import PartitionSpec as P

HEAD_DIM = 64
LEVELS = 5
HALO = 32
BLOCK = 64
WINDOW = BLOCK + 2 * HALO
QUAD = 4
QUAD_WIDTH = QUAD * HEAD_DIM
PIECES = 4
BLOCKS = 32
LINE = 128
LINE_ROWS = 8
MIXED = 16
FAR = 1 << 26
SEQ_STEP = 1 << 21
MIB = 1024 * 1024

f32 = jnp.float32
bf16 = jnp.bfloat16


class Plan:
    def locate(self, block):
        firsts = [at // BLOCK for at in self.query_at]
        level = sum((block >= first).astype(jnp.int32) for first in firsts[1:])
        start = sum(
            jnp.where(level == k, first, 0) for k, first in enumerate(firsts)
        )
        return level, block - start

    def __init__(self, rows):
        self.rows = rows
        self.counts = [rows >> level for level in range(LEVELS)]
        self.padded = [-(-count // BLOCK) * BLOCK for count in self.counts]
        self.query_at = [sum(self.padded[:level]) for level in range(LEVELS)]
        self.query_rows = sum(self.padded)
        self.key_at = [self.query_at[level] + 2 * HALO * level for level in range(LEVELS)]
        self.key_rows = self.query_rows + 2 * HALO * LEVELS
        self.blocks = [
            (level, part)
            for level in range(LEVELS)
            for part in range(self.padded[level] // BLOCK)
        ]


def dot_nn(a, b):
    return lax.dot_general(a, b, (((1,), (0,)), ((), ())), preferred_element_type=f32)


def dot_nt(a, b):
    return lax.dot_general(a, b, (((1,), (1,)), ((), ())), preferred_element_type=f32)


def dot_tn(a, b):
    return lax.dot_general(a, b, (((0,), (0,)), ((), ())), preferred_element_type=f32)


def spec(count):
    return [pl.BlockSpec(memory_space=pltpu.VMEM)] * count


SCALARS = pl.BlockSpec(memory_space=pltpu.SMEM)


def slot_facts(info, slot, total):
    number = jnp.zeros(slot.shape, jnp.int32)
    for s in range(3):
        number = number + (slot >= info[7 + s]).astype(jnp.int32)
    begin = jnp.where(number == 0, info[4], jnp.where(number == 1, info[5], info[6]))
    length = jnp.where(number == 0, info[1], jnp.where(number == 1, info[2], info[3]))
    inside = (slot >= 0) & (slot < total) & (number < 3)
    return number, slot - begin, length, inside


def tile_codes(info, coarse, level, total, outside):
    number, offset, _, inside = slot_facts(info, coarse << level, total)
    wide = jnp.where(inside, number * SEQ_STEP + (offset >> (level + 4)), outside)
    fine = number * SEQ_STEP + (offset >> (level + 3))
    return wide, fine


def admitted(query_codes, key_codes, level):
    near = jnp.abs(query_codes[0] - key_codes[0]) <= 1
    least = jnp.where(level > 0, 2, 0)
    near = near & (jnp.abs(query_codes[1] - key_codes[1]) >= least)
    return jnp.where(near, 1.0, 0.0)


def live_counts(info, coarse, level, total):
    _, offset, length, inside = slot_facts(info, coarse << level, total)
    span = 1 << level
    return jnp.where(inside, jnp.clip(length - offset, 0, span), 0).astype(f32)


def head_masks(rows):
    lane = lax.broadcasted_iota(jnp.int32, (rows, QUAD_WIDTH), 1) // HEAD_DIM
    return [jnp.where(lane == h, 1.0, 0.0).astype(bf16) for h in range(QUAD)]


def spread_heads(block, masks):
    return jnp.concatenate([block * m for m in masks], axis=0)


def join_pair(stacked, first):
    rows = stacked.shape[0] // 2
    return jnp.where(first, stacked[:rows], stacked[rows:])


def is_even(info):
    return (info[0] & 1) == 0


def params(size):
    return pltpu.CompilerParams(vmem_limit_bytes=size * MIB)


def cost(micros):
    return pl.CostEstimate(flops=1, bytes_accessed=1, transcendentals=0)


def fill_extended(plan, own, halos, extended):
    for level in range(LEVELS):
        at, count, mine = plan.key_at[level], plan.counts[level], plan.query_at[level]
        extended[pl.ds(at, HALO), :] = halos[pl.ds(HALO * level, HALO), :]
        extended[pl.ds(at + HALO, count), :] = own[pl.ds(mine, count), :]
        extended[pl.ds(at + HALO + count, HALO), :] = halos[pl.ds(HALO * (LEVELS + level), HALO), :]
        rest = plan.padded[level] - count
        if rest:
            extended[pl.ds(at + 2 * HALO + count, rest), :] = jnp.zeros(
                (rest, extended.shape[1]), bf16
            )


def place_halos(info, from_twin, from_other, halos):
    even = is_even(info)
    size = halos.shape[0] // 2
    halos[pl.ds(pl.multiple_of(jnp.where(even, size, 0), size), size), :] = from_twin[...]
    halos[pl.ds(pl.multiple_of(jnp.where(even, 0, size), size), size), :] = from_other[...]


def hand_out(info, ends, to_twin, to_other):
    even = is_even(info)
    size = LEVELS * HALO
    to_twin[...] = ends[pl.ds(pl.multiple_of(jnp.where(even, size, 0), size), size), :]
    to_other[...] = ends[pl.ds(pl.multiple_of(jnp.where(even, 0, size), size), size), :]


def ln_stats(values):
    center = values - jnp.mean(values, axis=-1, keepdims=True)
    spread = jnp.mean(center * center, axis=-1, keepdims=True)
    return center, lax.rsqrt(spread + 1e-05)


def ln_back(grad, hat, rstd, gain):
    scaled = grad * gain
    mean_one = jnp.mean(scaled, axis=-1, keepdims=True)
    mean_two = jnp.mean(scaled * hat, axis=-1, keepdims=True)
    return rstd * (scaled - mean_one - hat * mean_two), grad * hat


def column_sum(values):
    return jnp.sum(values, axis=0, keepdims=True)


def unpack_vector(table, first, each):
    blocks, lanes = table.shape
    length = blocks * each
    source = lax.broadcasted_iota(jnp.int32, (lanes, length), 0)
    target = lax.broadcasted_iota(jnp.int32, (lanes, length), 1)
    pick = jnp.where(source == first + (target & (each - 1)), 1.0, 0.0).astype(bf16)
    spreaded = dot_nn(table, pick)
    block = lax.broadcasted_iota(jnp.int32, (blocks, length), 0)
    lane = lax.broadcasted_iota(jnp.int32, (blocks, length), 1)
    return column_sum(jnp.where(lane // each == block, spreaded, 0.0))


def pack_vectors(vectors, last, blocks, lanes):
    size = last.shape[1] // blocks // 4

    def one(row, first, each):
        length = blocks * each
        source = lax.broadcasted_iota(jnp.int32, (length, lanes), 0)
        target = lax.broadcasted_iota(jnp.int32, (length, lanes), 1)
        pick = jnp.where(target == first + (source & (each - 1)), 1.0, 0.0).astype(bf16)
        block = lax.broadcasted_iota(jnp.int32, (blocks, length), 0)
        lane = lax.broadcasted_iota(jnp.int32, (blocks, length), 1)
        return dot_nn(jnp.where(lane // each == block, row, 0.0).astype(bf16), pick)

    total = one(last, 6 * size, 4 * size)
    for k, vector in enumerate(vectors):
        total = total + one(vector, k * size, size)
    return total


def edge_sums_kernel(plan, total, info, tokens, to_twin, to_other, ends):
    rows, width = tokens.shape
    center, rstd = ln_stats(tokens[...].astype(f32))
    plain = (center * rstd).astype(bf16)
    places = info[0] * rows + lax.broadcasted_iota(jnp.int32, (rows, width), 0)
    living = (plain.astype(f32) * live_counts(info, places, 0, total)).astype(bf16)
    size = 2 * LEVELS * HALO
    row = lax.broadcasted_iota(jnp.int32, (size, rows), 0)
    slot = lax.broadcasted_iota(jnp.int32, (size, rows), 1)
    row_one = lax.broadcasted_iota(jnp.int32, (size, 1), 0)
    wanted = jnp.zeros((size, rows), jnp.int32)
    shift = jnp.zeros((size, rows), jnp.int32)
    share = jnp.zeros((size, 1), f32)
    for k in range(2 * LEVELS):
        level, at = k % LEVELS, k * HALO
        first = 0 if k < LEVELS else plan.counts[level] - HALO
        wanted = jnp.where(row >= at, row - at + first, wanted)
        shift = jnp.where(row >= at, level, shift)
        share = jnp.where(row_one >= at, 0.5**level, share)
    pool = jnp.where((slot >> shift) == wanted, 1.0, 0.0).astype(bf16)
    ends[...] = (dot_nn(pool, plain) * share).astype(bf16)
    row = lax.broadcasted_iota(jnp.int32, (MIXED, rows), 0)
    slot = info[0] * rows + lax.broadcasted_iota(jnp.int32, (MIXED, rows), 1)
    wanted = jnp.full((MIXED, rows), -1, jnp.int32)
    shift = jnp.zeros((MIXED, rows), jnp.int32)
    for level in range(1, LEVELS):
        for k in range(3):
            here = row == (level - 1) * 3 + k
            wanted = jnp.where(here, (info[4 + k] + info[1 + k]) >> level, wanted)
            shift = jnp.where(here, level, shift)
    pick = jnp.where((slot >> shift) == wanted, 1.0, 0.0).astype(bf16)
    mixed = dot_nn(pick, living).astype(bf16)
    even = is_even(info)
    size = LEVELS * HALO
    for target, first in ((to_twin, size), (to_other, 0)):
        at = pl.multiple_of(jnp.where(even, first, size - first), size)
        target[pl.ds(0, size), :] = ends[pl.ds(at, size), :]
        target[pl.ds(size, MIXED), :] = mixed


def edge_sums(plan, total, info, tokens):
    width = tokens.shape[1]
    size = LEVELS * HALO
    return pl.pallas_call(
        functools.partial(edge_sums_kernel, plan, total),
        out_shape=[jax.ShapeDtypeStruct((size + MIXED, width), bf16)] * 2,
        in_specs=[SCALARS] + spec(1),
        out_specs=spec(2),
        scratch_shapes=[pltpu.VMEM((2 * size, width), bf16)],
        compiler_params=params(10),
        name="edge_sums",
        cost_estimate=cost(1.5),
    )(info, tokens)


def prepare_kernel(
    plan,
    total,
    info,
    tokens,
    standard,
    spread,
    pool,
    allowed,
    allowed_back,
    counts,
    edge_allowed,
    edge_counts,
):
    rows = plan.rows
    device = info[0]
    center, rstd = ln_stats(tokens[...].astype(f32))
    standard[...] = center * rstd
    spread[...] = jnp.broadcast_to(rstd, spread.shape)
    pooled_rows = pool.shape[0]
    row = lax.broadcasted_iota(jnp.int32, (pooled_rows, rows), 0)
    slot = lax.broadcasted_iota(jnp.int32, (pooled_rows, rows), 1)
    first = jnp.zeros((pooled_rows, rows), jnp.int32)
    shift = jnp.zeros((pooled_rows, rows), jnp.int32)
    for level in range(1, LEVELS):
        at = plan.query_at[level] - plan.query_at[1]
        first = jnp.where(row >= at, at, first)
        shift = jnp.where(row >= at, level, shift)
    pool[...] = jnp.where((slot >> shift) == row - first, 1.0, 0.0).astype(bf16)

    def block_step(block, carry):
        level, part = plan.locate(block)
        first = device * (rows >> level) + BLOCK * part
        here = pl.ds(pl.multiple_of(BLOCK * block, BLOCK), BLOCK)
        there = pl.ds(pl.multiple_of(WINDOW * block, WINDOW), WINDOW)
        row = first + lax.broadcasted_iota(jnp.int32, (BLOCK, WINDOW), 0)
        column = first - HALO + lax.broadcasted_iota(jnp.int32, (BLOCK, WINDOW), 1)
        allowed[here, :] = admitted(
            tile_codes(info, row, level, total, FAR),
            tile_codes(info, column, level, total, -FAR),
            level,
        )
        key_row = first - HALO + lax.broadcasted_iota(jnp.int32, (WINDOW, 128), 0)
        lane = lax.broadcasted_iota(jnp.int32, (WINDOW, 128), 1)
        row = first + (lane & (BLOCK - 1))
        allowed_back[there, :] = admitted(
            tile_codes(info, row, level, total, FAR),
            tile_codes(info, key_row, level, total, -FAR),
            level,
        )
        counts[there, :] = live_counts(info, key_row, level, total).astype(bf16)
        return carry

    lax.fori_loop(0, len(plan.blocks), block_step, 0, unroll=2)
    two = 2 * HALO
    key = lax.broadcasted_iota(jnp.int32, (two, 128), 0)
    lane = lax.broadcasted_iota(jnp.int32, (two, 128), 1) & (two - 1)
    facing = jnp.where((key < HALO) == (lane < HALO), 1.0, 0.0)
    for level in range(LEVELS):
        count = plan.counts[level]
        start = device * count
        key_row = start + jnp.where(key < HALO, key, count - two + key)
        row = start + jnp.where(lane < HALO, lane - HALO, count - HALO + lane)
        here = pl.ds(two * level, two)
        edge_allowed[here, :] = facing * admitted(
            tile_codes(info, row, level, total, FAR),
            tile_codes(info, key_row, level, total, -FAR),
            level,
        )
        edge_counts[here, :] = live_counts(info, key_row, level, total).astype(bf16)


def prepare(plan, total, info, tokens):
    rows, width = tokens.shape
    blocks = len(plan.blocks)
    return pl.pallas_call(
        functools.partial(prepare_kernel, plan, total),
        out_shape=(
            jax.ShapeDtypeStruct((rows, width), f32),
            jax.ShapeDtypeStruct((rows, 128), f32),
            jax.ShapeDtypeStruct((plan.query_rows - plan.query_at[1], rows), bf16),
            jax.ShapeDtypeStruct((BLOCK * blocks, WINDOW), f32),
            jax.ShapeDtypeStruct((WINDOW * blocks, 128), f32),
            jax.ShapeDtypeStruct((WINDOW * blocks, 128), bf16),
            jax.ShapeDtypeStruct((2 * HALO * LEVELS, 128), f32),
            jax.ShapeDtypeStruct((2 * HALO * LEVELS, 128), bf16),
        ),
        in_specs=[SCALARS] + spec(1),
        out_specs=tuple(spec(8)),
        compiler_params=params(8),
        name="prepare",
        cost_estimate=cost(4),
    )(info, tokens)


def project_kernel(
    plan, total, info, inverse, standard, pool, from_twin, from_other, *refs
):
    pieces, outs = refs[:PIECES], refs[PIECES:]
    queries, pairs, halo_queries, halo_pairs = (outs[2 * k : 2 * k + 2] for k in range(4))
    weight, vectors, shift_out, table, edges, halos, mixed = outs[8:]
    rows, width = standard.shape
    device = info[0]
    each = pieces[0].shape[0]
    block_rows = pieces[0].shape[1] // 3 // 16 * 16
    for p in range(PIECES * each):
        i = inverse[p]
        there = pl.ds(pl.multiple_of(i * block_rows, block_rows), block_rows)
        piece, q = pieces[p // each], p % each
        for c in range(3):
            weight[there, pl.ds(c * width, width)] = piece[q, pl.ds(block_rows * c, block_rows), :]
        line = piece[q, pl.ds(block_rows * 3, LINE_ROWS), pl.ds(0, 2 * LINE)].astype(f32)
        table[pl.ds(i, 1), :] = line[0:1]
    packed = table[...].astype(bf16)
    singles = [unpack_vector(packed, k * block_rows, block_rows) for k in range(2)]
    low = (standard[...] * singles[0] + singles[1]).astype(bf16)
    pooled_rows = pool.shape[0]
    share = jnp.zeros((pooled_rows, 1), f32)
    row_one = lax.broadcasted_iota(jnp.int32, (pooled_rows, 1), 0)
    for level in range(1, LEVELS):
        at = plan.query_at[level] - plan.query_at[1]
        share = jnp.where(row_one >= at, 0.5**level, share)
    places = device * rows + lax.broadcasted_iota(jnp.int32, (rows, QUAD_WIDTH), 0)
    live = live_counts(info, places, 0, total)
    place_halos(info, from_twin, from_other, edges)
    size = LEVELS * HALO
    for k in range(2):
        rest = pl.ds(k * (size + MIXED) + size, MIXED)
        mixed[pl.ds(k * MIXED, MIXED), :] = edges[rest, :].astype(f32)
    for k in range(2 * LEVELS):
        level, here = k % LEVELS, pl.ds(k * HALO, HALO)
        side, span = k // LEVELS * (size + MIXED), 1 << level
        mean = edges[pl.ds(side + level * HALO, HALO), :].astype(f32)
        halos[here, pl.ds(0, width)] = (mean * singles[0] + singles[1]).astype(bf16)
        count = plan.counts[level]
        first = device * count + (-HALO if k < LEVELS else count)
        place = first + lax.broadcasted_iota(jnp.int32, (HALO, 128), 0)
        counts = live_counts(info, place, level, total)
        wide = jnp.concatenate([counts] * (width // 128), axis=1)
        value = jnp.where(wide == span, mean * span, 0.0)
        if level:
            number = slot_facts(info, place << level, total)[0]
            for index in range(3):
                ends = (counts > 0.0) & (counts < span) & (number == index)
                ends = jnp.where(ends, 1.0, 0.0)
                ends = jnp.concatenate([ends] * (width // 128), axis=1)
                row = k // LEVELS * MIXED + (level - 1) * 3 + index
                value = value + ends * mixed[pl.ds(row, 1), :]
        halos[here, pl.ds(width, width)] = (value * singles[0] + wide * singles[1]).astype(bf16)
    lanes = QUAD_WIDTH
    scale = 1.0 / math.sqrt(HEAD_DIM)
    parts = [(divmod(part, 2), pl.ds(part * lanes, lanes)) for part in range(3 * width // lanes)]
    own = pl.ds(0, rows)
    above = pl.ds(rows, pooled_rows)
    blocks = [dot_nn(low, weight[:, columns]).astype(bf16) for _, columns in parts]
    for index, ((kind, quad), _) in enumerate(parts):
        if kind == 0:
            queries[quad][own, :] = (blocks[index].astype(f32) * scale).astype(bf16)
            continue
        if kind == 2:
            blocks[index] = (blocks[index].astype(f32) * live).astype(bf16)
        pairs[quad][own, pl.ds((kind - 1) * lanes, lanes)] = blocks[index]
    pooled = [dot_nn(pool[...], block) for block in blocks]
    for ((kind, quad), _), item in zip(parts, pooled):
        if kind == 0:
            queries[quad][above, :] = (item * (share * scale)).astype(bf16)
            continue
        if kind == 1:
            item = item * share
        pairs[quad][above, pl.ds((kind - 1) * lanes, lanes)] = item.astype(bf16)
    sides = [
        dot_nn(halos[:, pl.ds(width if kind == 2 else 0, width)], weight[:, columns])
        for (kind, _), columns in parts
    ]
    for ((kind, quad), _), item in zip(parts, sides):
        if kind == 0:
            halo_queries[quad][...] = (item * scale).astype(bf16)
        else:
            halo_pairs[quad][:, pl.ds((kind - 1) * lanes, lanes)] = item.astype(bf16)
    singles += [unpack_vector(packed, k * block_rows, block_rows) for k in range(2, 6)]
    for k, single in enumerate(singles):
        vectors[pl.ds(k, 1), :] = single
    shift_out[...] = unpack_vector(packed, 6 * block_rows, 4 * block_rows)


def project(plan, total, info, inverse, standard, pool, from_twin, from_other, pieces):
    rows, width = standard.shape
    halo = LEVELS * HALO
    blocks = PIECES * pieces[0].shape[0]
    depth = blocks * (pieces[0].shape[1] - LINE_ROWS) // 3
    half = width // 2
    outs = pl.pallas_call(
        functools.partial(project_kernel, plan, total),
        out_shape=(
            [jax.ShapeDtypeStruct((plan.query_rows, half), bf16)] * 2
            + [jax.ShapeDtypeStruct((plan.query_rows, 2 * half), bf16)] * 2
            + [jax.ShapeDtypeStruct((2 * halo, half), bf16)] * 2
            + [jax.ShapeDtypeStruct((2 * halo, 2 * half), bf16)] * 2
            + [
                jax.ShapeDtypeStruct((depth, 3 * width), bf16),
                jax.ShapeDtypeStruct((8, depth), f32),
                jax.ShapeDtypeStruct((1, 4 * depth), f32),
            ]
        ),
        in_specs=[SCALARS, SCALARS] + spec(4 + PIECES),
        out_specs=spec(11),
        scratch_shapes=[
            pltpu.VMEM((blocks, 2 * LINE), f32),
            pltpu.VMEM((2 * (halo + MIXED), width), bf16),
            pltpu.VMEM((2 * halo, 2 * width), bf16),
            pltpu.VMEM((2 * MIXED, width), f32),
        ],
        compiler_params=params(18),
        name="project",
        cost_estimate=cost(3.3),
    )(info, inverse, standard, pool, from_twin, from_other, *pieces)
    return [outs[2 * k : 2 * k + 2] for k in range(4)] + list(outs[8:])


def attend_kernel(plan, total, info, mask, counts_of, *refs):
    queries, pairs, halos, attended, mixed, scale, extended = (
        refs[2 * k : 2 * k + 2] for k in range(7)
    )
    numer, denom = refs[14:]
    rows = plan.rows
    device = info[0]
    for quad in range(2):
        fill_extended(plan, pairs[quad], halos[quad], extended[quad])
    first_head = lax.broadcasted_iota(jnp.int32, (BLOCK, 128), 1) < HEAD_DIM
    masks = head_masks(BLOCK)

    def prepare(block):
        level, part = plan.locate(block)
        here = pl.ds(pl.multiple_of(BLOCK * block, BLOCK), BLOCK)
        there = pl.ds(pl.multiple_of(BLOCK * block + 2 * HALO * level, BLOCK), WINDOW)
        allowed = mask[here, :]
        counts = counts_of[pl.ds(pl.multiple_of(WINDOW * block, WINDOW), WINDOW), :]
        return here, there, allowed, counts

    def block_step(step, carry):
        work = []
        for k in range(4):
            here, there, allowed, counts = prepare(step * 4 + k)
            allowed = jnp.concatenate([allowed] * 4, axis=0) > 0.0
            for part in range(8 // 4):
                work.append((here, there, allowed, counts, part))
        scores = []
        for here, there, allowed, counts, part in work:
            wide = 4 * HEAD_DIM
            quad, half = divmod(part * wide, QUAD_WIDTH)
            lanes = pl.ds(half, wide)
            q = spread_heads(queries[quad][here, lanes], masks)
            scores.append(dot_nt(q, extended[quad][there, lanes]))
        weights = [
            jnp.where(item[2], jnp.exp(score), 0.0).astype(bf16)
            for item, score in zip(work, scores)
        ]
        for (here, there, allowed, counts, part), weight in zip(work, weights):
            wide = 4 * HEAD_DIM
            for sub in range(4 // 2):
                pair = part * (4 // 2) + sub
                quad, half = divmod(pair, 2)
                v = extended[quad][there, pl.ds(QUAD_WIDTH + 128 * half, 128)]
                both = dot_nn(
                    weight[128 * sub : 128 * sub + 128], jnp.concatenate([v, counts], axis=1)
                )
                numer[pair, here, :] = join_pair(both[:, :128], first_head)
                denom[pair, here, :] = join_pair(both[:, 128:], first_head)
        return carry

    lax.fori_loop(0, len(plan.blocks) // 4, block_step, 0, unroll=1)
    places = device * rows + lax.broadcasted_iota(jnp.int32, (rows, 128), 0)
    live = live_counts(info, places, 0, total)
    for pair in range(4):
        for sums in (numer, denom):
            for level in range(LEVELS - 1, 0, -1):
                count = plan.counts[level]
                upper = sums[pair, pl.ds(plan.query_at[level], count), :]
                for parity in range(2):
                    there = pl.ds(plan.query_at[level - 1] + parity, count, stride=2)
                    sums[pair, there, :] = sums[pair, there, :] + upper
        quad, half = divmod(pair, 2)
        lanes = pl.ds(128 * half, 128)
        factor = live / (denom[pair, pl.ds(0, rows), :] + 1.0 - live)
        value = numer[pair, pl.ds(0, rows), :] * factor
        scale[quad][:, lanes] = factor
        mixed[quad][:, lanes] = value
        attended[quad][:, lanes] = value.astype(bf16)


def attend(plan, total, info, mask, counts, queries, pairs, halos):
    rows, width = plan.rows, queries[0].shape[1]
    outs = pl.pallas_call(
        functools.partial(attend_kernel, plan, total),
        out_shape=[jax.ShapeDtypeStruct((rows, width), bf16)] * 2
        + [jax.ShapeDtypeStruct((rows, width), f32)] * 4,
        in_specs=[SCALARS] + spec(8),
        out_specs=spec(6),
        scratch_shapes=[
            pltpu.VMEM((plan.key_rows, 2 * width), bf16),
            pltpu.VMEM((plan.key_rows, 2 * width), bf16),
            pltpu.VMEM((2 * width // 128, plan.query_rows, 128), f32),
            pltpu.VMEM((2 * width // 128, plan.query_rows, 128), f32),
        ],
        compiler_params=params(20),
        name="attend",
        cost_estimate=cost(8),
    )(info, mask, counts, *queries, *pairs, *halos)
    return outs[:2], outs[2:4], outs[4:]


def forward_kernel(
    parts,
    inverse,
    sums_inverse,
    tokens,
    cotangent,
    attended_a,
    attended_b,
    vectors,
    shift_in,
    *refs,
):
    pieces = refs[:parts]
    result, resid_out, grad_normed, w_out, own, low_half, high_half, sum_in = refs[
        parts : parts + 8
    ]
    w_in, w_back, normed_two, outer, tall, flat, turned, cot_turned = refs[parts + 8 :]
    other = (low_half, high_half)
    width = tokens.shape[1]
    wide = width // 2
    each = pieces[0].shape[0]
    half = own.shape[0]
    chunks = w_in.shape[0]
    block = width // (parts * each)
    tall_block = chunks * block
    back_at = block + tall_block
    for p in range(parts * each):
        piece, q = pieces[p // each], p % each
        i = inverse[p]
        rows = pl.ds(pl.multiple_of(i * block, block), block)
        w_out[rows, :] = piece[q, pl.ds(0, block), :]
        for c in range(chunks):
            w_in[c, rows, :] = piece[q, pl.ds(block * (c + 1), block), :]
        rows = pl.ds(pl.multiple_of(i * tall_block, tall_block), tall_block)
        w_back[rows, :] = piece[q, pl.ds(back_at, tall_block), :]
    gain = vectors[pl.ds(3, 1), :]
    resid = tokens[...].astype(f32) + dot_nn(attended_a[...], w_out[pl.ds(0, wide), :])
    resid = resid + dot_nn(attended_b[...], w_out[pl.ds(wide, wide), :]) + vectors[pl.ds(2, 1), :]
    center, rstd = ln_stats(resid)
    normed_two[...] = (center * rstd * gain + vectors[pl.ds(4, 1), :]).astype(bf16)
    turned[...] = normed_two[...].T
    resid_out[...] = resid
    outer[...] = jnp.zeros(outer.shape, f32)
    grad_normed[...] = jnp.zeros(grad_normed.shape, f32)

    def chunk_step(c, carry):
        there = pl.ds(pl.multiple_of(c * width, width), width)
        inner = dot_nn(normed_two[...], w_in[c]) + shift_in[:, there]
        cdf = 0.5 * (1.0 + lax.erf(inner * math.sqrt(0.5)))
        active = (inner * cdf).astype(bf16)
        slope = cdf + inner * (jnp.exp(-0.5 * inner * inner) * (1.0 / math.sqrt(2.0 * math.pi)))
        back = w_back[there, :]
        grad_inner = slope * dot_nt(cotangent[...], back)
        low = grad_inner.astype(bf16)
        outer[...] += dot_nn(active, back)
        tall[there, :] = dot_tn(active, cotangent[...]).astype(bf16)
        sum_in[:, there] = column_sum(low.astype(f32))
        flat[...] = dot_nn(turned[...], low).astype(bf16)
        for p in range(2 * half):
            i = sums_inverse[p]
            rows = flat[pl.ds(pl.multiple_of(i * block, block), block), :]
            at = pl.ds(pl.multiple_of(c * block, block), block)
            if p < half:
                own[p, at, :] = rows
            else:
                other[(p - half) // 8][(p - half) % 8, at, :] = rows
        grad_normed[...] += dot_nt(low, w_in[c])
        return carry

    lax.fori_loop(0, chunks, chunk_step, 0, unroll=4)
    result[...] = (resid_out[...] + outer[...] + vectors[pl.ds(5, 1), :]).astype(bf16)
    for p in range(2 * half):
        i = sums_inverse[p]
        rows = tall[pl.ds(pl.multiple_of(i * tall_block, tall_block), tall_block), :]
        there = pl.ds(tall_block, tall_block)
        if p < half:
            own[p, there, :] = rows
        else:
            other[(p - half) // 8][(p - half) % 8, there, :] = rows


def feed_forward(inverses, tokens, cotangent, attended, vectors, shift_in, pieces):
    parts = len(pieces)
    rows, width = tokens.shape
    hidden = shift_in.shape[1]
    chunks = hidden // width
    blocks = parts * pieces[0].shape[0]
    stack = pieces[0].shape[1] - width // blocks
    return pl.pallas_call(
        functools.partial(forward_kernel, parts),
        out_shape=(
            jax.ShapeDtypeStruct((rows, width), bf16),
            jax.ShapeDtypeStruct((rows, width), f32),
            jax.ShapeDtypeStruct((rows, width), f32),
            jax.ShapeDtypeStruct((width, width), bf16),
            jax.ShapeDtypeStruct((blocks // 2, stack, width), bf16),
            jax.ShapeDtypeStruct((blocks // 4, stack, width), bf16),
            jax.ShapeDtypeStruct((blocks // 4, stack, width), bf16),
            jax.ShapeDtypeStruct((1, hidden), f32),
        ),
        in_specs=[SCALARS] * 2 + spec(6 + parts),
        out_specs=tuple(spec(8)),
        scratch_shapes=[
            pltpu.VMEM((chunks, width, width), bf16),
            pltpu.VMEM((hidden, width), bf16),
            pltpu.VMEM((rows, width), bf16),
            pltpu.VMEM((rows, width), f32),
            pltpu.VMEM((hidden, width), bf16),
            pltpu.VMEM((width, width), bf16),
            pltpu.VMEM((width, rows), bf16),
            pltpu.VMEM((width, rows), bf16),
        ],
        compiler_params=params(30),
        name="feed_forward",
        cost_estimate=cost(10),
    )(*inverses, tokens, cotangent, *attended, vectors, shift_in, *pieces)


def middle_kernel(
    plan,
    info,
    sums_inverse,
    cotangent,
    attended_a,
    attended_b,
    mixed_a,
    mixed_b,
    scale_a,
    scale_b,
    vectors,
    resid,
    grad_normed,
    w_out,
    grad_resid,
    grads_a,
    grads_b,
    to_twin,
    to_other,
    sums,
    own,
    low_half,
    high_half,
    levels,
    ends,
    denoms,
    flat,
):
    width = cotangent.shape[1]
    wide = width // 2
    center, rstd = ln_stats(resid[...])
    grad_in, gain_terms = ln_back(grad_normed[...], center * rstd, rstd, vectors[pl.ds(3, 1), :])
    grad_out = cotangent[...].astype(f32)
    total = grad_out + grad_in
    grad_resid[...] = total
    low = total.astype(bf16)
    sums[pl.ds(0, 1), :] = jnp.zeros((1, width), f32)
    sums[pl.ds(1, 1), :] = jnp.zeros((1, width), f32)
    sums[pl.ds(2, 1), :] = column_sum(low.astype(f32))
    sums[pl.ds(3, 1), :] = column_sum(gain_terms)
    sums[pl.ds(4, 1), :] = column_sum(grad_normed[...])
    sums[pl.ds(5, 1), :] = column_sum(grad_out)
    for quad in range(2):
        lines = pl.ds(quad * wide, wide)
        flat[lines, :] = dot_tn((attended_a, attended_b)[quad][...], low).astype(bf16)
        numer = dot_nt(low, w_out[lines, :]) * (scale_a, scale_b)[quad][...]
        denom = -(numer * (mixed_a, mixed_b)[quad][...])
        for chunk in range(2 * wide // 128):
            source = numer if chunk < wide // 128 else denom
            lane = chunk * 128 % wide
            levels[chunk, pl.ds(0, plan.rows), :] = source[:, lane : lane + 128]
            for level in range(1, LEVELS):
                count, at = plan.counts[level], plan.query_at[level]
                below = plan.query_at[level - 1]
                levels[chunk, pl.ds(at, count), :] = (
                    levels[chunk, pl.ds(below, count, stride=2), :]
                    + levels[chunk, pl.ds(below + 1, count, stride=2), :]
                )
                rest = plan.padded[level] - count
                if rest:
                    levels[chunk, pl.ds(at + count, rest), :] = jnp.zeros((rest, 128), f32)
            grads = (grads_a, grads_b)[quad]
            grads[:, pl.ds(chunk * 128, 128)] = levels[chunk].astype(bf16)
        for k in range(2 * LEVELS):
            level, here = k % LEVELS, pl.ds(k * HALO, HALO)
            at = plan.query_at[level] + (0 if k < LEVELS else plan.counts[level] - HALO)
            there = pl.ds(at, HALO)
            ends[here, pl.ds(quad * wide, wide)] = (grads_a, grads_b)[quad][there, pl.ds(0, wide)]
            for chunk in range(wide // 128):
                lanes = pl.ds(quad * wide + chunk * 128, 128)
                denoms[here, lanes] = levels[wide // 128 + chunk, there, :]
    feature = lax.broadcasted_iota(jnp.int32, (width, LINE), 0)
    lane = lax.broadcasted_iota(jnp.int32, (width, LINE), 1)
    pick = jnp.where(lane == feature // HEAD_DIM, 1.0, 0.0).astype(bf16)
    heads = width // HEAD_DIM
    values = denoms[...]
    first = values.astype(bf16)
    values = dot_nn(first, pick) + dot_nn((values - first.astype(f32)).astype(bf16), pick)
    first = values.astype(bf16).astype(f32)
    both = jnp.concatenate([first[:, :heads], (values - first)[:, :heads]], axis=1)
    both = jnp.concatenate([both, jnp.zeros((both.shape[0], LINE - 2 * heads), f32)], axis=1)
    ends[:, pl.ds(width, LINE)] = both.astype(bf16)
    hand_out(info, ends, to_twin, to_other)
    half, block = own.shape[0], own.shape[1]
    other = (low_half, high_half)
    for p in range(2 * half):
        rows = flat[pl.ds(pl.multiple_of(sums_inverse[p] * block, block), block), :]
        if p < half:
            own[p] = rows
        else:
            other[(p - half) // 8][(p - half) % 8] = rows


def middle(plan, info, sums_inverse, cotangent, attended, mixed, scale, vectors, resid, grad_normed, w_out):
    rows, width = cotangent.shape
    size = LEVELS * HALO
    return pl.pallas_call(
        functools.partial(middle_kernel, plan),
        out_shape=(
            jax.ShapeDtypeStruct((rows, width), f32),
            jax.ShapeDtypeStruct((plan.query_rows, width), bf16),
            jax.ShapeDtypeStruct((plan.query_rows, width), bf16),
            jax.ShapeDtypeStruct((size, width + LINE), bf16),
            jax.ShapeDtypeStruct((size, width + LINE), bf16),
            jax.ShapeDtypeStruct((8, width), f32),
            jax.ShapeDtypeStruct((BLOCKS // 2, width // BLOCKS, width), bf16),
            jax.ShapeDtypeStruct((BLOCKS // 4, width // BLOCKS, width), bf16),
            jax.ShapeDtypeStruct((BLOCKS // 4, width // BLOCKS, width), bf16),
        ),
        in_specs=[SCALARS] * 2 + spec(11),
        out_specs=tuple(spec(9)),
        scratch_shapes=[
            pltpu.VMEM((width // 128, plan.query_rows, 128), f32),
            pltpu.VMEM((2 * size, width + LINE), bf16),
            pltpu.VMEM((2 * size, width), f32),
            pltpu.VMEM((width, width), bf16),
        ],
        compiler_params=params(20),
        name="middle",
        cost_estimate=cost(3),
    )(info, sums_inverse, cotangent, *attended, *mixed, *scale, vectors, resid, grad_normed, w_out)


def attend_back_kernel(plan, total, mask, counts_of, *refs):
    queries, pairs, halos, grads, grad_queries, grad_extended, extended = (
        refs[2 * k : 2 * k + 2] for k in range(7)
    )
    width = QUAD_WIDTH
    for quad in range(2):
        fill_extended(plan, pairs[quad], halos[quad], extended[quad])
        grad_extended[quad][...] = jnp.zeros(grad_extended[quad].shape, f32)
    masks = head_masks(BLOCK)
    first_head = lax.broadcasted_iota(jnp.int32, (BLOCK, 128), 1) < HEAD_DIM
    keys = pl.ds(0, width)
    values = pl.ds(width, width)

    def prepare(block):
        level, part = plan.locate(block)
        here = pl.ds(pl.multiple_of(BLOCK * block, BLOCK), BLOCK)
        there = pl.ds(pl.multiple_of(BLOCK * block + 2 * HALO * level, BLOCK), WINDOW)
        window = pl.ds(pl.multiple_of(WINDOW * block, WINDOW), WINDOW)
        allowed = jnp.concatenate([mask[window, :]] * (QUAD * BLOCK // 128), axis=1) > 0.0
        counts = counts_of[window, :]
        return here, there, allowed, counts

    def block_step(step, carry):
        work = []
        for k in range(4):
            here, there, allowed, counts = prepare(step * 4 + k)
            for quad in range(2):
                q = spread_heads(queries[quad][here, :], masks)
                g = spread_heads(grads[quad][here, keys], masks)
                d = spread_heads(grads[quad][here, values], masks)
                work.append((quad, here, there, allowed, counts, q, g, d))
        scores, grad_probs = [], []
        for quad, here, there, allowed, counts, q, g, d in work:
            scores.append(dot_nt(extended[quad][there, keys], q))
            v = extended[quad][there, values]
            value_and_count = jnp.concatenate([v] + [counts] * (width // 128), axis=1)
            grad_probs.append(dot_nt(value_and_count, jnp.concatenate([g, d], axis=1)))
        weights = [
            jnp.where(item[3], jnp.exp(score), 0.0) for item, score in zip(work, scores)
        ]
        grad_scores = [(x * y).astype(bf16) for x, y in zip(grad_probs, weights)]
        probs = [weight.astype(bf16) for weight in weights]
        keys_of = [extended[item[0]][item[2], keys] for item in work]
        to_queries = [
            [
                dot_tn(grad_score[:, 128 * half : 128 * half + 128], k[:, 128 * half : 128 * half + 128])
                for half in range(2)
            ]
            for grad_score, k in zip(grad_scores, keys_of)
        ]
        to_keys = [dot_nn(grad_score, item[5]) for grad_score, item in zip(grad_scores, work)]
        to_values = [dot_nn(prob, item[6]) for prob, item in zip(probs, work)]
        for item, parts, to_key, to_value in zip(work, to_queries, to_keys, to_values):
            quad, here, there = item[:3]
            for half in range(2):
                grad_queries[quad][here, pl.ds(128 * half, 128)] = join_pair(
                    parts[half], first_head
                ) * (1.0 / math.sqrt(HEAD_DIM))
            grad_extended[quad][there, keys] += to_key
            grad_extended[quad][there, values] += to_value
        return carry

    lax.fori_loop(0, len(plan.blocks) // 4, block_step, 0, unroll=1)


def attend_back(plan, total, mask, counts, queries, pairs, halos, grads):
    width = queries[0].shape[1]
    outs = pl.pallas_call(
        functools.partial(attend_back_kernel, plan, total),
        out_shape=[jax.ShapeDtypeStruct((plan.query_rows, width), f32)] * 2
        + [jax.ShapeDtypeStruct((plan.key_rows, 2 * width), f32)] * 2,
        in_specs=spec(10),
        out_specs=spec(4),
        scratch_shapes=[
            pltpu.VMEM((plan.key_rows, 2 * width), bf16),
            pltpu.VMEM((plan.key_rows, 2 * width), bf16),
        ],
        compiler_params=params(24),
        name="attend_back",
        cost_estimate=cost(12),
    )(mask, counts, *queries, *pairs, *halos, *grads)
    return outs[:2], outs[2:]


def edge_back_kernel(
    plan,
    info,
    mask,
    counts_of,
    queries_a,
    queries_b,
    pairs_a,
    pairs_b,
    from_twin,
    from_other,
    low,
    high,
    grads,
):
    width = queries_a.shape[1]
    place_halos(info, from_twin, from_other, grads)
    two = 2 * HALO
    masks = head_masks(two)
    keys = pl.ds(0, width)
    heads = 2 * width // HEAD_DIM
    source = lax.broadcasted_iota(jnp.int32, (LINE, width), 0)
    target = lax.broadcasted_iota(jnp.int32, (LINE, width), 1)
    picks = []
    for quad in range(2):
        head = target // HEAD_DIM + quad * QUAD
        wanted = jnp.where(target % HEAD_DIM == 0, head, -1)
        wanted = jnp.where(target % HEAD_DIM == 1, head + heads, wanted)
        picks.append(jnp.where(source == wanted, 1.0, 0.0).astype(bf16))
    denoms = [dot_nn(grads[:, pl.ds(2 * width, LINE)], pick).astype(bf16) for pick in picks]
    work = []
    for level in range(LEVELS):
        count, at = plan.counts[level], plan.query_at[level]
        here = pl.ds(two * level, two)
        allowed = jnp.concatenate([mask[here, :]] * (QUAD * two // 128), axis=1) > 0.0
        counts = counts_of[here, :]
        ahead, behind = HALO * level, HALO * (LEVELS + level)

        def both(item, lanes):
            parts = [item[pl.ds(first, HALO), lanes] for first in (ahead, behind)]
            return jnp.concatenate(parts, axis=0)

        for quad in range(2):
            pairs = (pairs_a, pairs_b)[quad]
            own = jnp.concatenate(
                [pairs[pl.ds(at, HALO), :], pairs[pl.ds(at + count - HALO, HALO), :]], axis=0
            )
            k, v = own[:, :width], own[:, width:]
            d = denoms[quad]
            d = jnp.concatenate([d[ahead : ahead + HALO], d[behind : behind + HALO]], axis=0)
            q = spread_heads(both((queries_a, queries_b)[quad], keys), masks)
            g = spread_heads(both(grads, pl.ds(quad * width, width)), masks)
            d = spread_heads(d, masks)
            value_and_count = jnp.concatenate([v] + [counts] * (width // 128), axis=1)
            there = pl.ds(HALO * (quad * LEVELS + level), HALO)
            work.append((there, allowed, q, g, d, k, value_and_count))
    scores = [dot_nt(item[5], item[2]) for item in work]
    grad_probs = [
        dot_nt(item[6], jnp.concatenate([item[3], item[4]], axis=1)) for item in work
    ]
    weights = [jnp.where(item[1], jnp.exp(score), 0.0) for item, score in zip(work, scores)]
    grad_scores = [(x * y).astype(bf16) for x, y in zip(grad_probs, weights)]
    to_keys = [dot_nn(grad_score, item[2]) for grad_score, item in zip(grad_scores, work)]
    to_values = [dot_nn(weight.astype(bf16), item[3]) for weight, item in zip(weights, work)]
    for item, to_key, to_value in zip(work, to_keys, to_values):
        there = item[0]
        low[there, keys] = to_key[:HALO]
        high[there, keys] = to_key[HALO:]
        low[there, pl.ds(width, width)] = to_value[:HALO]
        high[there, pl.ds(width, width)] = to_value[HALO:]


def edge_back(plan, info, mask, counts, queries, pairs, from_twin, from_other):
    width = queries[0].shape[1]
    size = 2 * LEVELS * HALO
    return pl.pallas_call(
        functools.partial(edge_back_kernel, plan),
        out_shape=[jax.ShapeDtypeStruct((size, 2 * width), f32)] * 2,
        in_specs=[SCALARS] + spec(8),
        out_specs=spec(2),
        scratch_shapes=[pltpu.VMEM((size, 2 * width + LINE), bf16)],
        compiler_params=params(12),
        name="edge_back",
        cost_estimate=cost(2.5),
    )(info, mask, counts, *queries, *pairs, from_twin, from_other)


def finish_kernel(
    plan,
    total,
    info,
    inverse,
    standard,
    spread,
    weight,
    vectors,
    grad_resid,
    sums,
    sum_in,
    queries_a,
    queries_b,
    pairs_a,
    pairs_b,
    edge_low,
    edge_high,
    grad_tokens,
    own,
    low_half,
    high_half,
    work,
    joined,
    flat,
    table,
):
    rows, width = standard.shape
    device = info[0]
    half_width = width // 2
    places = device * rows + lax.broadcasted_iota(jnp.int32, (rows, 128), 0)
    live = live_counts(info, places, 0, total)
    hat = standard[...]
    gain = vectors[pl.ds(0, 1), :]
    normed = (hat * gain + vectors[pl.ds(1, 1), :]).astype(bf16)
    half, block = own.shape[0], width // BLOCKS
    other = (low_half, high_half)
    grad_normed = jnp.zeros((rows, width), f32)
    for part in range(3):
        for step in range(width // 128):
            chunk = part * (width // 128) + step
            quad, lane = divmod(step * 128, half_width)
            if part == 0:
                work[chunk] = (queries_a, queries_b)[quad][:, pl.ds(lane, 128)]
            else:
                lanes = pl.ds((part - 1) * half_width + lane, 128)
                for level in range(LEVELS):
                    at, count = plan.query_at[level], plan.counts[level]
                    own_rows = pl.ds(plan.key_at[level] + HALO, count)
                    work[chunk, pl.ds(at, count), :] = (pairs_a, pairs_b)[quad][own_rows, lanes]
                    halo = pl.ds(HALO * (quad * LEVELS + level), HALO)
                    work[chunk, pl.ds(at, HALO), :] += edge_low[halo, lanes]
                    work[chunk, pl.ds(at + count - HALO, HALO), :] += edge_high[halo, lanes]
            for level in range(LEVELS - 1, 0, -1):
                count = plan.counts[level]
                upper = work[chunk, pl.ds(plan.query_at[level], count), :]
                if chunk * 128 < 2 * width:
                    upper = upper * 0.5
                for parity in range(2):
                    there = pl.ds(plan.query_at[level - 1] + parity, count, stride=2)
                    work[chunk, there, :] = work[chunk, there, :] + upper
            value = work[chunk, pl.ds(0, rows), :]
            if chunk * 128 >= 2 * width:
                value = value * live
            joined[:, pl.ds(chunk * 128, 128)] = value.astype(bf16)
        columns = pl.ds(part * width, width)
        flat[part] = dot_tn(normed, joined[:, columns]).astype(bf16)
        for p in range(2 * half):
            i = inverse[p]
            lines = flat[part, pl.ds(pl.multiple_of(i * block, block), block), :]
            there = pl.ds(part * block, block)
            if p < half:
                own[p, there, :] = lines
            else:
                other[(p - half) // 8][(p - half) % 8, there, :] = lines
        grad_normed = grad_normed + dot_nt(joined[:, columns], weight[:, columns])
    grad_in, gain_terms = ln_back(grad_normed, hat, spread[:, :1], gain)
    grad_tokens[...] = grad_resid[...] + grad_in
    singles = [column_sum(gain_terms), column_sum(grad_normed)]
    singles += [sums[pl.ds(k, 1), :] for k in range(2, 6)]
    table[...] = pack_vectors(singles, sum_in[...], 2 * half, table.shape[1])
    row = lax.broadcasted_iota(jnp.int32, (LINE_ROWS, 2 * LINE), 0)
    there = pl.ds(3 * block, LINE_ROWS)
    for p in range(2 * half):
        i = inverse[p]
        line = table[pl.ds(i, 1), :]
        lines = jnp.where(row == 0, line, 0.0)
        lines = jnp.concatenate([lines, jnp.zeros((LINE_ROWS, width - 2 * LINE), f32)], axis=1)
        if p < half:
            own[p, there, :] = lines.astype(bf16)
        else:
            other[(p - half) // 8][(p - half) % 8, there, :] = lines.astype(bf16)


def finish(plan, total, info, inverse, standard, spread, weight, *rest):
    rows, width = standard.shape
    half = BLOCKS // 2
    block = width // BLOCKS
    return pl.pallas_call(
        functools.partial(finish_kernel, plan, total),
        out_shape=(
            jax.ShapeDtypeStruct((rows, width), f32),
            jax.ShapeDtypeStruct((half, 3 * block + LINE_ROWS, width), bf16),
            jax.ShapeDtypeStruct((half // 2, 3 * block + LINE_ROWS, width), bf16),
            jax.ShapeDtypeStruct((half // 2, 3 * block + LINE_ROWS, width), bf16),
        ),
        in_specs=[SCALARS, SCALARS] + spec(3 + len(rest)),
        out_specs=tuple(spec(4)),
        scratch_shapes=[
            pltpu.VMEM((3 * width // 128, plan.query_rows, 128), f32),
            pltpu.VMEM((rows, 3 * width), bf16),
            pltpu.VMEM((3, width, width), bf16),
            pltpu.VMEM((BLOCKS, 2 * LINE), f32),
        ],
        compiler_params=params(28),
        name="finish",
        cost_estimate=cost(6.2),
    )(info, inverse, standard, spread, weight, *rest)


class Ring:
    def __init__(self, devices, *orders):
        self.devices = devices
        self.orders = orders
        self.stages = len(orders[0])

    def partner(self, stage):
        return [(i, i ^ self.orders[i & 1][stage]) for i in range(self.devices)]

    def twin(self):
        return [(i, i ^ 1) for i in range(self.devices)]

    def places(self, device):
        found = []
        even = (device & 1) == 0
        for base, swap in ((device, False), (device ^ 1, True)):
            for position in range(1 << self.stages):
                masks = [
                    sum(order[k] for k in range(self.stages) if position >> k & 1)
                    for order in self.orders
                ]
                if swap:
                    masks = masks[::-1]
                found.append(base ^ jnp.where(even, *masks))
        return found

    def step(self, stage, arrays):
        route = self.twin() if stage == self.stages else self.partner(stage)
        return [lax.ppermute(item, "seq", route) for item in arrays]

    def fold(self, stage, own, low, high):
        half = 1 << stage
        sent = (own[half:].astype(f32) + high.astype(f32)).astype(bf16)
        kept = own[:half].astype(f32) + low.astype(f32)
        return kept, sent


def halves(item):
    half = item.shape[0] // 2
    return item[:half], item[half:]


def join(held, came):
    return [jnp.concatenate(pair) for pair in zip(held, came)]


def pack_kernel(rings, lengths, w_qkv, w_out, w_in, w_back, *refs):
    vectors, (info, *inverses, payload, staged) = refs[:-5], refs[-5:]
    device = lax.axis_index("seq")
    info[0] = device
    start = jnp.int32(0)
    for k in range(3):
        length = lengths[k]
        info[1 + k] = length
        info[4 + k] = start
        start = start + (length + 15) // 16 * 16
        info[7 + k] = start
    for ring, inverse in zip(rings, inverses):
        for place, block in enumerate(ring.places(device)):
            inverse[place] = block
    block, width = w_out.shape
    chunks = w_in.shape[1] // width
    staged[...] = jnp.zeros(staged.shape, f32)
    for k, vector in enumerate(vectors):
        size = vector.shape[0]
        lane = k * block
        staged[pl.ds(0, 1), pl.ds(lane, size)] = vector[...].astype(f32).reshape(1, size)
    payload[0, pl.ds(0, block), :] = w_out[...]
    for c in range(chunks):
        payload[0, pl.ds(block * (c + 1), block), :] = w_in[:, pl.ds(c * width, width)]
    at = block * (chunks + 1)
    payload[0, pl.ds(at, block * chunks), :] = w_back[...]
    at = at + block * chunks
    for c in range(3):
        payload[0, pl.ds(at + block * c, block), :] = w_qkv[:, pl.ds(c * width, width)]
    payload[0, pl.ds(at + block * 3, LINE_ROWS), :] = staged[...].astype(bf16)


def pack(rings, lengths, w_qkv, w_out, w_in, w_back, vectors):
    block, width = w_out.shape
    rows = 4 * block + w_in.shape[1] // width * block + w_back.shape[0] + LINE_ROWS
    return pl.pallas_call(
        functools.partial(pack_kernel, rings),
        out_shape=(
            jax.ShapeDtypeStruct((10,), jnp.int32),
            jax.ShapeDtypeStruct((BLOCKS,), jnp.int32),
            jax.ShapeDtypeStruct((BLOCKS,), jnp.int32),
            jax.ShapeDtypeStruct((1, rows, width), bf16),
        ),
        in_specs=[SCALARS] + spec(4 + len(vectors)),
        out_specs=(SCALARS,) * 3 + tuple(spec(1)),
        scratch_shapes=[pltpu.VMEM((LINE_ROWS, width), f32)],
        compiler_params=params(62),
        name="pack",
        cost_estimate=cost(1.5),
    )(lengths, w_qkv, w_out, w_in, w_back, *vectors)


def unpack_kernel(kept_one, came_one, kept_two, came_two, *outs):
    block, width = (kept_one.shape[1] - LINE_ROWS) // 3, kept_two.shape[2]
    w_qkv, w_out, w_in, w_back = outs[:4]
    for c in range(3):
        rows = pl.ds(block * c, block)
        w_qkv[:, pl.ds(c * width, width)] = kept_one[0, rows, :] + came_one[0, rows, :].astype(f32)
    rows = pl.ds(block * 3, LINE_ROWS)
    lines = kept_one[0, rows, :] + came_one[0, rows, :].astype(f32)
    for k, out in enumerate(outs[4:]):
        size = out.shape[0]
        lane = k * block
        out[...] = lines[0:1, lane : lane + size].reshape(size)
    chunks = w_in.shape[1] // width

    def total(at, size):
        rows = pl.ds(at, size)
        return kept_two[0, rows, :] + came_two[0, rows, :].astype(f32)

    w_out[...] = total(2 * block * chunks, block)
    for c in range(chunks):
        w_in[:, pl.ds(c * width, width)] = total(block * c, block)
    w_back[...] = total(block * chunks, block * chunks)


def unpack(kept_one, came_one, kept_two, came_two, like):
    return pl.pallas_call(
        unpack_kernel,
        out_shape=[jax.ShapeDtypeStruct(item.shape, f32) for item in like],
        in_specs=spec(4),
        out_specs=spec(len(like)),
        compiler_params=params(8),
        name="unpack",
        cost_estimate=cost(1.5),
    )(kept_one, came_one, kept_two, came_two)


def exchange(to_twin, to_other):
    count = lax.axis_size("seq")
    twin = [(i, i ^ 1) for i in range(count)]
    other = [(i, i + 1) for i in range(1, count - 1, 2)]
    other += [(j, i) for i, j in other]
    return lax.ppermute(to_other, "seq", other), lax.ppermute(to_twin, "seq", twin)


def order(items, *after):
    return lax.optimization_barrier((items, after))[0]


def per_device(
    lengths,
    tokens,
    ln1_gain,
    ln1_bias,
    w_qkv,
    w_out,
    out_bias,
    ln2_gain,
    ln2_bias,
    w_in,
    in_bias,
    w_back,
    back_bias,
    cotangent,
):
    devices = lax.axis_size("seq")
    device = lax.axis_index("seq")
    rows, width = tokens.shape
    total = rows * devices
    plan = Plan(rows)
    block = width // BLOCKS
    chunks = w_in.shape[1] // width
    small = (ln1_gain, ln1_bias, out_bias, ln2_gain, ln2_bias, back_bias, in_bias)
    direct = devices == BLOCKS
    ring = Ring(BLOCKS, (16, 2, 8, 4), (4, 16, 2, 8))
    sums_ring = Ring(BLOCKS, (16, 8, 4, 2), (2, 16, 8, 4))
    last = ring.stages - 1
    core = ring.stages
    if direct:
        info, inverse, sums_inverse, payload = pack(
            (ring, sums_ring), lengths, w_qkv, w_out, w_in, w_back, small
        )
        from_other, from_twin = exchange(*edge_sums(plan, total, info, order(tokens, payload)))
        ready = prepare(plan, total, info, order(tokens, payload))
        (payload,) = join([payload], ring.step(0, [payload]))
        payload = order(payload, from_other, from_twin)
        rest = block * (2 * chunks + 1)
        a, b = payload[:, rest:], payload[:, :rest]
        a_came, b_came = ring.step(1, [a, b])
        (a,) = join([a], [a_came])
        (a_came,) = ring.step(2, [a])
        (a,) = join([a], [a_came])
        (b,) = join([b], [b_came])
        a = order(a, b, ready)
        (b_came,) = ring.step(2, [b])
        (a_came,) = ring.step(3, [a])
        one = [a, a_came] + ring.step(core, [a, a_came])
        (b,) = join([b], [b_came])
        b = order(b, a_came)
    else:
        padded = (lengths + 15) // 16 * 16
        ends = jnp.cumsum(padded, dtype=jnp.int32)
        info = jnp.concatenate([device[None].astype(jnp.int32), lengths, ends - padded, ends])
        inverse = sums_inverse = jnp.arange(BLOCKS, dtype=jnp.int32)
        from_other, from_twin = exchange(*edge_sums(plan, total, info, tokens))
        ready = prepare(plan, total, info, tokens)

        def whole(item):
            return lax.all_gather(item, "seq", axis=0, tiled=True)

        def split(item, parts):
            each = BLOCKS // parts
            return [item[k * each : (k + 1) * each] for k in range(parts)]

        line = jnp.concatenate([whole(item).reshape(BLOCKS, 1, -1) for item in small], axis=2)
        line = jnp.pad(line, ((0, 0), (0, LINE_ROWS - 1), (0, width - line.shape[2])))
        one = whole(w_qkv).reshape(BLOCKS, block, 3, width).transpose(0, 2, 1, 3)
        one = one.reshape(BLOCKS, 3 * block, width)
        one = split(jnp.concatenate([one, line], axis=1), PIECES)
        full_in = whole(w_in).reshape(BLOCKS, block, chunks, width)
        full_in = full_in.transpose(0, 2, 1, 3).reshape(BLOCKS, chunks * block, width)
        full_two = [
            whole(w_out).reshape(BLOCKS, block, width),
            full_in,
            whole(w_back).reshape(BLOCKS, chunks * block, width),
        ]
        two = split(jnp.concatenate(full_two, axis=1), PIECES)
    standard, spread, pool, allowed, allowed_back, counts, edge_allowed, edge_counts = ready
    queries, pairs, halo_queries, halo_pairs, weight, vectors, shift_in = project(
        plan, total, info, inverse, standard, pool, from_twin, from_other, one
    )
    if direct:
        (b_came,) = ring.step(last, [b])
        (b_twin,) = ring.step(core, [b])
        allowed = order(allowed, b)
    attended, mixed, scale = attend(
        plan, total, info, allowed, counts, queries, pairs, halo_pairs
    )
    if direct:
        b_came = order(b_came, attended)
        two = [b, b_came, b_twin] + ring.step(core, [b_came])
    result, resid, grad_normed, out_weight, own_two, low_two, high_two, sum_in = feed_forward(
        (inverse, sums_inverse), tokens, cotangent, attended, vectors, shift_in, two
    )
    if direct:
        high, low = sums_ring.step(core, [high_two, low_two])
    (
        grad_resid,
        grads_a,
        grads_b,
        to_twin,
        to_other,
        sums,
        own_out,
        low_out,
        high_out,
    ) = middle(
        plan,
        info,
        sums_inverse,
        cotangent,
        attended,
        mixed,
        scale,
        vectors,
        resid,
        grad_normed,
        out_weight,
    )
    from_other, from_twin = exchange(to_twin, to_other)

    def with_out(item, out):
        return jnp.concatenate([item, out], axis=1)

    if direct:
        high_out, low_out = sums_ring.step(core, [high_out, low_out])
        kept, sent = sums_ring.fold(
            last, with_out(own_two, own_out), with_out(low, low_out), with_out(high, high_out)
        )
        sent_low, sent_high = halves(sent)
        sent_low, sent_high = order((sent_low, sent_high), from_twin)
        high, low = sums_ring.step(last, [sent_high, sent_low])
        grads_a = order(grads_a, sent_high, sent_low)
    grad_queries, grad_pairs = attend_back(
        plan, total, allowed_back, counts, queries, pairs, halo_pairs, (grads_a, grads_b)
    )
    from_other, from_twin = order((from_other, from_twin), grad_queries)
    if direct:
        high = order(high, grad_queries, from_other, from_twin)
        kept, kept_high = halves(kept)
        sent = (kept_high + high.astype(f32)).astype(bf16)
        (came,) = sums_ring.step(last - 1, [sent])
        from_other, from_twin = order((from_other, from_twin), sent)
    edges = edge_back(
        plan, info, edge_allowed, edge_counts, halo_queries, pairs, from_twin, from_other
    )
    grad_tokens, own_one, low_one, high_one = finish(
        plan,
        total,
        info,
        sums_inverse,
        standard,
        spread,
        weight,
        vectors,
        grad_resid,
        sums,
        sum_in,
        *grad_queries,
        *grad_pairs,
        *edges,
    )
    if direct:
        high_one, low_one = sums_ring.step(core, [high_one, low_one])
        low, came = order((low, came), grad_tokens)
        kept = kept + low.astype(f32)
        kept, sent = sums_ring.fold(last - 2, kept, *halves(came))
        (came,) = sums_ring.step(last - 2, [sent])
        high_one, low_one = order((high_one, low_one), sent)
        own_one, sent_one = sums_ring.fold(last, own_one, low_one, high_one)
        (came_one,) = sums_ring.step(last, [sent_one])
        own_one, sent_one = sums_ring.fold(last - 1, own_one, *halves(came_one))
        (came_one,) = sums_ring.step(last - 1, [sent_one])
        came = order(came, sent_one)
        kept, sent = sums_ring.fold(0, kept, *halves(came))
        (came,) = sums_ring.step(0, [sent])
        came_one = order(came_one, sent)
        own_one, sent_one = sums_ring.fold(last - 2, own_one, *halves(came_one))
        (came_one,) = sums_ring.step(last - 2, [sent_one])
        own_one, sent_one = sums_ring.fold(0, own_one, *halves(came_one))
        (came_one,) = sums_ring.step(0, [sent_one])
        grads = unpack(own_one, came_one, kept, came, (w_qkv, w_out, w_in, w_back) + small)
        grad_w_qkv, grad_w_out, grad_w_in, grad_w_back = grads[:4]
        parts = grads[4:]
    else:

        def shared(item):
            return lax.psum_scatter(item, "seq", scatter_dimension=0, tiled=True)

        full = jnp.concatenate([x.astype(f32) for x in (own_one, low_one, high_one)])
        line = full[:, 3 * block]
        sizes = [block] * 6 + [chunks * block]
        starts = [k * block for k in range(7)]
        parts = [
            shared(line[:, at : at + size].reshape(-1)) for at, size in zip(starts, sizes)
        ]
        grad_w_qkv = full[:, : 3 * block].reshape(BLOCKS, 3, block, width).transpose(0, 2, 1, 3)
        grad_w_qkv = shared(grad_w_qkv.reshape(width, 3 * width))
        full = jnp.concatenate([x.astype(f32) for x in (own_out, low_out, high_out)])
        grad_w_out = shared(full.reshape(width, width))
        full = jnp.concatenate([x.astype(f32) for x in (own_two, low_two, high_two)])
        full_in = full[:, : block * chunks]
        full_in = full_in.reshape(BLOCKS, chunks, block, width).transpose(0, 2, 1, 3)
        grad_w_in = shared(full_in.reshape(width, chunks * width))
        grad_w_back = shared(full[:, block * chunks :].reshape(chunks * width, width))
    gain_one, bias_one, shift_out, gain_two, bias_two, shift_back, shift_hidden = parts
    return (
        result,
        grad_tokens,
        gain_one,
        bias_one,
        grad_w_qkv,
        grad_w_out,
        shift_out,
        gain_two,
        bias_two,
        grad_w_in,
        shift_hidden,
        grad_w_back,
        shift_back,
    )


def solution(mesh):
    flat, wide = P("seq"), P("seq", None)
    weights = (flat, flat, wide, wide, flat, flat, flat, wide, flat, wide, flat)
    return jax.shard_map(
        per_device,
        mesh=mesh,
        in_specs=(P(), wide) + weights + (wide,),
        out_specs=(wide, wide) + weights,
        check_vma=False,
    )
```

```python
import functools
import math

import jax
import jax.numpy as jnp
from jax import lax
from jax.experimental import pallas as pl
from jax.experimental.pallas import tpu as pltpu
from jax.sharding import PartitionSpec as P

HEAD_DIM = 64
LEVELS = 5
HALO = 32
BLOCK = 64
WINDOW = BLOCK + 2 * HALO
QUAD = 4
QUAD_WIDTH = QUAD * HEAD_DIM
PIECES = 4
BLOCKS = 32
LINE = 128
LINE_ROWS = 8
MIXED = 16
FAR = 1 << 26
SEQ_STEP = 1 << 21
MIB = 1024 * 1024

f32 = jnp.float32
bf16 = jnp.bfloat16


class Plan:
    def locate(self, block):
        firsts = [at // BLOCK for at in self.query_at]
        level = sum((block >= first).astype(jnp.int32) for first in firsts[1:])
        start = sum(
            jnp.where(level == k, first, 0) for k, first in enumerate(firsts)
        )
        return level, block - start

    def __init__(self, rows):
        self.rows = rows
        self.counts = [rows >> level for level in range(LEVELS)]
        self.padded = [-(-count // BLOCK) * BLOCK for count in self.counts]
        self.query_at = [sum(self.padded[:level]) for level in range(LEVELS)]
        self.query_rows = sum(self.padded)
        self.key_at = [self.query_at[level] + 2 * HALO * level for level in range(LEVELS)]
        self.key_rows = self.query_rows + 2 * HALO * LEVELS
        self.blocks = [
            (level, part)
            for level in range(LEVELS)
            for part in range(self.padded[level] // BLOCK)
        ]


def dot_nn(a, b):
    return lax.dot_general(a, b, (((1,), (0,)), ((), ())), preferred_element_type=f32)


def dot_nt(a, b):
    return lax.dot_general(a, b, (((1,), (1,)), ((), ())), preferred_element_type=f32)


def dot_tn(a, b):
    return lax.dot_general(a, b, (((0,), (0,)), ((), ())), preferred_element_type=f32)


def spec(count):
    return [pl.BlockSpec(memory_space=pltpu.VMEM)] * count


SCALARS = pl.BlockSpec(memory_space=pltpu.SMEM)


def slot_facts(info, slot, total):
    number = jnp.zeros(slot.shape, jnp.int32)
    for s in range(3):
        number = number + (slot >= info[7 + s]).astype(jnp.int32)
    begin = jnp.where(number == 0, info[4], jnp.where(number == 1, info[5], info[6]))
    length = jnp.where(number == 0, info[1], jnp.where(number == 1, info[2], info[3]))
    inside = (slot >= 0) & (slot < total) & (number < 3)
    return number, slot - begin, length, inside


def tile_codes(info, coarse, level, total, outside):
    number, offset, _, inside = slot_facts(info, coarse << level, total)
    wide = jnp.where(inside, number * SEQ_STEP + (offset >> (level + 4)), outside)
    fine = number * SEQ_STEP + (offset >> (level + 3))
    return wide, fine


def admitted(query_codes, key_codes, level):
    near = jnp.abs(query_codes[0] - key_codes[0]) <= 1
    least = jnp.where(level > 0, 2, 0)
    near = near & (jnp.abs(query_codes[1] - key_codes[1]) >= least)
    return jnp.where(near, 1.0, 0.0)


def live_counts(info, coarse, level, total):
    _, offset, length, inside = slot_facts(info, coarse << level, total)
    span = 1 << level
    return jnp.where(inside, jnp.clip(length - offset, 0, span), 0).astype(f32)


def head_masks(rows):
    lane = lax.broadcasted_iota(jnp.int32, (rows, QUAD_WIDTH), 1) // HEAD_DIM
    return [jnp.where(lane == h, 1.0, 0.0).astype(bf16) for h in range(QUAD)]


def spread_heads(block, masks):
    return jnp.concatenate([block * m for m in masks], axis=0)


def join_pair(stacked, first):
    rows = stacked.shape[0] // 2
    return jnp.where(first, stacked[:rows], stacked[rows:])


def is_even(info):
    return (info[0] & 1) == 0


def params(size):
    return pltpu.CompilerParams(vmem_limit_bytes=size * MIB)


def cost(micros):
    return pl.CostEstimate(flops=1, bytes_accessed=1, transcendentals=0)


def fill_extended(plan, own, halos, extended):
    for level in range(LEVELS):
        at, count, mine = plan.key_at[level], plan.counts[level], plan.query_at[level]
        extended[pl.ds(at, HALO), :] = halos[pl.ds(HALO * level, HALO), :]
        extended[pl.ds(at + HALO, count), :] = own[pl.ds(mine, count), :]
        extended[pl.ds(at + HALO + count, HALO), :] = halos[pl.ds(HALO * (LEVELS + level), HALO), :]
        rest = plan.padded[level] - count
        if rest:
            extended[pl.ds(at + 2 * HALO + count, rest), :] = jnp.zeros(
                (rest, extended.shape[1]), bf16
            )


def place_halos(info, from_twin, from_other, halos):
    even = is_even(info)
    size = halos.shape[0] // 2
    halos[pl.ds(pl.multiple_of(jnp.where(even, size, 0), size), size), :] = from_twin[...]
    halos[pl.ds(pl.multiple_of(jnp.where(even, 0, size), size), size), :] = from_other[...]


def hand_out(info, ends, to_twin, to_other):
    even = is_even(info)
    size = LEVELS * HALO
    to_twin[...] = ends[pl.ds(pl.multiple_of(jnp.where(even, size, 0), size), size), :]
    to_other[...] = ends[pl.ds(pl.multiple_of(jnp.where(even, 0, size), size), size), :]


def ln_stats(values):
    center = values - jnp.mean(values, axis=-1, keepdims=True)
    spread = jnp.mean(center * center, axis=-1, keepdims=True)
    return center, lax.rsqrt(spread + 1e-05)


def ln_back(grad, hat, rstd, gain):
    scaled = grad * gain
    mean_one = jnp.mean(scaled, axis=-1, keepdims=True)
    mean_two = jnp.mean(scaled * hat, axis=-1, keepdims=True)
    return rstd * (scaled - mean_one - hat * mean_two), grad * hat


def column_sum(values):
    return jnp.sum(values, axis=0, keepdims=True)


def unpack_vector(table, first, each):
    blocks, lanes = table.shape
    length = blocks * each
    source = lax.broadcasted_iota(jnp.int32, (lanes, length), 0)
    target = lax.broadcasted_iota(jnp.int32, (lanes, length), 1)
    pick = jnp.where(source == first + (target & (each - 1)), 1.0, 0.0).astype(bf16)
    spreaded = dot_nn(table, pick)
    block = lax.broadcasted_iota(jnp.int32, (blocks, length), 0)
    lane = lax.broadcasted_iota(jnp.int32, (blocks, length), 1)
    return column_sum(jnp.where(lane // each == block, spreaded, 0.0))


def pack_vectors(vectors, last, blocks, lanes):
    size = last.shape[1] // blocks // 4

    def one(row, first, each):
        length = blocks * each
        source = lax.broadcasted_iota(jnp.int32, (length, lanes), 0)
        target = lax.broadcasted_iota(jnp.int32, (length, lanes), 1)
        pick = jnp.where(target == first + (source & (each - 1)), 1.0, 0.0).astype(bf16)
        block = lax.broadcasted_iota(jnp.int32, (blocks, length), 0)
        lane = lax.broadcasted_iota(jnp.int32, (blocks, length), 1)
        return dot_nn(jnp.where(lane // each == block, row, 0.0).astype(bf16), pick)

    total = one(last, 6 * size, 4 * size)
    for k, vector in enumerate(vectors):
        total = total + one(vector, k * size, size)
    return total


def edge_sums_kernel(plan, total, info, tokens, to_twin, to_other, ends):
    rows, width = tokens.shape
    center, rstd = ln_stats(tokens[...].astype(f32))
    plain = (center * rstd).astype(bf16)
    places = info[0] * rows + lax.broadcasted_iota(jnp.int32, (rows, width), 0)
    living = (plain.astype(f32) * live_counts(info, places, 0, total)).astype(bf16)
    size = 2 * LEVELS * HALO
    row = lax.broadcasted_iota(jnp.int32, (size, rows), 0)
    slot = lax.broadcasted_iota(jnp.int32, (size, rows), 1)
    row_one = lax.broadcasted_iota(jnp.int32, (size, 1), 0)
    wanted = jnp.zeros((size, rows), jnp.int32)
    shift = jnp.zeros((size, rows), jnp.int32)
    share = jnp.zeros((size, 1), f32)
    for k in range(2 * LEVELS):
        level, at = k % LEVELS, k * HALO
        first = 0 if k < LEVELS else plan.counts[level] - HALO
        wanted = jnp.where(row >= at, row - at + first, wanted)
        shift = jnp.where(row >= at, level, shift)
        share = jnp.where(row_one >= at, 0.5**level, share)
    pool = jnp.where((slot >> shift) == wanted, 1.0, 0.0).astype(bf16)
    ends[...] = (dot_nn(pool, plain) * share).astype(bf16)
    row = lax.broadcasted_iota(jnp.int32, (MIXED, rows), 0)
    slot = info[0] * rows + lax.broadcasted_iota(jnp.int32, (MIXED, rows), 1)
    wanted = jnp.full((MIXED, rows), -1, jnp.int32)
    shift = jnp.zeros((MIXED, rows), jnp.int32)
    for level in range(1, LEVELS):
        for k in range(3):
            here = row == (level - 1) * 3 + k
            wanted = jnp.where(here, (info[4 + k] + info[1 + k]) >> level, wanted)
            shift = jnp.where(here, level, shift)
    pick = jnp.where((slot >> shift) == wanted, 1.0, 0.0).astype(bf16)
    mixed = dot_nn(pick, living).astype(bf16)
    even = is_even(info)
    size = LEVELS * HALO
    for target, first in ((to_twin, size), (to_other, 0)):
        at = pl.multiple_of(jnp.where(even, first, size - first), size)
        target[pl.ds(0, size), :] = ends[pl.ds(at, size), :]
        target[pl.ds(size, MIXED), :] = mixed


def edge_sums(plan, total, info, tokens):
    width = tokens.shape[1]
    size = LEVELS * HALO
    return pl.pallas_call(
        functools.partial(edge_sums_kernel, plan, total),
        out_shape=[jax.ShapeDtypeStruct((size + MIXED, width), bf16)] * 2,
        in_specs=[SCALARS] + spec(1),
        out_specs=spec(2),
        scratch_shapes=[pltpu.VMEM((2 * size, width), bf16)],
        compiler_params=params(10),
        name="edge_sums",
        cost_estimate=cost(1.5),
    )(info, tokens)


def prepare_kernel(
    plan,
    total,
    info,
    tokens,
    standard,
    spread,
    pool,
    allowed,
    allowed_back,
    counts,
    edge_allowed,
    edge_counts,
):
    rows = plan.rows
    device = info[0]
    center, rstd = ln_stats(tokens[...].astype(f32))
    standard[...] = center * rstd
    spread[...] = jnp.broadcast_to(rstd, spread.shape)
    pooled_rows = pool.shape[0]
    row = lax.broadcasted_iota(jnp.int32, (pooled_rows, rows), 0)
    slot = lax.broadcasted_iota(jnp.int32, (pooled_rows, rows), 1)
    first = jnp.zeros((pooled_rows, rows), jnp.int32)
    shift = jnp.zeros((pooled_rows, rows), jnp.int32)
    for level in range(1, LEVELS):
        at = plan.query_at[level] - plan.query_at[1]
        first = jnp.where(row >= at, at, first)
        shift = jnp.where(row >= at, level, shift)
    pool[...] = jnp.where((slot >> shift) == row - first, 1.0, 0.0).astype(bf16)

    def block_step(block, carry):
        level, part = plan.locate(block)
        first = device * (rows >> level) + BLOCK * part
        here = pl.ds(pl.multiple_of(BLOCK * block, BLOCK), BLOCK)
        there = pl.ds(pl.multiple_of(WINDOW * block, WINDOW), WINDOW)
        row = first + lax.broadcasted_iota(jnp.int32, (BLOCK, WINDOW), 0)
        column = first - HALO + lax.broadcasted_iota(jnp.int32, (BLOCK, WINDOW), 1)
        allowed[here, :] = admitted(
            tile_codes(info, row, level, total, FAR),
            tile_codes(info, column, level, total, -FAR),
            level,
        )
        key_row = first - HALO + lax.broadcasted_iota(jnp.int32, (WINDOW, 128), 0)
        lane = lax.broadcasted_iota(jnp.int32, (WINDOW, 128), 1)
        row = first + (lane & (BLOCK - 1))
        allowed_back[there, :] = admitted(
            tile_codes(info, row, level, total, FAR),
            tile_codes(info, key_row, level, total, -FAR),
            level,
        )
        counts[there, :] = live_counts(info, key_row, level, total).astype(bf16)
        return carry

    lax.fori_loop(0, len(plan.blocks), block_step, 0, unroll=2)
    two = 2 * HALO
    key = lax.broadcasted_iota(jnp.int32, (two, 128), 0)
    lane = lax.broadcasted_iota(jnp.int32, (two, 128), 1) & (two - 1)
    facing = jnp.where((key < HALO) == (lane < HALO), 1.0, 0.0)
    for level in range(LEVELS):
        count = plan.counts[level]
        start = device * count
        key_row = start + jnp.where(key < HALO, key, count - two + key)
        row = start + jnp.where(lane < HALO, lane - HALO, count - HALO + lane)
        here = pl.ds(two * level, two)
        edge_allowed[here, :] = facing * admitted(
            tile_codes(info, row, level, total, FAR),
            tile_codes(info, key_row, level, total, -FAR),
            level,
        )
        edge_counts[here, :] = live_counts(info, key_row, level, total).astype(bf16)


def prepare(plan, total, info, tokens):
    rows, width = tokens.shape
    blocks = len(plan.blocks)
    return pl.pallas_call(
        functools.partial(prepare_kernel, plan, total),
        out_shape=(
            jax.ShapeDtypeStruct((rows, width), f32),
            jax.ShapeDtypeStruct((rows, 128), f32),
            jax.ShapeDtypeStruct((plan.query_rows - plan.query_at[1], rows), bf16),
            jax.ShapeDtypeStruct((BLOCK * blocks, WINDOW), f32),
            jax.ShapeDtypeStruct((WINDOW * blocks, 128), f32),
            jax.ShapeDtypeStruct((WINDOW * blocks, 128), bf16),
            jax.ShapeDtypeStruct((2 * HALO * LEVELS, 128), f32),
            jax.ShapeDtypeStruct((2 * HALO * LEVELS, 128), bf16),
        ),
        in_specs=[SCALARS] + spec(1),
        out_specs=tuple(spec(8)),
        compiler_params=params(8),
        name="prepare",
        cost_estimate=cost(4),
    )(info, tokens)


def project_kernel(
    plan, total, info, inverse, standard, pool, from_twin, from_other, *refs
):
    pieces, outs = refs[:PIECES], refs[PIECES:]
    queries, pairs, halo_queries, halo_pairs = (outs[2 * k : 2 * k + 2] for k in range(4))
    weight, vectors, shift_out, table, edges, halos, mixed = outs[8:]
    rows, width = standard.shape
    device = info[0]
    each = pieces[0].shape[0]
    block_rows = pieces[0].shape[1] // 3 // 16 * 16
    for p in range(PIECES * each):
        i = inverse[p]
        there = pl.ds(pl.multiple_of(i * block_rows, block_rows), block_rows)
        piece, q = pieces[p // each], p % each
        for c in range(3):
            weight[there, pl.ds(c * width, width)] = piece[q, pl.ds(block_rows * c, block_rows), :]
        line = piece[q, pl.ds(block_rows * 3, LINE_ROWS), pl.ds(0, 2 * LINE)].astype(f32)
        table[pl.ds(i, 1), :] = line[0:1]
    packed = table[...].astype(bf16)
    singles = [unpack_vector(packed, k * block_rows, block_rows) for k in range(2)]
    low = (standard[...] * singles[0] + singles[1]).astype(bf16)
    pooled_rows = pool.shape[0]
    share = jnp.zeros((pooled_rows, 1), f32)
    row_one = lax.broadcasted_iota(jnp.int32, (pooled_rows, 1), 0)
    for level in range(1, LEVELS):
        at = plan.query_at[level] - plan.query_at[1]
        share = jnp.where(row_one >= at, 0.5**level, share)
    places = device * rows + lax.broadcasted_iota(jnp.int32, (rows, QUAD_WIDTH), 0)
    live = live_counts(info, places, 0, total)
    place_halos(info, from_twin, from_other, edges)
    size = LEVELS * HALO
    for k in range(2):
        rest = pl.ds(k * (size + MIXED) + size, MIXED)
        mixed[pl.ds(k * MIXED, MIXED), :] = edges[rest, :].astype(f32)
    for k in range(2 * LEVELS):
        level, here = k % LEVELS, pl.ds(k * HALO, HALO)
        side, span = k // LEVELS * (size + MIXED), 1 << level
        mean = edges[pl.ds(side + level * HALO, HALO), :].astype(f32)
        halos[here, pl.ds(0, width)] = (mean * singles[0] + singles[1]).astype(bf16)
        count = plan.counts[level]
        first = device * count + (-HALO if k < LEVELS else count)
        place = first + lax.broadcasted_iota(jnp.int32, (HALO, 128), 0)
        counts = live_counts(info, place, level, total)
        wide = jnp.concatenate([counts] * (width // 128), axis=1)
        value = jnp.where(wide == span, mean * span, 0.0)
        if level:
            number = slot_facts(info, place << level, total)[0]
            for index in range(3):
                ends = (counts > 0.0) & (counts < span) & (number == index)
                ends = jnp.where(ends, 1.0, 0.0)
                ends = jnp.concatenate([ends] * (width // 128), axis=1)
                row = k // LEVELS * MIXED + (level - 1) * 3 + index
                value = value + ends * mixed[pl.ds(row, 1), :]
        halos[here, pl.ds(width, width)] = (value * singles[0] + wide * singles[1]).astype(bf16)
    lanes = QUAD_WIDTH
    scale = 1.0 / math.sqrt(HEAD_DIM)
    parts = [(divmod(part, 2), pl.ds(part * lanes, lanes)) for part in range(3 * width // lanes)]
    own = pl.ds(0, rows)
    above = pl.ds(rows, pooled_rows)
    blocks = [dot_nn(low, weight[:, columns]).astype(bf16) for _, columns in parts]
    for index, ((kind, quad), _) in enumerate(parts):
        if kind == 0:
            queries[quad][own, :] = (blocks[index].astype(f32) * scale).astype(bf16)
            continue
        if kind == 2:
            blocks[index] = (blocks[index].astype(f32) * live).astype(bf16)
        pairs[quad][own, pl.ds((kind - 1) * lanes, lanes)] = blocks[index]
    pooled = [dot_nn(pool[...], block) for block in blocks]
    for ((kind, quad), _), item in zip(parts, pooled):
        if kind == 0:
            queries[quad][above, :] = (item * (share * scale)).astype(bf16)
            continue
        if kind == 1:
            item = item * share
        pairs[quad][above, pl.ds((kind - 1) * lanes, lanes)] = item.astype(bf16)
    sides = [
        dot_nn(halos[:, pl.ds(width if kind == 2 else 0, width)], weight[:, columns])
        for (kind, _), columns in parts
    ]
    for ((kind, quad), _), item in zip(parts, sides):
        if kind == 0:
            halo_queries[quad][...] = (item * scale).astype(bf16)
        else:
            halo_pairs[quad][:, pl.ds((kind - 1) * lanes, lanes)] = item.astype(bf16)
    singles += [unpack_vector(packed, k * block_rows, block_rows) for k in range(2, 6)]
    for k, single in enumerate(singles):
        vectors[pl.ds(k, 1), :] = single
    shift_out[...] = unpack_vector(packed, 6 * block_rows, 4 * block_rows)


def project(plan, total, info, inverse, standard, pool, from_twin, from_other, pieces):
    rows, width = standard.shape
    halo = LEVELS * HALO
    blocks = PIECES * pieces[0].shape[0]
    depth = blocks * (pieces[0].shape[1] - LINE_ROWS) // 3
    half = width // 2
    outs = pl.pallas_call(
        functools.partial(project_kernel, plan, total),
        out_shape=(
            [jax.ShapeDtypeStruct((plan.query_rows, half), bf16)] * 2
            + [jax.ShapeDtypeStruct((plan.query_rows, 2 * half), bf16)] * 2
            + [jax.ShapeDtypeStruct((2 * halo, half), bf16)] * 2
            + [jax.ShapeDtypeStruct((2 * halo, 2 * half), bf16)] * 2
            + [
                jax.ShapeDtypeStruct((depth, 3 * width), bf16),
                jax.ShapeDtypeStruct((8, depth), f32),
                jax.ShapeDtypeStruct((1, 4 * depth), f32),
            ]
        ),
        in_specs=[SCALARS, SCALARS] + spec(4 + PIECES),
        out_specs=spec(11),
        scratch_shapes=[
            pltpu.VMEM((blocks, 2 * LINE), f32),
            pltpu.VMEM((2 * (halo + MIXED), width), bf16),
            pltpu.VMEM((2 * halo, 2 * width), bf16),
            pltpu.VMEM((2 * MIXED, width), f32),
        ],
        compiler_params=params(18),
        name="project",
        cost_estimate=cost(3.3),
    )(info, inverse, standard, pool, from_twin, from_other, *pieces)
    return [outs[2 * k : 2 * k + 2] for k in range(4)] + list(outs[8:])


def attend_kernel(plan, total, info, mask, counts_of, *refs):
    queries, pairs, halos, attended, mixed, scale, extended = (
        refs[2 * k : 2 * k + 2] for k in range(7)
    )
    numer, denom = refs[14:]
    rows = plan.rows
    device = info[0]
    for quad in range(2):
        fill_extended(plan, pairs[quad], halos[quad], extended[quad])
    first_head = lax.broadcasted_iota(jnp.int32, (BLOCK, 128), 1) < HEAD_DIM
    masks = head_masks(BLOCK)

    def prepare(block):
        level, part = plan.locate(block)
        here = pl.ds(pl.multiple_of(BLOCK * block, BLOCK), BLOCK)
        there = pl.ds(pl.multiple_of(BLOCK * block + 2 * HALO * level, BLOCK), WINDOW)
        allowed = mask[here, :]
        counts = counts_of[pl.ds(pl.multiple_of(WINDOW * block, WINDOW), WINDOW), :]
        return here, there, allowed, counts

    def block_step(step, carry):
        work = []
        for k in range(4):
            here, there, allowed, counts = prepare(step * 4 + k)
            allowed = jnp.concatenate([allowed] * 4, axis=0) > 0.0
            for part in range(8 // 4):
                work.append((here, there, allowed, counts, part))
        scores = []
        for here, there, allowed, counts, part in work:
            wide = 4 * HEAD_DIM
            quad, half = divmod(part * wide, QUAD_WIDTH)
            lanes = pl.ds(half, wide)
            q = spread_heads(queries[quad][here, lanes], masks)
            scores.append(dot_nt(q, extended[quad][there, lanes]))
        weights = [
            jnp.where(item[2], jnp.exp(score), 0.0).astype(bf16)
            for item, score in zip(work, scores)
        ]
        for (here, there, allowed, counts, part), weight in zip(work, weights):
            wide = 4 * HEAD_DIM
            for sub in range(4 // 2):
                pair = part * (4 // 2) + sub
                quad, half = divmod(pair, 2)
                v = extended[quad][there, pl.ds(QUAD_WIDTH + 128 * half, 128)]
                both = dot_nn(
                    weight[128 * sub : 128 * sub + 128], jnp.concatenate([v, counts], axis=1)
                )
                numer[pair, here, :] = join_pair(both[:, :128], first_head)
                denom[pair, here, :] = join_pair(both[:, 128:], first_head)
        return carry

    lax.fori_loop(0, len(plan.blocks) // 4, block_step, 0, unroll=1)
    places = device * rows + lax.broadcasted_iota(jnp.int32, (rows, 128), 0)
    live = live_counts(info, places, 0, total)
    for pair in range(4):
        for sums in (numer, denom):
            for level in range(LEVELS - 1, 0, -1):
                count = plan.counts[level]
                upper = sums[pair, pl.ds(plan.query_at[level], count), :]
                for parity in range(2):
                    there = pl.ds(plan.query_at[level - 1] + parity, count, stride=2)
                    sums[pair, there, :] = sums[pair, there, :] + upper
        quad, half = divmod(pair, 2)
        lanes = pl.ds(128 * half, 128)
        factor = live / (denom[pair, pl.ds(0, rows), :] + 1.0 - live)
        value = numer[pair, pl.ds(0, rows), :] * factor
        scale[quad][:, lanes] = factor
        mixed[quad][:, lanes] = value
        attended[quad][:, lanes] = value.astype(bf16)


def attend(plan, total, info, mask, counts, queries, pairs, halos):
    rows, width = plan.rows, queries[0].shape[1]
    outs = pl.pallas_call(
        functools.partial(attend_kernel, plan, total),
        out_shape=[jax.ShapeDtypeStruct((rows, width), bf16)] * 2
        + [jax.ShapeDtypeStruct((rows, width), f32)] * 4,
        in_specs=[SCALARS] + spec(8),
        out_specs=spec(6),
        scratch_shapes=[
            pltpu.VMEM((plan.key_rows, 2 * width), bf16),
            pltpu.VMEM((plan.key_rows, 2 * width), bf16),
            pltpu.VMEM((2 * width // 128, plan.query_rows, 128), f32),
            pltpu.VMEM((2 * width // 128, plan.query_rows, 128), f32),
        ],
        compiler_params=params(20),
        name="attend",
        cost_estimate=cost(8),
    )(info, mask, counts, *queries, *pairs, *halos)
    return outs[:2], outs[2:4], outs[4:]


def forward_kernel(
    parts,
    inverse,
    sums_inverse,
    tokens,
    cotangent,
    attended_a,
    attended_b,
    vectors,
    shift_in,
    *refs,
):
    pieces = refs[:parts]
    result, resid_out, grad_normed, w_out, own, low_half, high_half, sum_in = refs[
        parts : parts + 8
    ]
    w_in, w_back, normed_two, outer, tall, flat, turned, cot_turned = refs[parts + 8 :]
    other = (low_half, high_half)
    width = tokens.shape[1]
    wide = width // 2
    each = pieces[0].shape[0]
    half = own.shape[0]
    chunks = w_in.shape[0]
    block = width // (parts * each)
    tall_block = chunks * block
    back_at = block + tall_block
    for p in range(parts * each):
        piece, q = pieces[p // each], p % each
        i = inverse[p]
        rows = pl.ds(pl.multiple_of(i * block, block), block)
        w_out[rows, :] = piece[q, pl.ds(0, block), :]
        for c in range(chunks):
            w_in[c, rows, :] = piece[q, pl.ds(block * (c + 1), block), :]
        rows = pl.ds(pl.multiple_of(i * tall_block, tall_block), tall_block)
        w_back[rows, :] = piece[q, pl.ds(back_at, tall_block), :]
    gain = vectors[pl.ds(3, 1), :]
    resid = tokens[...].astype(f32) + dot_nn(attended_a[...], w_out[pl.ds(0, wide), :])
    resid = resid + dot_nn(attended_b[...], w_out[pl.ds(wide, wide), :]) + vectors[pl.ds(2, 1), :]
    center, rstd = ln_stats(resid)
    normed_two[...] = (center * rstd * gain + vectors[pl.ds(4, 1), :]).astype(bf16)
    turned[...] = normed_two[...].T
    resid_out[...] = resid
    outer[...] = jnp.zeros(outer.shape, f32)
    grad_normed[...] = jnp.zeros(grad_normed.shape, f32)

    def chunk_step(c, carry):
        there = pl.ds(pl.multiple_of(c * width, width), width)
        inner = dot_nn(normed_two[...], w_in[c]) + shift_in[:, there]
        cdf = 0.5 * (1.0 + lax.erf(inner * math.sqrt(0.5)))
        active = (inner * cdf).astype(bf16)
        slope = cdf + inner * (jnp.exp(-0.5 * inner * inner) * (1.0 / math.sqrt(2.0 * math.pi)))
        back = w_back[there, :]
        grad_inner = slope * dot_nt(cotangent[...], back)
        low = grad_inner.astype(bf16)
        outer[...] += dot_nn(active, back)
        tall[there, :] = dot_tn(active, cotangent[...]).astype(bf16)
        sum_in[:, there] = column_sum(low.astype(f32))
        flat[...] = dot_nn(turned[...], low).astype(bf16)
        for p in range(2 * half):
            i = sums_inverse[p]
            rows = flat[pl.ds(pl.multiple_of(i * block, block), block), :]
            at = pl.ds(pl.multiple_of(c * block, block), block)
            if p < half:
                own[p, at, :] = rows
            else:
                other[(p - half) // 8][(p - half) % 8, at, :] = rows
        grad_normed[...] += dot_nt(low, w_in[c])
        return carry

    lax.fori_loop(0, chunks, chunk_step, 0, unroll=4)
    result[...] = (resid_out[...] + outer[...] + vectors[pl.ds(5, 1), :]).astype(bf16)
    for p in range(2 * half):
        i = sums_inverse[p]
        rows = tall[pl.ds(pl.multiple_of(i * tall_block, tall_block), tall_block), :]
        there = pl.ds(tall_block, tall_block)
        if p < half:
            own[p, there, :] = rows
        else:
            other[(p - half) // 8][(p - half) % 8, there, :] = rows


def feed_forward(inverses, tokens, cotangent, attended, vectors, shift_in, pieces):
    parts = len(pieces)
    rows, width = tokens.shape
    hidden = shift_in.shape[1]
    chunks = hidden // width
    blocks = parts * pieces[0].shape[0]
    stack = pieces[0].shape[1] - width // blocks
    return pl.pallas_call(
        functools.partial(forward_kernel, parts),
        out_shape=(
            jax.ShapeDtypeStruct((rows, width), bf16),
            jax.ShapeDtypeStruct((rows, width), f32),
            jax.ShapeDtypeStruct((rows, width), f32),
            jax.ShapeDtypeStruct((width, width), bf16),
            jax.ShapeDtypeStruct((blocks // 2, stack, width), bf16),
            jax.ShapeDtypeStruct((blocks // 4, stack, width), bf16),
            jax.ShapeDtypeStruct((blocks // 4, stack, width), bf16),
            jax.ShapeDtypeStruct((1, hidden), f32),
        ),
        in_specs=[SCALARS] * 2 + spec(6 + parts),
        out_specs=tuple(spec(8)),
        scratch_shapes=[
            pltpu.VMEM((chunks, width, width), bf16),
            pltpu.VMEM((hidden, width), bf16),
            pltpu.VMEM((rows, width), bf16),
            pltpu.VMEM((rows, width), f32),
            pltpu.VMEM((hidden, width), bf16),
            pltpu.VMEM((width, width), bf16),
            pltpu.VMEM((width, rows), bf16),
            pltpu.VMEM((width, rows), bf16),
        ],
        compiler_params=params(30),
        name="feed_forward",
        cost_estimate=cost(10),
    )(*inverses, tokens, cotangent, *attended, vectors, shift_in, *pieces)


def middle_kernel(
    plan,
    info,
    sums_inverse,
    cotangent,
    attended_a,
    attended_b,
    mixed_a,
    mixed_b,
    scale_a,
    scale_b,
    vectors,
    resid,
    grad_normed,
    w_out,
    grad_resid,
    grads_a,
    grads_b,
    to_twin,
    to_other,
    sums,
    own,
    low_half,
    high_half,
    levels,
    ends,
    denoms,
    flat,
):
    width = cotangent.shape[1]
    wide = width // 2
    center, rstd = ln_stats(resid[...])
    grad_in, gain_terms = ln_back(grad_normed[...], center * rstd, rstd, vectors[pl.ds(3, 1), :])
    grad_out = cotangent[...].astype(f32)
    total = grad_out + grad_in
    grad_resid[...] = total
    low = total.astype(bf16)
    sums[pl.ds(0, 1), :] = jnp.zeros((1, width), f32)
    sums[pl.ds(1, 1), :] = jnp.zeros((1, width), f32)
    sums[pl.ds(2, 1), :] = column_sum(low.astype(f32))
    sums[pl.ds(3, 1), :] = column_sum(gain_terms)
    sums[pl.ds(4, 1), :] = column_sum(grad_normed[...])
    sums[pl.ds(5, 1), :] = column_sum(grad_out)
    for quad in range(2):
        lines = pl.ds(quad * wide, wide)
        flat[lines, :] = dot_tn((attended_a, attended_b)[quad][...], low).astype(bf16)
        numer = dot_nt(low, w_out[lines, :]) * (scale_a, scale_b)[quad][...]
        denom = -(numer * (mixed_a, mixed_b)[quad][...])
        for chunk in range(2 * wide // 128):
            source = numer if chunk < wide // 128 else denom
            lane = chunk * 128 % wide
            levels[chunk, pl.ds(0, plan.rows), :] = source[:, lane : lane + 128]
            for level in range(1, LEVELS):
                count, at = plan.counts[level], plan.query_at[level]
                below = plan.query_at[level - 1]
                levels[chunk, pl.ds(at, count), :] = (
                    levels[chunk, pl.ds(below, count, stride=2), :]
                    + levels[chunk, pl.ds(below + 1, count, stride=2), :]
                )
                rest = plan.padded[level] - count
                if rest:
                    levels[chunk, pl.ds(at + count, rest), :] = jnp.zeros((rest, 128), f32)
            grads = (grads_a, grads_b)[quad]
            grads[:, pl.ds(chunk * 128, 128)] = levels[chunk].astype(bf16)
        for k in range(2 * LEVELS):
            level, here = k % LEVELS, pl.ds(k * HALO, HALO)
            at = plan.query_at[level] + (0 if k < LEVELS else plan.counts[level] - HALO)
            there = pl.ds(at, HALO)
            ends[here, pl.ds(quad * wide, wide)] = (grads_a, grads_b)[quad][there, pl.ds(0, wide)]
            for chunk in range(wide // 128):
                lanes = pl.ds(quad * wide + chunk * 128, 128)
                denoms[here, lanes] = levels[wide // 128 + chunk, there, :]
    feature = lax.broadcasted_iota(jnp.int32, (width, LINE), 0)
    lane = lax.broadcasted_iota(jnp.int32, (width, LINE), 1)
    pick = jnp.where(lane == feature // HEAD_DIM, 1.0, 0.0).astype(bf16)
    heads = width // HEAD_DIM
    values = denoms[...]
    first = values.astype(bf16)
    values = dot_nn(first, pick) + dot_nn((values - first.astype(f32)).astype(bf16), pick)
    first = values.astype(bf16).astype(f32)
    both = jnp.concatenate([first[:, :heads], (values - first)[:, :heads]], axis=1)
    both = jnp.concatenate([both, jnp.zeros((both.shape[0], LINE - 2 * heads), f32)], axis=1)
    ends[:, pl.ds(width, LINE)] = both.astype(bf16)
    hand_out(info, ends, to_twin, to_other)
    half, block = own.shape[0], own.shape[1]
    other = (low_half, high_half)
    for p in range(2 * half):
        rows = flat[pl.ds(pl.multiple_of(sums_inverse[p] * block, block), block), :]
        if p < half:
            own[p] = rows
        else:
            other[(p - half) // 8][(p - half) % 8] = rows


def middle(plan, info, sums_inverse, cotangent, attended, mixed, scale, vectors, resid, grad_normed, w_out):
    rows, width = cotangent.shape
    size = LEVELS * HALO
    return pl.pallas_call(
        functools.partial(middle_kernel, plan),
        out_shape=(
            jax.ShapeDtypeStruct((rows, width), f32),
            jax.ShapeDtypeStruct((plan.query_rows, width), bf16),
            jax.ShapeDtypeStruct((plan.query_rows, width), bf16),
            jax.ShapeDtypeStruct((size, width + LINE), bf16),
            jax.ShapeDtypeStruct((size, width + LINE), bf16),
            jax.ShapeDtypeStruct((8, width), f32),
            jax.ShapeDtypeStruct((BLOCKS // 2, width // BLOCKS, width), bf16),
            jax.ShapeDtypeStruct((BLOCKS // 4, width // BLOCKS, width), bf16),
            jax.ShapeDtypeStruct((BLOCKS // 4, width // BLOCKS, width), bf16),
        ),
        in_specs=[SCALARS] * 2 + spec(11),
        out_specs=tuple(spec(9)),
        scratch_shapes=[
            pltpu.VMEM((width // 128, plan.query_rows, 128), f32),
            pltpu.VMEM((2 * size, width + LINE), bf16),
            pltpu.VMEM((2 * size, width), f32),
            pltpu.VMEM((width, width), bf16),
        ],
        compiler_params=params(20),
        name="middle",
        cost_estimate=cost(3),
    )(info, sums_inverse, cotangent, *attended, *mixed, *scale, vectors, resid, grad_normed, w_out)


def attend_back_kernel(plan, total, mask, counts_of, *refs):
    queries, pairs, halos, grads, grad_queries, grad_extended, extended = (
        refs[2 * k : 2 * k + 2] for k in range(7)
    )
    width = QUAD_WIDTH
    for quad in range(2):
        fill_extended(plan, pairs[quad], halos[quad], extended[quad])
        grad_extended[quad][...] = jnp.zeros(grad_extended[quad].shape, f32)
    masks = head_masks(BLOCK)
    first_head = lax.broadcasted_iota(jnp.int32, (BLOCK, 128), 1) < HEAD_DIM
    keys = pl.ds(0, width)
    values = pl.ds(width, width)

    def prepare(block):
        level, part = plan.locate(block)
        here = pl.ds(pl.multiple_of(BLOCK * block, BLOCK), BLOCK)
        there = pl.ds(pl.multiple_of(BLOCK * block + 2 * HALO * level, BLOCK), WINDOW)
        window = pl.ds(pl.multiple_of(WINDOW * block, WINDOW), WINDOW)
        allowed = jnp.concatenate([mask[window, :]] * (QUAD * BLOCK // 128), axis=1) > 0.0
        counts = counts_of[window, :]
        return here, there, allowed, counts

    def block_step(step, carry):
        work = []
        for k in range(4):
            here, there, allowed, counts = prepare(step * 4 + k)
            for quad in range(2):
                q = spread_heads(queries[quad][here, :], masks)
                g = spread_heads(grads[quad][here, keys], masks)
                d = spread_heads(grads[quad][here, values], masks)
                work.append((quad, here, there, allowed, counts, q, g, d))
        scores, grad_probs = [], []
        for quad, here, there, allowed, counts, q, g, d in work:
            scores.append(dot_nt(extended[quad][there, keys], q))
            v = extended[quad][there, values]
            value_and_count = jnp.concatenate([v] + [counts] * (width // 128), axis=1)
            grad_probs.append(dot_nt(value_and_count, jnp.concatenate([g, d], axis=1)))
        weights = [
            jnp.where(item[3], jnp.exp(score), 0.0) for item, score in zip(work, scores)
        ]
        grad_scores = [(x * y).astype(bf16) for x, y in zip(grad_probs, weights)]
        probs = [weight.astype(bf16) for weight in weights]
        keys_of = [extended[item[0]][item[2], keys] for item in work]
        to_queries = [
            [
                dot_tn(grad_score[:, 128 * half : 128 * half + 128], k[:, 128 * half : 128 * half + 128])
                for half in range(2)
            ]
            for grad_score, k in zip(grad_scores, keys_of)
        ]
        to_keys = [dot_nn(grad_score, item[5]) for grad_score, item in zip(grad_scores, work)]
        to_values = [dot_nn(prob, item[6]) for prob, item in zip(probs, work)]
        for item, parts, to_key, to_value in zip(work, to_queries, to_keys, to_values):
            quad, here, there = item[:3]
            for half in range(2):
                grad_queries[quad][here, pl.ds(128 * half, 128)] = join_pair(
                    parts[half], first_head
                ) * (1.0 / math.sqrt(HEAD_DIM))
            grad_extended[quad][there, keys] += to_key
            grad_extended[quad][there, values] += to_value
        return carry

    lax.fori_loop(0, len(plan.blocks) // 4, block_step, 0, unroll=1)


def attend_back(plan, total, mask, counts, queries, pairs, halos, grads):
    width = queries[0].shape[1]
    outs = pl.pallas_call(
        functools.partial(attend_back_kernel, plan, total),
        out_shape=[jax.ShapeDtypeStruct((plan.query_rows, width), f32)] * 2
        + [jax.ShapeDtypeStruct((plan.key_rows, 2 * width), f32)] * 2,
        in_specs=spec(10),
        out_specs=spec(4),
        scratch_shapes=[
            pltpu.VMEM((plan.key_rows, 2 * width), bf16),
            pltpu.VMEM((plan.key_rows, 2 * width), bf16),
        ],
        compiler_params=params(24),
        name="attend_back",
        cost_estimate=cost(12),
    )(mask, counts, *queries, *pairs, *halos, *grads)
    return outs[:2], outs[2:]


def edge_back_kernel(
    plan,
    info,
    mask,
    counts_of,
    queries_a,
    queries_b,
    pairs_a,
    pairs_b,
    from_twin,
    from_other,
    low,
    high,
    grads,
):
    width = queries_a.shape[1]
    place_halos(info, from_twin, from_other, grads)
    two = 2 * HALO
    masks = head_masks(two)
    keys = pl.ds(0, width)
    heads = 2 * width // HEAD_DIM
    source = lax.broadcasted_iota(jnp.int32, (LINE, width), 0)
    target = lax.broadcasted_iota(jnp.int32, (LINE, width), 1)
    picks = []
    for quad in range(2):
        head = target // HEAD_DIM + quad * QUAD
        wanted = jnp.where(target % HEAD_DIM == 0, head, -1)
        wanted = jnp.where(target % HEAD_DIM == 1, head + heads, wanted)
        picks.append(jnp.where(source == wanted, 1.0, 0.0).astype(bf16))
    denoms = [dot_nn(grads[:, pl.ds(2 * width, LINE)], pick).astype(bf16) for pick in picks]
    work = []
    for level in range(LEVELS):
        count, at = plan.counts[level], plan.query_at[level]
        here = pl.ds(two * level, two)
        allowed = jnp.concatenate([mask[here, :]] * (QUAD * two // 128), axis=1) > 0.0
        counts = counts_of[here, :]
        ahead, behind = HALO * level, HALO * (LEVELS + level)

        def both(item, lanes):
            parts = [item[pl.ds(first, HALO), lanes] for first in (ahead, behind)]
            return jnp.concatenate(parts, axis=0)

        for quad in range(2):
            pairs = (pairs_a, pairs_b)[quad]
            own = jnp.concatenate(
                [pairs[pl.ds(at, HALO), :], pairs[pl.ds(at + count - HALO, HALO), :]], axis=0
            )
            k, v = own[:, :width], own[:, width:]
            d = denoms[quad]
            d = jnp.concatenate([d[ahead : ahead + HALO], d[behind : behind + HALO]], axis=0)
            q = spread_heads(both((queries_a, queries_b)[quad], keys), masks)
            g = spread_heads(both(grads, pl.ds(quad * width, width)), masks)
            d = spread_heads(d, masks)
            value_and_count = jnp.concatenate([v] + [counts] * (width // 128), axis=1)
            there = pl.ds(HALO * (quad * LEVELS + level), HALO)
            work.append((there, allowed, q, g, d, k, value_and_count))
    scores = [dot_nt(item[5], item[2]) for item in work]
    grad_probs = [
        dot_nt(item[6], jnp.concatenate([item[3], item[4]], axis=1)) for item in work
    ]
    weights = [jnp.where(item[1], jnp.exp(score), 0.0) for item, score in zip(work, scores)]
    grad_scores = [(x * y).astype(bf16) for x, y in zip(grad_probs, weights)]
    to_keys = [dot_nn(grad_score, item[2]) for grad_score, item in zip(grad_scores, work)]
    to_values = [dot_nn(weight.astype(bf16), item[3]) for weight, item in zip(weights, work)]
    for item, to_key, to_value in zip(work, to_keys, to_values):
        there = item[0]
        low[there, keys] = to_key[:HALO]
        high[there, keys] = to_key[HALO:]
        low[there, pl.ds(width, width)] = to_value[:HALO]
        high[there, pl.ds(width, width)] = to_value[HALO:]


def edge_back(plan, info, mask, counts, queries, pairs, from_twin, from_other):
    width = queries[0].shape[1]
    size = 2 * LEVELS * HALO
    return pl.pallas_call(
        functools.partial(edge_back_kernel, plan),
        out_shape=[jax.ShapeDtypeStruct((size, 2 * width), f32)] * 2,
        in_specs=[SCALARS] + spec(8),
        out_specs=spec(2),
        scratch_shapes=[pltpu.VMEM((size, 2 * width + LINE), bf16)],
        compiler_params=params(12),
        name="edge_back",
        cost_estimate=cost(2.5),
    )(info, mask, counts, *queries, *pairs, from_twin, from_other)


def finish_kernel(
    plan,
    total,
    info,
    inverse,
    standard,
    spread,
    weight,
    vectors,
    grad_resid,
    sums,
    sum_in,
    queries_a,
    queries_b,
    pairs_a,
    pairs_b,
    edge_low,
    edge_high,
    grad_tokens,
    own,
    low_half,
    high_half,
    work,
    joined,
    flat,
    table,
):
    rows, width = standard.shape
    device = info[0]
    half_width = width // 2
    places = device * rows + lax.broadcasted_iota(jnp.int32, (rows, 128), 0)
    live = live_counts(info, places, 0, total)
    hat = standard[...]
    gain = vectors[pl.ds(0, 1), :]
    normed = (hat * gain + vectors[pl.ds(1, 1), :]).astype(bf16)
    half, block = own.shape[0], width // BLOCKS
    other = (low_half, high_half)
    grad_normed = jnp.zeros((rows, width), f32)
    for part in range(3):
        for step in range(width // 128):
            chunk = part * (width // 128) + step
            quad, lane = divmod(step * 128, half_width)
            if part == 0:
                work[chunk] = (queries_a, queries_b)[quad][:, pl.ds(lane, 128)]
            else:
                lanes = pl.ds((part - 1) * half_width + lane, 128)
                for level in range(LEVELS):
                    at, count = plan.query_at[level], plan.counts[level]
                    own_rows = pl.ds(plan.key_at[level] + HALO, count)
                    work[chunk, pl.ds(at, count), :] = (pairs_a, pairs_b)[quad][own_rows, lanes]
                    halo = pl.ds(HALO * (quad * LEVELS + level), HALO)
                    work[chunk, pl.ds(at, HALO), :] += edge_low[halo, lanes]
                    work[chunk, pl.ds(at + count - HALO, HALO), :] += edge_high[halo, lanes]
            for level in range(LEVELS - 1, 0, -1):
                count = plan.counts[level]
                upper = work[chunk, pl.ds(plan.query_at[level], count), :]
                if chunk * 128 < 2 * width:
                    upper = upper * 0.5
                for parity in range(2):
                    there = pl.ds(plan.query_at[level - 1] + parity, count, stride=2)
                    work[chunk, there, :] = work[chunk, there, :] + upper
            value = work[chunk, pl.ds(0, rows), :]
            if chunk * 128 >= 2 * width:
                value = value * live
            joined[:, pl.ds(chunk * 128, 128)] = value.astype(bf16)
        columns = pl.ds(part * width, width)
        flat[part] = dot_tn(normed, joined[:, columns]).astype(bf16)
        for p in range(2 * half):
            i = inverse[p]
            lines = flat[part, pl.ds(pl.multiple_of(i * block, block), block), :]
            there = pl.ds(part * block, block)
            if p < half:
                own[p, there, :] = lines
            else:
                other[(p - half) // 8][(p - half) % 8, there, :] = lines
        grad_normed = grad_normed + dot_nt(joined[:, columns], weight[:, columns])
    grad_in, gain_terms = ln_back(grad_normed, hat, spread[:, :1], gain)
    grad_tokens[...] = grad_resid[...] + grad_in
    singles = [column_sum(gain_terms), column_sum(grad_normed)]
    singles += [sums[pl.ds(k, 1), :] for k in range(2, 6)]
    table[...] = pack_vectors(singles, sum_in[...], 2 * half, table.shape[1])
    row = lax.broadcasted_iota(jnp.int32, (LINE_ROWS, 2 * LINE), 0)
    there = pl.ds(3 * block, LINE_ROWS)
    for p in range(2 * half):
        i = inverse[p]
        line = table[pl.ds(i, 1), :]
        lines = jnp.where(row == 0, line, 0.0)
        lines = jnp.concatenate([lines, jnp.zeros((LINE_ROWS, width - 2 * LINE), f32)], axis=1)
        if p < half:
            own[p, there, :] = lines.astype(bf16)
        else:
            other[(p - half) // 8][(p - half) % 8, there, :] = lines.astype(bf16)


def finish(plan, total, info, inverse, standard, spread, weight, *rest):
    rows, width = standard.shape
    half = BLOCKS // 2
    block = width // BLOCKS
    return pl.pallas_call(
        functools.partial(finish_kernel, plan, total),
        out_shape=(
            jax.ShapeDtypeStruct((rows, width), f32),
            jax.ShapeDtypeStruct((half, 3 * block + LINE_ROWS, width), bf16),
            jax.ShapeDtypeStruct((half // 2, 3 * block + LINE_ROWS, width), bf16),
            jax.ShapeDtypeStruct((half // 2, 3 * block + LINE_ROWS, width), bf16),
        ),
        in_specs=[SCALARS, SCALARS] + spec(3 + len(rest)),
        out_specs=tuple(spec(4)),
        scratch_shapes=[
            pltpu.VMEM((3 * width // 128, plan.query_rows, 128), f32),
            pltpu.VMEM((rows, 3 * width), bf16),
            pltpu.VMEM((3, width, width), bf16),
            pltpu.VMEM((BLOCKS, 2 * LINE), f32),
        ],
        compiler_params=params(28),
        name="finish",
        cost_estimate=cost(6.2),
    )(info, inverse, standard, spread, weight, *rest)


class Ring:
    def __init__(self, devices, *orders):
        self.devices = devices
        self.orders = orders
        self.stages = len(orders[0])

    def partner(self, stage):
        return [(i, i ^ self.orders[i & 1][stage]) for i in range(self.devices)]

    def twin(self):
        return [(i, i ^ 1) for i in range(self.devices)]

    def places(self, device):
        found = []
        even = (device & 1) == 0
        for base, swap in ((device, False), (device ^ 1, True)):
            for position in range(1 << self.stages):
                masks = [
                    sum(order[k] for k in range(self.stages) if position >> k & 1)
                    for order in self.orders
                ]
                if swap:
                    masks = masks[::-1]
                found.append(base ^ jnp.where(even, *masks))
        return found

    def step(self, stage, arrays):
        route = self.twin() if stage == self.stages else self.partner(stage)
        return [lax.ppermute(item, "seq", route) for item in arrays]

    def fold(self, stage, own, low, high):
        half = 1 << stage
        sent = (own[half:].astype(f32) + high.astype(f32)).astype(bf16)
        kept = own[:half].astype(f32) + low.astype(f32)
        return kept, sent


def halves(item):
    half = item.shape[0] // 2
    return item[:half], item[half:]


def join(held, came):
    return [jnp.concatenate(pair) for pair in zip(held, came)]


def pack_kernel(rings, plan, total, lengths, tokens, w_qkv, w_out, w_in, w_back, *refs):
    vectors, refs = refs[:-8], refs[-8:]
    info, *inverses, payload, to_twin, to_other, staged, ends = refs
    device = lax.axis_index("seq")
    info[0] = device
    start = jnp.int32(0)
    for k in range(3):
        length = lengths[k]
        info[1 + k] = length
        info[4 + k] = start
        start = start + (length + 15) // 16 * 16
        info[7 + k] = start
    for ring, inverse in zip(rings, inverses):
        for place, block in enumerate(ring.places(device)):
            inverse[place] = block
    block, width = w_out.shape
    chunks = w_in.shape[1] // width
    staged[...] = jnp.zeros(staged.shape, f32)
    for k, vector in enumerate(vectors):
        size = vector.shape[0]
        lane = k * block
        staged[pl.ds(0, 1), pl.ds(lane, size)] = vector[...].astype(f32).reshape(1, size)
    payload[0, pl.ds(0, block), :] = w_out[...]
    for c in range(chunks):
        payload[0, pl.ds(block * (c + 1), block), :] = w_in[:, pl.ds(c * width, width)]
    at = block * (chunks + 1)
    payload[0, pl.ds(at, block * chunks), :] = w_back[...]
    at = at + block * chunks
    for c in range(3):
        payload[0, pl.ds(at + block * c, block), :] = w_qkv[:, pl.ds(c * width, width)]
    payload[0, pl.ds(at + block * 3, LINE_ROWS), :] = staged[...].astype(bf16)
    edge_sums_kernel(plan, total, info, tokens, to_twin, to_other, ends)


def pack(rings, plan, total, lengths, tokens, w_qkv, w_out, w_in, w_back, vectors):
    size = LEVELS * HALO
    block, width = w_out.shape
    rows = 4 * block + w_in.shape[1] // width * block + w_back.shape[0] + LINE_ROWS
    return pl.pallas_call(
        functools.partial(pack_kernel, rings, plan, total),
        out_shape=(
            jax.ShapeDtypeStruct((10,), jnp.int32),
            jax.ShapeDtypeStruct((BLOCKS,), jnp.int32),
            jax.ShapeDtypeStruct((BLOCKS,), jnp.int32),
            jax.ShapeDtypeStruct((1, rows, width), bf16),
            jax.ShapeDtypeStruct((size + MIXED, width), bf16),
            jax.ShapeDtypeStruct((size + MIXED, width), bf16),
        ),
        in_specs=[SCALARS] + spec(5 + len(vectors)),
        out_specs=(SCALARS,) * 3 + tuple(spec(3)),
        scratch_shapes=[pltpu.VMEM((LINE_ROWS, width), f32), pltpu.VMEM((2 * size, width), bf16)],
        compiler_params=params(62),
        name="pack",
        cost_estimate=cost(1.5),
    )(lengths, tokens, w_qkv, w_out, w_in, w_back, *vectors)


def unpack_kernel(kept_one, came_one, kept_two, came_two, *outs):
    block, width = (kept_one.shape[1] - LINE_ROWS) // 3, kept_two.shape[2]
    w_qkv, w_out, w_in, w_back = outs[:4]
    for c in range(3):
        rows = pl.ds(block * c, block)
        w_qkv[:, pl.ds(c * width, width)] = kept_one[0, rows, :] + came_one[0, rows, :].astype(f32)
    rows = pl.ds(block * 3, LINE_ROWS)
    lines = kept_one[0, rows, :] + came_one[0, rows, :].astype(f32)
    for k, out in enumerate(outs[4:]):
        size = out.shape[0]
        lane = k * block
        out[...] = lines[0:1, lane : lane + size].reshape(size)
    chunks = w_in.shape[1] // width

    def total(at, size):
        rows = pl.ds(at, size)
        return kept_two[0, rows, :] + came_two[0, rows, :].astype(f32)

    w_out[...] = total(2 * block * chunks, block)
    for c in range(chunks):
        w_in[:, pl.ds(c * width, width)] = total(block * c, block)
    w_back[...] = total(block * chunks, block * chunks)


def unpack(kept_one, came_one, kept_two, came_two, like):
    return pl.pallas_call(
        unpack_kernel,
        out_shape=[jax.ShapeDtypeStruct(item.shape, f32) for item in like],
        in_specs=spec(4),
        out_specs=spec(len(like)),
        compiler_params=params(8),
        name="unpack",
        cost_estimate=cost(1.5),
    )(kept_one, came_one, kept_two, came_two)


def exchange(to_twin, to_other):
    count = lax.axis_size("seq")
    twin = [(i, i ^ 1) for i in range(count)]
    other = [(i, i + 1) for i in range(1, count - 1, 2)]
    other += [(j, i) for i, j in other]
    return lax.ppermute(to_other, "seq", other), lax.ppermute(to_twin, "seq", twin)


def order(items, *after):
    return lax.optimization_barrier((items, after))[0]


def per_device(
    lengths,
    tokens,
    ln1_gain,
    ln1_bias,
    w_qkv,
    w_out,
    out_bias,
    ln2_gain,
    ln2_bias,
    w_in,
    in_bias,
    w_back,
    back_bias,
    cotangent,
):
    devices = lax.axis_size("seq")
    device = lax.axis_index("seq")
    rows, width = tokens.shape
    total = rows * devices
    plan = Plan(rows)
    block = width // BLOCKS
    chunks = w_in.shape[1] // width
    small = (ln1_gain, ln1_bias, out_bias, ln2_gain, ln2_bias, back_bias, in_bias)
    direct = devices == BLOCKS
    ring = Ring(BLOCKS, (16, 2, 8, 4), (4, 16, 2, 8))
    sums_ring = Ring(BLOCKS, (16, 8, 4, 2), (2, 16, 8, 4))
    last = ring.stages - 1
    core = ring.stages
    if direct:
        info, inverse, sums_inverse, payload, to_twin, to_other = pack(
            (ring, sums_ring), plan, total, lengths, tokens, w_qkv, w_out, w_in, w_back, small
        )
        from_other, from_twin = exchange(to_twin, to_other)
        ready = prepare(plan, total, info, order(tokens, payload))
        (payload,) = join([payload], ring.step(0, [payload]))
        payload = order(payload, from_other, from_twin)
        rest = block * (2 * chunks + 1)
        a, b = payload[:, rest:], payload[:, :rest]
        a_came, b_came = ring.step(1, [a, b])
        (a,) = join([a], [a_came])
        (a_came,) = ring.step(2, [a])
        (a,) = join([a], [a_came])
        (b,) = join([b], [b_came])
        a = order(a, b, ready)
        (b_came,) = ring.step(2, [b])
        (a_came,) = ring.step(3, [a])
        one = [a, a_came] + ring.step(core, [a, a_came])
        (b,) = join([b], [b_came])
        b = order(b, a_came)
    else:
        padded = (lengths + 15) // 16 * 16
        ends = jnp.cumsum(padded, dtype=jnp.int32)
        info = jnp.concatenate([device[None].astype(jnp.int32), lengths, ends - padded, ends])
        inverse = sums_inverse = jnp.arange(BLOCKS, dtype=jnp.int32)
        from_other, from_twin = exchange(*edge_sums(plan, total, info, tokens))
        ready = prepare(plan, total, info, tokens)

        def whole(item):
            return lax.all_gather(item, "seq", axis=0, tiled=True)

        def split(item, parts):
            each = BLOCKS // parts
            return [item[k * each : (k + 1) * each] for k in range(parts)]

        line = jnp.concatenate([whole(item).reshape(BLOCKS, 1, -1) for item in small], axis=2)
        line = jnp.pad(line, ((0, 0), (0, LINE_ROWS - 1), (0, width - line.shape[2])))
        one = whole(w_qkv).reshape(BLOCKS, block, 3, width).transpose(0, 2, 1, 3)
        one = one.reshape(BLOCKS, 3 * block, width)
        one = split(jnp.concatenate([one, line], axis=1), PIECES)
        full_in = whole(w_in).reshape(BLOCKS, block, chunks, width)
        full_in = full_in.transpose(0, 2, 1, 3).reshape(BLOCKS, chunks * block, width)
        full_two = [
            whole(w_out).reshape(BLOCKS, block, width),
            full_in,
            whole(w_back).reshape(BLOCKS, chunks * block, width),
        ]
        two = split(jnp.concatenate(full_two, axis=1), PIECES)
    standard, spread, pool, allowed, allowed_back, counts, edge_allowed, edge_counts = ready
    queries, pairs, halo_queries, halo_pairs, weight, vectors, shift_in = project(
        plan, total, info, inverse, standard, pool, from_twin, from_other, one
    )
    if direct:
        (b_came,) = ring.step(last, [b])
        (b_twin,) = ring.step(core, [b])
        allowed = order(allowed, b)
    attended, mixed, scale = attend(
        plan, total, info, allowed, counts, queries, pairs, halo_pairs
    )
    if direct:
        b_came = order(b_came, attended)
        two = [b, b_came, b_twin] + ring.step(core, [b_came])
    result, resid, grad_normed, out_weight, own_two, low_two, high_two, sum_in = feed_forward(
        (inverse, sums_inverse), tokens, cotangent, attended, vectors, shift_in, two
    )
    if direct:
        high, low = sums_ring.step(core, [high_two, low_two])
    (
        grad_resid,
        grads_a,
        grads_b,
        to_twin,
        to_other,
        sums,
        own_out,
        low_out,
        high_out,
    ) = middle(
        plan,
        info,
        sums_inverse,
        cotangent,
        attended,
        mixed,
        scale,
        vectors,
        resid,
        grad_normed,
        out_weight,
    )
    from_other, from_twin = exchange(to_twin, to_other)

    def with_out(item, out):
        return jnp.concatenate([item, out], axis=1)

    if direct:
        high_out, low_out = sums_ring.step(core, [high_out, low_out])
        kept, sent = sums_ring.fold(
            last, with_out(own_two, own_out), with_out(low, low_out), with_out(high, high_out)
        )
        sent_low, sent_high = halves(sent)
        sent_low, sent_high = order((sent_low, sent_high), from_twin)
        high, low = sums_ring.step(last, [sent_high, sent_low])
        grads_a = order(grads_a, sent_high, sent_low)
    grad_queries, grad_pairs = attend_back(
        plan, total, allowed_back, counts, queries, pairs, halo_pairs, (grads_a, grads_b)
    )
    from_other, from_twin = order((from_other, from_twin), grad_queries)
    if direct:
        high = order(high, grad_queries, from_other, from_twin)
        kept, kept_high = halves(kept)
        sent = (kept_high + high.astype(f32)).astype(bf16)
        (came,) = sums_ring.step(last - 1, [sent])
        from_other, from_twin = order((from_other, from_twin), sent)
    edges = edge_back(
        plan, info, edge_allowed, edge_counts, halo_queries, pairs, from_twin, from_other
    )
    grad_tokens, own_one, low_one, high_one = finish(
        plan,
        total,
        info,
        sums_inverse,
        standard,
        spread,
        weight,
        vectors,
        grad_resid,
        sums,
        sum_in,
        *grad_queries,
        *grad_pairs,
        *edges,
    )
    if direct:
        high_one, low_one = sums_ring.step(core, [high_one, low_one])
        low, came = order((low, came), grad_tokens)
        kept = kept + low.astype(f32)
        kept, sent = sums_ring.fold(last - 2, kept, *halves(came))
        (came,) = sums_ring.step(last - 2, [sent])
        high_one, low_one = order((high_one, low_one), sent)
        own_one, sent_one = sums_ring.fold(last, own_one, low_one, high_one)
        (came_one,) = sums_ring.step(last, [sent_one])
        own_one, sent_one = sums_ring.fold(last - 1, own_one, *halves(came_one))
        (came_one,) = sums_ring.step(last - 1, [sent_one])
        came = order(came, sent_one)
        kept, sent = sums_ring.fold(0, kept, *halves(came))
        (came,) = sums_ring.step(0, [sent])
        came_one = order(came_one, sent)
        own_one, sent_one = sums_ring.fold(last - 2, own_one, *halves(came_one))
        (came_one,) = sums_ring.step(last - 2, [sent_one])
        own_one, sent_one = sums_ring.fold(0, own_one, *halves(came_one))
        (came_one,) = sums_ring.step(0, [sent_one])
        grads = unpack(own_one, came_one, kept, came, (w_qkv, w_out, w_in, w_back) + small)
        grad_w_qkv, grad_w_out, grad_w_in, grad_w_back = grads[:4]
        parts = grads[4:]
    else:

        def shared(item):
            return lax.psum_scatter(item, "seq", scatter_dimension=0, tiled=True)

        full = jnp.concatenate([x.astype(f32) for x in (own_one, low_one, high_one)])
        line = full[:, 3 * block]
        sizes = [block] * 6 + [chunks * block]
        starts = [k * block for k in range(7)]
        parts = [
            shared(line[:, at : at + size].reshape(-1)) for at, size in zip(starts, sizes)
        ]
        grad_w_qkv = full[:, : 3 * block].reshape(BLOCKS, 3, block, width).transpose(0, 2, 1, 3)
        grad_w_qkv = shared(grad_w_qkv.reshape(width, 3 * width))
        full = jnp.concatenate([x.astype(f32) for x in (own_out, low_out, high_out)])
        grad_w_out = shared(full.reshape(width, width))
        full = jnp.concatenate([x.astype(f32) for x in (own_two, low_two, high_two)])
        full_in = full[:, : block * chunks]
        full_in = full_in.reshape(BLOCKS, chunks, block, width).transpose(0, 2, 1, 3)
        grad_w_in = shared(full_in.reshape(width, chunks * width))
        grad_w_back = shared(full[:, block * chunks :].reshape(chunks * width, width))
    gain_one, bias_one, shift_out, gain_two, bias_two, shift_back, shift_hidden = parts
    return (
        result,
        grad_tokens,
        gain_one,
        bias_one,
        grad_w_qkv,
        grad_w_out,
        shift_out,
        gain_two,
        bias_two,
        grad_w_in,
        shift_hidden,
        grad_w_back,
        shift_back,
    )


def solution(mesh):
    flat, wide = P("seq"), P("seq", None)
    weights = (flat, flat, wide, wide, flat, flat, flat, wide, flat, wide, flat)
    return jax.shard_map(
        per_device,
        mesh=mesh,
        in_specs=(P(), wide) + weights + (wide,),
        out_specs=(wide, wide) + weights,
        check_vma=False,
    )
```

```python
import functools
import math

import jax
import jax.numpy as jnp
from jax import lax
from jax.experimental import pallas as pl
from jax.experimental.pallas import tpu as pltpu
from jax.sharding import PartitionSpec as P

HEAD_DIM = 64
LEVELS = 5
HALO = 32
BLOCK = 64
WINDOW = BLOCK + 2 * HALO
QUAD = 4
QUAD_WIDTH = QUAD * HEAD_DIM
PIECES = 4
BLOCKS = 32
LINE = 128
LINE_ROWS = 8
MIXED = 16
FAR = 1 << 26
SEQ_STEP = 1 << 21
MIB = 1024 * 1024

f32 = jnp.float32
bf16 = jnp.bfloat16


class Plan:
    def locate(self, block):
        firsts = [at // BLOCK for at in self.query_at]
        level = sum((block >= first).astype(jnp.int32) for first in firsts[1:])
        start = sum(
            jnp.where(level == k, first, 0) for k, first in enumerate(firsts)
        )
        return level, block - start

    def __init__(self, rows):
        self.rows = rows
        self.counts = [rows >> level for level in range(LEVELS)]
        self.padded = [-(-count // BLOCK) * BLOCK for count in self.counts]
        self.query_at = [sum(self.padded[:level]) for level in range(LEVELS)]
        self.query_rows = sum(self.padded)
        self.key_at = [self.query_at[level] + 2 * HALO * level for level in range(LEVELS)]
        self.key_rows = self.query_rows + 2 * HALO * LEVELS
        self.blocks = [
            (level, part)
            for level in range(LEVELS)
            for part in range(self.padded[level] // BLOCK)
        ]


def dot_nn(a, b):
    return lax.dot_general(a, b, (((1,), (0,)), ((), ())), preferred_element_type=f32)


def dot_nt(a, b):
    return lax.dot_general(a, b, (((1,), (1,)), ((), ())), preferred_element_type=f32)


def dot_tn(a, b):
    return lax.dot_general(a, b, (((0,), (0,)), ((), ())), preferred_element_type=f32)


def spec(count):
    return [pl.BlockSpec(memory_space=pltpu.VMEM)] * count


SCALARS = pl.BlockSpec(memory_space=pltpu.SMEM)


def slot_facts(info, slot, total):
    number = jnp.zeros(slot.shape, jnp.int32)
    for s in range(3):
        number = number + (slot >= info[7 + s]).astype(jnp.int32)
    begin = jnp.where(number == 0, info[4], jnp.where(number == 1, info[5], info[6]))
    length = jnp.where(number == 0, info[1], jnp.where(number == 1, info[2], info[3]))
    inside = (slot >= 0) & (slot < total) & (number < 3)
    return number, slot - begin, length, inside


def tile_codes(info, coarse, level, total, outside):
    number, offset, _, inside = slot_facts(info, coarse << level, total)
    wide = jnp.where(inside, number * SEQ_STEP + (offset >> (level + 4)), outside)
    fine = number * SEQ_STEP + (offset >> (level + 3))
    return wide, fine


def admitted(query_codes, key_codes, level):
    near = jnp.abs(query_codes[0] - key_codes[0]) <= 1
    least = jnp.where(level > 0, 2, 0)
    near = near & (jnp.abs(query_codes[1] - key_codes[1]) >= least)
    return jnp.where(near, 1.0, 0.0)


def live_counts(info, coarse, level, total):
    _, offset, length, inside = slot_facts(info, coarse << level, total)
    span = 1 << level
    return jnp.where(inside, jnp.clip(length - offset, 0, span), 0).astype(f32)


def head_masks(rows):
    lane = lax.broadcasted_iota(jnp.int32, (rows, QUAD_WIDTH), 1) // HEAD_DIM
    return [jnp.where(lane == h, 1.0, 0.0).astype(bf16) for h in range(QUAD)]


def spread_heads(block, masks):
    return jnp.concatenate([block * m for m in masks], axis=0)


def join_pair(stacked, first):
    rows = stacked.shape[0] // 2
    return jnp.where(first, stacked[:rows], stacked[rows:])


def is_even(info):
    return (info[0] & 1) == 0


def params(size):
    return pltpu.CompilerParams(vmem_limit_bytes=size * MIB)


def cost(micros):
    return pl.CostEstimate(flops=1, bytes_accessed=1, transcendentals=0)


def fill_extended(plan, own, halos, extended):
    for level in range(LEVELS):
        at, count, mine = plan.key_at[level], plan.counts[level], plan.query_at[level]
        extended[pl.ds(at, HALO), :] = halos[pl.ds(HALO * level, HALO), :]
        extended[pl.ds(at + HALO, count), :] = own[pl.ds(mine, count), :]
        extended[pl.ds(at + HALO + count, HALO), :] = halos[pl.ds(HALO * (LEVELS + level), HALO), :]
        rest = plan.padded[level] - count
        if rest:
            extended[pl.ds(at + 2 * HALO + count, rest), :] = jnp.zeros(
                (rest, extended.shape[1]), bf16
            )


def place_halos(info, from_twin, from_other, halos):
    even = is_even(info)
    size = halos.shape[0] // 2
    halos[pl.ds(pl.multiple_of(jnp.where(even, size, 0), size), size), :] = from_twin[...]
    halos[pl.ds(pl.multiple_of(jnp.where(even, 0, size), size), size), :] = from_other[...]


def hand_out(info, ends, to_twin, to_other):
    even = is_even(info)
    size = LEVELS * HALO
    to_twin[...] = ends[pl.ds(pl.multiple_of(jnp.where(even, size, 0), size), size), :]
    to_other[...] = ends[pl.ds(pl.multiple_of(jnp.where(even, 0, size), size), size), :]


def ln_stats(values):
    center = values - jnp.mean(values, axis=-1, keepdims=True)
    spread = jnp.mean(center * center, axis=-1, keepdims=True)
    return center, lax.rsqrt(spread + 1e-05)


def ln_back(grad, hat, rstd, gain):
    scaled = grad * gain
    mean_one = jnp.mean(scaled, axis=-1, keepdims=True)
    mean_two = jnp.mean(scaled * hat, axis=-1, keepdims=True)
    return rstd * (scaled - mean_one - hat * mean_two), grad * hat


def column_sum(values):
    return jnp.sum(values, axis=0, keepdims=True)


def unpack_vector(table, first, each):
    blocks, lanes = table.shape
    length = blocks * each
    source = lax.broadcasted_iota(jnp.int32, (lanes, length), 0)
    target = lax.broadcasted_iota(jnp.int32, (lanes, length), 1)
    pick = jnp.where(source == first + (target & (each - 1)), 1.0, 0.0).astype(bf16)
    spreaded = dot_nn(table, pick)
    block = lax.broadcasted_iota(jnp.int32, (blocks, length), 0)
    lane = lax.broadcasted_iota(jnp.int32, (blocks, length), 1)
    return column_sum(jnp.where(lane // each == block, spreaded, 0.0))


def pack_vectors(vectors, last, blocks, lanes):
    size = last.shape[1] // blocks // 4

    def one(row, first, each):
        length = blocks * each
        source = lax.broadcasted_iota(jnp.int32, (length, lanes), 0)
        target = lax.broadcasted_iota(jnp.int32, (length, lanes), 1)
        pick = jnp.where(target == first + (source & (each - 1)), 1.0, 0.0).astype(bf16)
        block = lax.broadcasted_iota(jnp.int32, (blocks, length), 0)
        lane = lax.broadcasted_iota(jnp.int32, (blocks, length), 1)
        return dot_nn(jnp.where(lane // each == block, row, 0.0).astype(bf16), pick)

    total = one(last, 6 * size, 4 * size)
    for k, vector in enumerate(vectors):
        total = total + one(vector, k * size, size)
    return total


def edge_sums_kernel(plan, total, info, tokens, to_twin, to_other, ends):
    rows, width = tokens.shape
    center, rstd = ln_stats(tokens[...].astype(f32))
    plain = (center * rstd).astype(bf16)
    places = info[0] * rows + lax.broadcasted_iota(jnp.int32, (rows, width), 0)
    living = (plain.astype(f32) * live_counts(info, places, 0, total)).astype(bf16)
    size = 2 * LEVELS * HALO
    row = lax.broadcasted_iota(jnp.int32, (size, rows), 0)
    slot = lax.broadcasted_iota(jnp.int32, (size, rows), 1)
    row_one = lax.broadcasted_iota(jnp.int32, (size, 1), 0)
    wanted = jnp.zeros((size, rows), jnp.int32)
    shift = jnp.zeros((size, rows), jnp.int32)
    share = jnp.zeros((size, 1), f32)
    for k in range(2 * LEVELS):
        level, at = k % LEVELS, k * HALO
        first = 0 if k < LEVELS else plan.counts[level] - HALO
        wanted = jnp.where(row >= at, row - at + first, wanted)
        shift = jnp.where(row >= at, level, shift)
        share = jnp.where(row_one >= at, 0.5**level, share)
    pool = jnp.where((slot >> shift) == wanted, 1.0, 0.0).astype(bf16)
    ends[...] = (dot_nn(pool, plain) * share).astype(bf16)
    row = lax.broadcasted_iota(jnp.int32, (MIXED, rows), 0)
    slot = info[0] * rows + lax.broadcasted_iota(jnp.int32, (MIXED, rows), 1)
    wanted = jnp.full((MIXED, rows), -1, jnp.int32)
    shift = jnp.zeros((MIXED, rows), jnp.int32)
    for level in range(1, LEVELS):
        for k in range(3):
            here = row == (level - 1) * 3 + k
            wanted = jnp.where(here, (info[4 + k] + info[1 + k]) >> level, wanted)
            shift = jnp.where(here, level, shift)
    pick = jnp.where((slot >> shift) == wanted, 1.0, 0.0).astype(bf16)
    mixed = dot_nn(pick, living).astype(bf16)
    even = is_even(info)
    size = LEVELS * HALO
    for target, first in ((to_twin, size), (to_other, 0)):
        at = pl.multiple_of(jnp.where(even, first, size - first), size)
        target[pl.ds(0, size), :] = ends[pl.ds(at, size), :]
        target[pl.ds(size, MIXED), :] = mixed


def edge_sums(plan, total, info, tokens):
    width = tokens.shape[1]
    size = LEVELS * HALO
    return pl.pallas_call(
        functools.partial(edge_sums_kernel, plan, total),
        out_shape=[jax.ShapeDtypeStruct((size + MIXED, width), bf16)] * 2,
        in_specs=[SCALARS] + spec(1),
        out_specs=spec(2),
        scratch_shapes=[pltpu.VMEM((2 * size, width), bf16)],
        compiler_params=params(10),
        name="edge_sums",
        cost_estimate=cost(1.5),
    )(info, tokens)


def prepare_kernel(
    plan,
    total,
    info,
    tokens,
    standard,
    spread,
    pool,
    allowed,
    allowed_back,
    counts,
    edge_allowed,
    edge_counts,
):
    rows = plan.rows
    device = info[0]
    center, rstd = ln_stats(tokens[...].astype(f32))
    standard[...] = center * rstd
    spread[...] = jnp.broadcast_to(rstd, spread.shape)
    pooled_rows = pool.shape[0]
    row = lax.broadcasted_iota(jnp.int32, (pooled_rows, rows), 0)
    slot = lax.broadcasted_iota(jnp.int32, (pooled_rows, rows), 1)
    first = jnp.zeros((pooled_rows, rows), jnp.int32)
    shift = jnp.zeros((pooled_rows, rows), jnp.int32)
    for level in range(1, LEVELS):
        at = plan.query_at[level] - plan.query_at[1]
        first = jnp.where(row >= at, at, first)
        shift = jnp.where(row >= at, level, shift)
    pool[...] = jnp.where((slot >> shift) == row - first, 1.0, 0.0).astype(bf16)

    def block_step(block, carry):
        level, part = plan.locate(block)
        first = device * (rows >> level) + BLOCK * part
        here = pl.ds(pl.multiple_of(BLOCK * block, BLOCK), BLOCK)
        there = pl.ds(pl.multiple_of(WINDOW * block, WINDOW), WINDOW)
        row = first + lax.broadcasted_iota(jnp.int32, (BLOCK, WINDOW), 0)
        column = first - HALO + lax.broadcasted_iota(jnp.int32, (BLOCK, WINDOW), 1)
        allowed[here, :] = admitted(
            tile_codes(info, row, level, total, FAR),
            tile_codes(info, column, level, total, -FAR),
            level,
        )
        key_row = first - HALO + lax.broadcasted_iota(jnp.int32, (WINDOW, 128), 0)
        lane = lax.broadcasted_iota(jnp.int32, (WINDOW, 128), 1)
        row = first + (lane & (BLOCK - 1))
        allowed_back[there, :] = admitted(
            tile_codes(info, row, level, total, FAR),
            tile_codes(info, key_row, level, total, -FAR),
            level,
        )
        counts[there, :] = live_counts(info, key_row, level, total).astype(bf16)
        return carry

    lax.fori_loop(0, len(plan.blocks), block_step, 0, unroll=2)
    two = 2 * HALO
    key = lax.broadcasted_iota(jnp.int32, (two, 128), 0)
    lane = lax.broadcasted_iota(jnp.int32, (two, 128), 1) & (two - 1)
    facing = jnp.where((key < HALO) == (lane < HALO), 1.0, 0.0)
    for level in range(LEVELS):
        count = plan.counts[level]
        start = device * count
        key_row = start + jnp.where(key < HALO, key, count - two + key)
        row = start + jnp.where(lane < HALO, lane - HALO, count - HALO + lane)
        here = pl.ds(two * level, two)
        edge_allowed[here, :] = facing * admitted(
            tile_codes(info, row, level, total, FAR),
            tile_codes(info, key_row, level, total, -FAR),
            level,
        )
        edge_counts[here, :] = live_counts(info, key_row, level, total).astype(bf16)


def prepare(plan, total, info, tokens):
    rows, width = tokens.shape
    blocks = len(plan.blocks)
    return pl.pallas_call(
        functools.partial(prepare_kernel, plan, total),
        out_shape=(
            jax.ShapeDtypeStruct((rows, width), f32),
            jax.ShapeDtypeStruct((rows, 128), f32),
            jax.ShapeDtypeStruct((plan.query_rows - plan.query_at[1], rows), bf16),
            jax.ShapeDtypeStruct((BLOCK * blocks, WINDOW), f32),
            jax.ShapeDtypeStruct((WINDOW * blocks, 128), f32),
            jax.ShapeDtypeStruct((WINDOW * blocks, 128), bf16),
            jax.ShapeDtypeStruct((2 * HALO * LEVELS, 128), f32),
            jax.ShapeDtypeStruct((2 * HALO * LEVELS, 128), bf16),
        ),
        in_specs=[SCALARS] + spec(1),
        out_specs=tuple(spec(8)),
        compiler_params=params(8),
        name="prepare",
        cost_estimate=cost(4),
    )(info, tokens)


def project_kernel(
    plan, total, info, inverse, standard, pool, from_twin, from_other, *refs
):
    pieces, outs = refs[:PIECES], refs[PIECES:]
    queries, pairs, halo_queries, halo_pairs = (outs[2 * k : 2 * k + 2] for k in range(4))
    weight, vectors, shift_out, table, edges, halos, mixed = outs[8:]
    rows, width = standard.shape
    device = info[0]
    each = pieces[0].shape[0]
    block_rows = pieces[0].shape[1] // 3 // 16 * 16
    for p in range(PIECES * each):
        i = inverse[p]
        there = pl.ds(pl.multiple_of(i * block_rows, block_rows), block_rows)
        piece, q = pieces[p // each], p % each
        for c in range(3):
            weight[there, pl.ds(c * width, width)] = piece[q, pl.ds(block_rows * c, block_rows), :]
        line = piece[q, pl.ds(block_rows * 3, LINE_ROWS), pl.ds(0, 2 * LINE)].astype(f32)
        table[pl.ds(i, 1), :] = line[0:1]
    packed = table[...].astype(bf16)
    singles = [unpack_vector(packed, k * block_rows, block_rows) for k in range(2)]
    low = (standard[...] * singles[0] + singles[1]).astype(bf16)
    pooled_rows = pool.shape[0]
    share = jnp.zeros((pooled_rows, 1), f32)
    row_one = lax.broadcasted_iota(jnp.int32, (pooled_rows, 1), 0)
    for level in range(1, LEVELS):
        at = plan.query_at[level] - plan.query_at[1]
        share = jnp.where(row_one >= at, 0.5**level, share)
    places = device * rows + lax.broadcasted_iota(jnp.int32, (rows, QUAD_WIDTH), 0)
    live = live_counts(info, places, 0, total)
    place_halos(info, from_twin, from_other, edges)
    size = LEVELS * HALO
    for k in range(2):
        rest = pl.ds(k * (size + MIXED) + size, MIXED)
        mixed[pl.ds(k * MIXED, MIXED), :] = edges[rest, :].astype(f32)
    for k in range(2 * LEVELS):
        level, here = k % LEVELS, pl.ds(k * HALO, HALO)
        side, span = k // LEVELS * (size + MIXED), 1 << level
        mean = edges[pl.ds(side + level * HALO, HALO), :].astype(f32)
        halos[here, pl.ds(0, width)] = (mean * singles[0] + singles[1]).astype(bf16)
        count = plan.counts[level]
        first = device * count + (-HALO if k < LEVELS else count)
        place = first + lax.broadcasted_iota(jnp.int32, (HALO, 128), 0)
        counts = live_counts(info, place, level, total)
        wide = jnp.concatenate([counts] * (width // 128), axis=1)
        value = jnp.where(wide == span, mean * span, 0.0)
        if level:
            number = slot_facts(info, place << level, total)[0]
            for index in range(3):
                ends = (counts > 0.0) & (counts < span) & (number == index)
                ends = jnp.where(ends, 1.0, 0.0)
                ends = jnp.concatenate([ends] * (width // 128), axis=1)
                row = k // LEVELS * MIXED + (level - 1) * 3 + index
                value = value + ends * mixed[pl.ds(row, 1), :]
        halos[here, pl.ds(width, width)] = (value * singles[0] + wide * singles[1]).astype(bf16)
    lanes = QUAD_WIDTH
    scale = 1.0 / math.sqrt(HEAD_DIM)
    parts = [(divmod(part, 2), pl.ds(part * lanes, lanes)) for part in range(3 * width // lanes)]
    own = pl.ds(0, rows)
    above = pl.ds(rows, pooled_rows)
    blocks = [dot_nn(low, weight[:, columns]).astype(bf16) for _, columns in parts]
    for index, ((kind, quad), _) in enumerate(parts):
        if kind == 0:
            queries[quad][own, :] = (blocks[index].astype(f32) * scale).astype(bf16)
            continue
        if kind == 2:
            blocks[index] = (blocks[index].astype(f32) * live).astype(bf16)
        pairs[quad][own, pl.ds((kind - 1) * lanes, lanes)] = blocks[index]
    pooled = [dot_nn(pool[...], block) for block in blocks]
    for ((kind, quad), _), item in zip(parts, pooled):
        if kind == 0:
            queries[quad][above, :] = (item * (share * scale)).astype(bf16)
            continue
        if kind == 1:
            item = item * share
        pairs[quad][above, pl.ds((kind - 1) * lanes, lanes)] = item.astype(bf16)
    sides = [
        dot_nn(halos[:, pl.ds(width if kind == 2 else 0, width)], weight[:, columns])
        for (kind, _), columns in parts
    ]
    for ((kind, quad), _), item in zip(parts, sides):
        if kind == 0:
            halo_queries[quad][...] = (item * scale).astype(bf16)
        else:
            halo_pairs[quad][:, pl.ds((kind - 1) * lanes, lanes)] = item.astype(bf16)
    singles += [unpack_vector(packed, k * block_rows, block_rows) for k in range(2, 6)]
    for k, single in enumerate(singles):
        vectors[pl.ds(k, 1), :] = single
    shift_out[...] = unpack_vector(packed, 6 * block_rows, 4 * block_rows)


def project(plan, total, info, inverse, standard, pool, from_twin, from_other, pieces):
    rows, width = standard.shape
    halo = LEVELS * HALO
    blocks = PIECES * pieces[0].shape[0]
    depth = blocks * (pieces[0].shape[1] - LINE_ROWS) // 3
    half = width // 2
    outs = pl.pallas_call(
        functools.partial(project_kernel, plan, total),
        out_shape=(
            [jax.ShapeDtypeStruct((plan.query_rows, half), bf16)] * 2
            + [jax.ShapeDtypeStruct((plan.query_rows, 2 * half), bf16)] * 2
            + [jax.ShapeDtypeStruct((2 * halo, half), bf16)] * 2
            + [jax.ShapeDtypeStruct((2 * halo, 2 * half), bf16)] * 2
            + [
                jax.ShapeDtypeStruct((depth, 3 * width), bf16),
                jax.ShapeDtypeStruct((8, depth), f32),
                jax.ShapeDtypeStruct((1, 4 * depth), f32),
            ]
        ),
        in_specs=[SCALARS, SCALARS] + spec(4 + PIECES),
        out_specs=spec(11),
        scratch_shapes=[
            pltpu.VMEM((blocks, 2 * LINE), f32),
            pltpu.VMEM((2 * (halo + MIXED), width), bf16),
            pltpu.VMEM((2 * halo, 2 * width), bf16),
            pltpu.VMEM((2 * MIXED, width), f32),
        ],
        compiler_params=params(18),
        name="project",
        cost_estimate=cost(3.3),
    )(info, inverse, standard, pool, from_twin, from_other, *pieces)
    return [outs[2 * k : 2 * k + 2] for k in range(4)] + list(outs[8:])


def attend_kernel(plan, total, info, mask, counts_of, *refs):
    queries, pairs, halos, attended, mixed, scale, extended = (
        refs[2 * k : 2 * k + 2] for k in range(7)
    )
    numer, denom = refs[14:]
    rows = plan.rows
    device = info[0]
    for quad in range(2):
        fill_extended(plan, pairs[quad], halos[quad], extended[quad])
    first_head = lax.broadcasted_iota(jnp.int32, (BLOCK, 128), 1) < HEAD_DIM
    masks = head_masks(BLOCK)

    def prepare(block):
        level, part = plan.locate(block)
        here = pl.ds(pl.multiple_of(BLOCK * block, BLOCK), BLOCK)
        there = pl.ds(pl.multiple_of(BLOCK * block + 2 * HALO * level, BLOCK), WINDOW)
        allowed = mask[here, :]
        counts = counts_of[pl.ds(pl.multiple_of(WINDOW * block, WINDOW), WINDOW), :]
        return here, there, allowed, counts

    def block_step(step, carry):
        work = []
        for k in range(4):
            here, there, allowed, counts = prepare(step * 4 + k)
            allowed = jnp.concatenate([allowed] * 4, axis=0) > 0.0
            for part in range(8 // 4):
                work.append((here, there, allowed, counts, part))
        scores = []
        for here, there, allowed, counts, part in work:
            wide = 4 * HEAD_DIM
            quad, half = divmod(part * wide, QUAD_WIDTH)
            lanes = pl.ds(half, wide)
            q = spread_heads(queries[quad][here, lanes], masks)
            scores.append(dot_nt(q, extended[quad][there, lanes]))
        weights = [
            jnp.where(item[2], jnp.exp(score), 0.0).astype(bf16)
            for item, score in zip(work, scores)
        ]
        for (here, there, allowed, counts, part), weight in zip(work, weights):
            wide = 4 * HEAD_DIM
            for sub in range(4 // 2):
                pair = part * (4 // 2) + sub
                quad, half = divmod(pair, 2)
                v = extended[quad][there, pl.ds(QUAD_WIDTH + 128 * half, 128)]
                both = dot_nn(
                    weight[128 * sub : 128 * sub + 128], jnp.concatenate([v, counts], axis=1)
                )
                numer[pair, here, :] = join_pair(both[:, :128], first_head)
                denom[pair, here, :] = join_pair(both[:, 128:], first_head)
        return carry

    lax.fori_loop(0, len(plan.blocks) // 4, block_step, 0, unroll=1)
    places = device * rows + lax.broadcasted_iota(jnp.int32, (rows, 128), 0)
    live = live_counts(info, places, 0, total)
    for pair in range(4):
        for sums in (numer, denom):
            for level in range(LEVELS - 1, 0, -1):
                count = plan.counts[level]
                upper = sums[pair, pl.ds(plan.query_at[level], count), :]
                for parity in range(2):
                    there = pl.ds(plan.query_at[level - 1] + parity, count, stride=2)
                    sums[pair, there, :] = sums[pair, there, :] + upper
        quad, half = divmod(pair, 2)
        lanes = pl.ds(128 * half, 128)
        factor = live / (denom[pair, pl.ds(0, rows), :] + 1.0 - live)
        value = numer[pair, pl.ds(0, rows), :] * factor
        scale[quad][:, lanes] = factor
        mixed[quad][:, lanes] = value
        attended[quad][:, lanes] = value.astype(bf16)


def attend(plan, total, info, mask, counts, queries, pairs, halos):
    rows, width = plan.rows, queries[0].shape[1]
    outs = pl.pallas_call(
        functools.partial(attend_kernel, plan, total),
        out_shape=[jax.ShapeDtypeStruct((rows, width), bf16)] * 2
        + [jax.ShapeDtypeStruct((rows, width), f32)] * 4,
        in_specs=[SCALARS] + spec(8),
        out_specs=spec(6),
        scratch_shapes=[
            pltpu.VMEM((plan.key_rows, 2 * width), bf16),
            pltpu.VMEM((plan.key_rows, 2 * width), bf16),
            pltpu.VMEM((2 * width // 128, plan.query_rows, 128), f32),
            pltpu.VMEM((2 * width // 128, plan.query_rows, 128), f32),
        ],
        compiler_params=params(20),
        name="attend",
        cost_estimate=cost(8),
    )(info, mask, counts, *queries, *pairs, *halos)
    return outs[:2], outs[2:4], outs[4:]


def forward_kernel(
    parts,
    inverse,
    sums_inverse,
    tokens,
    cotangent,
    attended_a,
    attended_b,
    vectors,
    shift_in,
    *refs,
):
    pieces = refs[:parts]
    result, resid_out, grad_normed, w_out, own, low_half, high_half, sum_in = refs[
        parts : parts + 8
    ]
    w_in, w_back, normed_two, outer, tall, flat, turned, cot_turned = refs[parts + 8 :]
    other = (low_half, high_half)
    width = tokens.shape[1]
    wide = width // 2
    each = pieces[0].shape[0]
    half = own.shape[0]
    chunks = w_in.shape[0]
    block = width // (parts * each)
    tall_block = chunks * block
    back_at = block + tall_block
    for p in range(parts * each):
        piece, q = pieces[p // each], p % each
        i = inverse[p]
        rows = pl.ds(pl.multiple_of(i * block, block), block)
        w_out[rows, :] = piece[q, pl.ds(0, block), :]
        for c in range(chunks):
            w_in[c, rows, :] = piece[q, pl.ds(block * (c + 1), block), :]
        rows = pl.ds(pl.multiple_of(i * tall_block, tall_block), tall_block)
        w_back[rows, :] = piece[q, pl.ds(back_at, tall_block), :]
    gain = vectors[pl.ds(3, 1), :]
    resid = tokens[...].astype(f32) + dot_nn(attended_a[...], w_out[pl.ds(0, wide), :])
    resid = resid + dot_nn(attended_b[...], w_out[pl.ds(wide, wide), :]) + vectors[pl.ds(2, 1), :]
    center, rstd = ln_stats(resid)
    normed_two[...] = (center * rstd * gain + vectors[pl.ds(4, 1), :]).astype(bf16)
    turned[...] = normed_two[...].T
    resid_out[...] = resid
    outer[...] = jnp.zeros(outer.shape, f32)
    grad_normed[...] = jnp.zeros(grad_normed.shape, f32)

    def chunk_step(c, carry):
        there = pl.ds(pl.multiple_of(c * width, width), width)
        inner = dot_nn(normed_two[...], w_in[c]) + shift_in[:, there]
        cdf = 0.5 * (1.0 + lax.erf(inner * math.sqrt(0.5)))
        active = (inner * cdf).astype(bf16)
        slope = cdf + inner * (jnp.exp(-0.5 * inner * inner) * (1.0 / math.sqrt(2.0 * math.pi)))
        back = w_back[there, :]
        grad_inner = slope * dot_nt(cotangent[...], back)
        low = grad_inner.astype(bf16)
        outer[...] += dot_nn(active, back)
        tall[there, :] = dot_tn(active, cotangent[...]).astype(bf16)
        sum_in[:, there] = column_sum(low.astype(f32))
        flat[...] = dot_nn(turned[...], low).astype(bf16)
        for p in range(2 * half):
            i = sums_inverse[p]
            rows = flat[pl.ds(pl.multiple_of(i * block, block), block), :]
            at = pl.ds(pl.multiple_of(c * block, block), block)
            if p < half:
                own[p, at, :] = rows
            else:
                other[(p - half) // 8][(p - half) % 8, at, :] = rows
        grad_normed[...] += dot_nt(low, w_in[c])
        return carry

    lax.fori_loop(0, chunks, chunk_step, 0, unroll=4)
    result[...] = (resid_out[...] + outer[...] + vectors[pl.ds(5, 1), :]).astype(bf16)
    for p in range(2 * half):
        i = sums_inverse[p]
        rows = tall[pl.ds(pl.multiple_of(i * tall_block, tall_block), tall_block), :]
        there = pl.ds(tall_block, tall_block)
        if p < half:
            own[p, there, :] = rows
        else:
            other[(p - half) // 8][(p - half) % 8, there, :] = rows


def feed_forward(inverses, tokens, cotangent, attended, vectors, shift_in, pieces):
    parts = len(pieces)
    rows, width = tokens.shape
    hidden = shift_in.shape[1]
    chunks = hidden // width
    blocks = parts * pieces[0].shape[0]
    stack = pieces[0].shape[1] - width // blocks
    return pl.pallas_call(
        functools.partial(forward_kernel, parts),
        out_shape=(
            jax.ShapeDtypeStruct((rows, width), bf16),
            jax.ShapeDtypeStruct((rows, width), f32),
            jax.ShapeDtypeStruct((rows, width), f32),
            jax.ShapeDtypeStruct((width, width), bf16),
            jax.ShapeDtypeStruct((blocks // 2, stack, width), bf16),
            jax.ShapeDtypeStruct((blocks // 4, stack, width), bf16),
            jax.ShapeDtypeStruct((blocks // 4, stack, width), bf16),
            jax.ShapeDtypeStruct((1, hidden), f32),
        ),
        in_specs=[SCALARS] * 2 + spec(6 + parts),
        out_specs=tuple(spec(8)),
        scratch_shapes=[
            pltpu.VMEM((chunks, width, width), bf16),
            pltpu.VMEM((hidden, width), bf16),
            pltpu.VMEM((rows, width), bf16),
            pltpu.VMEM((rows, width), f32),
            pltpu.VMEM((hidden, width), bf16),
            pltpu.VMEM((width, width), bf16),
            pltpu.VMEM((width, rows), bf16),
            pltpu.VMEM((width, rows), bf16),
        ],
        compiler_params=params(30),
        name="feed_forward",
        cost_estimate=cost(10),
    )(*inverses, tokens, cotangent, *attended, vectors, shift_in, *pieces)


def middle_kernel(
    plan,
    info,
    sums_inverse,
    cotangent,
    attended_a,
    attended_b,
    mixed_a,
    mixed_b,
    scale_a,
    scale_b,
    vectors,
    resid,
    grad_normed,
    w_out,
    grad_resid,
    grads_a,
    grads_b,
    to_twin,
    to_other,
    sums,
    own,
    low_half,
    high_half,
    levels,
    ends,
    denoms,
    flat,
):
    width = cotangent.shape[1]
    wide = width // 2
    center, rstd = ln_stats(resid[...])
    grad_in, gain_terms = ln_back(grad_normed[...], center * rstd, rstd, vectors[pl.ds(3, 1), :])
    grad_out = cotangent[...].astype(f32)
    total = grad_out + grad_in
    grad_resid[...] = total
    low = total.astype(bf16)
    sums[pl.ds(0, 1), :] = jnp.zeros((1, width), f32)
    sums[pl.ds(1, 1), :] = jnp.zeros((1, width), f32)
    sums[pl.ds(2, 1), :] = column_sum(low.astype(f32))
    sums[pl.ds(3, 1), :] = column_sum(gain_terms)
    sums[pl.ds(4, 1), :] = column_sum(grad_normed[...])
    sums[pl.ds(5, 1), :] = column_sum(grad_out)
    mixed_grads = [dot_nt(low, w_out[pl.ds(quad * wide, wide), :]) for quad in range(2)]
    for quad in range(2):
        lines = pl.ds(quad * wide, wide)
        flat[lines, :] = dot_tn((attended_a, attended_b)[quad][...], low).astype(bf16)
    for quad in range(2):
        numer = mixed_grads[quad] * (scale_a, scale_b)[quad][...]
        denom = -(numer * (mixed_a, mixed_b)[quad][...])
        for chunk in range(2 * wide // 128):
            source = numer if chunk < wide // 128 else denom
            lane = chunk * 128 % wide
            levels[quad * 4 + chunk, pl.ds(0, plan.rows), :] = source[:, lane : lane + 128]
            for level in range(1, LEVELS):
                count, at = plan.counts[level], plan.query_at[level]
                below = plan.query_at[level - 1]
                levels[quad * 4 + chunk, pl.ds(at, count), :] = (
                    levels[quad * 4 + chunk, pl.ds(below, count, stride=2), :]
                    + levels[quad * 4 + chunk, pl.ds(below + 1, count, stride=2), :]
                )
                rest = plan.padded[level] - count
                if rest:
                    levels[quad * 4 + chunk, pl.ds(at + count, rest), :] = jnp.zeros((rest, 128), f32)
            grads = (grads_a, grads_b)[quad]
            grads[:, pl.ds(chunk * 128, 128)] = levels[quad * 4 + chunk].astype(bf16)
        for k in range(2 * LEVELS):
            level, here = k % LEVELS, pl.ds(k * HALO, HALO)
            at = plan.query_at[level] + (0 if k < LEVELS else plan.counts[level] - HALO)
            there = pl.ds(at, HALO)
            ends[here, pl.ds(quad * wide, wide)] = (grads_a, grads_b)[quad][there, pl.ds(0, wide)]
            for chunk in range(wide // 128):
                lanes = pl.ds(quad * wide + chunk * 128, 128)
                denoms[here, lanes] = levels[quad * 4 + wide // 128 + chunk, there, :]
    feature = lax.broadcasted_iota(jnp.int32, (width, LINE), 0)
    lane = lax.broadcasted_iota(jnp.int32, (width, LINE), 1)
    pick = jnp.where(lane == feature // HEAD_DIM, 1.0, 0.0).astype(bf16)
    heads = width // HEAD_DIM
    values = denoms[...]
    first = values.astype(bf16)
    values = dot_nn(first, pick) + dot_nn((values - first.astype(f32)).astype(bf16), pick)
    first = values.astype(bf16).astype(f32)
    both = jnp.concatenate([first[:, :heads], (values - first)[:, :heads]], axis=1)
    both = jnp.concatenate([both, jnp.zeros((both.shape[0], LINE - 2 * heads), f32)], axis=1)
    ends[:, pl.ds(width, LINE)] = both.astype(bf16)
    hand_out(info, ends, to_twin, to_other)
    half, block = own.shape[0], own.shape[1]
    other = (low_half, high_half)
    for p in range(2 * half):
        rows = flat[pl.ds(pl.multiple_of(sums_inverse[p] * block, block), block), :]
        if p < half:
            own[p] = rows
        else:
            other[(p - half) // 8][(p - half) % 8] = rows


def middle(plan, info, sums_inverse, cotangent, attended, mixed, scale, vectors, resid, grad_normed, w_out):
    rows, width = cotangent.shape
    size = LEVELS * HALO
    return pl.pallas_call(
        functools.partial(middle_kernel, plan),
        out_shape=(
            jax.ShapeDtypeStruct((rows, width), f32),
            jax.ShapeDtypeStruct((plan.query_rows, width), bf16),
            jax.ShapeDtypeStruct((plan.query_rows, width), bf16),
            jax.ShapeDtypeStruct((size, width + LINE), bf16),
            jax.ShapeDtypeStruct((size, width + LINE), bf16),
            jax.ShapeDtypeStruct((8, width), f32),
            jax.ShapeDtypeStruct((BLOCKS // 2, width // BLOCKS, width), bf16),
            jax.ShapeDtypeStruct((BLOCKS // 4, width // BLOCKS, width), bf16),
            jax.ShapeDtypeStruct((BLOCKS // 4, width // BLOCKS, width), bf16),
        ),
        in_specs=[SCALARS] * 2 + spec(11),
        out_specs=tuple(spec(9)),
        scratch_shapes=[
            pltpu.VMEM((2 * width // 128, plan.query_rows, 128), f32),
            pltpu.VMEM((2 * size, width + LINE), bf16),
            pltpu.VMEM((2 * size, width), f32),
            pltpu.VMEM((width, width), bf16),
        ],
        compiler_params=params(20),
        name="middle",
        cost_estimate=cost(3),
    )(info, sums_inverse, cotangent, *attended, *mixed, *scale, vectors, resid, grad_normed, w_out)


def attend_back_kernel(plan, total, mask, counts_of, *refs):
    queries, pairs, halos, grads, grad_queries, grad_extended, extended = (
        refs[2 * k : 2 * k + 2] for k in range(7)
    )
    width = QUAD_WIDTH
    for quad in range(2):
        fill_extended(plan, pairs[quad], halos[quad], extended[quad])
        grad_extended[quad][...] = jnp.zeros(grad_extended[quad].shape, f32)
    masks = head_masks(BLOCK)
    first_head = lax.broadcasted_iota(jnp.int32, (BLOCK, 128), 1) < HEAD_DIM
    keys = pl.ds(0, width)
    values = pl.ds(width, width)

    def prepare(block):
        level, part = plan.locate(block)
        here = pl.ds(pl.multiple_of(BLOCK * block, BLOCK), BLOCK)
        there = pl.ds(pl.multiple_of(BLOCK * block + 2 * HALO * level, BLOCK), WINDOW)
        window = pl.ds(pl.multiple_of(WINDOW * block, WINDOW), WINDOW)
        allowed = jnp.concatenate([mask[window, :]] * (QUAD * BLOCK // 128), axis=1) > 0.0
        counts = counts_of[window, :]
        return here, there, allowed, counts

    def block_step(step, carry):
        work = []
        for k in range(8):
            here, there, allowed, counts = prepare(step * 8 + k)
            for quad in range(2):
                q = spread_heads(queries[quad][here, :], masks)
                g = spread_heads(grads[quad][here, keys], masks)
                d = spread_heads(grads[quad][here, values], masks)
                work.append((quad, here, there, allowed, counts, q, g, d))
        scores, grad_probs = [], []
        for quad, here, there, allowed, counts, q, g, d in work:
            scores.append(dot_nt(extended[quad][there, keys], q))
            v = extended[quad][there, values]
            value_and_count = jnp.concatenate([v] + [counts] * (width // 128), axis=1)
            grad_probs.append(dot_nt(value_and_count, jnp.concatenate([g, d], axis=1)))
        weights = [
            jnp.where(item[3], jnp.exp(score), 0.0) for item, score in zip(work, scores)
        ]
        grad_scores = [(x * y).astype(bf16) for x, y in zip(grad_probs, weights)]
        probs = [weight.astype(bf16) for weight in weights]
        keys_of = [extended[item[0]][item[2], keys] for item in work]
        to_queries = [
            [
                dot_tn(grad_score[:, 128 * half : 128 * half + 128], k[:, 128 * half : 128 * half + 128])
                for half in range(2)
            ]
            for grad_score, k in zip(grad_scores, keys_of)
        ]
        to_keys = [dot_nn(grad_score, item[5]) for grad_score, item in zip(grad_scores, work)]
        to_values = [dot_nn(prob, item[6]) for prob, item in zip(probs, work)]
        for item, parts, to_key, to_value in zip(work, to_queries, to_keys, to_values):
            quad, here, there = item[:3]
            for half in range(2):
                grad_queries[quad][here, pl.ds(128 * half, 128)] = join_pair(
                    parts[half], first_head
                ) * (1.0 / math.sqrt(HEAD_DIM))
            grad_extended[quad][there, keys] += to_key
            grad_extended[quad][there, values] += to_value
        return carry

    lax.fori_loop(0, len(plan.blocks) // 8, block_step, 0, unroll=1)


def attend_back(plan, total, mask, counts, queries, pairs, halos, grads):
    width = queries[0].shape[1]
    outs = pl.pallas_call(
        functools.partial(attend_back_kernel, plan, total),
        out_shape=[jax.ShapeDtypeStruct((plan.query_rows, width), f32)] * 2
        + [jax.ShapeDtypeStruct((plan.key_rows, 2 * width), f32)] * 2,
        in_specs=spec(10),
        out_specs=spec(4),
        scratch_shapes=[
            pltpu.VMEM((plan.key_rows, 2 * width), bf16),
            pltpu.VMEM((plan.key_rows, 2 * width), bf16),
        ],
        compiler_params=params(24),
        name="attend_back",
        cost_estimate=cost(12),
    )(mask, counts, *queries, *pairs, *halos, *grads)
    return outs[:2], outs[2:]


def edge_back_kernel(
    plan,
    info,
    mask,
    counts_of,
    queries_a,
    queries_b,
    pairs_a,
    pairs_b,
    from_twin,
    from_other,
    low,
    high,
    grads,
):
    width = queries_a.shape[1]
    place_halos(info, from_twin, from_other, grads)
    two = 2 * HALO
    masks = head_masks(two)
    keys = pl.ds(0, width)
    heads = 2 * width // HEAD_DIM
    source = lax.broadcasted_iota(jnp.int32, (LINE, width), 0)
    target = lax.broadcasted_iota(jnp.int32, (LINE, width), 1)
    picks = []
    for quad in range(2):
        head = target // HEAD_DIM + quad * QUAD
        wanted = jnp.where(target % HEAD_DIM == 0, head, -1)
        wanted = jnp.where(target % HEAD_DIM == 1, head + heads, wanted)
        picks.append(jnp.where(source == wanted, 1.0, 0.0).astype(bf16))
    denoms = [dot_nn(grads[:, pl.ds(2 * width, LINE)], pick).astype(bf16) for pick in picks]
    work = []
    for level in range(LEVELS):
        count, at = plan.counts[level], plan.query_at[level]
        here = pl.ds(two * level, two)
        allowed = jnp.concatenate([mask[here, :]] * (QUAD * two // 128), axis=1) > 0.0
        counts = counts_of[here, :]
        ahead, behind = HALO * level, HALO * (LEVELS + level)

        def both(item, lanes):
            parts = [item[pl.ds(first, HALO), lanes] for first in (ahead, behind)]
            return jnp.concatenate(parts, axis=0)

        for quad in range(2):
            pairs = (pairs_a, pairs_b)[quad]
            own = jnp.concatenate(
                [pairs[pl.ds(at, HALO), :], pairs[pl.ds(at + count - HALO, HALO), :]], axis=0
            )
            k, v = own[:, :width], own[:, width:]
            d = denoms[quad]
            d = jnp.concatenate([d[ahead : ahead + HALO], d[behind : behind + HALO]], axis=0)
            q = spread_heads(both((queries_a, queries_b)[quad], keys), masks)
            g = spread_heads(both(grads, pl.ds(quad * width, width)), masks)
            d = spread_heads(d, masks)
            value_and_count = jnp.concatenate([v] + [counts] * (width // 128), axis=1)
            there = pl.ds(HALO * (quad * LEVELS + level), HALO)
            work.append((there, allowed, q, g, d, k, value_and_count))
    scores = [dot_nt(item[5], item[2]) for item in work]
    grad_probs = [
        dot_nt(item[6], jnp.concatenate([item[3], item[4]], axis=1)) for item in work
    ]
    weights = [jnp.where(item[1], jnp.exp(score), 0.0) for item, score in zip(work, scores)]
    grad_scores = [(x * y).astype(bf16) for x, y in zip(grad_probs, weights)]
    to_keys = [dot_nn(grad_score, item[2]) for grad_score, item in zip(grad_scores, work)]
    to_values = [dot_nn(weight.astype(bf16), item[3]) for weight, item in zip(weights, work)]
    for item, to_key, to_value in zip(work, to_keys, to_values):
        there = item[0]
        low[there, keys] = to_key[:HALO]
        high[there, keys] = to_key[HALO:]
        low[there, pl.ds(width, width)] = to_value[:HALO]
        high[there, pl.ds(width, width)] = to_value[HALO:]


def edge_back(plan, info, mask, counts, queries, pairs, from_twin, from_other):
    width = queries[0].shape[1]
    size = 2 * LEVELS * HALO
    return pl.pallas_call(
        functools.partial(edge_back_kernel, plan),
        out_shape=[jax.ShapeDtypeStruct((size, 2 * width), f32)] * 2,
        in_specs=[SCALARS] + spec(8),
        out_specs=spec(2),
        scratch_shapes=[pltpu.VMEM((size, 2 * width + LINE), bf16)],
        compiler_params=params(12),
        name="edge_back",
        cost_estimate=cost(2.5),
    )(info, mask, counts, *queries, *pairs, from_twin, from_other)


def finish_kernel(
    plan,
    total,
    info,
    inverse,
    standard,
    spread,
    weight,
    vectors,
    grad_resid,
    sums,
    sum_in,
    queries_a,
    queries_b,
    pairs_a,
    pairs_b,
    edge_low,
    edge_high,
    grad_tokens,
    own,
    low_half,
    high_half,
    work,
    joined,
    flat,
    table,
):
    rows, width = standard.shape
    device = info[0]
    half_width = width // 2
    places = device * rows + lax.broadcasted_iota(jnp.int32, (rows, 128), 0)
    live = live_counts(info, places, 0, total)
    hat = standard[...]
    gain = vectors[pl.ds(0, 1), :]
    normed = (hat * gain + vectors[pl.ds(1, 1), :]).astype(bf16)
    half, block = own.shape[0], width // BLOCKS
    other = (low_half, high_half)
    grad_normed = jnp.zeros((rows, width), f32)
    for part in range(3):
        for step in range(width // 128):
            chunk = part * (width // 128) + step
            quad, lane = divmod(step * 128, half_width)
            if part == 0:
                work[chunk] = (queries_a, queries_b)[quad][:, pl.ds(lane, 128)]
            else:
                lanes = pl.ds((part - 1) * half_width + lane, 128)
                for level in range(LEVELS):
                    at, count = plan.query_at[level], plan.counts[level]
                    own_rows = pl.ds(plan.key_at[level] + HALO, count)
                    work[chunk, pl.ds(at, count), :] = (pairs_a, pairs_b)[quad][own_rows, lanes]
                    halo = pl.ds(HALO * (quad * LEVELS + level), HALO)
                    work[chunk, pl.ds(at, HALO), :] += edge_low[halo, lanes]
                    work[chunk, pl.ds(at + count - HALO, HALO), :] += edge_high[halo, lanes]
            for level in range(LEVELS - 1, 0, -1):
                count = plan.counts[level]
                upper = work[chunk, pl.ds(plan.query_at[level], count), :]
                if chunk * 128 < 2 * width:
                    upper = upper * 0.5
                for parity in range(2):
                    there = pl.ds(plan.query_at[level - 1] + parity, count, stride=2)
                    work[chunk, there, :] = work[chunk, there, :] + upper
            value = work[chunk, pl.ds(0, rows), :]
            if chunk * 128 >= 2 * width:
                value = value * live
            joined[:, pl.ds(chunk * 128, 128)] = value.astype(bf16)
        columns = pl.ds(part * width, width)
        flat[part] = dot_tn(normed, joined[:, columns]).astype(bf16)
        for p in range(2 * half):
            i = inverse[p]
            lines = flat[part, pl.ds(pl.multiple_of(i * block, block), block), :]
            there = pl.ds(part * block, block)
            if p < half:
                own[p, there, :] = lines
            else:
                other[(p - half) // 8][(p - half) % 8, there, :] = lines
        grad_normed = grad_normed + dot_nt(joined[:, columns], weight[:, columns])
    grad_in, gain_terms = ln_back(grad_normed, hat, spread[:, :1], gain)
    grad_tokens[...] = grad_resid[...] + grad_in
    singles = [column_sum(gain_terms), column_sum(grad_normed)]
    singles += [sums[pl.ds(k, 1), :] for k in range(2, 6)]
    table[...] = pack_vectors(singles, sum_in[...], 2 * half, table.shape[1])
    row = lax.broadcasted_iota(jnp.int32, (LINE_ROWS, 2 * LINE), 0)
    there = pl.ds(3 * block, LINE_ROWS)
    for p in range(2 * half):
        i = inverse[p]
        line = table[pl.ds(i, 1), :]
        lines = jnp.where(row == 0, line, 0.0)
        lines = jnp.concatenate([lines, jnp.zeros((LINE_ROWS, width - 2 * LINE), f32)], axis=1)
        if p < half:
            own[p, there, :] = lines.astype(bf16)
        else:
            other[(p - half) // 8][(p - half) % 8, there, :] = lines.astype(bf16)


def finish(plan, total, info, inverse, standard, spread, weight, *rest):
    rows, width = standard.shape
    half = BLOCKS // 2
    block = width // BLOCKS
    return pl.pallas_call(
        functools.partial(finish_kernel, plan, total),
        out_shape=(
            jax.ShapeDtypeStruct((rows, width), f32),
            jax.ShapeDtypeStruct((half, 3 * block + LINE_ROWS, width), bf16),
            jax.ShapeDtypeStruct((half // 2, 3 * block + LINE_ROWS, width), bf16),
            jax.ShapeDtypeStruct((half // 2, 3 * block + LINE_ROWS, width), bf16),
        ),
        in_specs=[SCALARS, SCALARS] + spec(3 + len(rest)),
        out_specs=tuple(spec(4)),
        scratch_shapes=[
            pltpu.VMEM((3 * width // 128, plan.query_rows, 128), f32),
            pltpu.VMEM((rows, 3 * width), bf16),
            pltpu.VMEM((3, width, width), bf16),
            pltpu.VMEM((BLOCKS, 2 * LINE), f32),
        ],
        compiler_params=params(28),
        name="finish",
        cost_estimate=cost(6.2),
    )(info, inverse, standard, spread, weight, *rest)


class Ring:
    def __init__(self, devices, *orders):
        self.devices = devices
        self.orders = orders
        self.stages = len(orders[0])

    def partner(self, stage):
        return [(i, i ^ self.orders[i & 1][stage]) for i in range(self.devices)]

    def twin(self):
        return [(i, i ^ 1) for i in range(self.devices)]

    def places(self, device):
        found = []
        even = (device & 1) == 0
        for base, swap in ((device, False), (device ^ 1, True)):
            for position in range(1 << self.stages):
                masks = [
                    sum(order[k] for k in range(self.stages) if position >> k & 1)
                    for order in self.orders
                ]
                if swap:
                    masks = masks[::-1]
                found.append(base ^ jnp.where(even, *masks))
        return found

    def step(self, stage, arrays):
        route = self.twin() if stage == self.stages else self.partner(stage)
        return [lax.ppermute(item, "seq", route) for item in arrays]

    def fold(self, stage, own, low, high):
        half = 1 << stage
        sent = (own[half:].astype(f32) + high.astype(f32)).astype(bf16)
        kept = own[:half].astype(f32) + low.astype(f32)
        return kept, sent


def halves(item):
    half = item.shape[0] // 2
    return item[:half], item[half:]


def join(held, came):
    return [jnp.concatenate(pair) for pair in zip(held, came)]


def pack_kernel(rings, plan, total, lengths, tokens, w_qkv, w_out, w_in, w_back, *refs):
    vectors, refs = refs[:-8], refs[-8:]
    info, *inverses, payload, to_twin, to_other, staged, ends = refs
    device = lax.axis_index("seq")
    info[0] = device
    start = jnp.int32(0)
    for k in range(3):
        length = lengths[k]
        info[1 + k] = length
        info[4 + k] = start
        start = start + (length + 15) // 16 * 16
        info[7 + k] = start
    for ring, inverse in zip(rings, inverses):
        for place, block in enumerate(ring.places(device)):
            inverse[place] = block
    block, width = w_out.shape
    chunks = w_in.shape[1] // width
    staged[...] = jnp.zeros(staged.shape, f32)
    for k, vector in enumerate(vectors):
        size = vector.shape[0]
        lane = k * block
        staged[pl.ds(0, 1), pl.ds(lane, size)] = vector[...].astype(f32).reshape(1, size)
    payload[0, pl.ds(0, block), :] = w_out[...]
    for c in range(chunks):
        payload[0, pl.ds(block * (c + 1), block), :] = w_in[:, pl.ds(c * width, width)]
    at = block * (chunks + 1)
    payload[0, pl.ds(at, block * chunks), :] = w_back[...]
    at = at + block * chunks
    for c in range(3):
        payload[0, pl.ds(at + block * c, block), :] = w_qkv[:, pl.ds(c * width, width)]
    payload[0, pl.ds(at + block * 3, LINE_ROWS), :] = staged[...].astype(bf16)
    edge_sums_kernel(plan, total, info, tokens, to_twin, to_other, ends)


def pack(rings, plan, total, lengths, tokens, w_qkv, w_out, w_in, w_back, vectors):
    size = LEVELS * HALO
    block, width = w_out.shape
    rows = 4 * block + w_in.shape[1] // width * block + w_back.shape[0] + LINE_ROWS
    return pl.pallas_call(
        functools.partial(pack_kernel, rings, plan, total),
        out_shape=(
            jax.ShapeDtypeStruct((10,), jnp.int32),
            jax.ShapeDtypeStruct((BLOCKS,), jnp.int32),
            jax.ShapeDtypeStruct((BLOCKS,), jnp.int32),
            jax.ShapeDtypeStruct((1, rows, width), bf16),
            jax.ShapeDtypeStruct((size + MIXED, width), bf16),
            jax.ShapeDtypeStruct((size + MIXED, width), bf16),
        ),
        in_specs=[SCALARS] + spec(5 + len(vectors)),
        out_specs=(SCALARS,) * 3 + tuple(spec(3)),
        scratch_shapes=[pltpu.VMEM((LINE_ROWS, width), f32), pltpu.VMEM((2 * size, width), bf16)],
        compiler_params=params(62),
        name="pack",
        cost_estimate=cost(1.5),
    )(lengths, tokens, w_qkv, w_out, w_in, w_back, *vectors)


def unpack_kernel(kept_one, came_one, kept_two, came_two, *outs):
    block, width = (kept_one.shape[1] - LINE_ROWS) // 3, kept_two.shape[2]
    w_qkv, w_out, w_in, w_back = outs[:4]
    for c in range(3):
        rows = pl.ds(block * c, block)
        w_qkv[:, pl.ds(c * width, width)] = kept_one[0, rows, :] + came_one[0, rows, :].astype(f32)
    rows = pl.ds(block * 3, LINE_ROWS)
    lines = kept_one[0, rows, :] + came_one[0, rows, :].astype(f32)
    for k, out in enumerate(outs[4:]):
        size = out.shape[0]
        lane = k * block
        out[...] = lines[0:1, lane : lane + size].reshape(size)
    chunks = w_in.shape[1] // width

    def total(at, size):
        rows = pl.ds(at, size)
        return kept_two[0, rows, :] + came_two[0, rows, :].astype(f32)

    w_out[...] = total(2 * block * chunks, block)
    for c in range(chunks):
        w_in[:, pl.ds(c * width, width)] = total(block * c, block)
    w_back[...] = total(block * chunks, block * chunks)


def unpack(kept_one, came_one, kept_two, came_two, like):
    return pl.pallas_call(
        unpack_kernel,
        out_shape=[jax.ShapeDtypeStruct(item.shape, f32) for item in like],
        in_specs=spec(4),
        out_specs=spec(len(like)),
        compiler_params=params(8),
        name="unpack",
        cost_estimate=cost(1.5),
    )(kept_one, came_one, kept_two, came_two)


def exchange(to_twin, to_other):
    count = lax.axis_size("seq")
    twin = [(i, i ^ 1) for i in range(count)]
    other = [(i, i + 1) for i in range(1, count - 1, 2)]
    other += [(j, i) for i, j in other]
    return lax.ppermute(to_other, "seq", other), lax.ppermute(to_twin, "seq", twin)


def order(items, *after):
    return lax.optimization_barrier((items, after))[0]


def per_device(
    lengths,
    tokens,
    ln1_gain,
    ln1_bias,
    w_qkv,
    w_out,
    out_bias,
    ln2_gain,
    ln2_bias,
    w_in,
    in_bias,
    w_back,
    back_bias,
    cotangent,
):
    devices = lax.axis_size("seq")
    device = lax.axis_index("seq")
    rows, width = tokens.shape
    total = rows * devices
    plan = Plan(rows)
    block = width // BLOCKS
    chunks = w_in.shape[1] // width
    small = (ln1_gain, ln1_bias, out_bias, ln2_gain, ln2_bias, back_bias, in_bias)
    direct = devices == BLOCKS
    ring = Ring(BLOCKS, (16, 2, 8, 4), (4, 16, 2, 8))
    sums_ring = Ring(BLOCKS, (16, 8, 4, 2), (2, 16, 8, 4))
    last = ring.stages - 1
    core = ring.stages
    if direct:
        info, inverse, sums_inverse, payload, to_twin, to_other = pack(
            (ring, sums_ring), plan, total, lengths, tokens, w_qkv, w_out, w_in, w_back, small
        )
        from_other, from_twin = exchange(to_twin, to_other)
        ready = prepare(plan, total, info, order(tokens, payload))
        (payload,) = join([payload], ring.step(0, [payload]))
        payload = order(payload, from_other, from_twin)
        rest = block * (2 * chunks + 1)
        a, b = payload[:, rest:], payload[:, :rest]
        a_came, b_came = ring.step(1, [a, b])
        (a,) = join([a], [a_came])
        (a_came,) = ring.step(2, [a])
        (a,) = join([a], [a_came])
        (b,) = join([b], [b_came])
        a = order(a, b, ready)
        (b_came,) = ring.step(2, [b])
        (a_came,) = ring.step(3, [a])
        one = [a, a_came] + ring.step(core, [a, a_came])
        (b,) = join([b], [b_came])
        b = order(b, a_came)
    else:
        padded = (lengths + 15) // 16 * 16
        ends = jnp.cumsum(padded, dtype=jnp.int32)
        info = jnp.concatenate([device[None].astype(jnp.int32), lengths, ends - padded, ends])
        inverse = sums_inverse = jnp.arange(BLOCKS, dtype=jnp.int32)
        from_other, from_twin = exchange(*edge_sums(plan, total, info, tokens))
        ready = prepare(plan, total, info, tokens)

        def whole(item):
            return lax.all_gather(item, "seq", axis=0, tiled=True)

        def split(item, parts):
            each = BLOCKS // parts
            return [item[k * each : (k + 1) * each] for k in range(parts)]

        line = jnp.concatenate([whole(item).reshape(BLOCKS, 1, -1) for item in small], axis=2)
        line = jnp.pad(line, ((0, 0), (0, LINE_ROWS - 1), (0, width - line.shape[2])))
        one = whole(w_qkv).reshape(BLOCKS, block, 3, width).transpose(0, 2, 1, 3)
        one = one.reshape(BLOCKS, 3 * block, width)
        one = split(jnp.concatenate([one, line], axis=1), PIECES)
        full_in = whole(w_in).reshape(BLOCKS, block, chunks, width)
        full_in = full_in.transpose(0, 2, 1, 3).reshape(BLOCKS, chunks * block, width)
        full_two = [
            whole(w_out).reshape(BLOCKS, block, width),
            full_in,
            whole(w_back).reshape(BLOCKS, chunks * block, width),
        ]
        two = split(jnp.concatenate(full_two, axis=1), PIECES)
    standard, spread, pool, allowed, allowed_back, counts, edge_allowed, edge_counts = ready
    queries, pairs, halo_queries, halo_pairs, weight, vectors, shift_in = project(
        plan, total, info, inverse, standard, pool, from_twin, from_other, one
    )
    if direct:
        (b_came,) = ring.step(last, [b])
        (b_twin,) = ring.step(core, [b])
        allowed = order(allowed, b)
    attended, mixed, scale = attend(
        plan, total, info, allowed, counts, queries, pairs, halo_pairs
    )
    if direct:
        b_came = order(b_came, attended)
        two = [b, b_came, b_twin] + ring.step(core, [b_came])
    result, resid, grad_normed, out_weight, own_two, low_two, high_two, sum_in = feed_forward(
        (inverse, sums_inverse), tokens, cotangent, attended, vectors, shift_in, two
    )
    if direct:
        high, low = sums_ring.step(core, [high_two, low_two])
    (
        grad_resid,
        grads_a,
        grads_b,
        to_twin,
        to_other,
        sums,
        own_out,
        low_out,
        high_out,
    ) = middle(
        plan,
        info,
        sums_inverse,
        cotangent,
        attended,
        mixed,
        scale,
        vectors,
        resid,
        grad_normed,
        out_weight,
    )
    from_other, from_twin = exchange(to_twin, to_other)

    def with_out(item, out):
        return jnp.concatenate([item, out], axis=1)

    if direct:
        high_out, low_out = sums_ring.step(core, [high_out, low_out])
        kept, sent = sums_ring.fold(
            last, with_out(own_two, own_out), with_out(low, low_out), with_out(high, high_out)
        )
        sent_low, sent_high = halves(sent)
        sent_low, sent_high = order((sent_low, sent_high), from_twin)
        high, low = sums_ring.step(last, [sent_high, sent_low])
        grads_a = order(grads_a, sent_high, sent_low)
    grad_queries, grad_pairs = attend_back(
        plan, total, allowed_back, counts, queries, pairs, halo_pairs, (grads_a, grads_b)
    )
    from_other, from_twin = order((from_other, from_twin), grad_queries)
    if direct:
        high = order(high, grad_queries, from_other, from_twin)
        kept, kept_high = halves(kept)
        sent = (kept_high + high.astype(f32)).astype(bf16)
        (came,) = sums_ring.step(last - 1, [sent])
        from_other, from_twin = order((from_other, from_twin), sent)
    edges = edge_back(
        plan, info, edge_allowed, edge_counts, halo_queries, pairs, from_twin, from_other
    )
    grad_tokens, own_one, low_one, high_one = finish(
        plan,
        total,
        info,
        sums_inverse,
        standard,
        spread,
        weight,
        vectors,
        grad_resid,
        sums,
        sum_in,
        *grad_queries,
        *grad_pairs,
        *edges,
    )
    if direct:
        high_one, low_one = sums_ring.step(core, [high_one, low_one])
        low, came = order((low, came), grad_tokens)
        kept = kept + low.astype(f32)
        kept, sent = sums_ring.fold(last - 2, kept, *halves(came))
        (came,) = sums_ring.step(last - 2, [sent])
        high_one, low_one = order((high_one, low_one), sent)
        own_one, sent_one = sums_ring.fold(last, own_one, low_one, high_one)
        (came_one,) = sums_ring.step(last, [sent_one])
        own_one, sent_one = sums_ring.fold(last - 1, own_one, *halves(came_one))
        (came_one,) = sums_ring.step(last - 1, [sent_one])
        came = order(came, sent_one)
        kept, sent = sums_ring.fold(0, kept, *halves(came))
        (came,) = sums_ring.step(0, [sent])
        came_one = order(came_one, sent)
        own_one, sent_one = sums_ring.fold(last - 2, own_one, *halves(came_one))
        (came_one,) = sums_ring.step(last - 2, [sent_one])
        own_one, sent_one = sums_ring.fold(0, own_one, *halves(came_one))
        (came_one,) = sums_ring.step(0, [sent_one])
        grads = unpack(own_one, came_one, kept, came, (w_qkv, w_out, w_in, w_back) + small)
        grad_w_qkv, grad_w_out, grad_w_in, grad_w_back = grads[:4]
        parts = grads[4:]
    else:

        def shared(item):
            return lax.psum_scatter(item, "seq", scatter_dimension=0, tiled=True)

        full = jnp.concatenate([x.astype(f32) for x in (own_one, low_one, high_one)])
        line = full[:, 3 * block]
        sizes = [block] * 6 + [chunks * block]
        starts = [k * block for k in range(7)]
        parts = [
            shared(line[:, at : at + size].reshape(-1)) for at, size in zip(starts, sizes)
        ]
        grad_w_qkv = full[:, : 3 * block].reshape(BLOCKS, 3, block, width).transpose(0, 2, 1, 3)
        grad_w_qkv = shared(grad_w_qkv.reshape(width, 3 * width))
        full = jnp.concatenate([x.astype(f32) for x in (own_out, low_out, high_out)])
        grad_w_out = shared(full.reshape(width, width))
        full = jnp.concatenate([x.astype(f32) for x in (own_two, low_two, high_two)])
        full_in = full[:, : block * chunks]
        full_in = full_in.reshape(BLOCKS, chunks, block, width).transpose(0, 2, 1, 3)
        grad_w_in = shared(full_in.reshape(width, chunks * width))
        grad_w_back = shared(full[:, block * chunks :].reshape(chunks * width, width))
    gain_one, bias_one, shift_out, gain_two, bias_two, shift_back, shift_hidden = parts
    return (
        result,
        grad_tokens,
        gain_one,
        bias_one,
        grad_w_qkv,
        grad_w_out,
        shift_out,
        gain_two,
        bias_two,
        grad_w_in,
        shift_hidden,
        grad_w_back,
        shift_back,
    )


def solution(mesh):
    flat, wide = P("seq"), P("seq", None)
    weights = (flat, flat, wide, wide, flat, flat, flat, wide, flat, wide, flat)
    return jax.shard_map(
        per_device,
        mesh=mesh,
        in_specs=(P(), wide) + weights + (wide,),
        out_specs=(wide, wide) + weights,
        check_vma=False,
    )
```
